32 devices in a mesh: dp: 8 (over z, y), mp: 4 (over x, core).
Axes of the slice: x: 2, y: 2, z: 4, core: 2. Of those that a mesh axis runs over, the one named last changes fastest.
Arguments:
- encoder_input: bfloat16 [16384, 768], P(('dp', 'mp')), may hold values from -6 to 6
- corrupted: bfloat16 [16384, 768], P(('dp', 'mp')), may hold values from -6 to 6
- lengths: int32 [128], P(('dp', 'mp')), may hold values from 65 to 512, as said below
- buckets: int32 [32], P(('dp', 'mp')), may hold values from 0 to 2, as said below
- qkv_weight: bfloat16 [2, 768, 2304], P(None, ('dp', 'mp')), may hold values from -0.21875 to 0.21875
- out_weight: bfloat16 [2, 768, 768], P(None, ('dp', 'mp')), may hold values from -0.875 to 0.875
- up_weight: bfloat16 [2, 768, 3072], P(None, ('dp', 'mp')), may hold values from -0.21875 to 0.21875
- down_weight: bfloat16 [2, 3072, 768], P(None, ('dp', 'mp')), may hold values from -0.109375 to 0.109375
- norm_gains: bfloat16 [2, 2, 768], P(None, None, ('dp', 'mp')), may hold values from 0.5 to 1.5
- bias_rows: bfloat16 [2, 6, 768], P(None, None, ('dp', 'mp')), may hold values from -3 to 3
- up_bias: bfloat16 [2, 3072], P(None, ('dp', 'mp')), may hold values from -3 to 3
- encoder_cot: bfloat16 [16384, 768], P(('dp', 'mp')), may hold values from -6 to 6
- decoder_cot: bfloat16 [16384, 768], P(('dp', 'mp')), may hold values from -6 to 6
Outputs:
- encoder_output: bfloat16 [16384, 768], P(('dp', 'mp'))
- decoder_output: bfloat16 [16384, 768], P(('dp', 'mp'))
- encoder_grad: bfloat16 [16384, 768], P(('dp', 'mp'))
- corrupted_grad: bfloat16 [16384, 768], P(('dp', 'mp'))
- qkv_grad: float32 [2, 768, 2304], P(None, ('dp', 'mp'))
- out_grad: float32 [2, 768, 768], P(None, ('dp', 'mp'))
- up_grad: float32 [2, 768, 3072], P(None, ('dp', 'mp'))
- down_grad: float32 [2, 3072, 768], P(None, ('dp', 'mp'))
- gains_grad: float32 [2, 2, 768], P(None, None, ('dp', 'mp'))
- biases_grad: float32 [2, 6, 768], P(None, None, ('dp', 'mp'))
- up_bias_grad: float32 [2, 3072], P(None, ('dp', 'mp'))
The draws below stay inside these ranges and needn't reach their ends.
Inputs may be any that keep to these rules, and one draw needn't show every extreme that they name: `buckets`: 0, 1 or 2; a group's passages all span 2**id slots of 128 tokens. `lengths`: equal over the slots of one passage; more than half of the passage's 2**id * 128 slots, at most all of them.
All inputs are finite; a program needn't handle non-finite values.
Results may differ from the reference program's by a relative error of at most 0.014.
Values may be sent and summed in bfloat16 or wider, within the bound.
No kernel may reach another device: no remote copies, remote signals or barrier semaphores. Data moves between devices by JAX's collectives and lax.ppermute only.
A program may use at most 256 MiB of HBM per device.

```python
import jax
import jax.numpy as jnp
from jax import lax

D = 768
H = 12
HD = 64
FF = 3072
SLOT = 128
GROUP = 512
TOKENS = 16384
GROUPS = 32


def passage_layout(key):
    slot_count = GROUP // SLOT
    drawn_bucket = jax.random.randint(jax.random.fold_in(key, 101), (GROUPS,), 0, 3)
    bucket_ids = drawn_bucket.at[0].set(2)
    span = jnp.left_shift(jnp.int32(1), bucket_ids)
    slot_ids = jnp.arange(slot_count, dtype=jnp.int32)
    seg_start = slot_ids[None, :] // span[:, None] * span[:, None]
    capacity = span[:, None] * SLOT
    drawn = jax.random.randint(jax.random.fold_in(key, 102), (GROUPS, slot_count), 0, 1 << 20)
    picked = jnp.take_along_axis(drawn, seg_start, axis=1)
    half_cap = capacity // 2
    slot_lengths = half_cap + 1 + picked % half_cap
    slot_lengths = slot_lengths.at[0, :].set(4 * SLOT)
    return (bucket_ids.astype(jnp.int32), slot_lengths.reshape(-1).astype(jnp.int32))


def draw_buckets(key, part):
    bucket_ids, slot_lengths = passage_layout(key)
    return bucket_ids


def draw_lengths(key, part):
    bucket_ids, slot_lengths = passage_layout(key)
    return slot_lengths


def block_scale(rng, shape, pieces, low, top_value):
    def one(axis_at, blocks):
        heights = jax.random.uniform(jax.random.fold_in(jax.random.fold_in(rng, 6), axis_at), (blocks,), jnp.float32, low / len(pieces), top_value / len(pieces))
        return jnp.repeat(jnp.exp(heights), shape[axis_at] // blocks).reshape((-1,) + (1,) * (len(shape) - axis_at - 1))

    level = one(*pieces[0])
    for cut in pieces[1:]:
        level = level * one(*cut)
    return level


def gaussian(rng, dims, scale, most, split=(), held_as=jnp.bfloat16):
    values = scale * jax.random.normal(rng, dims, jnp.float32)
    if split:
        values = values * block_scale(rng, dims, split, -0.22, 0.18)
    return jnp.clip(values, -most, most).astype(held_as)


def setup_inputs(seed: int = 0) -> dict:
    arg_keys = jax.random.split(jax.random.key(seed), 14)
    encoder_input = gaussian(arg_keys[0], (TOKENS, D), 1.0, 6.0, ((0, 32),))
    corrupted = gaussian(arg_keys[1], (TOKENS, D), 1.0, 6.0, ((0, 32),))
    lengths = draw_lengths(jax.random.fold_in(arg_keys[13], 71), 0)
    buckets = draw_buckets(jax.random.fold_in(arg_keys[13], 71), 0)
    qkv_weight = gaussian(arg_keys[4], (2, D, 3 * D), D ** -0.5, 0.21875, ((1, 32),))
    out_weight = gaussian(arg_keys[5], (2, D, D), (D // 16) ** -0.5, 0.875, ((1, 32),))
    up_weight = gaussian(arg_keys[6], (2, D, FF), D ** -0.5, 0.21875, ((1, 32),))
    down_weight = gaussian(arg_keys[7], (2, FF, D), FF ** -0.5, 0.109375, ((1, 32),))
    norm_gains = jnp.clip(1.0 + 0.1 * jax.random.normal(arg_keys[8], (2, 2, D), jnp.float32), 0.5, 1.5).astype(jnp.bfloat16)
    bias_rows = gaussian(arg_keys[9], (2, 6, D), 0.3, 3.0, ((2, 32),))
    up_bias = gaussian(arg_keys[10], (2, FF), 0.3, 3.0, ((1, 32),))
    encoder_cot = gaussian(arg_keys[11], (TOKENS, D), 1.0, 6.0, ((0, 32),))
    decoder_cot = gaussian(arg_keys[12], (TOKENS, D), 1.0, 6.0, ((0, 32),))
    return {"encoder_input": encoder_input, "corrupted": corrupted, "lengths": lengths, "buckets": buckets, "qkv_weight": qkv_weight, "out_weight": out_weight, "up_weight": up_weight, "down_weight": down_weight, "norm_gains": norm_gains, "bias_rows": bias_rows, "up_bias": up_bias, "encoder_cot": encoder_cot, "decoder_cot": decoder_cot}


EPSILON = 1e-06
NEGATIVE = -1e+30
HIGH = lax.Precision.HIGHEST

@jax.custom_vjp
def low(v):
    return lax.optimization_barrier(v.astype(jnp.bfloat16)).astype(jnp.float32)

@jax.custom_vjp
def low_back(v):
    return v

def low_keep(v):
    return (low(v), None)

def low_pass(kept, grad):
    return (grad,)

def back_keep(v):
    return (v, None)

def back_low(kept, grad):
    return (low(grad),)
low.defvjp(low_keep, low_pass)
low_back.defvjp(back_keep, back_low)

def layout_mask(slot_lengths, bucket_id):
    token = jnp.arange(GROUP, dtype=jnp.int32)
    slot_of = token // SLOT
    span = jnp.left_shift(jnp.int32(1), bucket_id)
    passage = slot_of // span
    position = token - passage * span * SLOT
    valid = position < slot_lengths[slot_of]
    allowed = (passage[:, None] == passage[None, :]) & valid[None, :]
    return (allowed, position == 0)

def normalize(resid, gain, shift):
    center = lax.optimization_barrier(jnp.mean(resid, axis=-1, keepdims=True))
    shifted = resid - center
    spread = lax.optimization_barrier(jnp.mean(shifted * shifted, axis=-1, keepdims=True))
    return shifted * lax.rsqrt(spread + EPSILON) * gain + shift

def block(block_in, allowed, params):
    qkv_w, out_w, up_w, down_w, gains, biases, up_b = params
    row_count = block_in.shape[0]
    low_in = low(block_in)
    bias_row = jnp.concatenate([biases[0], jnp.zeros((D,), jnp.float32), biases[1]])
    packed = jnp.dot(low_in, qkv_w, precision=HIGH) + bias_row
    packed = low(low_back(packed))
    split_heads = packed.reshape(row_count, 3, H, HD)
    scores = jnp.einsum('qhd,khd->hqk', split_heads[:, 0], split_heads[:, 1], precision=HIGH) * HD ** (-0.5)
    scores = low_back(scores)
    masked = jnp.where(allowed[None], scores, NEGATIVE)
    peak_score = lax.optimization_barrier(jnp.max(masked, axis=-1, keepdims=True))
    exp_scores = jnp.exp(masked - peak_score)
    soft_weights = exp_scores / lax.optimization_barrier(jnp.sum(exp_scores, axis=-1, keepdims=True))
    mixed_heads = jnp.einsum('hqk,khd->qhd', low(soft_weights), split_heads[:, 2], precision=HIGH)
    mixed_heads = low(low_back(mixed_heads.reshape(row_count, D)))
    attended = low_back(jnp.dot(mixed_heads, out_w, precision=HIGH)) + biases[2]
    normed_one = normalize(block_in + attended, gains[0], biases[3])
    hidden = low_back(jnp.dot(low(normed_one), up_w, precision=HIGH) + up_b)
    active = low(jax.nn.gelu(hidden, approximate=False))
    branch = low_back(jnp.dot(active, down_w, precision=HIGH)) + biases[4]
    return normalize(normed_one + branch, gains[1], biases[5])

def reference(encoder_input, corrupted, lengths, buckets, qkv_weight, out_weight, up_weight, down_weight, norm_gains, bias_rows, up_bias, encoder_cot, decoder_cot):
    slot_lengths = lengths.reshape(GROUPS, GROUP // SLOT)
    floats = tuple((item.astype(jnp.float32) for item in (qkv_weight, out_weight, up_weight, down_weight, norm_gains, bias_rows, up_bias)))
    enc_rows = encoder_input.astype(jnp.float32).reshape(GROUPS, GROUP, D)
    cor_rows = corrupted.astype(jnp.float32).reshape(GROUPS, GROUP, D)

    def forward(enc_x, cor_x, params):
        first_layer = tuple((item[0] for item in params))
        second_layer = tuple((item[1] for item in params))

        def one_group(entry):
            block_in, cor_in, lens_group, bucket_id = entry
            allowed, starts = layout_mask(lens_group, bucket_id)
            encoded = block(block_in, allowed, first_layer)
            decoded = block(jnp.where(starts[:, None], encoded, cor_in), allowed, second_layer)
            return (encoded, decoded)
        return lax.map(jax.checkpoint(one_group), (enc_x, cor_x, slot_lengths, buckets))
    outputs, pullback = jax.vjp(forward, enc_rows, cor_rows, floats)
    cot = (encoder_cot.astype(jnp.float32).reshape(GROUPS, GROUP, D), decoder_cot.astype(jnp.float32).reshape(GROUPS, GROUP, D))
    enc_grad, cor_grad, weight_grads = pullback(cot)
    return (outputs[0].reshape(TOKENS, D).astype(jnp.bfloat16), outputs[1].reshape(TOKENS, D).astype(jnp.bfloat16), enc_grad.reshape(TOKENS, D).astype(jnp.bfloat16), cor_grad.reshape(TOKENS, D).astype(jnp.bfloat16), weight_grads[0], weight_grads[1], weight_grads[2], weight_grads[3], weight_grads[4], weight_grads[5], weight_grads[6])
```

```python
import functools

import jax
import jax.numpy as jnp
from jax import lax
from jax.experimental import pallas as pl
from jax.experimental.pallas import tpu as pltpu
from jax.sharding import Mesh
from jax.sharding import PartitionSpec as P

HD = 64
SLOT = 128
EPSILON = 1e-06
NEGATIVE = -1e30
F32 = jnp.float32
BF16 = jnp.bfloat16
VMEM_LIMIT = 56 * 1024 * 1024

T = 512
D = 768
HALF = D // 2
ROWS = 48
DROWS = 192
Q_AT, O_AT, SMALL_AT, U_AT, D_AT = 0, 144, 192, 208, 400
PACK = 592

VM = pl.BlockSpec(memory_space=pltpu.VMEM)
SM = pl.BlockSpec(memory_space=pltpu.SMEM)
ANY = pl.BlockSpec(memory_space=pl.ANY)


def dot(left, right):
    return lax.dot_general(left, right, (((1,), (0,)), ((), ())), preferred_element_type=F32)


def dot_rt(left, right):
    return lax.dot_general(left, right, (((1,), (1,)), ((), ())), preferred_element_type=F32)


def call(kernel, outs, in_specs, out_specs, scratch, flops, nbytes, name):
    return pl.pallas_call(
        kernel,
        out_shape=outs,
        in_specs=in_specs,
        out_specs=out_specs,
        scratch_shapes=scratch,
        compiler_params=pltpu.CompilerParams(vmem_limit_bytes=VMEM_LIMIT),
        cost_estimate=pl.CostEstimate(flops=flops, bytes_accessed=nbytes, transcendentals=0),
        name=name,
    )


def sds(shape, dtype):
    return jax.ShapeDtypeStruct(shape, dtype)


def panel_copies(w, dst, sems, row_at, rows):
    copies = []
    for y in range(2):
        for x in range(2):
            for h in range(2):
                copies.append(
                    pltpu.make_async_copy(
                        w.at[:, y, x, h, row_at : row_at + rows, :],
                        dst.at[:, 2 * y + x, :, h * HALF : (h + 1) * HALF],
                        sems.at[len(copies)],
                    )
                )
    return copies


def start(copies):
    for copy in copies:
        copy.start()


def wait(copies):
    for copy in copies:
        copy.wait()


def starts_column(bucket):
    span = lax.shift_left(jnp.int32(SLOT), bucket)
    token = lax.broadcasted_iota(jnp.int32, (T, 1), 0)
    return jnp.bitwise_and(token, span - 1) == 0


def fill_bias(bias, lens, buck):
    bucket = buck[0]
    key = lax.broadcasted_iota(jnp.int32, (T, T), 0)
    query = lax.broadcasted_iota(jnp.int32, (T, T), 1)
    shift = bucket + 7
    same = lax.shift_right_logical(key, shift) == lax.shift_right_logical(query, shift)
    position = jnp.bitwise_and(key, lax.shift_left(jnp.int32(SLOT), bucket) - 1)
    slot = lax.shift_right_logical(key, 7)
    length = jnp.where(
        slot < 2,
        jnp.where(slot == 0, lens[0], lens[1]),
        jnp.where(slot == 2, lens[2], lens[3]),
    )
    bias[...] = jnp.where(same & (position < length), 0.0, NEGATIVE)


def halves(block):
    lane = lax.broadcasted_iota(jnp.int32, block.shape, 1)
    zero = jnp.zeros_like(block)
    return jnp.where(lane < HD, block, zero), jnp.where(lane < HD, zero, block)


def attend_kernel(x, vec, w, lens, buck, p, m, stat, wq, bias, sems):
    copies = [panel_copies(w, wq.at[j], sems.at[j], Q_AT + j * ROWS, ROWS) for j in range(3)]
    for group in copies:
        start(group)
    fill_bias(bias, lens, buck)
    for j in range(3):
        wait(copies[j])
        weight = wq[j].reshape(D, D)
        if j == 1:
            row = jnp.zeros((1, D), F32)
        else:
            row = vec[2 : 3, :] if j == 0 else vec[3 : 4, :]
        for half in range(2):
            rows = slice(half * 256, half * 256 + 256)
            out = (dot(x[rows, :], weight) + row).astype(BF16)
            for s in range(6):
                p[6 * j + s, rows, :] = out[:, 128 * s : 128 * s + 128]

    def pair(i, carry):
        q = p[i] * jnp.asarray(HD**-0.5, BF16)
        v_t = p[12 + i].T
        keys = halves(p[6 + i])
        parts = []
        for a in range(2):
            scores = dot_rt(keys[a], q) + bias[...]
            peak = jnp.max(scores, axis=0, keepdims=True)
            weights = jnp.exp(scores - peak)
            inverse = 1.0 / jnp.sum(weights, axis=0, keepdims=True)
            stat[2 * i + a, 0:1, :] = peak
            stat[2 * i + a, 1:2, :] = inverse
            soft = (weights * inverse).astype(BF16)
            parts.append(dot(v_t[HD * a : HD * a + HD, :], soft))
        m[i] = jnp.concatenate(parts, axis=0).T.astype(BF16)
        return carry

    lax.fori_loop(0, 6, pair, 0)


def attend(x, vec, w, lens, buck):
    return call(
        attend_kernel,
        [sds((18, T, 128), BF16), sds((6, T, 128), BF16), sds((12, 8, T), F32)],
        [VM, VM, ANY, SM, SM],
        [VM, VM, VM],
        [
            pltpu.VMEM((3, 4, 4, ROWS, D), BF16),
            pltpu.VMEM((T, T), F32),
            pltpu.SemaphoreType.DMA((3, 8)),
        ],
        2 * T * D * 3 * D + 4 * T * T * D * 4,
        12 * 1024 * 1024,
        "attend",
    )(x, vec, w, lens, buck)


def unit_norm(resid):
    center = jnp.mean(resid, axis=-1, keepdims=True)
    shifted = resid - center
    spread = jnp.mean(shifted * shifted, axis=-1, keepdims=True)
    inverse = lax.rsqrt(spread + EPSILON)
    return shifted * inverse, inverse


def row_loop(size, body):
    def step(i, carry):
        body(pl.ds(pl.multiple_of(i * size, size), size))
        return carry

    lax.fori_loop(0, T // size, step, 0)


def feed_kernel(encoder, *refs):
    if encoder:
        (x, m, vec, w, cor, buck, out, xd, xdl, n1, r1, n2, r2, y1l, g, gp) = refs[:16]
        (wo, wu, wd, scr, y1, sems) = refs[16:]
    else:
        (x, m, vec, w, out, n1, r1, n2, r2, y1l, g, gp) = refs[:12]
        (wo, wu, wd, scr, y1, sems) = refs[12:]
    o_copies = panel_copies(w, wo, sems.at[0], O_AT, ROWS)
    u_copies = [panel_copies(w, wu.at[j], sems.at[1 + j], U_AT + j * ROWS, ROWS) for j in range(4)]
    d_copies = panel_copies(w, wd, sems.at[5], D_AT, DROWS)
    start(o_copies)
    for group in u_copies:
        start(group)
    start(d_copies)
    wait(o_copies)
    weight = wo[...].reshape(D, D)
    for half in range(2):
        rows = slice(half * 256, half * 256 + 256)
        left = jnp.concatenate([m[s, rows, :] for s in range(6)], axis=1)
        scr[rows, :] = dot(left, weight)

    def first(rows):
        resid = x[rows, :].astype(F32) + (scr[rows, :] + vec[4:5, :])
        unit, inverse = unit_norm(resid)
        n1[rows, :] = unit
        r1[rows, :] = jnp.broadcast_to(inverse, (inverse.shape[0], 128))
        normed = unit * vec[0:1, :] + vec[5:6, :]
        y1[rows, :] = normed
        y1l[rows, :] = normed.astype(BF16)

    row_loop(64, first)

    for j in range(4):
        wait(u_copies[j])

        def up(rows, j=j):
            left = y1l[rows, :]
            for k in range(3):
                cols = slice(256 * k, 256 * k + 256)
                right = wu[j, :, :, :, cols].reshape(D, 256)
                hidden = dot(left, right) + vec[8 + j : 9 + j, cols]
                cdf = 0.5 * (1.0 + lax.erf(hidden * (0.5**0.5)))
                g[j, rows, cols] = (hidden * cdf).astype(BF16)
                density = jnp.exp(hidden * hidden * -0.5) * 0.3989422804014327
                gp[j, rows, cols] = (cdf + hidden * density).astype(gp.dtype)

        row_loop(128, up)

    wait(d_copies)
    for half in range(2):
        rows = slice(half * 256, half * 256 + 256)
        total = dot(g[0, rows, :], wd[0].reshape(D, D))
        for j in range(1, 4):
            total = total + dot(g[j, rows, :], wd[j].reshape(D, D))
        scr[rows, :] = total

    def second(rows):
        resid = y1[rows, :] + (scr[rows, :] + vec[6:7, :])
        unit, inverse = unit_norm(resid)
        n2[rows, :] = unit
        r2[rows, :] = jnp.broadcast_to(inverse, (inverse.shape[0], 128))
        result = unit * vec[1:2, :] + vec[7:8, :]
        out[rows, :] = result.astype(BF16)
        if encoder:
            span = lax.shift_left(jnp.int32(SLOT), buck[0])
            token = lax.broadcasted_iota(jnp.int32, (64, 1), 0) + rows.start
            mixed = jnp.where(
                jnp.bitwise_and(token, span - 1) == 0, result, cor[rows, :].astype(F32)
            )
            xd[rows, :] = mixed
            xdl[rows, :] = mixed.astype(BF16)

    row_loop(64, second)


def feed(encoder, x, m, vec, w, cor=None, buck=None):
    saved = [
        sds((T, D), F32),
        sds((T, 128), F32),
        sds((T, D), F32),
        sds((T, 128), F32),
        sds((T, D), BF16),
        sds((4, T, D), BF16),
        sds((4, T, D), BF16),
    ]
    if encoder:
        args = (x, m, vec, w, cor, buck)
        in_specs = [VM, VM, VM, ANY, VM, SM]
        outs = [sds((T, D), BF16), sds((T, D), F32), sds((T, D), BF16)] + saved
    else:
        args = (x, m, vec, w)
        in_specs = [VM, VM, VM, ANY]
        outs = [sds((T, D), BF16)] + saved
    return call(
        functools.partial(feed_kernel, encoder),
        outs,
        in_specs,
        [VM] * len(outs),
        [
            pltpu.VMEM((4, 4, ROWS, D), BF16),
            pltpu.VMEM((4, 4, 4, ROWS, D), BF16),
            pltpu.VMEM((4, 4, DROWS, D), BF16),
            pltpu.VMEM((T, D), F32),
            pltpu.VMEM((T, D), F32),
            pltpu.SemaphoreType.DMA((6, 8)),
        ],
        2 * T * D * 9 * D,
        25 * 1024 * 1024,
        "feed",
    )(*args)


def norm_back(grad, unit, inverse, gain):
    scaled = grad * gain
    mean = jnp.mean(scaled, axis=-1, keepdims=True)
    along = jnp.mean(scaled * unit, axis=-1, keepdims=True)
    return inverse * (scaled - mean - unit * along)


def column_sum(value):
    return jnp.sum(value, axis=0, keepdims=True)


def feed_back_kernel(encoder, *refs):
    if encoder:
        (cot, dxd, buck, n1, r1, n2, r2, gp, vec, w) = refs[:10]
        refs = refs[10:]
    else:
        (cot, n1, r1, n2, r2, gp, vec, w) = refs[:8]
        refs = refs[8:]
    (dr2l, dul, dr1, dr1l, dml, small, wo, wu, wd, dr2, scr, sems) = refs
    o_copies = panel_copies(w, wo, sems.at[0], O_AT, ROWS)
    u_copies = [panel_copies(w, wu.at[j], sems.at[1 + j], U_AT + j * ROWS, ROWS) for j in range(4)]
    d_copies = panel_copies(w, wd, sems.at[5], D_AT, DROWS)
    start(d_copies)
    for group in u_copies:
        start(group)
    start(o_copies)
    small[...] = jnp.zeros_like(small)

    def second(rows):
        grad = cot[rows, :].astype(F32)
        if encoder:
            span = lax.shift_left(jnp.int32(SLOT), buck[0])
            token = lax.broadcasted_iota(jnp.int32, (64, 1), 0) + rows.start
            grad = grad + jnp.where(jnp.bitwise_and(token, span - 1) == 0, dxd[rows, :], 0.0)
        unit = n2[rows, :]
        resid = norm_back(grad, unit, r2[rows, 0:1], vec[1:2, :])
        small[1:2, :] += column_sum(grad * unit)
        small[7:8, :] += column_sum(grad)
        small[6:7, :] += column_sum(resid)
        dr2[rows, :] = resid
        dr2l[rows, :] = resid.astype(BF16)

    row_loop(64, second)
    wait(d_copies)
    for j in range(4):

        def up(rows, j=j):
            left = dr2l[rows, :]
            weight = wd[j].reshape(D, D)
            for k in range(3):
                cols = slice(256 * k, 256 * k + 256)
                grad = dot_rt(left, weight[cols, :])
                hidden = (grad * gp[j, rows, cols].astype(F32)).astype(BF16)
                dul[j, rows, cols] = hidden
                small[8 + j : 9 + j, cols] += column_sum(hidden.astype(F32))

        row_loop(256, up)
    for group in u_copies:
        wait(group)
    for half in range(2):
        rows = slice(half * 256, half * 256 + 256)
        total = dot_rt(dul[0, rows, :], wu[0].reshape(D, D))
        for j in range(1, 4):
            total = total + dot_rt(dul[j, rows, :], wu[j].reshape(D, D))
        scr[rows, :] = total

    def first(rows):
        grad = dr2[rows, :] + scr[rows, :]
        unit = n1[rows, :]
        resid = norm_back(grad, unit, r1[rows, 0:1], vec[0:1, :])
        small[0:1, :] += column_sum(grad * unit)
        small[5:6, :] += column_sum(grad)
        small[4:5, :] += column_sum(resid)
        dr1[rows, :] = resid
        dr1l[rows, :] = resid.astype(BF16)

    row_loop(64, first)
    wait(o_copies)
    weight = wo[...].reshape(D, D)
    for half in range(2):
        rows = slice(half * 256, half * 256 + 256)
        out = dot_rt(dr1l[rows, :], weight).astype(BF16)
        for s in range(6):
            dml[s, rows, :] = out[:, 128 * s : 128 * s + 128]


def feed_back(encoder, cot, saved, vec, w, dxd=None, buck=None):
    n1, r1, n2, r2, _, _, gp = saved
    if encoder:
        args = (cot, dxd, buck, n1, r1, n2, r2, gp, vec, w)
        in_specs = [VM, VM, SM] + [VM] * 6 + [ANY]
    else:
        args = (cot, n1, r1, n2, r2, gp, vec, w)
        in_specs = [VM] * 7 + [ANY]
    outs = [
        sds((T, D), BF16),
        sds((4, T, D), BF16),
        sds((T, D), F32),
        sds((T, D), BF16),
        sds((6, T, 128), BF16),
        sds((16, D), F32),
    ]
    return call(
        functools.partial(feed_back_kernel, encoder),
        outs,
        in_specs,
        [VM] * len(outs),
        [
            pltpu.VMEM((4, 4, ROWS, D), BF16),
            pltpu.VMEM((4, 4, 4, ROWS, D), BF16),
            pltpu.VMEM((4, 4, DROWS, D), BF16),
            pltpu.VMEM((T, D), F32),
            pltpu.VMEM((T, D), F32),
            pltpu.SemaphoreType.DMA((6, 8)),
        ],
        2 * T * D * 9 * D,
        28 * 1024 * 1024,
        "feed_back",
    )(*args)


def attend_back_kernel(p, dml, stat, lens, buck, dpl, small, bias):
    fill_bias(bias, lens, buck)
    scale = jnp.asarray(HD**-0.5, BF16)

    def pair(i, carry):
        q = p[i] * scale
        k_t = p[6 + i].T
        keys = halves(p[6 + i])
        values = halves(p[12 + i])
        grad = dml[i]
        grads = halves(grad)
        queries = halves(q)
        dq = []
        dk = jnp.zeros((T, 128), F32)
        dv = jnp.zeros((T, 128), F32)
        for a in range(2):
            scores = dot_rt(keys[a], q) + bias[...]
            peak = stat[2 * i + a, 0:1, :]
            inverse = stat[2 * i + a, 1:2, :]
            soft = jnp.exp(scores - peak) * inverse
            dv = dv + dot(soft.astype(BF16), grads[a])
            dsoft = dot_rt(values[a], grad)
            total = jnp.sum(soft * dsoft, axis=0, keepdims=True)
            dscore = (soft * (dsoft - total)).astype(BF16)
            dk = dk + dot(dscore, queries[a])
            dq.append(dot(k_t[HD * a : HD * a + HD, :], dscore))
        dq = (jnp.concatenate(dq, axis=0).T * (HD**-0.5)).astype(BF16)
        dv = dv.astype(BF16)
        dpl[i] = dq
        dpl[6 + i] = dk.astype(BF16)
        dpl[12 + i] = dv
        small[i, 0:1, :] = column_sum(dq.astype(F32))
        small[i, 1:2, :] = column_sum(dv.astype(F32))
        return carry

    lax.fori_loop(0, 6, pair, 0)


def attend_back(p, dml, stat, lens, buck):
    return call(
        attend_back_kernel,
        [sds((18, T, 128), BF16), sds((6, 8, 128), F32)],
        [VM, VM, VM, SM, SM],
        [VM, VM],
        [pltpu.VMEM((T, T), F32)],
        8 * T * T * D * 3,
        6 * 1024 * 1024,
        "attend_back",
    )(p, dml, stat, lens, buck)


def input_back_kernel(encoder, *refs):
    if encoder:
        (dpl, dr1, w, out, wq, scr, sems) = refs
    else:
        (dpl, dr1, w, buck, dxd, out, wq, scr, sems) = refs
    copies = [panel_copies(w, wq.at[j], sems.at[j], Q_AT + j * ROWS, ROWS) for j in range(3)]
    for group in copies:
        start(group)
    for group in copies:
        wait(group)
    for half in range(2):
        rows = slice(half * 256, half * 256 + 256)
        total = dr1[rows, :]
        for j in range(3):
            left = jnp.concatenate([dpl[6 * j + s, rows, :] for s in range(6)], axis=1)
            total = total + dot_rt(left, wq[j].reshape(D, D))
        if encoder:
            out[rows, :] = total.astype(BF16)
        else:
            dxd[rows, :] = total
            span = lax.shift_left(jnp.int32(SLOT), buck[0])
            token = lax.broadcasted_iota(jnp.int32, (256, 1), 0) + half * 256
            first = jnp.bitwise_and(token, span - 1) == 0
            out[rows, :] = jnp.where(first, 0.0, total).astype(BF16)


def input_back(encoder, dpl, dr1, w, buck=None):
    if encoder:
        args, in_specs = (dpl, dr1, w), [VM, VM, ANY]
        outs = [sds((T, D), BF16)]
    else:
        args, in_specs = (dpl, dr1, w, buck), [VM, VM, ANY, SM]
        outs = [sds((T, D), F32), sds((T, D), BF16)]
    return call(
        functools.partial(input_back_kernel, encoder),
        outs,
        in_specs,
        [VM] * len(outs),
        [
            pltpu.VMEM((3, 4, 4, ROWS, D), BF16),
            pltpu.VMEM((T, D), F32),
            pltpu.SemaphoreType.DMA((3, 8)),
        ],
        2 * T * D * 3 * D,
        10 * 1024 * 1024,
        "input_back",
    )(*args)


def feed_grads(left_u, right_u, left_d, right_d, h, put):
    cols = pl.ds(pl.multiple_of(h * HALF, HALF), HALF)
    left = left_u[...].T
    for j in range(4):
        put(slice(None), slice(j * ROWS, j * ROWS + ROWS), dot(left, right_u[j, :, cols]))
        put(j, slice(4 * ROWS, 4 * ROWS + DROWS), dot(left_d[j].T, right_d[:, cols]))


def attend_grads(left_q, right_q, left_o, right_o, small, h, put):
    left = left_q[...].T
    for j in range(3):
        right = jnp.concatenate([right_q[6 * j + 3 * h + s] for s in range(3)], axis=1)
        put(slice(None), slice(j * ROWS, j * ROWS + ROWS), dot(left, right))
    left = jnp.concatenate([left_o[s] for s in range(6)], axis=1).T
    cols = pl.ds(pl.multiple_of(h * HALF, HALF), HALF)
    put(slice(None), slice(O_AT, O_AT + ROWS), dot(left, right_o[:, cols]))
    put(slice(None), slice(SMALL_AT, SMALL_AT + 16), small[h].astype(F32))


def grads_kernel(fill, count, rows, own, *refs):
    inputs, refs = refs[:count], refs[count:]
    if own:
        (place, other, a_send, a_keep, b_send, b_keep, block, theirs, sems) = refs
        h = place[0]
        fetch = pltpu.make_async_copy(other, theirs, sems.at[4])
        fetch.start()
    else:
        (place, out, block, sems) = refs
        h = 1 - place[0]
    waited = []

    def put(z, at, value):
        if own and not waited:
            fetch.wait()
            waited.append(True)
        if isinstance(z, int):
            value = value.reshape(4, at.stop - at.start, HALF)
        else:
            value = value.reshape(4, 4, at.stop - at.start, HALF)
        if own:
            value = value + theirs[z, :, at, :].astype(F32)
        block[z, :, at, :] = value.astype(BF16)

    fill(*inputs, h, put)
    if own:
        x, y = place[1], place[2]
        copies = []
        for n, (dst, side) in enumerate(((a_send, 1 - x), (a_keep, x))):
            for row in range(2):
                copies.append((block.at[0:2, 2 * row + side], dst.at[:, row], n))
        for n, (dst, side) in enumerate(((b_send, 1 - y), (b_keep, y))):
            for col in range(2):
                copies.append((block.at[2:4, 2 * side + col], dst.at[:, col], 2 + n))
        copies = [
            pltpu.make_async_copy(src, dst, sems.at[5 + n]) for n, (src, dst, _) in enumerate(copies)
        ]
        start(copies)
        wait(copies)
    else:
        copy = pltpu.make_async_copy(block, out, sems.at[0])
        copy.start()
        copy.wait()


def grads(fill, rows, place, inputs, in_specs, other=None):
    own = other is not None
    scratch = [pltpu.VMEM((4, 4, rows, HALF), BF16)]
    if own:
        outs = [sds((2, 2, rows, HALF), BF16)] * 4
        args, in_specs = (*inputs, place, other), [*in_specs, SM, ANY]
        scratch = scratch * 2
    else:
        outs = [sds((4, 4, rows, HALF), BF16)]
        args, in_specs = (*inputs, place), [*in_specs, SM]
    return call(
        functools.partial(grads_kernel, fill, len(inputs), rows, own),
        outs,
        in_specs,
        [ANY] * len(outs),
        [*scratch, pltpu.SemaphoreType.DMA((16,))],
        2 * T * 16 * rows * HALF,
        14 * 1024 * 1024,
        "weight_grads",
    )(*args)


AXES = ("z", "y", "x", "c", "e")


def links(flip):
    pairs = []
    for d in range(32):
        pairs.append((d, d ^ flip))
    return pairs


def swap(value, axis):
    return lax.ppermute(value, axis, [(0, 1), (1, 0)])


def pick(value, index, axis):
    return lax.dynamic_index_in_dim(value, index, axis, keepdims=False)


def scatter(fill, rows, place, inputs, in_specs, x, y):
    (theirs,) = grads(fill, rows, place, inputs, in_specs)
    theirs = swap(theirs, "c")
    a_send, a_keep, b_send, b_keep = grads(fill, rows, place, inputs, in_specs, theirs)
    a_got = swap(a_send, "x")
    b_got = swap(b_send, "y")
    a_next = (pick(a_keep, 1 - y, 1).astype(F32) + pick(a_got, 1 - y, 1).astype(F32)).astype(BF16)
    b_next = (pick(b_keep, 1 - x, 1).astype(F32) + pick(b_got, 1 - x, 1).astype(F32)).astype(BF16)
    a_last = swap(a_next, "y")
    b_last = swap(b_next, "x")
    a = pick(a_keep, y, 1).astype(F32) + pick(a_got, y, 1).astype(F32) + a_last.astype(F32)
    b = pick(b_keep, x, 1).astype(F32) + pick(b_got, x, 1).astype(F32) + b_last.astype(F32)
    line = jnp.concatenate([a.astype(BF16), b.astype(BF16)], axis=0)
    return lax.psum_scatter(line, "z", scatter_dimension=0, tiled=False)


def pack_weights(qkv, out, up, down, gains, biases, up_b, c):
    rows = out.shape[1]
    panels = jnp.concatenate([qkv, out, up], axis=2).reshape(2, rows, 8, 2, HALF)
    panels = jnp.transpose(panels, (0, 3, 2, 1, 4)).reshape(2, 2, 8 * rows, HALF)
    downs = jnp.transpose(down.reshape(2, 4 * rows, 2, HALF), (0, 2, 1, 3))
    both = jnp.concatenate([panels, downs], axis=2)
    mine = pick(both, c, 1)
    got = swap(pick(both, 1 - c, 1), "c")
    low = jnp.where(c == 0, mine, got)
    high = jnp.where(c == 0, got, mine)

    def merge(n):
        size = low.shape[1] if n == 0 else n
        return size

    panels = jnp.stack(
        [low[:, : 8 * rows].reshape(2, 8, rows, HALF), high[:, : 8 * rows].reshape(2, 8, rows, HALF)],
        axis=2,
    ).reshape(2, 16 * rows, HALF)
    downs = jnp.concatenate([low[:, 8 * rows :], high[:, 8 * rows :]], axis=1)
    small = jnp.concatenate(
        [gains.reshape(2, 2 * rows), biases.reshape(2, 6 * rows), up_b], axis=1
    )
    small = jnp.pad(small[:, None, :], ((0, 0), (0, 15), (0, HALF - 12 * rows)))
    return jnp.concatenate([panels[:, : 8 * rows], small, panels[:, 8 * rows :], downs], axis=1)


def small_rows(values, rows):
    heads = values[:, : 8 * rows].reshape(32, 8, rows)
    heads = jnp.transpose(heads, (1, 0, 2)).reshape(8, D)
    tail = values[:, 8 * rows : 12 * rows].reshape(4, D)
    return jnp.concatenate([heads, tail, jnp.zeros((4, D), values.dtype)], axis=0).astype(F32)


def small_back(values, rows):
    heads = values[:8].reshape(8, 16, 2, rows)
    heads = jnp.transpose(heads, (2, 1, 0, 3)).reshape(2, 16, 8 * rows)
    tail = jnp.transpose(values[8:12].reshape(16, 2, 4 * rows), (1, 0, 2))
    both = jnp.concatenate([heads, tail], axis=2).astype(BF16)
    both = jnp.pad(both[:, :, None, :], ((0, 0), (0, 0), (0, 15), (0, HALF - 12 * rows)))
    return both.reshape(2, 4, 4, 16, HALF)


def body(
    encoder_input,
    corrupted,
    lengths,
    buckets,
    qkv_weight,
    out_weight,
    up_weight,
    down_weight,
    norm_gains,
    bias_rows,
    up_bias,
    encoder_cot,
    decoder_cot,
):
    extra = lax.axis_size("e")
    weights = [qkv_weight, out_weight, up_weight, down_weight, norm_gains, bias_rows, up_bias]
    if extra > 1:
        weights = [
            lax.all_gather(w, "e", axis=at, tiled=True)
            for w, at in zip(weights, (1, 1, 1, 1, 2, 2, 1))
        ]
    rows = weights[1].shape[1]
    x, y, c = lax.axis_index("x"), lax.axis_index("y"), lax.axis_index("c")
    place = jnp.stack([c, x, y]).astype(jnp.int32)
    packed = pack_weights(*weights, c)
    gathered = [
        lax.all_gather(packed[l], ("z", "y", "x", "c"), axis=0, tiled=False).reshape(
            4, 2, 2, 2, PACK, HALF
        )
        for l in range(2)
    ]
    vecs = [small_rows(g[:, :, :, :, SMALL_AT, :].reshape(32, HALF), rows) for g in gathered]

    p0, m0, stat0 = attend(encoder_input, vecs[0], gathered[0], lengths, buckets)
    enc_out, xd, xdl, *saved0 = feed(
        True, encoder_input, m0, vecs[0], gathered[0], corrupted, buckets
    )
    p1, m1, stat1 = attend(xdl, vecs[1], gathered[1], lengths, buckets)
    dec_out, *saved1 = feed(False, xd, m1, vecs[1], gathered[1])

    results = []
    dxd = None
    for l, (xb, p, m, stat, saved) in ((1, (xdl, p1, m1, stat1, saved1)), (0, (encoder_input, p0, m0, stat0, saved0))):
        encoder = l == 0
        if encoder:
            back = feed_back(True, encoder_cot, saved, vecs[l], gathered[l], dxd, buckets)
        else:
            back = feed_back(False, decoder_cot, saved, vecs[l], gathered[l])
        dr2l, dul, dr1, dr1l, dml, small = back
        y1l, g = saved[4], saved[5]
        feed_part = scatter(
            feed_grads, 4 * ROWS + DROWS, place, (y1l, dul, g, dr2l), [VM] * 4, x, y
        )
        dpl, sums = attend_back(p, dml, stat, lengths, buckets)
        if encoder:
            (enc_grad,) = input_back(True, dpl, dr1, gathered[l])
        else:
            dxd, cor_grad = input_back(False, dpl, dr1, gathered[l], buckets)
        q_bias = sums[:, 0, :].reshape(1, D)
        v_bias = sums[:, 1, :].reshape(1, D)
        small = jnp.concatenate([small[0:2], q_bias, v_bias, small[4:12]], axis=0)
        attend_part = scatter(
            attend_grads,
            SMALL_AT + 16,
            place,
            (xb, dpl, m, dr1l, small_back(small, rows)),
            [VM] * 5,
            x,
            y,
        )
        results.append((attend_part, feed_part))

    attend_part = jnp.stack([results[1][0], results[0][0]])
    feed_part = jnp.stack([results[1][1], results[0][1]])
    panels = jnp.concatenate(
        [attend_part[:, :SMALL_AT], feed_part[:, : 4 * ROWS]], axis=1
    ).reshape(2, 8, 2, rows, HALF)
    downs = feed_part[:, 4 * ROWS :].reshape(2, 2, 4 * rows, HALF)
    send = jnp.concatenate(
        [pick(panels, 1 - c, 2).reshape(2, 8 * rows, HALF), pick(downs, 1 - c, 1)], axis=1
    )
    mine = jnp.concatenate(
        [pick(panels, c, 2).reshape(2, 8 * rows, HALF), pick(downs, c, 1)], axis=1
    )
    got = swap(send, "c")
    full = jnp.concatenate([jnp.where(c == 0, mine, got), jnp.where(c == 0, got, mine)], axis=2)
    full = full.astype(F32)
    panels = full[:, : 8 * rows].reshape(2, 8, rows, D)
    qkv_grad = jnp.concatenate([panels[:, 0], panels[:, 1], panels[:, 2]], axis=2)
    out_grad = panels[:, 3]
    up_grad = jnp.concatenate([panels[:, 4], panels[:, 5], panels[:, 6], panels[:, 7]], axis=2)
    down_grad = full[:, 8 * rows :]
    small = attend_part[:, SMALL_AT, :].astype(F32)
    gains_grad = small[:, : 2 * rows].reshape(2, 2, rows)
    biases_grad = small[:, 2 * rows : 8 * rows].reshape(2, 6, rows)
    up_b_grad = small[:, 8 * rows : 12 * rows]
    grads_out = [qkv_grad, out_grad, up_grad, down_grad, gains_grad, biases_grad, up_b_grad]
    if extra > 1:
        grads_out = [
            lax.psum_scatter(v, "e", scatter_dimension=at, tiled=True)
            for v, at in zip(grads_out, (1, 1, 1, 1, 2, 2, 1))
        ]
    return (enc_out, dec_out, enc_grad, cor_grad, *grads_out)


def solution(mesh):
    devices = mesh.devices.reshape(4, 2, 2, 2, -1)
    inner = Mesh(devices, AXES)
    token = P(AXES, None)
    line = P(AXES)
    wide = P(None, AXES, None)
    vector = P(None, None, AXES)
    return jax.shard_map(
        body,
        mesh=inner,
        in_specs=(
            token, token, line, line, wide, wide, wide, wide, vector, vector, P(None, AXES), token, token,
        ),
        out_specs=(
            token, token, token, token, wide, wide, wide, wide, vector, vector, P(None, AXES),
        ),
        check_vma=False,
    )
```

```python
import functools

import jax
import jax.numpy as jnp
from jax import lax
from jax.experimental import pallas as pl
from jax.experimental.pallas import tpu as pltpu
from jax.sharding import Mesh
from jax.sharding import PartitionSpec as P

HD = 64
SLOT = 128
EPSILON = 1e-06
NEGATIVE = -1e30
F32 = jnp.float32
BF16 = jnp.bfloat16
VMEM_LIMIT = 60 * 1024 * 1024

T = 512
D = 768
HALF = D // 2
ROWS = 48
DROWS = 192
O_AT, SMALL_AT, PART_A = 144, 192, 224
D_AT, PART_B = 192, 384

VM = pl.BlockSpec(memory_space=pltpu.VMEM)
SM = pl.BlockSpec(memory_space=pltpu.SMEM)
HBM = pl.BlockSpec(memory_space=pl.ANY)


def dot(left, right):
    return lax.dot_general(left, right, (((1,), (0,)), ((), ())), preferred_element_type=F32)


def dot_rt(left, right):
    return lax.dot_general(left, right, (((1,), (1,)), ((), ())), preferred_element_type=F32)


def sds(shape, dtype):
    return jax.ShapeDtypeStruct(shape, dtype)


def call(kernel, name, args, in_specs, outs, out_specs, scratch, after=(), aliases=None):
    n, m = len(args), len(after)

    def ordered(*refs):
        kernel(*refs[:n], *refs[n + m :])

    return pl.pallas_call(
        ordered,
        out_shape=outs,
        in_specs=[*in_specs, *([HBM] * m)],
        out_specs=out_specs,
        scratch_shapes=scratch,
        input_output_aliases=aliases or {},
        compiler_params=pltpu.CompilerParams(vmem_limit_bytes=VMEM_LIMIT),
        cost_estimate=pl.CostEstimate(flops=1000, bytes_accessed=1000, transcendentals=0),
        name=name,
    )(*args, *after)


def start(copies):
    for copy in copies:
        copy.start()


def wait(copies):
    for copy in copies:
        copy.wait()


def part_slots(place):
    c, x, y = place[0], place[1], place[2]
    across = 2 * (1 - y) + (1 - x)
    slots = ((2 * y + x, 0, 4), (2 * y + 1 - x, 0, 4), (2 * (1 - y) + x, 0, 4), (across, 0, 2), (across, 2, 4))
    return [(half, *slot) for half in (c, 1 - c) for slot in slots]


def panel_copies(parts, place, dst, sems, row_at, rows):
    copies = []
    for n, (ref, (half, at, low, high)) in enumerate(zip(parts, part_slots(place))):
        cols = pl.ds(pl.multiple_of(half * HALF, HALF), HALF)
        copies.append(
            pltpu.make_async_copy(
                ref.at[:, row_at : row_at + rows, :], dst.at[low:high, at, :, cols], sems.at[n]
            )
        )
    return copies


def fill_bias(bias, lens, buck):
    bucket = buck[0]
    key = lax.broadcasted_iota(jnp.int32, (T, T), 0)
    query = lax.broadcasted_iota(jnp.int32, (T, T), 1)
    shift = bucket + 7
    same = lax.shift_right_logical(key, shift) == lax.shift_right_logical(query, shift)
    position = jnp.bitwise_and(key, lax.shift_left(jnp.int32(SLOT), bucket) - 1)
    slot = lax.shift_right_logical(key, 7)
    length = jnp.where(
        slot < 2,
        jnp.where(slot == 0, lens[0], lens[1]),
        jnp.where(slot == 2, lens[2], lens[3]),
    )
    bias[...] = jnp.where(same & (position < length), 0.0, NEGATIVE)


def first_tokens(buck, low, size):
    span = lax.shift_left(jnp.int32(SLOT), buck[0])
    token = lax.broadcasted_iota(jnp.int32, (size, 1), 0) + low
    return jnp.bitwise_and(token, span - 1) == 0


def halves(block):
    lane = lax.broadcasted_iota(jnp.int32, block.shape, 1)
    zero = jnp.zeros_like(block)
    return jnp.where(lane < HD, block, zero), jnp.where(lane < HD, zero, block)


def row_loop(size, body):
    def step(i, carry):
        body(pl.ds(pl.multiple_of(i * size, size), size))
        return carry

    lax.fori_loop(0, T // size, step, 0)


def attend_kernel(*refs):
    x, lens, buck, place = refs[:4]
    parts = refs[4:14]
    p, m, mt, stat, xt, vec, wq, bias, heap, sems = refs[14:]
    copies = [panel_copies(parts, place, wq.at[j], sems.at[j], j * ROWS, ROWS) for j in range(3)]
    smalls = []
    for n, part in enumerate(parts):
        at = (0, 4, 8, 12, 14)[n % 5] + 16 * (n // 5)
        count = 4 if n % 5 < 3 else 2
        smalls.append(
            pltpu.make_async_copy(
                part.at[:, SMALL_AT : SMALL_AT + 32, :], heap.at[at : at + count], sems.at[3, n]
            )
        )
    start(smalls)
    for group in copies:
        start(group)
    xt[...] = x[...].T
    fill_bias(bias, lens, buck)
    wait(smalls)
    total = heap[0].astype(F32)
    for n in range(1, 32):
        total = total + heap[n].astype(F32)
    vec[...] = jnp.concatenate([total[:16], total[16:]], axis=1)
    for j in range(3):
        wait(copies[j])
        weight = wq[j].reshape(D, D)
        for half in range(2):
            rows = slice(half * 256, half * 256 + 256)
            out = dot(x[rows, :], weight)
            if j != 1:
                out = out + (vec[2:3, :] if j == 0 else vec[3:4, :])
            out = out.astype(BF16)
            for s in range(6):
                p[6 * j + s, rows, :] = out[:, 128 * s : 128 * s + 128]

    def pair(i, carry):
        q = p[i] * jnp.asarray(HD**-0.5, BF16)
        v_t = p[12 + i].T
        keys = halves(p[6 + i])
        mixed = []
        for a in range(2):
            scores = dot_rt(keys[a], q) + bias[...]
            peak = jnp.max(scores, axis=0, keepdims=True)
            weights = jnp.exp(scores - peak)
            inverse = 1.0 / jnp.sum(weights, axis=0, keepdims=True)
            stat[2 * i + a, 0:1, :] = peak
            stat[2 * i + a, 1:2, :] = inverse
            soft = (weights * inverse).astype(BF16)
            mixed.append(dot(v_t[HD * a : HD * a + HD, :], soft))
        mixed = jnp.concatenate(mixed, axis=0)
        mt[i] = mixed.astype(BF16)
        m[i] = mixed.T.astype(BF16)
        return carry

    lax.fori_loop(0, 6, pair, 0)


def attend(x, lens, buck, place, parts, after):
    return call(
        attend_kernel,
        "attend",
        (x, lens, buck, place, *parts),
        [VM, SM, SM, SM] + [HBM] * 10,
        [
            sds((18, T, 128), BF16),
            sds((6, T, 128), BF16),
            sds((6, 128, T), BF16),
            sds((12, 8, T), F32),
            sds((D, T), BF16),
            sds((16, D), F32),
        ],
        [VM] * 6,
        [
            pltpu.VMEM((3, 4, 4, ROWS, D), BF16),
            pltpu.VMEM((T, T), F32),
            pltpu.VMEM((32, 32, HALF), BF16),
            pltpu.SemaphoreType.DMA((4, 10)),
        ],
        after,
    )


def unit_norm(resid):
    center = jnp.mean(resid, axis=-1, keepdims=True)
    shifted = resid - center
    spread = jnp.mean(shifted * shifted, axis=-1, keepdims=True)
    inverse = lax.rsqrt(spread + EPSILON)
    return shifted * inverse, inverse


def feed_kernel(encoder, *refs):
    x, m, vec, place = refs[:4]
    refs = refs[4:]
    if encoder:
        cor, buck = refs[:2]
        refs = refs[2:]
    parts_a, parts_b, refs = refs[:10], refs[10:20], refs[20:]
    out, n1, r1, n2, r2, y1t, gt, gp = refs[:8]
    refs = refs[8:]
    if encoder:
        xd, xdl = refs[:2]
        refs = refs[2:]
    wo, wu, wd, scr, y1, y1l, g, sems = refs
    o_copies = panel_copies(parts_a, place, wo, sems.at[0], O_AT, ROWS)
    u_copies = [
        panel_copies(parts_b, place, wu.at[j], sems.at[1 + j], j * ROWS, ROWS) for j in range(4)
    ]
    d_copies = panel_copies(parts_b, place, wd, sems.at[5], D_AT, DROWS)
    start(o_copies)
    for group in u_copies:
        start(group)
    start(d_copies)
    wait(o_copies)
    weight = wo[...].reshape(D, D)
    for half in range(2):
        rows = slice(half * 256, half * 256 + 256)
        left = jnp.concatenate([m[s, rows, :] for s in range(6)], axis=1)
        scr[rows, :] = dot(left, weight)

    def first(rows):
        resid = x[rows, :].astype(F32) + (scr[rows, :] + vec[4:5, :])
        unit, inverse = unit_norm(resid)
        n1[rows, :] = unit
        r1[rows, :] = jnp.broadcast_to(inverse, (inverse.shape[0], 128))
        normed = unit * vec[0:1, :] + vec[5:6, :]
        y1[rows, :] = normed
        y1l[rows, :] = normed.astype(BF16)

    row_loop(64, first)

    for j in range(4):
        wait(u_copies[j])

        def up(rows, j=j):
            left = y1l[rows, :]
            for k in range(3):
                cols = slice(256 * k, 256 * k + 256)
                right = wu[j, :, :, :, cols].reshape(D, 256)
                hidden = dot(left, right) + vec[8 + j : 9 + j, cols]
                cdf = 0.5 * (1.0 + lax.erf(hidden * (0.5**0.5)))
                g[j, rows, cols] = (hidden * cdf).astype(BF16)
                density = jnp.exp(hidden * hidden * -0.5) * 0.3989422804014327
                gp[j, rows, cols] = (cdf + hidden * density).astype(BF16)

        row_loop(128, up)

    wait(d_copies)
    for half in range(2):
        rows = slice(half * 256, half * 256 + 256)
        total = dot(g[0, rows, :], wd[0].reshape(D, D))
        for j in range(1, 4):
            total = total + dot(g[j, rows, :], wd[j].reshape(D, D))
        scr[rows, :] = total

    def second(rows):
        resid = y1[rows, :] + (scr[rows, :] + vec[6:7, :])
        unit, inverse = unit_norm(resid)
        n2[rows, :] = unit
        r2[rows, :] = jnp.broadcast_to(inverse, (inverse.shape[0], 128))
        result = unit * vec[1:2, :] + vec[7:8, :]
        out[rows, :] = result.astype(BF16)
        if encoder:
            mixed = jnp.where(
                first_tokens(buck, rows.start, 64), result, cor[rows, :].astype(F32)
            )
            xd[rows, :] = mixed
            xdl[rows, :] = mixed.astype(BF16)

    row_loop(64, second)
    y1t[...] = y1l[...].T
    for j in range(4):
        gt[j] = g[j].T


def feed(encoder, x, m, vec, place, parts_a, parts_b, after, cor=None, buck=None):
    args = (x, m, vec, place)
    in_specs = [VM, VM, VM, SM]
    outs = [
        sds((T, D), BF16),
        sds((T, D), F32),
        sds((T, 128), F32),
        sds((T, D), F32),
        sds((T, 128), F32),
        sds((D, T), BF16),
        sds((4, D, T), BF16),
        sds((4, T, D), BF16),
    ]
    if encoder:
        args = (*args, cor, buck)
        in_specs = [*in_specs, VM, SM]
        outs = [*outs, sds((T, D), F32), sds((T, D), BF16)]
    return call(
        functools.partial(feed_kernel, encoder),
        "feed",
        (*args, *parts_a, *parts_b),
        in_specs + [HBM] * 20,
        outs,
        [VM] * len(outs),
        [
            pltpu.VMEM((4, 4, ROWS, D), BF16),
            pltpu.VMEM((4, 4, 4, ROWS, D), BF16),
            pltpu.VMEM((4, 4, DROWS, D), BF16),
            pltpu.VMEM((T, D), F32),
            pltpu.VMEM((T, D), F32),
            pltpu.VMEM((T, D), BF16),
            pltpu.VMEM((4, T, D), BF16),
            pltpu.SemaphoreType.DMA((6, 10)),
        ],
        after,
    )


def norm_back(grad, unit, inverse, gain):
    scaled = grad * gain
    mean = jnp.mean(scaled, axis=-1, keepdims=True)
    along = jnp.mean(scaled * unit, axis=-1, keepdims=True)
    return inverse * (scaled - mean - unit * along)


def column_sum(value):
    return jnp.sum(value, axis=0, keepdims=True)


def half_cols(h):
    return pl.ds(pl.multiple_of(h * HALF, HALF), HALF)


def down_grads(h, put, gt, dr2l):
    for j in range(4):
        put(j, slice(0, DROWS), dot(gt[j], dr2l[:, half_cols(h)]))


def up_grads(h, put, y1t, dul):
    for j in range(4):
        put(None, slice(j * ROWS, j * ROWS + ROWS), dot(y1t[...], dul[j, :, half_cols(h)]))


def attend_grads(h, put, xt, dpl, mt, dr1l, small_a, small_b, small_c, small_d):
    for j in range(3):
        right = jnp.concatenate([dpl[6 * j + 3 * h + s] for s in range(3)], axis=1)
        put(None, slice(j * ROWS, j * ROWS + ROWS), dot(xt[...], right))
    left = jnp.concatenate([mt[s] for s in range(6)], axis=0)
    put(None, slice(O_AT, O_AT + ROWS), dot(left, dr1l[:, half_cols(h)]))
    small = small_a[...] + small_b[...] + small_c[...] + small_d[...]
    small = jnp.concatenate([small[:, :HALF], small[:, HALF:]], axis=0)
    put(None, slice(SMALL_AT, SMALL_AT + 32), jnp.broadcast_to(small, (16, 32, HALF)))


def placed(z, at, value):
    rows = at.stop - at.start
    return value.reshape((4, rows, HALF) if z is not None else (4, 4, rows, HALF))


PIECES = [(z, y) for z in range(4) for y in range(2)]


def give_grads(fill, inputs, place, outs, block, sems):
    copies = []

    def put(z, at, value):
        block[(slice(None) if z is None else z, slice(None), at)] = placed(z, at, value).astype(BF16)
        for n, (at_z, at_y) in enumerate(PIECES):
            if z is None or z == at_z:
                src = block.at[at_z, 2 * at_y : 2 * at_y + 2, at]
                copy = pltpu.make_async_copy(src, outs[n].at[:, at], sems.at[len(copies)])
                copy.start()
                copies.append(copy)

    fill(1 - place[0], put, *inputs)
    return copies


def give_kernel(fill, count, *refs):
    place, outs, block, sems = refs[count], refs[count + 1 : count + 9], *refs[count + 9 :]
    wait(give_grads(fill, refs[:count], place, outs, block, sems))


def give(fill, inputs, rows, place, after):
    return call(
        functools.partial(give_kernel, fill, len(inputs)),
        "give_grads",
        (*inputs, place),
        [VM] * len(inputs) + [SM],
        [sds((2, rows, HALF), BF16)] * 8,
        [HBM] * 8,
        [pltpu.VMEM((4, 4, rows, HALF), BF16), pltpu.SemaphoreType.DMA((48,))],
        after,
    )


def keep_kernel(fill, count, *refs):
    place, got, refs_out = refs[count], refs[count + 1 : count + 9], refs[count + 9 :]
    a_send, a_keep, b_send, b_keep, block, theirs, sems = refs_out
    fetch = [
        pltpu.make_async_copy(got[n], theirs.at[z, 2 * y : 2 * y + 2], sems.at[8 + n])
        for n, (z, y) in enumerate(PIECES)
    ]
    start(fetch)
    waited = []

    def put(z, at, value):
        if not waited:
            wait(fetch)
            waited.append(True)
        index = (slice(None) if z is None else z, slice(None), at)
        block[index] = (placed(z, at, value) + theirs[index].astype(F32)).astype(BF16)

    fill(place[0], put, *refs[:count])
    x, y = place[1], place[2]
    copies = []
    for dst, side in ((a_send, 1 - x), (a_keep, x)):
        for row in range(2):
            copies.append((block.at[0:2, 2 * row + side], dst.at[row]))
    for dst, side in ((b_send, 1 - y), (b_keep, y)):
        for col in range(2):
            copies.append((block.at[2:4, 2 * side + col], dst.at[col]))
    copies = [pltpu.make_async_copy(src, dst, sems.at[n]) for n, (src, dst) in enumerate(copies)]
    start(copies)
    wait(copies)


def keep(fill, inputs, rows, place, got, after):
    return call(
        functools.partial(keep_kernel, fill, len(inputs)),
        "keep_grads",
        (*inputs, place, *got),
        [VM] * len(inputs) + [SM] + [HBM] * 8,
        [sds((2, 2, rows, HALF), BF16)] * 4,
        [HBM] * 4,
        [
            pltpu.VMEM((4, 4, rows, HALF), BF16),
            pltpu.VMEM((4, 4, rows, HALF), BF16),
            pltpu.SemaphoreType.DMA((16,)),
        ],
        after,
    )


def add_next_kernel(a_keep, a_got, b_keep, b_got, place, a_next, b_next, blocks, sems):
    x, y = place[1], place[2]
    refs = (a_keep.at[1 - y], a_got.at[1 - y], b_keep.at[1 - x], b_got.at[1 - x])
    copies = [pltpu.make_async_copy(ref, blocks.at[n], sems.at[n]) for n, ref in enumerate(refs)]
    start(copies)
    wait(copies)
    a_next[...] = (blocks[0].astype(F32) + blocks[1].astype(F32)).astype(BF16)
    b_next[...] = (blocks[2].astype(F32) + blocks[3].astype(F32)).astype(BF16)


def add_next(a_keep, a_got, b_keep, b_got, place, after):
    rows = a_keep.shape[2]
    return call(
        add_next_kernel,
        "add_next",
        (a_keep, a_got, b_keep, b_got, place),
        [HBM] * 4 + [SM],
        [sds((2, rows, HALF), BF16)] * 2,
        [VM] * 2,
        [pltpu.VMEM((4, 2, rows, HALF), BF16), pltpu.SemaphoreType.DMA((4,))],
        after,
    )


def add_last_kernel(a_keep, a_got, a_last, b_keep, b_got, b_last, place, line, blocks, sems):
    x, y = place[1], place[2]
    refs = (a_keep.at[y], a_got.at[y], a_last, b_keep.at[x], b_got.at[x], b_last)
    copies = [pltpu.make_async_copy(ref, blocks.at[n], sems.at[n]) for n, ref in enumerate(refs)]
    start(copies)
    wait(copies)
    for n in range(2):
        total = blocks[3 * n].astype(F32) + blocks[3 * n + 1].astype(F32)
        line[2 * n : 2 * n + 2] = (total + blocks[3 * n + 2].astype(F32)).astype(BF16)


def add_last(a_keep, a_got, a_last, b_keep, b_got, b_last, place, after):
    rows = a_keep.shape[2]
    (line,) = call(
        add_last_kernel,
        "add_last",
        (a_keep, a_got, a_last, b_keep, b_got, b_last, place),
        [HBM] * 6 + [SM],
        [sds((4, rows, HALF), BF16)],
        [VM],
        [pltpu.VMEM((6, 2, rows, HALF), BF16), pltpu.SemaphoreType.DMA((6,))],
        after,
    )
    return line


def down_back_kernel(encoder, *refs):
    cot, n2, r2, vec, gt, place = refs[:6]
    refs = refs[6:]
    if encoder:
        dxd, buck = refs[:2]
        refs = refs[2:]
    dr2, dr2l, small = refs[:3]
    outs, gts, block, sems, out_sems = refs[3:11], *refs[11:]
    copies = [pltpu.make_async_copy(gt.at[j], gts.at[j], sems.at[j]) for j in range(4)]
    start(copies)
    small[...] = jnp.zeros_like(small)

    def second(rows):
        grad = cot[rows, :].astype(F32)
        if encoder:
            grad = grad + jnp.where(first_tokens(buck, rows.start, 64), dxd[rows, :], 0.0)
        unit = n2[rows, :]
        resid = norm_back(grad, unit, r2[rows, 0:1], vec[1:2, :])
        small[1:2, :] += column_sum(grad * unit)
        small[7:8, :] += column_sum(grad)
        small[6:7, :] += column_sum(resid)
        dr2[rows, :] = resid
        dr2l[rows, :] = resid.astype(BF16)

    row_loop(64, second)
    wait(copies)
    wait(give_grads(down_grads, (gts, dr2l), place, outs, block, out_sems))


def down_back(encoder, cot, n2, r2, vec, gt, place, after, dxd=None, buck=None):
    args = (cot, n2, r2, vec, gt, place)
    in_specs = [VM, VM, VM, VM, HBM, SM]
    if encoder:
        args = (*args, dxd, buck)
        in_specs = [*in_specs, VM, SM]
    return call(
        functools.partial(down_back_kernel, encoder),
        "down_back",
        args,
        in_specs,
        [sds((T, D), F32), sds((T, D), BF16), sds((16, D), F32)] + [sds((2, DROWS, HALF), BF16)] * 8,
        [VM] * 3 + [HBM] * 8,
        [
            pltpu.VMEM((4, D, T), BF16),
            pltpu.VMEM((4, 4, DROWS, HALF), BF16),
            pltpu.SemaphoreType.DMA((4,)),
            pltpu.SemaphoreType.DMA((48,)),
        ],
        after,
    )


def up_back_kernel(*refs):
    dr2l, gp, y1t, place = refs[:4]
    parts = refs[4:14]
    dul, small = refs[14:16]
    outs, wd, block, sems, out_sems = refs[16:24], *refs[24:]
    copies = panel_copies(parts, place, wd, sems, D_AT, DROWS)
    start(copies)
    small[...] = jnp.zeros_like(small)
    wait(copies)
    for j in range(4):

        def up(rows, j=j):
            left = dr2l[rows, :]
            weight = wd[j].reshape(D, D)
            for k in range(3):
                cols = slice(256 * k, 256 * k + 256)
                grad = dot_rt(left, weight[cols, :])
                hidden = (grad * gp[j, rows, cols].astype(F32)).astype(BF16)
                dul[j, rows, cols] = hidden
                small[8 + j : 9 + j, cols] += column_sum(hidden.astype(F32))

        row_loop(256, up)
    wait(give_grads(up_grads, (y1t, dul), place, outs, block, out_sems))


def up_back(dr2l, gp, y1t, place, parts_b, after):
    return call(
        up_back_kernel,
        "up_back",
        (dr2l, gp, y1t, place, *parts_b),
        [VM, VM, VM, SM] + [HBM] * 10,
        [sds((4, T, D), BF16), sds((16, D), F32)] + [sds((2, 4 * ROWS, HALF), BF16)] * 8,
        [VM] * 2 + [HBM] * 8,
        [
            pltpu.VMEM((4, 4, DROWS, D), BF16),
            pltpu.VMEM((4, 4, 4 * ROWS, HALF), BF16),
            pltpu.SemaphoreType.DMA((10,)),
            pltpu.SemaphoreType.DMA((48,)),
        ],
        after,
    )


def mid_back_kernel(*refs):
    dul, dr2, n1, r1, vec, place = refs[:6]
    parts_a, parts_b = refs[6:16], refs[16:26]
    dr1, dr1l, dml, small, wo, wu, scr, sems = refs[26:]
    u_copies = [
        panel_copies(parts_b, place, wu.at[j], sems.at[1 + j], j * ROWS, ROWS) for j in range(4)
    ]
    o_copies = panel_copies(parts_a, place, wo, sems.at[0], O_AT, ROWS)
    for group in u_copies:
        start(group)
    start(o_copies)
    small[...] = jnp.zeros_like(small)
    for j in range(4):
        wait(u_copies[j])
        for half in range(2):
            rows = slice(half * 256, half * 256 + 256)
            part = dot_rt(dul[j, rows, :], wu[j].reshape(D, D))
            scr[rows, :] = (dr2[rows, :] if j == 0 else scr[rows, :]) + part

    def first(rows):
        grad = scr[rows, :]
        unit = n1[rows, :]
        resid = norm_back(grad, unit, r1[rows, 0:1], vec[0:1, :])
        small[0:1, :] += column_sum(grad * unit)
        small[5:6, :] += column_sum(grad)
        small[4:5, :] += column_sum(resid)
        dr1[rows, :] = resid
        dr1l[rows, :] = resid.astype(BF16)

    row_loop(64, first)
    wait(o_copies)
    weight = wo[...].reshape(D, D)
    for half in range(2):
        rows = slice(half * 256, half * 256 + 256)
        out = dot_rt(dr1l[rows, :], weight).astype(BF16)
        for s in range(6):
            dml[s, rows, :] = out[:, 128 * s : 128 * s + 128]


def mid_back(dul, dr2, n1, r1, vec, place, parts_a, parts_b, after):
    return call(
        mid_back_kernel,
        "mid_back",
        (dul, dr2, n1, r1, vec, place, *parts_a, *parts_b),
        [VM] * 5 + [SM] + [HBM] * 20,
        [sds((T, D), F32), sds((T, D), BF16), sds((6, T, 128), BF16), sds((16, D), F32)],
        [VM] * 4,
        [
            pltpu.VMEM((4, 4, ROWS, D), BF16),
            pltpu.VMEM((4, 4, 4, ROWS, D), BF16),
            pltpu.VMEM((T, D), F32),
            pltpu.SemaphoreType.DMA((5, 10)),
        ],
        after,
    )


def attend_back_kernel(p, dml, stat, lens, buck, dpl, small, bias):
    fill_bias(bias, lens, buck)
    scale = jnp.asarray(HD**-0.5, BF16)
    small[...] = jnp.zeros_like(small)

    def pair(i, carry):
        q = p[i] * scale
        k_t = p[6 + i].T
        keys = halves(p[6 + i])
        values = halves(p[12 + i])
        grad = dml[i]
        grads = halves(grad)
        queries = halves(q)
        dq = []
        dk = jnp.zeros((T, 128), F32)
        dv = jnp.zeros((T, 128), F32)
        for a in range(2):
            scores = dot_rt(keys[a], q) + bias[...]
            peak = stat[2 * i + a, 0:1, :]
            inverse = stat[2 * i + a, 1:2, :]
            soft = jnp.exp(scores - peak) * inverse
            dv = dv + dot(soft.astype(BF16), grads[a])
            dsoft = dot_rt(values[a], grad)
            total = jnp.sum(soft * dsoft, axis=0, keepdims=True)
            dscore = (soft * (dsoft - total)).astype(BF16)
            dk = dk + dot(dscore, queries[a])
            dq.append(dot(k_t[HD * a : HD * a + HD, :], dscore))
        dq = (jnp.concatenate(dq, axis=0).T * (HD**-0.5)).astype(BF16)
        dv = dv.astype(BF16)
        dpl[i] = dq
        dpl[6 + i] = dk.astype(BF16)
        dpl[12 + i] = dv
        cols = pl.ds(pl.multiple_of(i * 128, 128), 128)
        small[2:3, cols] = column_sum(dq.astype(F32))
        small[3:4, cols] = column_sum(dv.astype(F32))
        return carry

    lax.fori_loop(0, 6, pair, 0)


def attend_back(p, dml, stat, lens, buck, after):
    return call(
        attend_back_kernel,
        "attend_back",
        (p, dml, stat, lens, buck),
        [VM, VM, VM, SM, SM],
        [sds((18, T, 128), BF16), sds((16, D), F32)],
        [VM, VM],
        [pltpu.VMEM((T, T), F32)],
        after,
    )


def input_back_kernel(encoder, *refs):
    dpl, dr1, place = refs[:3]
    refs = refs[3:]
    if not encoder:
        buck, refs = refs[0], refs[1:]
    parts, refs = refs[:10], refs[10:]
    if not encoder:
        dxd, refs = refs[0], refs[1:]
    out, wq, sems = refs
    copies = [panel_copies(parts, place, wq.at[j], sems.at[j], j * ROWS, ROWS) for j in range(3)]
    for group in copies:
        start(group)
    for group in copies:
        wait(group)
    for half in range(2):
        rows = slice(half * 256, half * 256 + 256)
        total = dr1[rows, :]
        for j in range(3):
            left = jnp.concatenate([dpl[6 * j + s, rows, :] for s in range(6)], axis=1)
            total = total + dot_rt(left, wq[j].reshape(D, D))
        if encoder:
            out[rows, :] = total.astype(BF16)
        else:
            dxd[rows, :] = total
            out[rows, :] = jnp.where(first_tokens(buck, half * 256, 256), 0.0, total).astype(BF16)


def input_back(encoder, dpl, dr1, place, parts_a, after, buck=None):
    args, in_specs = (dpl, dr1, place), [VM, VM, SM]
    outs = [sds((T, D), BF16)]
    if not encoder:
        args, in_specs = (*args, buck), [*in_specs, SM]
        outs = [sds((T, D), F32), *outs]
    return call(
        functools.partial(input_back_kernel, encoder),
        "input_back",
        (*args, *parts_a),
        in_specs + [HBM] * 10,
        outs,
        [VM] * len(outs),
        [pltpu.VMEM((3, 4, 4, ROWS, D), BF16), pltpu.SemaphoreType.DMA((3, 10))],
        after,
    )


def gate_kernel(*refs):
    pass


def gate(values, after):
    outs = call(
        gate_kernel,
        "gate",
        tuple(values),
        [HBM] * len(values),
        [sds(v.shape, v.dtype) for v in values],
        [HBM] * len(values),
        [],
        after,
        {n: n for n in range(len(values))},
    )
    return list(outs)


def split_kernel(bx, by, ax, ay, held, sems):
    refs = ((bx.at[0:2], held.at[0], ax), (by.at[2:4], held.at[1], ay))
    into = [pltpu.make_async_copy(src, mid, sems.at[n]) for n, (src, mid, _) in enumerate(refs)]
    out = [pltpu.make_async_copy(mid, dst, sems.at[2 + n]) for n, (_, mid, dst) in enumerate(refs)]
    start(into)
    for n in range(2):
        into[n].wait()
        out[n].start()
    wait(out)


def split(bx, by, after):
    shape = (2, *bx.shape[1:])
    return call(
        split_kernel,
        "split",
        (bx, by),
        [HBM, HBM],
        [sds(shape, BF16)] * 2,
        [HBM] * 2,
        [pltpu.VMEM((2, *shape), BF16), pltpu.SemaphoreType.DMA((4,))],
        after,
    )


AXES = ("z", "y", "x", "c", "e")


def swap(value, axis):
    return lax.ppermute(value, axis, [(0, 1), (1, 0)])


def pick(value, index, axis):
    return lax.dynamic_index_in_dim(value, index, axis, keepdims=False)


class Gather:
    def __init__(self, line):
        self.line = line

    def plane(self, after):
        (self.own,) = gate([self.line], after)
        self.bx, self.by = swap(self.own, "x"), swap(self.own, "y")
        self.own_c = swap(self.own, "c")
        return (self.own,)

    def forward(self, after):
        ax, ay = split(self.bx, self.by, after)
        self.dx, self.dy = swap(ax, "y"), swap(ay, "x")
        self.bx_c, self.by_c = swap(self.bx, "c"), swap(self.by, "c")
        return (ax, ay)

    def across(self, after):
        self.dx, self.dy = gate([self.dx, self.dy], after)
        self.parts = (
            self.own, self.bx, self.by, self.dx, self.dy,
            self.own_c, self.bx_c, self.by_c, swap(self.dx, "c"), swap(self.dy, "c"),
        )
        return (self.dx, self.dy)


class Scatter:
    def __init__(self, fill, rows, place):
        self.fill, self.rows, self.place = fill, rows, place

    def give(self, inputs, after):
        self.inputs = inputs
        return self.given(give(self.fill, inputs, self.rows, self.place, after), inputs)

    def given(self, outs, inputs):
        self.inputs = inputs
        self.got = [swap(out, "c") for out in outs]
        return (outs[0],)

    def keep(self, after):
        a_send, self.a_keep, b_send, self.b_keep = keep(
            self.fill, self.inputs, self.rows, self.place, self.got, after
        )
        self.a_got, self.b_got = swap(a_send, "x"), swap(b_send, "y")
        return (a_send, b_send)

    def next(self, after):
        a_next, b_next = add_next(
            self.a_keep, self.a_got, self.b_keep, self.b_got, self.place, after
        )
        self.a_last, self.b_last = swap(a_next, "y"), swap(b_next, "x")
        return (a_next, b_next)

    def last(self, after):
        line = add_last(
            self.a_keep, self.a_got, self.a_last, self.b_keep, self.b_got, self.b_last, self.place, after
        )
        self.total = lax.psum_scatter(line, "z", scatter_dimension=0, tiled=False)
        return (line,)

    def end(self, after):
        (self.total,) = gate([self.total], after)
        return (self.total,)


def pack_weights(qkv, out, up, down, gains, biases, up_b, c, device):
    rows = out.shape[1]
    panels = jnp.concatenate([qkv, out, up], axis=2).reshape(2, rows, 8, 2, HALF)
    panels = jnp.transpose(panels, (0, 3, 2, 1, 4)).reshape(2, 2, 8 * rows, HALF)
    downs = jnp.transpose(down.reshape(2, 4 * rows, 2, HALF), (0, 2, 1, 3))
    both = jnp.concatenate([panels, downs], axis=2)
    mine = pick(both, c, 1)
    got = swap(pick(both, 1 - c, 1), "c")
    low = jnp.where(c == 0, mine, got)
    high = jnp.where(c == 0, got, mine)
    panels = jnp.stack(
        [low[:, : 8 * rows].reshape(2, 8, rows, HALF), high[:, : 8 * rows].reshape(2, 8, rows, HALF)],
        axis=2,
    ).reshape(2, 16 * rows, HALF)
    downs = jnp.concatenate([low[:, 8 * rows :], high[:, 8 * rows :]], axis=1)
    small = jnp.zeros((2, 16, D), BF16)
    small = lax.dynamic_update_slice(
        small, jnp.concatenate([gains, biases], axis=1), (0, 0, device * rows)
    )
    small = lax.dynamic_update_slice(
        small, up_b[:, None, :], (0, 8 + device // 8, device % 8 * (4 * rows))
    )
    small = jnp.concatenate([small[:, :, :HALF], small[:, :, HALF:]], axis=1)
    part_a = jnp.concatenate([panels[:, : 8 * rows], small], axis=1)
    part_b = jnp.concatenate([panels[:, 8 * rows :], downs], axis=1)
    return part_a, part_b


def body(
    encoder_input,
    corrupted,
    lengths,
    buckets,
    qkv_weight,
    out_weight,
    up_weight,
    down_weight,
    norm_gains,
    bias_rows,
    up_bias,
    encoder_cot,
    decoder_cot,
):
    extra = lax.axis_size("e")
    weights = [qkv_weight, out_weight, up_weight, down_weight, norm_gains, bias_rows, up_bias]
    if extra > 1:
        weights = [
            lax.all_gather(w, "e", axis=at, tiled=True)
            for w, at in zip(weights, (1, 1, 1, 1, 2, 2, 1))
        ]
    rows = weights[1].shape[1]
    x, y, c = lax.axis_index("x"), lax.axis_index("y"), lax.axis_index("c")
    device = ((lax.axis_index("z") * 2 + y) * 2 + x) * 2 + c
    place = jnp.stack([c, x, y]).astype(jnp.int32)
    part_a, part_b = pack_weights(*weights, c, device)
    a0 = Gather(lax.all_gather(part_a[0], "z", axis=0, tiled=False))
    tok = a0.plane(())
    (part_b0,) = gate([part_b[0]], tok)
    b0 = Gather(lax.all_gather(part_b0, "z", axis=0, tiled=False))
    rest = lax.all_gather(jnp.concatenate([part_a[1], part_b[1]]), "z", axis=0, tiled=False)
    a1, b1 = Gather(rest[:, :PART_A]), Gather(rest[:, PART_A:])
    tok = a0.forward(tok)
    tok = a0.across(tok)
    tok = b0.plane(tok)
    p0, m0, mt0, stat0, xt0, vec0 = attend(encoder_input, lengths, buckets, place, a0.parts, tok)
    tok = b0.forward((stat0,))
    tok = a1.plane(tok)
    tok = b0.across(tok)
    tok = b1.plane(tok)
    enc_out, *saved0, xd, xdl = feed(
        True, encoder_input, m0, vec0, place, a0.parts, b0.parts, tok, corrupted, buckets
    )
    tok = a1.forward((enc_out,))
    tok = a1.across(tok)
    tok = b1.forward(tok)
    p1, m1, mt1, stat1, xt1, vec1 = attend(xdl, lengths, buckets, place, a1.parts, tok)
    tok = b1.across((stat1,))
    dec_out, *saved1 = feed(False, xd, m1, vec1, place, a1.parts, b1.parts, tok)

    n1, r1, n2, r2, y1t, gt, gp = saved1
    d1, u1, q1 = (
        Scatter(down_grads, DROWS, place),
        Scatter(up_grads, 4 * ROWS, place),
        Scatter(attend_grads, PART_A, place),
    )
    dr2, dr2l, small_a, *out = down_back(False, decoder_cot, n2, r2, vec1, gt, place, (dec_out,))
    d1.given(out, (gt, dr2l))
    dul, small_b, *out = up_back(dr2l, gp, y1t, place, b1.parts, (small_a,))
    u1.given(out, (y1t, dul))
    tok = d1.keep((small_b,))
    dr1, dr1l, dml, small_c = mid_back(dul, dr2, n1, r1, vec1, place, a1.parts, b1.parts, tok)
    tok = u1.keep((small_c,))
    dpl, small_d = attend_back(p1, dml, stat1, lengths, buckets, tok)
    tok = d1.next((small_d,))
    tok = q1.give((xt1, dpl, mt1, dr1l, small_a, small_b, small_c, small_d), tok)
    tok = u1.next(tok)
    dxd, cor_grad = input_back(False, dpl, dr1, place, a1.parts, tok, buckets)
    tok = q1.keep((cor_grad,))
    tok = d1.last(tok)

    n1, r1, n2, r2, y1t, gt, gp = saved0
    d0, u0, q0 = (
        Scatter(down_grads, DROWS, place),
        Scatter(up_grads, 4 * ROWS, place),
        Scatter(attend_grads, PART_A, place),
    )
    dr2, dr2l, small_a, *out = down_back(
        True, encoder_cot, n2, r2, vec0, gt, place, tok, dxd, buckets
    )
    d0.given(out, (gt, dr2l))
    tok = u1.last((small_a,))
    dul, small_b, *out = up_back(dr2l, gp, y1t, place, b0.parts, tok)
    u0.given(out, (y1t, dul))
    tok = q1.next((small_b,))
    tok = d1.end(tok)
    tok = d0.keep(tok)
    dr1, dr1l, dml, small_c = mid_back(dul, dr2, n1, r1, vec0, place, a0.parts, b0.parts, tok)
    tok = u0.keep((small_c,))
    tok = u1.end(tok)
    tok = q1.last(tok)
    dpl, small_d = attend_back(p0, dml, stat0, lengths, buckets, tok)
    tok = q0.give((xt0, dpl, mt0, dr1l, small_a, small_b, small_c, small_d), (small_d,))
    tok = d0.next(tok)
    tok = q0.keep(tok)
    tok = u0.next(tok)
    (enc_grad,) = input_back(True, dpl, dr1, place, a0.parts, tok)
    tok = q1.end((enc_grad,))
    tok = d0.last(tok)
    tok = u0.last(tok)
    tok = q0.next(tok)
    tok = d0.end(tok)
    tok = u0.end(tok)
    tok = q0.last(tok)

    attend_part = jnp.stack([q0.total, q1.total])
    panels = jnp.concatenate(
        [attend_part[:, :SMALL_AT], jnp.stack([u0.total, u1.total])], axis=1
    ).reshape(2, 8, 2, rows, HALF)
    downs = jnp.stack([d0.total, d1.total]).reshape(2, 2, 4 * rows, HALF)
    send = jnp.concatenate(
        [pick(panels, 1 - c, 2).reshape(2, 8 * rows, HALF), pick(downs, 1 - c, 1)], axis=1
    )
    mine = jnp.concatenate(
        [pick(panels, c, 2).reshape(2, 8 * rows, HALF), pick(downs, c, 1)], axis=1
    )
    got = swap(send, "c")
    full = jnp.concatenate([jnp.where(c == 0, mine, got), jnp.where(c == 0, got, mine)], axis=2)
    full = full.astype(F32)
    panels = full[:, : 8 * rows].reshape(2, 8, rows, D)
    qkv_grad = jnp.concatenate([panels[:, 0], panels[:, 1], panels[:, 2]], axis=2)
    out_grad = panels[:, 3]
    up_grad = jnp.concatenate([panels[:, 4], panels[:, 5], panels[:, 6], panels[:, 7]], axis=2)
    down_grad = full[:, 8 * rows :]
    small = attend_part[:, SMALL_AT:].astype(F32)
    small = jnp.concatenate([small[:, :16], small[:, 16:]], axis=2)
    heads = lax.dynamic_slice(small, (0, 0, device * rows), (2, 8, rows))
    up_b_grad = lax.dynamic_slice(
        small, (0, 8 + device // 8, device % 8 * (4 * rows)), (2, 1, 4 * rows)
    )[:, 0]
    grads_out = [qkv_grad, out_grad, up_grad, down_grad, heads[:, :2], heads[:, 2:], up_b_grad]
    if extra > 1:
        grads_out = [
            lax.psum_scatter(v, "e", scatter_dimension=at, tiled=True)
            for v, at in zip(grads_out, (1, 1, 1, 1, 2, 2, 1))
        ]
    return (enc_out, dec_out, enc_grad, cor_grad, *grads_out)


def solution(mesh):
    devices = mesh.devices.reshape(4, 2, 2, 2, -1)
    inner = Mesh(devices, AXES)
    token = P(AXES, None)
    line = P(AXES)
    wide = P(None, AXES, None)
    vector = P(None, None, AXES)
    return jax.shard_map(
        body,
        mesh=inner,
        in_specs=(
            token, token, line, line, wide, wide, wide, wide, vector, vector, P(None, AXES), token, token,
        ),
        out_specs=(
            token, token, token, token, wide, wide, wide, wide, vector, vector, P(None, AXES),
        ),
        check_vma=False,
    )
```

```python
import functools

import jax
import jax.numpy as jnp
from jax import lax
from jax.experimental import pallas as pl
from jax.experimental.pallas import tpu as pltpu
from jax.sharding import Mesh
from jax.sharding import PartitionSpec as P

HD = 64
SLOT = 128
EPSILON = 1e-06
NEGATIVE = -1e30
F32 = jnp.float32
BF16 = jnp.bfloat16
VMEM_LIMIT = 64 * 1024 * 1024

T = 512
D = 768
HALF = D // 2
ROWS = 48
DROWS = 192
O_AT, SMALL_AT, PART_A = 144, 192, 224
D_AT, PART_B = 192, 384

NORM_ROWS = 256
ATTEND_BACK_PAIRS = 2
SM = pl.BlockSpec(memory_space=pltpu.SMEM)
HBM = pl.BlockSpec(memory_space=pl.ANY)
SPAN = {
    "attend": 35,
    "feed": 20,
    "split": 0,
    "mid_back": 12,
    "input_back": 14,
    "up_back": 6,
    "add_next": 1.5,
}


def dot(left, right):
    return lax.dot_general(left, right, (((1,), (0,)), ((), ())), preferred_element_type=F32)


def dot_rt(left, right):
    return lax.dot_general(left, right, (((1,), (1,)), ((), ())), preferred_element_type=F32)


def sds(shape, dtype):
    return jax.ShapeDtypeStruct(shape, dtype)


class In:
    def __init__(self, source, held, sem):
        self.held, self.copy, self.there = held, pltpu.make_async_copy(source, held, sem), False
        self.copy.start()

    def __call__(self):
        if not self.there:
            self.copy.wait()
            self.there = True
        return self.held


class Out:
    def __init__(self, target, held, sems):
        self.target, self.held, self.sems, self.copies = target, held, sems, []

    def send(self, index=None):
        source = self.held if index is None else self.held.at[index]
        target = self.target if index is None else self.target.at[index]
        copy = pltpu.make_async_copy(source, target, self.sems.at[len(self.copies)])
        copy.start()
        self.copies.append(copy)

    def wait(self):
        for copy in self.copies:
            copy.wait()


def call(kernel, name, args, in_kinds, outs, out_kinds, scratch, after=(), aliases=None):
    n, m, k = len(args), len(after), len(outs)
    spec = {"i": HBM, "o": HBM, "h": HBM, "s": SM}
    ins = [a for a, kind in zip(args, in_kinds) if kind == "i"]
    sent = [o for o, kind in zip(outs, out_kinds) if kind == "o"]

    def ordered(*refs):
        inputs, results, rest = refs[:n], refs[n + m : n + m + k], refs[n + m + k :]
        held_in, held_out = rest[: len(ins)], rest[len(ins) : len(ins) + len(sent)]
        own = rest[len(ins) + len(sent) : len(ins) + len(sent) + len(scratch)]
        sems = rest[len(ins) + len(sent) + len(scratch) :]
        lazy, at = [], 0
        for ref, kind in zip(inputs, in_kinds):
            if kind == "i":
                ref, at = In(ref, held_in[at], sems[0].at[at]), at + 1
            lazy.append(ref)
        flow, at = [], 0
        for ref, kind in zip(results, out_kinds):
            if kind == "o":
                ref, at = Out(ref, held_out[at], sems[-1].at[at]), at + 1
            flow.append(ref)
        kernel(*lazy, *flow, *own)
        for ref in lazy:
            if isinstance(ref, In):
                ref()
        flow = [ref for ref in flow if isinstance(ref, Out)]
        for ref in flow:
            if not ref.copies:
                ref.send()
        for ref in flow:
            ref.wait()

    sems = []
    if ins:
        sems.append(pltpu.SemaphoreType.DMA((len(ins),)))
    if sent:
        sems.append(pltpu.SemaphoreType.DMA((len(sent), 4)))
    return pl.pallas_call(
        ordered,
        out_shape=outs,
        in_specs=[*(spec[kind] for kind in in_kinds), *([HBM] * m)],
        out_specs=[HBM] * k,
        scratch_shapes=[
            *(pltpu.VMEM(a.shape, a.dtype) for a in ins),
            *(pltpu.VMEM(o.shape, o.dtype) for o in sent),
            *scratch,
            *sems,
        ],
        input_output_aliases=aliases or {},
        compiler_params=pltpu.CompilerParams(vmem_limit_bytes=VMEM_LIMIT),
        cost_estimate=pl.CostEstimate(
            flops=int(1000 + 1.1e9 * SPAN.get(name, 0)), bytes_accessed=1000, transcendentals=0
        ),
        name=name,
    )(*args, *after)


def start(copies):
    for copy in copies:
        copy.start()


def wait(copies):
    for copy in copies:
        copy.wait()


PIECES = 7


def piece_refs(pieces):
    own, bx, by, dx, dy, near, far = pieces
    return (own, bx, by, dx, dy, near.at[0], near.at[1], near.at[2], far.at[0], far.at[1])


def piece_slots(place):
    c, x, y = place[0], place[1], place[2]
    across = 2 * (1 - y) + (1 - x)
    slots = ((2 * y + x, 0, 4), (2 * y + 1 - x, 0, 4), (2 * (1 - y) + x, 0, 4), (across, 0, 2), (across, 2, 4))
    return [(half, *slot) for half in (c, 1 - c) for slot in slots]


def panel_copies(pieces, base, place, dst, sems, row_at, rows):
    copies = []
    for n, (ref, (half, at, low, high)) in enumerate(zip(piece_refs(pieces), piece_slots(place))):
        cols = pl.ds(pl.multiple_of(half * HALF, HALF), HALF)
        first = row_at + (base if n < 3 else 0)
        copies.append(
            pltpu.make_async_copy(
                ref.at[:, first : first + rows, :], dst.at[low:high, at, :, cols], sems.at[n]
            )
        )
    return copies


def fill_bias(bias, lens, buck):
    bucket = buck[0]
    key = lax.broadcasted_iota(jnp.int32, (T, T), 0)
    query = lax.broadcasted_iota(jnp.int32, (T, T), 1)
    shift = bucket + 7
    same = lax.shift_right_logical(key, shift) == lax.shift_right_logical(query, shift)
    position = jnp.bitwise_and(key, lax.shift_left(jnp.int32(SLOT), bucket) - 1)
    slot = lax.shift_right_logical(key, 7)
    length = jnp.where(
        slot < 2,
        jnp.where(slot == 0, lens[0], lens[1]),
        jnp.where(slot == 2, lens[2], lens[3]),
    )
    bias[...] = jnp.where(same & (position < length), 0.0, NEGATIVE)


def first_tokens(buck, low, size):
    span = lax.shift_left(jnp.int32(SLOT), buck[0])
    token = lax.broadcasted_iota(jnp.int32, (size, 1), 0) + low
    return jnp.bitwise_and(token, span - 1) == 0


def halves(block):
    lane = lax.broadcasted_iota(jnp.int32, block.shape, 1)
    zero = jnp.zeros_like(block)
    return jnp.where(lane < HD, block, zero), jnp.where(lane < HD, zero, block)


def row_loop(size, body):
    if size == T:
        return body(pl.ds(0, T))

    def step(i, carry):
        body(pl.ds(pl.multiple_of(i * size, size), size))
        return carry

    lax.fori_loop(0, T // size, step, 0)


def attend_kernel(base, *refs):
    x, lens, buck, place = refs[:4]
    pieces, refs = refs[4 : 4 + PIECES], refs[4 + PIECES :]
    flow, (wq, bias, heap, sems) = refs[:5], refs[5:]
    p, m, xm, stat, vec = (ref.held for ref in flow)
    copies = [
        panel_copies(pieces, base, place, wq.at[j], sems.at[j], j * ROWS, ROWS) for j in range(3)
    ]
    smalls = []
    for n, piece in enumerate(piece_refs(pieces)):
        at = (0, 4, 8, 12, 14)[n % 5] + 16 * (n // 5)
        count = 4 if n % 5 < 3 else 2
        first = SMALL_AT + (base if n < 3 else 0)
        smalls.append(
            pltpu.make_async_copy(
                piece.at[:, first : first + 32, :], heap.at[at : at + count], sems.at[3, n]
            )
        )
    start(smalls)
    for group in copies:
        start(group)
    fill_bias(bias, lens, buck)
    x = x()
    xm[0] = x[...].T
    wait(smalls)
    total = heap[0].astype(F32)
    for n in range(1, 32):
        total = total + heap[n].astype(F32)
    vec[...] = jnp.concatenate([total[:16], total[16:]], axis=1)
    flow[4].send()
    for j in range(3):
        wait(copies[j])
        weight = wq[j].reshape(D, D)
        for half in range(2):
            rows = slice(half * 256, half * 256 + 256)
            out = dot(x[rows, :], weight)
            if j != 1:
                out = out + (vec[2:3, :] if j == 0 else vec[3:4, :])
            out = out.astype(BF16)
            for s in range(6):
                p[6 * j + s, rows, :] = out[:, 128 * s : 128 * s + 128]
        flow[0].send(slice(6 * j, 6 * j + 6))

    def pair(i):
        q = p[i] * jnp.asarray(HD**-0.5, BF16)
        v_t = p[12 + i].T
        both = dot_rt(jnp.concatenate(halves(p[6 + i]), axis=0), q)
        mixed = []
        for a in range(2):
            scores = both[T * a : T * a + T] + bias[...]
            peak = jnp.max(scores, axis=0, keepdims=True)
            weights = jnp.exp(scores - peak)
            inverse = 1.0 / jnp.sum(weights, axis=0, keepdims=True)
            stat[2 * i + a, 0:1, :] = peak
            stat[2 * i + a, 1:2, :] = inverse
            soft = (weights * inverse).astype(BF16)
            mixed.append(dot(v_t[HD * a : HD * a + HD, :], soft))
        mixed = jnp.concatenate(mixed, axis=0)
        xm[1, pl.ds(pl.multiple_of(i * 128, 128), 128), :] = mixed.astype(BF16)
        m[i] = mixed.T.astype(BF16)

    def pairs(n, carry):
        for k in range(3):
            pair(3 * n + k)
        return carry

    lax.fori_loop(0, 2, pairs, 0)


def attend(x, lens, buck, place, part, after):
    pieces, base = part
    return call(
        functools.partial(attend_kernel, base),
        "attend",
        (x, lens, buck, place, *pieces),
        "isss" + "h" * PIECES,
        [
            sds((18, T, 128), BF16),
            sds((6, T, 128), BF16),
            sds((2, D, T), BF16),
            sds((12, 8, T), F32),
            sds((16, D), F32),
        ],
        "o" * 5,
        [
            pltpu.VMEM((3, 4, 4, ROWS, D), BF16),
            pltpu.VMEM((T, T), F32),
            pltpu.VMEM((32, 32, HALF), BF16),
            pltpu.SemaphoreType.DMA((4, 10)),
        ],
        after,
    )


def unit_norm(resid):
    center = jnp.mean(resid, axis=-1, keepdims=True)
    shifted = resid - center
    spread = jnp.mean(shifted * shifted, axis=-1, keepdims=True)
    inverse = lax.rsqrt(spread + EPSILON)
    return shifted * inverse, inverse


def feed_kernel(encoder, base_a, base_b, *refs):
    x, m, vec, place = refs[:4]
    refs = refs[4:]
    if encoder:
        cor, buck = refs[:2]
        refs = refs[2:]
    pieces_a, pieces_b, refs = refs[:PIECES], refs[PIECES : 2 * PIECES], refs[2 * PIECES :]
    flow, refs = refs[: 8 if encoder else 6], refs[8 if encoder else 6 :]
    out, n1, r1, n2, r2, gp = (ref.held for ref in flow[:6])
    if encoder:
        xd, xdl = (ref.held for ref in flow[6:])
    y1t_out, gt_out, give_out, wo, wu, wd, scr, y1, y1l, g, y1t, gt, sems, out_sems = refs
    c = place[0]
    sent = []

    def send(source, target):
        copy = pltpu.make_async_copy(source, target, out_sems.at[len(sent)])
        copy.start()
        sent.append(copy)

    o_copies = panel_copies(pieces_a, base_a, place, wo, sems.at[0], O_AT, ROWS)
    u_copies = [
        panel_copies(pieces_b, base_b, place, wu.at[j], sems.at[1 + j], j * ROWS, ROWS)
        for j in range(4)
    ]
    d_copies = panel_copies(pieces_b, base_b, place, wd, sems.at[5], D_AT, DROWS)
    start(o_copies)
    for group in u_copies:
        start(group)
    start(d_copies)
    wait(o_copies)
    m, x, vec = m(), x(), vec()
    weight = wo[...].reshape(D, D)
    for half in range(2):
        rows = slice(half * 256, half * 256 + 256)
        left = jnp.concatenate([m[s, rows, :] for s in range(6)], axis=1)
        scr[rows, :] = dot(left, weight)

    def first(rows):
        resid = x[rows, :].astype(F32) + (scr[rows, :] + vec[4:5, :])
        unit, inverse = unit_norm(resid)
        n1[rows, :] = unit
        r1[rows, :] = jnp.broadcast_to(inverse, (inverse.shape[0], 128))
        normed = unit * vec[0:1, :] + vec[5:6, :]
        y1[rows, :] = normed
        y1l[rows, :] = normed.astype(BF16)

    row_loop(NORM_ROWS, first)
    y1t[...] = y1l[...].T.reshape(8, 96, T)
    send(y1t, y1t_out)
    send(y1t, give_out.at[0:8])
    for n in (1, 2):
        flow[n].send()

    for j in range(4):
        wait(u_copies[j])

        def up(rows, j=j):
            left = y1l[rows, :]
            for k in range(3):
                cols = slice(256 * k, 256 * k + 256)
                right = wu[j, :, :, :, cols].reshape(D, 256)
                hidden = dot(left, right) + vec[8 + j : 9 + j, cols]
                cdf = 0.5 * (1.0 + lax.erf(hidden * (0.5**0.5)))
                g[j, rows, cols] = (hidden * cdf).astype(BF16)
                density = jnp.exp(hidden * hidden * -0.5) * 0.3989422804014327
                gp[j, rows, cols] = (cdf + hidden * density).astype(BF16)

        row_loop(128, up)
        gt[j] = g[j].T.reshape(4, 2, 96, T)
        send(gt.at[j, :, c], gt_out.at[j])
        send(gt.at[j, :, 1 - c], give_out.at[8 + 4 * j : 12 + 4 * j])
        flow[5].send(j)

    wait(d_copies)
    if encoder:
        cor = cor()
    for half in range(2):
        rows = slice(half * 256, half * 256 + 256)
        total = dot(g[0, rows, :], wd[0].reshape(D, D))
        for j in range(1, 4):
            total = total + dot(g[j, rows, :], wd[j].reshape(D, D))
        scr[rows, :] = total

    def second(rows):
        resid = y1[rows, :] + (scr[rows, :] + vec[6:7, :])
        unit, inverse = unit_norm(resid)
        n2[rows, :] = unit
        r2[rows, :] = jnp.broadcast_to(inverse, (inverse.shape[0], 128))
        result = unit * vec[1:2, :] + vec[7:8, :]
        out[rows, :] = result.astype(BF16)
        if encoder:
            mixed = jnp.where(
                first_tokens(buck, rows.start, NORM_ROWS), result, cor[rows, :].astype(F32)
            )
            xd[rows, :] = mixed
            xdl[rows, :] = mixed.astype(BF16)

    row_loop(NORM_ROWS, second)
    wait(sent)


def feed(encoder, x, m, vec, place, part_a, part_b, after, cor=None, buck=None):
    (pieces_a, base_a), (pieces_b, base_b) = part_a, part_b
    args, kinds = (x, m, vec, place), "iiis"
    outs = [
        sds((T, D), BF16),
        sds((T, D), F32),
        sds((T, 128), F32),
        sds((T, D), F32),
        sds((T, 128), F32),
        sds((4, T, D), BF16),
    ]
    if encoder:
        args, kinds = (*args, cor, buck), kinds + "is"
        outs = [*outs, sds((T, D), F32), sds((T, D), BF16)]
    return call(
        functools.partial(feed_kernel, encoder, base_a, base_b),
        "feed",
        (*args, *pieces_a, *pieces_b),
        kinds + "h" * (2 * PIECES),
        [*outs, sds((8, 96, T), BF16), sds((4, 4, 96, T), BF16), sds((24, 96, T), BF16)],
        "o" * len(outs) + "hhh",
        [
            pltpu.VMEM((4, 4, ROWS, D), BF16),
            pltpu.VMEM((4, 4, 4, ROWS, D), BF16),
            pltpu.VMEM((4, 4, DROWS, D), BF16),
            pltpu.VMEM((T, D), F32),
            pltpu.VMEM((T, D), F32),
            pltpu.VMEM((T, D), BF16),
            pltpu.VMEM((4, T, D), BF16),
            pltpu.VMEM((8, 96, T), BF16),
            pltpu.VMEM((4, 4, 2, 96, T), BF16),
            pltpu.SemaphoreType.DMA((6, 10)),
            pltpu.SemaphoreType.DMA((10,)),
        ],
        after,
    )


def norm_back(grad, unit, inverse, gain):
    scaled = grad * gain
    mean = jnp.mean(scaled, axis=-1, keepdims=True)
    along = jnp.mean(scaled * unit, axis=-1, keepdims=True)
    return inverse * (scaled - mean - unit * along)


def column_sum(value):
    return jnp.sum(value, axis=0, keepdims=True)


def down_grads(put, place, gt, dr2l, dr2l_other, given, held, sems):
    copies = [
        pltpu.make_async_copy(given.at[8 + 4 * j : 12 + 4 * j], held.at[4 * j : 4 * j + 4], sems.at[j])
        for j in range(4)
    ]
    start(copies)
    gt, dr2l, dr2l_other = gt(), dr2l(), dr2l_other()
    for j in range(4):
        mine = dot(gt[j].reshape(4 * 96, T), dr2l[...])
        copies[j].wait()
        other = dot(held[4 * j : 4 * j + 4].reshape(4 * 96, T), dr2l_other[...])
        put(j, slice(0, 96), (mine + other).reshape(4, 96, D))


def up_grads(put, place, y1t, dul, dul_other, given, held, sems):
    copy = pltpu.make_async_copy(given.at[0:8], held.at[0:8], sems.at[0])
    copy.start()
    y1t, dul = y1t(), dul()
    left = y1t[...].reshape(D, T)
    for j in range(4):
        mine = dot(left, dul[j])
        if j == 0:
            copy.wait()
            dul_other = dul_other()
            left_other = held[0:8].reshape(D, T)
        other = dot(left_other, dul_other[j])
        put(None, slice(j * ROWS, j * ROWS + ROWS), (mine + other).reshape(4, 4, ROWS, HALF))


def attend_grads(put, place, xm, xm_other, part, part_other, small):
    xm, part = xm(), part()
    for j in range(4):
        kind = 0 if j < 3 else 1
        mine = dot(xm[kind], jnp.concatenate([part[s] for s in range(3 * j, 3 * j + 3)], axis=1))
        if j == 0:
            xm_other, part_other = xm_other(), part_other()
        right = jnp.concatenate([part_other[s] for s in range(3 * j, 3 * j + 3)], axis=1)
        other = dot(xm_other[kind], right)
        put(None, slice(j * ROWS, j * ROWS + ROWS), (mine + other).reshape(4, 4, ROWS, HALF))
    other = [part_other[12, 16 * k : 16 * k + 16, :].astype(F32) for k in range(6)]
    small = small()[...] + jnp.concatenate(other, axis=1)
    small = jnp.concatenate([small[:, :HALF], small[:, HALF:]], axis=0)
    put(None, slice(SMALL_AT, SMALL_AT + 32), jnp.broadcast_to(small, (4, 4, 32, HALF)))


def keep_kernel(fill, count, *refs):
    place, a_send, a_keep, b_send, b_keep, block, out_sems = refs[count : count + 7]

    def put(z, at, value):
        block[slice(None) if z is None else z, :, at] = value.astype(BF16)

    fill(put, place, *refs[:count], *refs[count + 7 :])
    x, y = place[1], place[2]
    copies = []
    for dst, side in ((a_send, 1 - x), (a_keep, x)):
        for row in range(2):
            copies.append((block.at[0:2, 2 * row + side], dst.at[row]))
    for dst, side in ((b_send, 1 - y), (b_keep, y)):
        for col in range(2):
            copies.append((block.at[2:4, 2 * side + col], dst.at[col]))
    copies = [
        pltpu.make_async_copy(src, dst, out_sems.at[n]) for n, (src, dst) in enumerate(copies)
    ]
    start(copies)
    wait(copies)


def keep(fill, inputs, kinds, shape, place, scratch, after):
    return call(
        functools.partial(keep_kernel, fill, len(inputs)),
        "keep_grads",
        (*inputs, place),
        kinds + "s",
        [sds((2, 2, *shape), BF16)] * 4,
        "hhhh",
        [pltpu.VMEM((4, 4, *shape), BF16), pltpu.SemaphoreType.DMA((8,)), *scratch],
        after,
    )


def add_next_kernel(a_keep, a_got, b_keep, b_got, place, a_next, b_next, blocks, sems):
    x, y = place[1], place[2]
    refs = (a_keep.at[1 - y], a_got.at[1 - y], b_keep.at[1 - x], b_got.at[1 - x])
    copies = [pltpu.make_async_copy(ref, blocks.at[n], sems.at[n]) for n, ref in enumerate(refs)]
    start(copies)
    for n, out in enumerate((a_next, b_next)):
        wait(copies[2 * n : 2 * n + 2])
        out.held[...] = (blocks[2 * n].astype(F32) + blocks[2 * n + 1].astype(F32)).astype(BF16)
        out.send()


def add_next(a_keep, a_got, b_keep, b_got, place, after):
    shape = a_keep.shape[2:]
    return call(
        add_next_kernel,
        "add_next",
        (a_keep, a_got, b_keep, b_got, place),
        "hhhhs",
        [sds((2, *shape), BF16)] * 2,
        "oo",
        [pltpu.VMEM((4, 2, *shape), BF16), pltpu.SemaphoreType.DMA((4,))],
        after,
    )


def add_last_kernel(a_keep, a_got, a_last, b_keep, b_got, b_last, place, line, blocks, sems):
    x, y = place[1], place[2]
    refs = (a_keep.at[y], a_got.at[y], a_last, b_keep.at[x], b_got.at[x], b_last)
    copies = [pltpu.make_async_copy(ref, blocks.at[n], sems.at[n]) for n, ref in enumerate(refs)]
    start(copies)
    for n in range(2):
        wait(copies[3 * n : 3 * n + 3])
        total = blocks[3 * n].astype(F32) + blocks[3 * n + 1].astype(F32)
        line.held[2 * n : 2 * n + 2] = (total + blocks[3 * n + 2].astype(F32)).astype(BF16)
        line.send(slice(2 * n, 2 * n + 2))


def add_last(a_keep, a_got, a_last, b_keep, b_got, b_last, place, after):
    shape = a_keep.shape[2:]
    (line,) = call(
        add_last_kernel,
        "add_last",
        (a_keep, a_got, a_last, b_keep, b_got, b_last, place),
        "hhhhhhs",
        [sds((4, *shape), BF16)],
        "o",
        [pltpu.VMEM((6, 2, *shape), BF16), pltpu.SemaphoreType.DMA((6,))],
        after,
    )
    return line


def down_back_kernel(encoder, *refs):
    cot, n2, r2, vec = refs[:4]
    refs = refs[4:]
    if encoder:
        dxd, buck = refs[:2]
        refs = refs[2:]
    dr2, dr2l, small = (ref.held for ref in refs)
    small[...] = jnp.zeros_like(small)
    cot, n2, r2, vec = cot(), n2(), r2(), vec()
    if encoder:
        dxd = dxd()

    def second(rows):
        grad = cot[rows, :].astype(F32)
        if encoder:
            grad = grad + jnp.where(first_tokens(buck, rows.start, NORM_ROWS), dxd[rows, :], 0.0)
        unit = n2[rows, :]
        resid = norm_back(grad, unit, r2[rows, 0:1], vec[1:2, :])
        small[1:2, :] += column_sum(grad * unit)
        small[7:8, :] += column_sum(grad)
        small[6:7, :] += column_sum(resid)
        dr2[rows, :] = resid
        dr2l[rows, :] = resid.astype(BF16)

    row_loop(NORM_ROWS, second)


def down_back(encoder, cot, n2, r2, vec, after, dxd=None, buck=None):
    args, kinds = (cot, n2, r2, vec), "iiii"
    if encoder:
        args, kinds = (*args, dxd, buck), kinds + "is"
    return call(
        functools.partial(down_back_kernel, encoder),
        "down_back",
        args,
        kinds,
        [sds((T, D), F32), sds((T, D), BF16), sds((16, D), F32)],
        "ooo",
        [],
        after,
    )


def half_cols(h):
    return pl.ds(pl.multiple_of(h * HALF, HALF), HALF)


def up_back_kernel(base, *refs):
    dr2l, gp, place = refs[:3]
    pieces, refs = refs[3 : 3 + PIECES], refs[3 + PIECES :]
    small_out, keep_out, give_out, dul, wd, sems, out_sems = refs
    small = small_out.held
    c = place[0]
    copies = panel_copies(pieces, base, place, wd, sems, D_AT, DROWS)
    start(copies)
    small[...] = jnp.zeros_like(small)
    dr2l, gp = dr2l(), gp()
    wait(copies)
    sent = []
    for j in range(4):

        def up(rows, j=j):
            left = dr2l[rows, :]
            weight = wd[j].reshape(D, D)
            for k in range(3):
                cols = slice(256 * k, 256 * k + 256)
                grad = dot_rt(left, weight[cols, :])
                hidden = (grad * gp[j, rows, cols].astype(F32)).astype(BF16)
                dul[j, rows, cols] = hidden
                small[8 + j : 9 + j, cols] += column_sum(hidden.astype(F32))

        row_loop(256, up)
        for n, (half, out) in enumerate(((1 - c, give_out), (c, keep_out))):
            sent.append(
                pltpu.make_async_copy(
                    dul.at[j, :, half_cols(half)], out.at[j], out_sems.at[2 * j + n]
                )
            )
            sent[-1].start()
    wait(sent)


def up_back(dr2l, gp, place, part_b, after):
    pieces, base = part_b
    return call(
        functools.partial(up_back_kernel, base),
        "up_back",
        (dr2l, gp, place, *pieces),
        "iis" + "h" * PIECES,
        [sds((16, D), F32), sds((4, T, HALF), BF16), sds((4, T, HALF), BF16)],
        "ohh",
        [
            pltpu.VMEM((4, T, D), BF16),
            pltpu.VMEM((4, 4, DROWS, D), BF16),
            pltpu.SemaphoreType.DMA((10,)),
            pltpu.SemaphoreType.DMA((8,)),
        ],
        after,
    )


def mid_back_kernel(base_a, base_b, *refs):
    dul_keep, dul_give, dr2, n1, r1, vec, place = refs[:7]
    pieces_a, pieces_b, refs = refs[7 : 7 + PIECES], refs[7 + PIECES : 7 + 2 * PIECES], refs[7 + 2 * PIECES :]
    flow = refs[:4]
    dr1, dr1l, dml, small = (ref.held for ref in flow)
    wo, wu, scr, dul, low_rows, sems = refs[4:]
    c = place[0]
    dul_copies = [
        [
            pltpu.make_async_copy(
                source.at[j], dul.at[j, :, half_cols(half)], sems.at[5, 2 * j + n]
            )
            for n, (half, source) in enumerate(((c, dul_keep), (1 - c, dul_give)))
        ]
        for j in range(4)
    ]
    u_copies = [
        panel_copies(pieces_b, base_b, place, wu.at[j], sems.at[1 + j], j * ROWS, ROWS)
        for j in range(4)
    ]
    o_copies = panel_copies(pieces_a, base_a, place, wo, sems.at[0], O_AT, ROWS)
    for j in range(4):
        start(dul_copies[j])
        start(u_copies[j])
    start(o_copies)
    small[...] = jnp.zeros_like(small)
    dr2 = dr2()
    for j in range(4):
        wait(dul_copies[j])
        wait(u_copies[j])
        for half in range(2):
            rows = slice(half * 256, half * 256 + 256)
            part = dot_rt(dul[j, rows, :], wu[j].reshape(D, D))
            scr[rows, :] = (dr2[rows, :] if j == 0 else scr[rows, :]) + part

    n1, r1, vec = n1(), r1(), vec()

    def first(rows):
        grad = scr[rows, :]
        unit = n1[rows, :]
        resid = norm_back(grad, unit, r1[rows, 0:1], vec[0:1, :])
        small[0:1, :] += column_sum(grad * unit)
        small[5:6, :] += column_sum(grad)
        small[4:5, :] += column_sum(resid)
        dr1[rows, :] = resid
        low = resid.astype(BF16)
        low_rows[rows, :] = low
        for s in range(6):
            dr1l[s, rows, :] = low[:, 128 * s : 128 * s + 128]

    row_loop(NORM_ROWS, first)
    for n in (0, 1, 3):
        flow[n].send()
    wait(o_copies)
    weight = wo[...].reshape(D, D)
    for half in range(2):
        rows = slice(half * 256, half * 256 + 256)
        out = dot_rt(low_rows[rows, :], weight).astype(BF16)
        for s in range(6):
            dml[s, rows, :] = out[:, 128 * s : 128 * s + 128]


def mid_back(dul_keep, dul_give, dr2, n1, r1, vec, place, part_a, part_b, after):
    (pieces_a, base_a), (pieces_b, base_b) = part_a, part_b
    return call(
        functools.partial(mid_back_kernel, base_a, base_b),
        "mid_back",
        (dul_keep, dul_give, dr2, n1, r1, vec, place, *pieces_a, *pieces_b),
        "hhiiiis" + "h" * (2 * PIECES),
        [sds((T, D), F32), sds((6, T, 128), BF16), sds((6, T, 128), BF16), sds((16, D), F32)],
        "oooo",
        [
            pltpu.VMEM((4, 4, ROWS, D), BF16),
            pltpu.VMEM((4, 4, 4, ROWS, D), BF16),
            pltpu.VMEM((T, D), F32),
            pltpu.VMEM((4, T, D), BF16),
            pltpu.VMEM((T, D), BF16),
            pltpu.SemaphoreType.DMA((6, 10)),
        ],
        after,
    )


def attend_back_kernel(*refs):
    p, dml, stat, dr1l, small_a, small_b, small_c, lens, buck, place = refs[:10]
    keep_out, give_out, small_out, dpl, slab, bias, out_sems = refs[10:]
    small = small_out.held
    c = place[0]
    fill_bias(bias, lens, buck)
    p, dml, stat = p(), dml(), stat()
    scale = jnp.asarray(HD**-0.5, BF16)
    small[...] = small_a()[...] + small_b()[...] + small_c()[...]

    def pair(i):
        q = p[i] * scale
        k_t = p[6 + i].T
        both = dot_rt(jnp.concatenate(halves(p[6 + i]), axis=0), q)
        grad = dml[i]
        dboth = dot_rt(jnp.concatenate(halves(p[12 + i]), axis=0), grad)
        softs, dscores, dq = [], [], []
        for a in range(2):
            scores = both[T * a : T * a + T] + bias[...]
            peak = stat[2 * i + a, 0:1, :]
            inverse = stat[2 * i + a, 1:2, :]
            soft = jnp.exp(scores - peak) * inverse
            dsoft = dboth[T * a : T * a + T]
            total = jnp.sum(soft * dsoft, axis=0, keepdims=True)
            dscore = (soft * (dsoft - total)).astype(BF16)
            softs.append(soft.astype(BF16))
            dscores.append(dscore)
            dq.append(dot(k_t[HD * a : HD * a + HD, :], dscore))
        grads, queries = halves(grad), halves(q)
        dv = (dot(softs[0], grads[0]) + dot(softs[1], grads[1])).astype(BF16)
        dk = (dot(dscores[0], queries[0]) + dot(dscores[1], queries[1])).astype(BF16)
        dq = (jnp.concatenate(dq, axis=0).T * (HD**-0.5)).astype(BF16)
        dpl[i] = dq
        dpl[6 + i] = dk
        dpl[12 + i] = dv
        cols = pl.ds(pl.multiple_of(i * 128, 128), 128)
        small[2:3, cols] = column_sum(dq.astype(F32))
        small[3:4, cols] = column_sum(dv.astype(F32))

    def pairs(n, carry):
        for k in range(ATTEND_BACK_PAIRS):
            pair(ATTEND_BACK_PAIRS * n + k)
        return carry

    lax.fori_loop(0, 6 // ATTEND_BACK_PAIRS, pairs, 0)
    slab[...] = jnp.zeros_like(slab)
    for k in range(6):
        slab[16 * k : 16 * k + 16, :] = small[:, 128 * k : 128 * k + 128].astype(BF16)
    dr1l = dr1l()
    sent = []
    for half, out in ((1 - c, give_out), (c, keep_out)):
        for j in range(3):
            sent.append((dpl.at[pl.ds(6 * j + 3 * half, 3)], out.at[3 * j : 3 * j + 3]))
        sent.append((dr1l.at[pl.ds(3 * half, 3)], out.at[9:12]))
        sent.append((slab, out.at[12]))
    sent = [pltpu.make_async_copy(src, dst, out_sems.at[n]) for n, (src, dst) in enumerate(sent)]
    start(sent)
    wait(sent)


def attend_back(p, dml, stat, dr1l, smalls, lens, buck, place, after):
    return call(
        attend_back_kernel,
        "attend_back",
        (p, dml, stat, dr1l, *smalls, lens, buck, place),
        "iiiiiiisss",
        [sds((13, T, 128), BF16), sds((13, T, 128), BF16), sds((16, D), F32)],
        "hho",
        [
            pltpu.VMEM((18, T, 128), BF16),
            pltpu.VMEM((T, 128), BF16),
            pltpu.VMEM((T, T), F32),
            pltpu.SemaphoreType.DMA((10,)),
        ],
        after,
    )


def input_back_kernel(encoder, base, *refs):
    dpl_keep, dpl_give, dr1, place = refs[:4]
    refs = refs[4:]
    if not encoder:
        buck, refs = refs[0], refs[1:]
    pieces, refs = refs[:PIECES], refs[PIECES:]
    if not encoder:
        dxd_out, refs = refs[0], refs[1:]
        dxd = dxd_out.held
    out_flow, dpl, wq, sems = refs
    out = out_flow.held
    c = place[0]
    copies = []
    for j in range(3):
        group = panel_copies(pieces, base, place, wq.at[j], sems.at[j], j * ROWS, ROWS)
        for n, (half, source) in enumerate(((c, dpl_keep), (1 - c, dpl_give))):
            group.append(
                pltpu.make_async_copy(
                    source.at[3 * j : 3 * j + 3], dpl.at[pl.ds(6 * j + 3 * half, 3)], sems.at[j, 10 + n]
                )
            )
        start(group)
        copies.append(group)
    dr1 = dr1()
    for group in copies:
        wait(group)
    for half in range(2):
        rows = slice(half * 256, half * 256 + 256)
        total = dr1[rows, :]
        for j in range(3):
            left = jnp.concatenate([dpl[6 * j + s, rows, :] for s in range(6)], axis=1)
            total = total + dot_rt(left, wq[j].reshape(D, D))
        if encoder:
            out[rows, :] = total.astype(BF16)
        else:
            dxd[rows, :] = total
            out[rows, :] = jnp.where(first_tokens(buck, half * 256, 256), 0.0, total).astype(BF16)
            dxd_out.send(rows)
        out_flow.send(rows)


def input_back(encoder, dpl_keep, dpl_give, dr1, place, part_a, after, buck=None):
    pieces, base = part_a
    args, kinds = (dpl_keep, dpl_give, dr1, place), "hhis"
    outs = [sds((T, D), BF16)]
    if not encoder:
        args, kinds = (*args, buck), kinds + "s"
        outs = [sds((T, D), F32), *outs]
    return call(
        functools.partial(input_back_kernel, encoder, base),
        "input_back",
        (*args, *pieces),
        kinds + "h" * PIECES,
        outs,
        "o" * len(outs),
        [
            pltpu.VMEM((18, T, 128), BF16),
            pltpu.VMEM((3, 4, 4, ROWS, D), BF16),
            pltpu.SemaphoreType.DMA((3, 12)),
        ],
        after,
    )


def gate_kernel(*refs):
    pass


def gate(values, after):
    outs = call(
        gate_kernel,
        "gate",
        tuple(values),
        "h" * len(values),
        [sds(v.shape, v.dtype) for v in values],
        "h" * len(values),
        [],
        after,
        {n: n for n in range(len(values))},
    )
    return list(outs)


def split_kernel(base, own, bx, by, ax, ay, near, held, sems):
    rows = held.shape[2]
    part = slice(base, base + rows)
    into = [
        pltpu.make_async_copy(ref.at[:, part], held.at[n], sems.at[n])
        for n, ref in ((1, bx), (2, by), (0, own))
    ]
    start(into)
    out = []
    for k, n in enumerate((1, 2, 0)):
        into[k].wait()
        out.append(pltpu.make_async_copy(held.at[n], near.at[n], sems.at[3 + n]))
        if n:
            half = slice(0, 2) if n == 1 else slice(2, 4)
            out.append(pltpu.make_async_copy(held.at[n, half], (ax, ay)[n - 1], sems.at[5 + n]))
        start(out[-2:] if n else out[-1:])
    wait(out)


def split(base, rows, own, bx, by, after):
    return call(
        functools.partial(split_kernel, base),
        "split",
        (own, bx, by),
        "hhh",
        [sds((2, rows, HALF), BF16)] * 2 + [sds((3, 4, rows, HALF), BF16)],
        "hhh",
        [pltpu.VMEM((3, 4, rows, HALF), BF16), pltpu.SemaphoreType.DMA((8,))],
        after,
    )


def join_kernel(dx, dy, far, held, sems):
    into = [pltpu.make_async_copy(ref, held.at[n], sems.at[n]) for n, ref in enumerate((dx, dy))]
    out = [pltpu.make_async_copy(held.at[n], far.at[n], sems.at[2 + n]) for n in range(2)]
    start(into)
    for n in range(2):
        into[n].wait()
        out[n].start()
    wait(out)


def join(dx, dy, after):
    (far,) = call(
        join_kernel,
        "join",
        (dx, dy),
        "hh",
        [sds((2, *dx.shape), BF16)],
        "h",
        [pltpu.VMEM((2, *dx.shape), BF16), pltpu.SemaphoreType.DMA((4,))],
        after,
    )
    return far


AXES = ("z", "y", "x", "c", "e")


def swap(value, axis):
    return lax.ppermute(value, axis, [(0, 1), (1, 0)])


def pick(value, index, axis):
    return lax.dynamic_index_in_dim(value, index, axis, keepdims=False)


class Line:
    def __init__(self, own):
        self.own = own

    def plane(self, after):
        (self.own,) = gate([self.own], after)
        self.bx, self.by = swap(self.own, "x"), swap(self.own, "y")
        return (self.own,)


class Gather:
    def __init__(self, line, base, rows):
        self.line, self.base, self.rows = line, base, rows

    def forward(self, after):
        line = self.line
        ax, ay, near = split(self.base, self.rows, line.own, line.bx, line.by, after)
        self.dx, self.dy = swap(ax, "y"), swap(ay, "x")
        self.near = swap(near, "c")
        return (ax,)

    def across(self, after):
        line = self.line
        far = join(self.dx, self.dy, after)
        pieces = (line.own, line.bx, line.by, self.dx, self.dy, self.near, swap(far, "c"))
        self.part = (pieces, self.base)
        return (far,)


class Scatter:
    def __init__(self, fill, kinds, shape, place, scratch=()):
        self.fill, self.kinds, self.shape, self.place, self.scratch = fill, kinds, shape, place, scratch

    def keep(self, inputs, after):
        a_send, self.a_keep, b_send, self.b_keep = keep(
            self.fill, inputs, self.kinds, self.shape, self.place, self.scratch, after
        )
        self.a_got, self.b_got = swap(a_send, "x"), swap(b_send, "y")
        return (a_send,)

    def next(self, after):
        a_next, b_next = add_next(
            self.a_keep, self.a_got, self.b_keep, self.b_got, self.place, after
        )
        self.a_last, self.b_last = swap(a_next, "y"), swap(b_next, "x")
        return (a_next,)

    def last(self, after):
        line = add_last(
            self.a_keep, self.a_got, self.a_last, self.b_keep, self.b_got, self.b_last, self.place, after
        )
        self.total = lax.psum_scatter(line, "z", scatter_dimension=0, tiled=False)
        return (line,)

    def end(self, after):
        (self.total,) = gate([self.total], after)
        return (self.total,)


def scatters(place):
    held = (pltpu.VMEM((16, 96, T), BF16), pltpu.SemaphoreType.DMA((4,)))
    return (
        Scatter(down_grads, "iiih", (96, D), place, held),
        Scatter(up_grads, "iiih", (4 * ROWS, HALF), place, held),
        Scatter(attend_grads, "iiiii", (PART_A, HALF), place),
    )


def pack_weights(qkv, out, up, down, gains, biases, up_b, c, device):
    rows = out.shape[1]
    panels = jnp.concatenate([qkv, out, up], axis=2).reshape(2, rows, 8, 2, HALF)
    panels = jnp.transpose(panels, (0, 3, 2, 1, 4)).reshape(2, 2, 8 * rows, HALF)
    downs = jnp.transpose(down.reshape(2, 4 * rows, 2, HALF), (0, 2, 1, 3))
    both = jnp.concatenate([panels, downs], axis=2)
    mine = pick(both, c, 1)
    got = swap(pick(both, 1 - c, 1), "c")
    low = jnp.where(c == 0, mine, got)
    high = jnp.where(c == 0, got, mine)
    panels = jnp.stack(
        [low[:, : 8 * rows].reshape(2, 8, rows, HALF), high[:, : 8 * rows].reshape(2, 8, rows, HALF)],
        axis=2,
    ).reshape(2, 16 * rows, HALF)
    downs = jnp.concatenate([low[:, 8 * rows :], high[:, 8 * rows :]], axis=1)
    small = jnp.zeros((2, 16, D), BF16)
    small = lax.dynamic_update_slice(
        small, jnp.concatenate([gains, biases], axis=1), (0, 0, device * rows)
    )
    small = lax.dynamic_update_slice(
        small, up_b[:, None, :], (0, 8 + device // 8, device % 8 * (4 * rows))
    )
    small = jnp.concatenate([small[:, :, :HALF], small[:, :, HALF:]], axis=1)
    part_a = jnp.concatenate([panels[:, : 8 * rows], small], axis=1)
    part_b = jnp.concatenate([panels[:, 8 * rows :], downs], axis=1)
    return part_a, part_b


def body(
    encoder_input,
    corrupted,
    lengths,
    buckets,
    qkv_weight,
    out_weight,
    up_weight,
    down_weight,
    norm_gains,
    bias_rows,
    up_bias,
    encoder_cot,
    decoder_cot,
):
    extra = lax.axis_size("e")
    weights = [qkv_weight, out_weight, up_weight, down_weight, norm_gains, bias_rows, up_bias]
    if extra > 1:
        weights = [
            lax.all_gather(w, "e", axis=at, tiled=True)
            for w, at in zip(weights, (1, 1, 1, 1, 2, 2, 1))
        ]
    rows = weights[1].shape[1]
    x, y, c = lax.axis_index("x"), lax.axis_index("y"), lax.axis_index("c")
    device = ((lax.axis_index("z") * 2 + y) * 2 + x) * 2 + c
    place = jnp.stack([c, x, y]).astype(jnp.int32)
    part_a, part_b = pack_weights(*weights, c, device)
    line_a0 = Line(lax.all_gather(part_a[0], "z", axis=0, tiled=False))
    tok = line_a0.plane(())
    line_b0 = Line(lax.all_gather(part_b[0], "z", axis=0, tiled=False))
    rest = jnp.concatenate([part_a[1], part_b[1]])
    line_1 = Line(lax.all_gather(rest, "z", axis=0, tiled=False))
    a0, b0 = Gather(line_a0, 0, PART_A), Gather(line_b0, 0, PART_B)
    a1, b1 = Gather(line_1, 0, PART_A), Gather(line_1, PART_A, PART_B)

    tok = a0.forward(tok)
    tok = a0.across(tok)
    tok = line_b0.plane(tok)
    p0, m0, xm0, stat0, vec0 = attend(encoder_input, lengths, buckets, place, a0.part, tok)
    xm0_other = swap(xm0, "c")
    tok = b0.forward((stat0,))
    tok = line_1.plane(tok)
    tok = b0.across(tok)
    enc_out, *saved0, xd, xdl, y1t0, gt0, give0 = feed(
        True, encoder_input, m0, vec0, place, a0.part, b0.part, tok, corrupted, buckets
    )
    given0 = swap(give0, "c")
    tok = a1.forward((enc_out, xm0_other))
    tok = a1.across(tok)
    tok = b1.forward(tok)
    p1, m1, xm1, stat1, vec1 = attend(xdl, lengths, buckets, place, a1.part, tok)
    xm1_other = swap(xm1, "c")
    tok = b1.across((stat1, given0))
    dec_out, *saved1, y1t1, gt1, give1 = feed(
        False, xd, m1, vec1, place, a1.part, b1.part, (*tok, xm1_other)
    )
    given1 = swap(give1, "c")

    n1, r1, n2, r2, gp = saved1
    d1, u1, q1 = scatters(place)
    dr2, dr2l, small_a = down_back(False, decoder_cot, n2, r2, vec1, (dec_out,))
    dr2l_other = swap(dr2l, "c")
    small_b, dul, dul_give = up_back(dr2l, gp, place, b1.part, (small_a,))
    dul_other = swap(dul_give, "c")
    tok = d1.keep((gt1, dr2l, dr2l_other, given1), (small_b,))
    dr1, dr1l, dml, small_c = mid_back(
        dul, dul_give, dr2, n1, r1, vec1, place, a1.part, b1.part, tok
    )
    tok = u1.keep((y1t1, dul, dul_other, given1), (small_c,))
    part, part_give, small = attend_back(
        p1, dml, stat1, dr1l, (small_a, small_b, small_c), lengths, buckets, place, tok
    )
    part_other = swap(part_give, "c")
    tok = d1.next((small,))
    tok = u1.next(tok)
    dxd, cor_grad = input_back(False, part, part_give, dr1, place, a1.part, tok, buckets)
    tok = d1.last((cor_grad,))
    tok = q1.keep((xm1, xm1_other, part, part_other, small), tok)

    n1, r1, n2, r2, gp = saved0
    d0, u0, q0 = scatters(place)
    dr2, dr2l, small_a = down_back(True, encoder_cot, n2, r2, vec0, tok, dxd, buckets)
    dr2l_other = swap(dr2l, "c")
    tok = u1.last((small_a,))
    small_b, dul, dul_give = up_back(dr2l, gp, place, b0.part, tok)
    dul_other = swap(dul_give, "c")
    tok = q1.next((small_b,))
    tok = d1.end(tok)
    tok = d0.keep((gt0, dr2l, dr2l_other, given0), tok)
    tok = q1.last(tok)
    dr1, dr1l, dml, small_c = mid_back(
        dul, dul_give, dr2, n1, r1, vec0, place, a0.part, b0.part, tok
    )
    tok = (small_c,)
    tok = u0.keep((y1t0, dul, dul_other, given0), tok)
    tok = u1.end(tok)
    part, part_give, small = attend_back(
        p0, dml, stat0, dr1l, (small_a, small_b, small_c), lengths, buckets, place, tok
    )
    part_other = swap(part_give, "c")
    tok = d0.next((small,))
    tok = u0.next(tok)
    tok = q1.end(tok)
    (enc_grad,) = input_back(True, part, part_give, dr1, place, a0.part, tok)
    tok = d0.last((enc_grad,))
    tok = q0.keep((xm0, xm0_other, part, part_other, small), tok)
    tok = u0.last(tok)
    tok = q0.next(tok)
    tok = d0.end(tok)
    tok = q0.last(tok)
    tok = u0.end(tok)

    attend_part = jnp.stack([q0.total, q1.total])
    panels = jnp.concatenate(
        [attend_part[:, :SMALL_AT], jnp.stack([u0.total, u1.total])], axis=1
    ).reshape(2, 8, 2, rows, HALF)
    mine = pick(panels, c, 2)
    got = swap(pick(panels, 1 - c, 2), "c")
    panels = jnp.concatenate([jnp.where(c == 0, mine, got), jnp.where(c == 0, got, mine)], axis=3)
    panels = panels.astype(F32)
    qkv_grad = jnp.concatenate([panels[:, 0], panels[:, 1], panels[:, 2]], axis=2)
    out_grad = panels[:, 3]
    up_grad = jnp.concatenate([panels[:, 4], panels[:, 5], panels[:, 6], panels[:, 7]], axis=2)
    down_grad = jnp.stack([d0.total, d1.total]).astype(F32)
    small = attend_part[:, SMALL_AT:].astype(F32)
    small = jnp.concatenate([small[:, :16], small[:, 16:]], axis=2)
    heads = lax.dynamic_slice(small, (0, 0, device * rows), (2, 8, rows))
    up_b_grad = lax.dynamic_slice(
        small, (0, 8 + device // 8, device % 8 * (4 * rows)), (2, 1, 4 * rows)
    )[:, 0]
    grads_out = [qkv_grad, out_grad, up_grad, down_grad, heads[:, :2], heads[:, 2:], up_b_grad]
    if extra > 1:
        grads_out = [
            lax.psum_scatter(v, "e", scatter_dimension=at, tiled=True)
            for v, at in zip(grads_out, (1, 1, 1, 1, 2, 2, 1))
        ]
    return (enc_out, dec_out, enc_grad, cor_grad, *grads_out)


def solution(mesh):
    devices = mesh.devices.reshape(4, 2, 2, 2, -1)
    inner = Mesh(devices, AXES)
    token = P(AXES, None)
    line = P(AXES)
    wide = P(None, AXES, None)
    vector = P(None, None, AXES)
    return jax.shard_map(
        body,
        mesh=inner,
        in_specs=(
            token, token, line, line, wide, wide, wide, wide, vector, vector, P(None, AXES), token, token,
        ),
        out_specs=(
            token, token, token, token, wide, wide, wide, wide, vector, vector, P(None, AXES),
        ),
        check_vma=False,
    )
```

```python
import functools

import jax
import jax.numpy as jnp
from jax import lax
from jax.experimental import pallas as pl
from jax.experimental.pallas import tpu as pltpu
from jax.sharding import Mesh
from jax.sharding import PartitionSpec as P

HD = 64
SLOT = 128
EPSILON = 1e-06
NEGATIVE = -1e30
F32 = jnp.float32
BF16 = jnp.bfloat16
VMEM_LIMIT = 64 * 1024 * 1024

T = 512
D = 768
HALF = D // 2
ROWS = 48
DROWS = 192
O_AT, SMALL_AT, PART_A = 144, 192, 224
D_AT, PART_B = 192, 384

NORM_ROWS = 256
ATTEND_BACK_PAIRS = 2
SM = pl.BlockSpec(memory_space=pltpu.SMEM)
HBM = pl.BlockSpec(memory_space=pl.ANY)
SPAN = {
    "feed": 20,
    "input_back": 12,
    "add_next": 12,
}


def dot(left, right):
    return lax.dot_general(left, right, (((1,), (0,)), ((), ())), preferred_element_type=F32)


def dot_rt(left, right):
    return lax.dot_general(left, right, (((1,), (1,)), ((), ())), preferred_element_type=F32)


def sds(shape, dtype):
    return jax.ShapeDtypeStruct(shape, dtype)


class In:
    def __init__(self, source, held, sem, late):
        self.held, self.copy, self.there = held, pltpu.make_async_copy(source, held, sem), False
        self.begun = False
        if not late:
            self.start()

    def start(self):
        self.begun = True
        self.copy.start()

    def __call__(self):
        if not self.begun:
            self.start()
        if not self.there:
            self.copy.wait()
            self.there = True
        return self.held


class Out:
    def __init__(self, target, held, sems):
        self.target, self.held, self.sems, self.copies = target, held, sems, []

    def send(self, index=None):
        source = self.held if index is None else self.held.at[index]
        target = self.target if index is None else self.target.at[index]
        copy = pltpu.make_async_copy(source, target, self.sems.at[len(self.copies)])
        copy.start()
        self.copies.append(copy)

    def wait(self):
        for copy in self.copies:
            copy.wait()


def call(kernel, name, args, in_kinds, outs, out_kinds, scratch, after=(), aliases=None, span=None):
    n, m, k = len(args), len(after), len(outs)
    spec = {"i": HBM, "l": HBM, "o": HBM, "h": HBM, "s": SM}
    ins = [a for a, kind in zip(args, in_kinds) if kind in "il"]
    sent = [o for o, kind in zip(outs, out_kinds) if kind == "o"]

    def ordered(*refs):
        inputs, results, rest = refs[:n], refs[n + m : n + m + k], refs[n + m + k :]
        held_in, held_out = rest[: len(ins)], rest[len(ins) : len(ins) + len(sent)]
        own = rest[len(ins) + len(sent) : len(ins) + len(sent) + len(scratch)]
        sems = rest[len(ins) + len(sent) + len(scratch) :]
        lazy, at = [], 0
        for ref, kind in zip(inputs, in_kinds):
            if kind in "il":
                ref, at = In(ref, held_in[at], sems[0].at[at], kind == "l"), at + 1
            lazy.append(ref)
        flow, at = [], 0
        for ref, kind in zip(results, out_kinds):
            if kind == "o":
                ref, at = Out(ref, held_out[at], sems[-1].at[at]), at + 1
            flow.append(ref)
        kernel(*lazy, *flow, *own)
        for ref in lazy:
            if isinstance(ref, In):
                ref()
        flow = [ref for ref in flow if isinstance(ref, Out)]
        for ref in flow:
            if not ref.copies:
                ref.send()
        for ref in flow:
            ref.wait()

    sems = []
    if ins:
        sems.append(pltpu.SemaphoreType.DMA((len(ins),)))
    if sent:
        sems.append(pltpu.SemaphoreType.DMA((len(sent), 4)))
    return pl.pallas_call(
        ordered,
        out_shape=outs,
        in_specs=[*(spec[kind] for kind in in_kinds), *([HBM] * m)],
        out_specs=[HBM] * k,
        scratch_shapes=[
            *(pltpu.VMEM(a.shape, a.dtype) for a in ins),
            *(pltpu.VMEM(o.shape, o.dtype) for o in sent),
            *scratch,
            *sems,
        ],
        input_output_aliases=aliases or {},
        compiler_params=pltpu.CompilerParams(vmem_limit_bytes=VMEM_LIMIT),
        cost_estimate=pl.CostEstimate(
            flops=int(1000 + 1.1e9 * (SPAN.get(name, 0) if span is None else span)), bytes_accessed=1000, transcendentals=0
        ),
        name=name,
    )(*args, *after)


def start(copies):
    for copy in copies:
        copy.start()


def wait(copies):
    for copy in copies:
        copy.wait()


class Spread:
    count = 9

    def __init__(self, base):
        self.base = base

    def slabs(self, refs, place, row_at, rows):
        c, x, y = place[0], place[1], place[2]
        own, bx, by, dx, dy, own_c, bx_c, by_c, far = refs
        across = 2 * (1 - y) + (1 - x)
        slots = ((2 * y + x, 0, 4), (2 * y + 1 - x, 0, 4), (2 * (1 - y) + x, 0, 4), (across, 0, 2), (across, 2, 4))
        first = self.base + row_at
        groups = (
            (c, (own, bx, by, dx, dy)),
            (1 - c, (own_c, bx_c, by_c, far.at[0], far.at[1])),
        )
        for half, group in groups:
            for ref, (at, low, high) in zip(group, slots):
                yield ref.at[:, first : first + rows, :], at, low, high, half


class Mixed:
    count = 6

    def __init__(self, cut, size):
        self.cut, self.size = cut, size

    def slabs(self, refs, place, row_at, rows):
        c, x, y = place[0], place[1], place[2]
        own, near_x, near_y = 2 * y + x, 2 * y + 1 - x, 2 * (1 - y) + x
        across = 2 * (1 - y) + (1 - x)
        rest = self.size - self.cut
        for half, (line, low, high) in ((c, refs[:3]), (1 - c, refs[3:])):
            if row_at < self.cut:
                places = ((line, row_at, own), (line, self.cut + row_at, near_x))
                places += ((low, row_at, near_y), (low, self.cut + row_at, across))
            else:
                first, base = row_at - self.cut, 2 * self.cut
                places = ((line, base + first, own), (line, base + rest + first, near_y))
                places += ((high, first, near_x), (high, rest + first, across))
            for ref, first, at in places:
                yield ref.at[:, first : first + rows, :], at, 0, 4, half


def half_cols(h):
    return pl.ds(pl.multiple_of(h * HALF, HALF), HALF)


def panel_copies(layout, refs, place, dst, sems, row_at, rows):
    copies = []
    for n, (src, at, low, high, half) in enumerate(layout.slabs(refs, place, row_at, rows)):
        copies.append(
            pltpu.make_async_copy(src, dst.at[low:high, at, :, half_cols(half)], sems.at[n])
        )
    return copies


def fill_bias(bias, lens, buck):
    bucket = buck[0]
    key = lax.broadcasted_iota(jnp.int32, (T, T), 0)
    query = lax.broadcasted_iota(jnp.int32, (T, T), 1)
    shift = bucket + 7
    same = lax.shift_right_logical(key, shift) == lax.shift_right_logical(query, shift)
    position = jnp.bitwise_and(key, lax.shift_left(jnp.int32(SLOT), bucket) - 1)
    slot = lax.shift_right_logical(key, 7)
    length = jnp.where(
        slot < 2,
        jnp.where(slot == 0, lens[0], lens[1]),
        jnp.where(slot == 2, lens[2], lens[3]),
    )
    bias[...] = jnp.where(same & (position < length), 0.0, NEGATIVE)


def first_tokens(buck, low, size):
    span = lax.shift_left(jnp.int32(SLOT), buck[0])
    token = lax.broadcasted_iota(jnp.int32, (size, 1), 0) + low
    return jnp.bitwise_and(token, span - 1) == 0


def halves(block):
    lane = lax.broadcasted_iota(jnp.int32, block.shape, 1)
    zero = jnp.zeros_like(block)
    return jnp.where(lane < HD, block, zero), jnp.where(lane < HD, zero, block)


def row_loop(size, body):
    if size == T:
        return body(pl.ds(0, T))

    def step(i, carry):
        body(pl.ds(pl.multiple_of(i * size, size), size))
        return carry

    lax.fori_loop(0, T // size, step, 0)


def attend_kernel(layout, *refs):
    x, lens, buck, place = refs[:4]
    pieces, refs = refs[4 : 4 + layout.count], refs[4 + layout.count :]
    flow, (wq, bias, heap, sems) = refs[:6], refs[6:]
    p, m, xt, mt, stat, vec = (ref.held for ref in flow)
    copies = [
        panel_copies(layout, pieces, place, wq.at[j], sems.at[j], j * ROWS, ROWS) for j in range(3)
    ]
    smalls, at = [], 0
    for n, (src, _, low, high, _) in enumerate(layout.slabs(pieces, place, SMALL_AT, 32)):
        smalls.append(pltpu.make_async_copy(src, heap.at[at : at + high - low], sems.at[3, n]))
        at += high - low
    start(smalls)
    for group in copies:
        start(group)
    fill_bias(bias, lens, buck)
    x = x()
    xt[...] = x[...].T
    flow[2].send()
    wait(smalls)
    total = heap[0].astype(F32)
    for n in range(1, 32):
        total = total + heap[n].astype(F32)
    vec[...] = jnp.concatenate([total[:16], total[16:]], axis=1)
    flow[5].send()
    for j in range(3):
        wait(copies[j])
        weight = wq[j].reshape(D, D)
        for half in range(2):
            rows = slice(half * 256, half * 256 + 256)
            out = dot(x[rows, :], weight)
            if j != 1:
                out = out + (vec[2:3, :] if j == 0 else vec[3:4, :])
            out = out.astype(BF16)
            for s in range(6):
                p[6 * j + s, rows, :] = out[:, 128 * s : 128 * s + 128]
        flow[0].send(slice(6 * j, 6 * j + 6))

    def pair(i):
        q = p[i] * jnp.asarray(HD**-0.5, BF16)
        v_t = p[12 + i].T
        both = dot_rt(jnp.concatenate(halves(p[6 + i]), axis=0), q)
        mixed = []
        for a in range(2):
            scores = both[T * a : T * a + T] + bias[...]
            peak = jnp.max(scores, axis=0, keepdims=True)
            weights = jnp.exp(scores - peak)
            inverse = 1.0 / jnp.sum(weights, axis=0, keepdims=True)
            stat[2 * i + a, 0:1, :] = peak
            stat[2 * i + a, 1:2, :] = inverse
            soft = (weights * inverse).astype(BF16)
            mixed.append(dot(v_t[HD * a : HD * a + HD, :], soft))
        mixed = jnp.concatenate(mixed, axis=0)
        mt[pl.ds(pl.multiple_of(i * 128, 128), 128), :] = mixed.astype(BF16)
        m[i] = mixed.T.astype(BF16)

    def pairs(n, carry):
        for k in range(3):
            pair(3 * n + k)
        return carry

    lax.fori_loop(0, 2, pairs, 0)


def attend(x, lens, buck, place, part, after, span):
    layout, pieces = part
    return call(
        functools.partial(attend_kernel, layout),
        "attend",
        (x, lens, buck, place, *pieces),
        "isss" + "h" * layout.count,
        [
            sds((18, T, 128), BF16),
            sds((6, T, 128), BF16),
            sds((D, T), BF16),
            sds((D, T), BF16),
            sds((12, 8, T), F32),
            sds((16, D), F32),
        ],
        "o" * 6,
        [
            pltpu.VMEM((3, 4, 4, ROWS, D), BF16),
            pltpu.VMEM((T, T), F32),
            pltpu.VMEM((32, 32, HALF), BF16),
            pltpu.SemaphoreType.DMA((4, 10)),
        ],
        after,
        span=span,
    )


def unit_norm(resid):
    center = jnp.mean(resid, axis=-1, keepdims=True)
    shifted = resid - center
    spread = jnp.mean(shifted * shifted, axis=-1, keepdims=True)
    inverse = lax.rsqrt(spread + EPSILON)
    return shifted * inverse, inverse


def feed_kernel(encoder, layout_a, layout_b, *refs):
    x, m, vec, place = refs[:4]
    refs = refs[4:]
    if encoder:
        cor, buck = refs[:2]
        refs = refs[2:]
    pieces_a, refs = refs[: layout_a.count], refs[layout_a.count :]
    pieces_b, refs = refs[: layout_b.count], refs[layout_b.count :]
    flow, refs = refs[: 8 if encoder else 6], refs[8 if encoder else 6 :]
    out, n1, r1, n2, r2, gp = (ref.held for ref in flow[:6])
    if encoder:
        xd, xdl = (ref.held for ref in flow[6:])
    y1t_out, gt_out, give_out, wo, wu, wd, scr, y1, y1l, g, y1t, gt, sems, out_sems = refs
    c = place[0]
    sent = []

    def send(source, target):
        copy = pltpu.make_async_copy(source, target, out_sems.at[len(sent)])
        copy.start()
        sent.append(copy)

    o_copies = panel_copies(layout_a, pieces_a, place, wo, sems.at[0], O_AT, ROWS)
    u_copies = [
        panel_copies(layout_b, pieces_b, place, wu.at[j], sems.at[1 + j], j * ROWS, ROWS)
        for j in range(4)
    ]
    d_copies = panel_copies(layout_b, pieces_b, place, wd, sems.at[5], D_AT, DROWS)
    start(o_copies)
    for group in u_copies:
        start(group)
    start(d_copies)
    wait(o_copies)
    m, x, vec = m(), x(), vec()
    weight = wo[...].reshape(D, D)
    for half in range(2):
        rows = slice(half * 256, half * 256 + 256)
        left = jnp.concatenate([m[s, rows, :] for s in range(6)], axis=1)
        scr[rows, :] = dot(left, weight)

    def first(rows):
        resid = x[rows, :].astype(F32) + (scr[rows, :] + vec[4:5, :])
        unit, inverse = unit_norm(resid)
        n1[rows, :] = unit
        r1[rows, :] = jnp.broadcast_to(inverse, (inverse.shape[0], 128))
        normed = unit * vec[0:1, :] + vec[5:6, :]
        y1[rows, :] = normed
        y1l[rows, :] = normed.astype(BF16)

    row_loop(NORM_ROWS, first)
    y1t[...] = y1l[...].T.reshape(8, 96, T)
    send(y1t, y1t_out)
    send(y1t, give_out.at[0:8])
    for n in (1, 2):
        flow[n].send()

    for j in range(4):
        wait(u_copies[j])

        def up(rows, j=j):
            left = y1l[rows, :]
            for k in range(3):
                cols = slice(256 * k, 256 * k + 256)
                right = wu[j, :, :, :, cols].reshape(D, 256)
                hidden = dot(left, right) + vec[8 + j : 9 + j, cols]
                cdf = 0.5 * (1.0 + lax.erf(hidden * (0.5**0.5)))
                g[j, rows, cols] = (hidden * cdf).astype(BF16)
                density = jnp.exp(hidden * hidden * -0.5) * 0.3989422804014327
                gp[j, rows, cols] = (cdf + hidden * density).astype(BF16)

        row_loop(128, up)
        gt[j] = g[j].T.reshape(4, 2, 96, T)
        send(gt.at[j, :, c], gt_out.at[j])
        send(gt.at[j, :, 1 - c], give_out.at[8 + 4 * j : 12 + 4 * j])
        flow[5].send(j)

    wait(d_copies)
    if encoder:
        cor = cor()
    for half in range(2):
        rows = slice(half * 256, half * 256 + 256)
        total = dot(g[0, rows, :], wd[0].reshape(D, D))
        for j in range(1, 4):
            total = total + dot(g[j, rows, :], wd[j].reshape(D, D))
        scr[rows, :] = total

    def second(rows):
        resid = y1[rows, :] + (scr[rows, :] + vec[6:7, :])
        unit, inverse = unit_norm(resid)
        n2[rows, :] = unit
        r2[rows, :] = jnp.broadcast_to(inverse, (inverse.shape[0], 128))
        result = unit * vec[1:2, :] + vec[7:8, :]
        out[rows, :] = result.astype(BF16)
        if encoder:
            mixed = jnp.where(
                first_tokens(buck, rows.start, NORM_ROWS), result, cor[rows, :].astype(F32)
            )
            xd[rows, :] = mixed
            xdl[rows, :] = mixed.astype(BF16)

    row_loop(NORM_ROWS, second)
    wait(sent)


def feed(encoder, x, m, vec, place, part_a, part_b, after, cor=None, buck=None):
    (layout_a, pieces_a), (layout_b, pieces_b) = part_a, part_b
    args, kinds = (x, m, vec, place), "iiis"
    outs = [
        sds((T, D), BF16),
        sds((T, D), F32),
        sds((T, 128), F32),
        sds((T, D), F32),
        sds((T, 128), F32),
        sds((4, T, D), BF16),
    ]
    if encoder:
        args, kinds = (*args, cor, buck), kinds + "is"
        outs = [*outs, sds((T, D), F32), sds((T, D), BF16)]
    return call(
        functools.partial(feed_kernel, encoder, layout_a, layout_b),
        "feed",
        (*args, *pieces_a, *pieces_b),
        kinds + "h" * (layout_a.count + layout_b.count),
        [*outs, sds((8, 96, T), BF16), sds((4, 4, 96, T), BF16), sds((24, 96, T), BF16)],
        "o" * len(outs) + "hhh",
        [
            pltpu.VMEM((4, 4, ROWS, D), BF16),
            pltpu.VMEM((4, 4, 4, ROWS, D), BF16),
            pltpu.VMEM((4, 4, DROWS, D), BF16),
            pltpu.VMEM((T, D), F32),
            pltpu.VMEM((T, D), F32),
            pltpu.VMEM((T, D), BF16),
            pltpu.VMEM((4, T, D), BF16),
            pltpu.VMEM((8, 96, T), BF16),
            pltpu.VMEM((4, 4, 2, 96, T), BF16),
            pltpu.SemaphoreType.DMA((6, 10)),
            pltpu.SemaphoreType.DMA((10,)),
        ],
        after,
    )


def norm_back(grad, unit, inverse, gain):
    scaled = grad * gain
    mean = jnp.mean(scaled, axis=-1, keepdims=True)
    along = jnp.mean(scaled * unit, axis=-1, keepdims=True)
    return inverse * (scaled - mean - unit * along)


def column_sum(value):
    return jnp.sum(value, axis=0, keepdims=True)


GROUPS = {"do": (240, "iiihlll"), "u": (192, "lllh"), "q": (176, "iiiiii")}


def down_out_grads(more, block, at, held, sems, gt, dr2l, resid_other, given, xm, xm_other, dr1l):
    copies = [
        pltpu.make_async_copy(given.at[8 + 4 * j : 12 + 4 * j], held.at[4 * j : 4 * j + 4], sems.at[j])
        for j in range(4)
    ]
    start(copies)
    gt, dr2l, resid_other = gt(), dr2l(), resid_other()
    for ref in (xm, xm_other, dr1l, *more):
        ref.start()
    dr2l_other = jnp.concatenate([resid_other[0], resid_other[1]], axis=1)
    for j in range(4):
        mine = dot(gt[j].reshape(4 * 96, T), dr2l[...])
        copies[j].wait()
        other = dot(held[4 * j : 4 * j + 4].reshape(4 * 96, T), dr2l_other)
        value = (mine + other).astype(BF16)
        for half in range(2):
            rows = slice(at + 96 * half, at + 96 * half + 96)
            block[j, :, rows] = value[:, half * HALF : half * HALF + HALF].reshape(4, 96, HALF)
    xm, xm_other, dr1l = xm(), xm_other(), dr1l()
    panel_grad(block, at + 192, dot(xm[...], dr1l[...]), dot(xm_other[...], resid_other[2]))


def panel_grad(block, at, mine, other):
    block[:, :, at : at + ROWS] = (mine + other).astype(BF16).reshape(4, 4, ROWS, HALF)


def up_grads(more, block, at, held, sems, y1t, dul, dul_other, given):
    copy = pltpu.make_async_copy(given.at[0:8], held.at[16:24], sems.at[4])
    copy.start()
    y1t, dul, dul_other = y1t(), dul(), dul_other()
    left = y1t[...].reshape(D, T)
    copy.wait()
    left_other = held[16:24].reshape(D, T)
    for j in range(4):
        panel_grad(block, at + j * ROWS, dot(left, dul[j]), dot(left_other, dul_other[j]))


def qkv_grads(more, block, at, held, sems, xt, xt_other, part, part_low, part_high, small):
    xt, xt_other, part = xt(), xt_other(), part()
    part_other = [p[s] for p in (part_low(), part_high()) for s in range(5)]
    for j in range(3):
        mine, other = (
            jnp.concatenate([p[s] for s in range(3 * j, 3 * j + 3)], axis=1)
            for p in (part, part_other)
        )
        panel_grad(block, at + j * ROWS, dot(xt[...], mine), dot(xt_other[...], other))
    other = [part_other[9][16 * k : 16 * k + 16, :].astype(F32) for k in range(6)]
    small = small()[...] + jnp.concatenate(other, axis=1)
    small = jnp.concatenate([small[:, :HALF], small[:, HALF:]], axis=0)
    block[:, :, at + 144 : at + 176] = jnp.broadcast_to(small.astype(BF16), (4, 4, 32, HALF))


FILLS = {"do": down_out_grads, "u": up_grads, "q": qkv_grads}


def keep_kernel(groups, *refs):
    inputs, refs = refs[: sum(len(GROUPS[g][1]) for g in groups)], refs[sum(len(GROUPS[g][1]) for g in groups) :]
    place, a_send, a_keep, b_send, b_keep, block, held, sems, out_sems = refs
    x, y = place[1], place[2]
    copies, at, first = [], 0, 0
    for g in groups:
        rows, kinds = GROUPS[g]
        more = [ref for ref in inputs[first + len(kinds) :] if isinstance(ref, In)]
        FILLS[g](more, block, at, held, sems, *inputs[first : first + len(kinds)])
        part = slice(at, at + rows)
        pairs = []
        for side, a, b in ((1, a_send, b_send), (0, a_keep, b_keep)):
            for n in range(2):
                pairs.append((block.at[0:2, 2 * n + lax.bitwise_xor(x, side), part], a.at[n, :, part]))
                pairs.append((block.at[2:4, 2 * lax.bitwise_xor(y, side) + n, part], b.at[n, :, part]))
        new = [
            pltpu.make_async_copy(src, dst, out_sems.at[len(copies) + n])
            for n, (src, dst) in enumerate(pairs)
        ]
        start(new)
        copies += new
        at, first = at + rows, first + len(kinds)
    wait(copies)


def keep(groups, inputs, place, after, span=None):
    rows = sum(GROUPS[g][0] for g in groups)
    return call(
        functools.partial(keep_kernel, groups),
        "keep_grads",
        (*inputs, place),
        "".join(GROUPS[g][1] for g in groups) + "s",
        [sds((2, 2, rows, HALF), BF16)] * 4,
        "hhhh",
        [
            pltpu.VMEM((4, 4, rows, HALF), BF16),
            pltpu.VMEM((24, 96, T), BF16),
            pltpu.SemaphoreType.DMA((5,)),
            pltpu.SemaphoreType.DMA((8 * len(groups),)),
        ],
        after,
        span=span,
    )


def add_next_kernel(a_keep, a_got, b_keep, b_got, place, a_next, b_next, blocks, sems):
    x, y = place[1], place[2]
    refs = (a_keep.at[1 - y], a_got.at[1 - y], b_keep.at[1 - x], b_got.at[1 - x])
    copies = [pltpu.make_async_copy(ref, blocks.at[n], sems.at[n]) for n, ref in enumerate(refs)]
    start(copies)
    for n, out in enumerate((a_next, b_next)):
        wait(copies[2 * n : 2 * n + 2])
        out.held[...] = (blocks[2 * n].astype(F32) + blocks[2 * n + 1].astype(F32)).astype(BF16)
        out.send()


def add_next(a_keep, a_got, b_keep, b_got, place, after):
    shape = a_keep.shape[2:]
    return call(
        add_next_kernel,
        "add_next",
        (a_keep, a_got, b_keep, b_got, place),
        "hhhhs",
        [sds((2, *shape), BF16)] * 2,
        "oo",
        [pltpu.VMEM((4, 2, *shape), BF16), pltpu.SemaphoreType.DMA((4,))],
        after,
    )


def add_last_kernel(sizes, *refs):
    place, line, sems = refs[6 * len(sizes)], refs[6 * len(sizes) + 1], refs[-1]
    blocks = refs[6 * len(sizes) + 2 : -1]
    x, y = place[1], place[2]
    copies = []
    for g in range(len(sizes)):
        a_keep, a_got, a_last, b_keep, b_got, b_last = refs[6 * g : 6 * g + 6]
        for n, ref in enumerate((a_keep.at[y], a_got.at[y], a_last, b_keep.at[x], b_got.at[x], b_last)):
            copies.append(pltpu.make_async_copy(ref, blocks[g].at[n], sems.at[6 * g + n]))
    start(copies)
    at = 0
    for g, rows in enumerate(sizes):
        for n in range(2):
            wait(copies[6 * g + 3 * n : 6 * g + 3 * n + 3])
            block = blocks[g]
            total = block[3 * n].astype(F32) + block[3 * n + 1].astype(F32)
            total = total + block[3 * n + 2].astype(F32)
            line.held[2 * n : 2 * n + 2, at : at + rows] = total.astype(BF16)
        at += rows


def add_last(groups, place, after):
    sizes = [group[0].shape[2] for group in groups]
    (line,) = call(
        functools.partial(add_last_kernel, sizes),
        "add_last",
        (*(array for group in groups for array in group), place),
        "h" * (6 * len(groups)) + "s",
        [sds((4, sum(sizes), HALF), BF16)],
        "o",
        [
            *(pltpu.VMEM((6, 2, rows, HALF), BF16) for rows in sizes),
            pltpu.SemaphoreType.DMA((6 * len(groups),)),
        ],
        after,
    )
    return line


def feed_back_kernel(encoder, layout_a, layout_b, *refs):
    cot, n2, r2, vec, gp, n1, r1, place = refs[:8]
    refs = refs[8:]
    if encoder:
        dxd, buck = refs[:2]
        refs = refs[2:]
    pieces_a, refs = refs[: layout_a.count], refs[layout_a.count :]
    pieces_b, refs = refs[: layout_b.count], refs[layout_b.count :]
    flow, refs = refs[:4], refs[4:]
    dr2l, dr1, dml, small = (ref.held for ref in flow)
    dul_keep, dul_give, dr1_keep, resid_give, wo, wu, wd, scr, dul, dr1l, sems, out_sems = refs
    c = place[0]
    sent = []

    def send(source, target):
        sent.append(pltpu.make_async_copy(source, target, out_sems.at[len(sent)]))
        sent[-1].start()

    d_copies = panel_copies(layout_b, pieces_b, place, wd, sems.at[5], D_AT, DROWS)
    u_copies = [
        panel_copies(layout_b, pieces_b, place, wu.at[j], sems.at[1 + j], j * ROWS, ROWS)
        for j in range(4)
    ]
    o_copies = panel_copies(layout_a, pieces_a, place, wo, sems.at[0], O_AT, ROWS)
    start(d_copies)
    gp.start()
    for group in u_copies:
        start(group)
    n1.start()
    r1.start()
    start(o_copies)
    small[...] = jnp.zeros_like(small)
    cot, n2, r2, vec = cot(), n2(), r2(), vec()
    if encoder:
        dxd = dxd()

    def second(rows):
        grad = cot[rows, :].astype(F32)
        if encoder:
            grad = grad + jnp.where(first_tokens(buck, rows.start, NORM_ROWS), dxd[rows, :], 0.0)
        unit = n2[rows, :]
        resid = norm_back(grad, unit, r2[rows, 0:1], vec[1:2, :])
        small[1:2, :] += column_sum(grad * unit)
        small[7:8, :] += column_sum(grad)
        small[6:7, :] += column_sum(resid)
        scr[rows, :] = resid
        dr2l[rows, :] = resid.astype(BF16)

    row_loop(NORM_ROWS, second)
    flow[0].send()
    for half in range(2):
        send(dr2l.at[:, half * HALF : half * HALF + HALF], resid_give.at[half])
    wait(d_copies)
    gp = gp()
    for j in range(4):

        def up(rows, j=j):
            left = dr2l[rows, :]
            weight = wd[j].reshape(D, D)
            for k in range(3):
                cols = slice(256 * k, 256 * k + 256)
                grad = dot_rt(left, weight[cols, :])
                hidden = (grad * gp[j, rows, cols].astype(F32)).astype(BF16)
                dul[j, rows, cols] = hidden
                small[8 + j : 9 + j, cols] += column_sum(hidden.astype(F32))

        row_loop(256, up)
        send(dul.at[j, :, half_cols(1 - c)], dul_give.at[j])
        send(dul.at[j, :, half_cols(c)], dul_keep.at[j])
        wait(u_copies[j])
        for half in range(2):
            rows = slice(half * 256, half * 256 + 256)
            scr[rows, :] += dot_rt(dul[j, rows, :], wu[j].reshape(D, D))
    n1, r1 = n1(), r1()

    def first(rows):
        grad = scr[rows, :]
        unit = n1[rows, :]
        resid = norm_back(grad, unit, r1[rows, 0:1], vec[0:1, :])
        small[0:1, :] += column_sum(grad * unit)
        small[5:6, :] += column_sum(grad)
        small[4:5, :] += column_sum(resid)
        dr1[rows, :] = resid
        dr1l[rows, :] = resid.astype(BF16)

    row_loop(NORM_ROWS, first)
    send(dr1l.at[:, half_cols(1 - c)], resid_give.at[2])
    send(dr1l.at[:, half_cols(c)], dr1_keep)
    for n in (1, 3):
        flow[n].send()
    wait(o_copies)
    weight = wo[...].reshape(D, D)
    for half in range(2):
        rows = slice(half * 256, half * 256 + 256)
        out = dot_rt(dr1l[rows, :], weight).astype(BF16)
        for s in range(6):
            dml[s, rows, :] = out[:, 128 * s : 128 * s + 128]
    wait(sent)


def feed_back(encoder, cot, n2, r2, vec, gp, n1, r1, place, part_a, part_b, after, dxd=None, buck=None):
    (layout_a, pieces_a), (layout_b, pieces_b) = part_a, part_b
    args, kinds = (cot, n2, r2, vec, gp, n1, r1, place), "iiiillls"
    if encoder:
        args, kinds = (*args, dxd, buck), kinds + "is"
    half = sds((4, T, HALF), BF16)
    narrow = sds((T, HALF), BF16)
    return call(
        functools.partial(feed_back_kernel, encoder, layout_a, layout_b),
        "feed_back",
        (*args, *pieces_a, *pieces_b),
        kinds + "h" * (layout_a.count + layout_b.count),
        [
            sds((T, D), BF16),
            sds((T, D), F32),
            sds((6, T, 128), BF16),
            sds((16, D), F32),
            half,
            half,
            narrow,
            sds((3, T, HALF), BF16),
        ],
        "oooohhhh",
        [
            pltpu.VMEM((4, 4, ROWS, D), BF16),
            pltpu.VMEM((4, 4, 4, ROWS, D), BF16),
            pltpu.VMEM((4, 4, DROWS, D), BF16),
            pltpu.VMEM((T, D), F32),
            pltpu.VMEM((4, T, D), BF16),
            pltpu.VMEM((T, D), BF16),
            pltpu.SemaphoreType.DMA((6, 10)),
            pltpu.SemaphoreType.DMA((12,)),
        ],
        after,
    )


def attend_back_kernel(*refs):
    p, dml, stat, small_in, lens, buck, place = refs[:7]
    keep_out, low_out, high_out, small_out, dpl, slab, bias, out_sems = refs[7:]
    small = small_out.held
    c = place[0]
    fill_bias(bias, lens, buck)
    p, dml, stat = p(), dml(), stat()
    scale = jnp.asarray(HD**-0.5, BF16)
    small[...] = small_in()[...]

    def pair(i):
        q = p[i] * scale
        k_t = p[6 + i].T
        both = dot_rt(jnp.concatenate(halves(p[6 + i]), axis=0), q)
        grad = dml[i]
        dboth = dot_rt(jnp.concatenate(halves(p[12 + i]), axis=0), grad)
        softs, dscores, dq = [], [], []
        for a in range(2):
            scores = both[T * a : T * a + T] + bias[...]
            peak = stat[2 * i + a, 0:1, :]
            inverse = stat[2 * i + a, 1:2, :]
            soft = jnp.exp(scores - peak) * inverse
            dsoft = dboth[T * a : T * a + T]
            total = jnp.sum(soft * dsoft, axis=0, keepdims=True)
            dscore = (soft * (dsoft - total)).astype(BF16)
            softs.append(soft.astype(BF16))
            dscores.append(dscore)
            dq.append(dot(k_t[HD * a : HD * a + HD, :], dscore))
        grads, queries = halves(grad), halves(q)
        dv = (dot(softs[0], grads[0]) + dot(softs[1], grads[1])).astype(BF16)
        dk = (dot(dscores[0], queries[0]) + dot(dscores[1], queries[1])).astype(BF16)
        dq = (jnp.concatenate(dq, axis=0).T * (HD**-0.5)).astype(BF16)
        dpl[i] = dq
        dpl[6 + i] = dk
        dpl[12 + i] = dv
        cols = pl.ds(pl.multiple_of(i * 128, 128), 128)
        small[2:3, cols] = column_sum(dq.astype(F32))
        small[3:4, cols] = column_sum(dv.astype(F32))

    def pairs(n, carry):
        for k in range(ATTEND_BACK_PAIRS):
            pair(ATTEND_BACK_PAIRS * n + k)
        return carry

    lax.fori_loop(0, 6 // ATTEND_BACK_PAIRS, pairs, 0)
    slab[...] = jnp.zeros_like(slab)
    for k in range(6):
        slab[16 * k : 16 * k + 16, :] = small[:, 128 * k : 128 * k + 128].astype(BF16)
    h = 3 * (1 - c)
    sent = [
        (dpl.at[pl.ds(h, 3)], low_out.at[0:3]),
        (dpl.at[pl.ds(6 + h, 2)], low_out.at[3:5]),
        (dpl.at[pl.ds(8 + h, 1)], high_out.at[0:1]),
        (dpl.at[pl.ds(12 + h, 3)], high_out.at[1:4]),
        (slab, high_out.at[4]),
    ]
    for j in range(3):
        sent.append((dpl.at[pl.ds(6 * j + 3 * c, 3)], keep_out.at[3 * j : 3 * j + 3]))
    sent = [pltpu.make_async_copy(src, dst, out_sems.at[n]) for n, (src, dst) in enumerate(sent)]
    start(sent)
    wait(sent)


def attend_back(p, dml, stat, small, lens, buck, place, after):
    return call(
        attend_back_kernel,
        "attend_back",
        (p, dml, stat, small, lens, buck, place),
        "iiiisss",
        [sds((9, T, 128), BF16), sds((5, T, 128), BF16), sds((5, T, 128), BF16), sds((16, D), F32)],
        "hhho",
        [
            pltpu.VMEM((18, T, 128), BF16),
            pltpu.VMEM((T, 128), BF16),
            pltpu.VMEM((T, T), F32),
            pltpu.SemaphoreType.DMA((10,)),
        ],
        after,
    )


def input_back_kernel(encoder, layout, *refs):
    dpl_keep, dpl_low, dpl_high, dr1, place = refs[:5]
    refs = refs[5:]
    if not encoder:
        buck, refs = refs[0], refs[1:]
    pieces, refs = refs[: layout.count], refs[layout.count :]
    if not encoder:
        dxd_out, refs = refs[0], refs[1:]
        dxd = dxd_out.held
    out_flow, dpl, wq, sems = refs
    out = out_flow.held
    c = place[0]
    copies = []
    for j in range(3):
        group = panel_copies(layout, pieces, place, wq.at[j], sems.at[j], j * ROWS, ROWS)
        other = 6 * j + 3 * (1 - c)
        pairs = [(dpl_keep.at[3 * j : 3 * j + 3], pl.ds(6 * j + 3 * c, 3))]
        if j == 0:
            pairs.append((dpl_low.at[0:3], pl.ds(other, 3)))
        elif j == 1:
            pairs += [(dpl_low.at[3:5], pl.ds(other, 2)), (dpl_high.at[0:1], pl.ds(other + 2, 1))]
        else:
            pairs.append((dpl_high.at[1:4], pl.ds(other, 3)))
        for n, (src, at) in enumerate(pairs):
            group.append(pltpu.make_async_copy(src, dpl.at[at], sems.at[j, 10 + n]))
        start(group)
        copies.append(group)
    dr1 = dr1()
    for group in copies:
        wait(group)
    for half in range(2):
        rows = slice(half * 256, half * 256 + 256)
        total = dr1[rows, :]
        for j in range(3):
            left = jnp.concatenate([dpl[6 * j + s, rows, :] for s in range(6)], axis=1)
            total = total + dot_rt(left, wq[j].reshape(D, D))
        if encoder:
            out[rows, :] = total.astype(BF16)
        else:
            dxd[rows, :] = total
            out[rows, :] = jnp.where(first_tokens(buck, half * 256, 256), 0.0, total).astype(BF16)
            dxd_out.send(rows)
        out_flow.send(rows)


def input_back(encoder, slabs, dr1, place, part_a, after, buck=None):
    layout, pieces = part_a
    args, kinds = (*slabs, dr1, place), "hhhis"
    outs = [sds((T, D), BF16)]
    if not encoder:
        args, kinds = (*args, buck), kinds + "s"
        outs = [sds((T, D), F32), *outs]
    return call(
        functools.partial(input_back_kernel, encoder, layout),
        "input_back",
        (*args, *pieces),
        kinds + "h" * layout.count,
        outs,
        "o" * len(outs),
        [
            pltpu.VMEM((18, T, 128), BF16),
            pltpu.VMEM((3, 4, 4, ROWS, D), BF16),
            pltpu.SemaphoreType.DMA((3, 13)),
        ],
        after,
    )


def gate_kernel(*refs):
    pass


def gate(values, after):
    outs = call(
        gate_kernel,
        "gate",
        tuple(values),
        "h" * len(values),
        [sds(v.shape, v.dtype) for v in values],
        "h" * len(values),
        [],
        after,
        {n: n for n in range(len(values))},
    )
    return list(outs)


def split_kernel(bx, by, ax, ay, held, sems):
    refs = ((bx.at[0:2], held.at[0], ax), (by.at[2:4], held.at[1], ay))
    into = [pltpu.make_async_copy(src, mid, sems.at[n]) for n, (src, mid, _) in enumerate(refs)]
    out = [pltpu.make_async_copy(mid, dst, sems.at[2 + n]) for n, (_, mid, dst) in enumerate(refs)]
    start(into)
    for n in range(2):
        into[n].wait()
        out[n].start()
    wait(out)


def split(bx, by, after):
    shape = (2, *bx.shape[1:])
    return call(
        split_kernel,
        "split",
        (bx, by),
        "hh",
        [sds(shape, BF16)] * 2,
        "hh",
        [pltpu.VMEM((2, *shape), BF16), pltpu.SemaphoreType.DMA((4,))],
        after,
    )


def cut_kernel(at, line, low, high, held, sems):
    into, out = [], []
    for n, (rows, dst) in enumerate(((slice(0, at), low), (slice(at, held.shape[1]), high))):
        into.append(pltpu.make_async_copy(line.at[:, rows], held.at[:, rows], sems.at[n]))
        out.append(pltpu.make_async_copy(held.at[:, rows], dst, sems.at[2 + n]))
    start(into)
    for n in range(2):
        into[n].wait()
        out[n].start()
    wait(out)


def cut(line, at, after):
    rows = line.shape[1]
    return call(
        functools.partial(cut_kernel, at),
        "cut",
        (line,),
        "h",
        [sds((4, at, HALF), BF16), sds((4, rows - at, HALF), BF16)],
        "hh",
        [pltpu.VMEM((4, rows, HALF), BF16), pltpu.SemaphoreType.DMA((4,))],
        after,
    )


def join_kernel(dx, dy, far, held, sems):
    into = [pltpu.make_async_copy(ref, held.at[n], sems.at[n]) for n, ref in enumerate((dx, dy))]
    out = [pltpu.make_async_copy(held.at[n], far.at[n], sems.at[2 + n]) for n in range(2)]
    start(into)
    for n in range(2):
        into[n].wait()
        out[n].start()
    wait(out)


def join(dx, dy, after):
    (far,) = call(
        join_kernel,
        "join",
        (dx, dy),
        "hh",
        [sds((2, *dx.shape), BF16)],
        "h",
        [pltpu.VMEM((2, *dx.shape), BF16), pltpu.SemaphoreType.DMA((4,))],
        after,
    )
    return far


AXES = ("z", "y", "x", "c", "e")


def swap(value, axis):
    return lax.ppermute(value, axis, [(0, 1), (1, 0)])


def pick(value, index, axis):
    return lax.dynamic_index_in_dim(value, index, axis, keepdims=False)


class SpreadGather:
    def __init__(self, rows):
        self.own = lax.all_gather(rows, "z", axis=0, tiled=False)

    def plane(self, after):
        (self.own,) = gate([self.own], after)
        self.bx, self.by = swap(self.own, "x"), swap(self.own, "y")
        self.own_c = swap(self.own, "c")
        return (self.own,)

    def forward(self, after):
        ax, ay = split(self.bx, self.by, (*after, self.own_c))
        self.dx, self.dy = swap(ax, "y"), swap(ay, "x")
        self.bx_c, self.by_c = swap(self.bx, "c"), swap(self.by, "c")
        return (ax,)

    def across(self, after):
        far = join(self.dx, self.dy, after)
        self.pieces = (
            self.own, self.bx, self.by, self.dx, self.dy, self.own_c, self.bx_c, self.by_c, swap(far, "c"),
        )
        return (far,)


class MixedGather:
    def __init__(self, rows, at, along_x, along_y):
        self.at, self.size = at, rows.shape[0]
        self.rows = jnp.concatenate([rows[:at], along_x, rows[at:], along_y])

    def line(self, after):
        (rows,) = gate([self.rows], after)
        self.own = lax.all_gather(rows, "z", axis=0, tiled=False)
        return (rows,)

    def arrive(self, after):
        (self.own,) = gate([self.own], after)
        return (self.own,)

    def plane(self, after):
        low, high = cut(self.own, 2 * self.at, after)
        self.low, self.high = swap(low, "y"), swap(high, "x")
        return (low,)

    def near(self, after):
        tok = self.arrive(after)
        self.own_c = swap(self.own, "c")
        return tok

    def across(self, after):
        self.low, self.high = gate([self.low, self.high], after)
        self.low_c, self.high_c = swap(self.low, "c"), swap(self.high, "c")
        self.pieces = (self.own, self.low, self.high, self.own_c, self.low_c, self.high_c)
        self.part = (Mixed(self.at, self.size), self.pieces)
        return (self.low,)


class Scatter:
    def __init__(self, groups, place):
        self.groups, self.place = groups, place

    def keep(self, inputs, after, span=None):
        a_send, self.a_keep, b_send, self.b_keep = keep(
            self.groups, inputs, self.place, after, span
        )
        self.a_got, self.b_got = swap(a_send, "x"), swap(b_send, "y")
        return (a_send,)

    def next(self, after):
        a_next, b_next = add_next(
            self.a_keep, self.a_got, self.b_keep, self.b_got, self.place, after
        )
        self.a_last, self.b_last = swap(a_next, "y"), swap(b_next, "x")
        return (a_next,)

    def sums(self):
        return (self.a_keep, self.a_got, self.a_last, self.b_keep, self.b_got, self.b_last)


def finish(scatters, place, after):
    line = add_last([scatter.sums() for scatter in scatters], place, after)
    return (line,), lax.psum_scatter(line, "z", scatter_dimension=0, tiled=False)


def pack_weights(qkv, out, up, down, gains, biases, up_b, c, device):
    rows = out.shape[1]
    panels = jnp.concatenate([qkv, out, up], axis=2).reshape(2, rows, 8, 2, HALF)
    panels = jnp.transpose(panels, (0, 3, 2, 1, 4)).reshape(2, 2, 8 * rows, HALF)
    downs = jnp.transpose(down.reshape(2, 4 * rows, 2, HALF), (0, 2, 1, 3))
    both = jnp.concatenate([panels, downs], axis=2)
    mine = pick(both, c, 1)
    got = swap(pick(both, 1 - c, 1), "c")
    low = jnp.where(c == 0, mine, got)
    high = jnp.where(c == 0, got, mine)
    panels = jnp.stack(
        [low[:, : 8 * rows].reshape(2, 8, rows, HALF), high[:, : 8 * rows].reshape(2, 8, rows, HALF)],
        axis=2,
    ).reshape(2, 16 * rows, HALF)
    downs = jnp.concatenate([low[:, 8 * rows :], high[:, 8 * rows :]], axis=1)
    small = jnp.zeros((2, 16, D), BF16)
    small = lax.dynamic_update_slice(
        small, jnp.concatenate([gains, biases], axis=1), (0, 0, device * rows)
    )
    small = lax.dynamic_update_slice(
        small, up_b[:, None, :], (0, 8 + device // 8, device % 8 * (4 * rows))
    )
    small = jnp.concatenate([small[:, :, :HALF], small[:, :, HALF:]], axis=1)
    part_a = jnp.concatenate([panels[:, : 8 * rows], small], axis=1)
    part_b = jnp.concatenate([panels[:, 8 * rows :], downs], axis=1)
    return part_a, part_b


def body(
    encoder_input,
    corrupted,
    lengths,
    buckets,
    qkv_weight,
    out_weight,
    up_weight,
    down_weight,
    norm_gains,
    bias_rows,
    up_bias,
    encoder_cot,
    decoder_cot,
):
    extra = lax.axis_size("e")
    weights = [qkv_weight, out_weight, up_weight, down_weight, norm_gains, bias_rows, up_bias]
    if extra > 1:
        weights = [
            lax.all_gather(w, "e", axis=at, tiled=True)
            for w, at in zip(weights, (1, 1, 1, 1, 2, 2, 1))
        ]
    rows = weights[1].shape[1]
    x, y, c = lax.axis_index("x"), lax.axis_index("y"), lax.axis_index("c")
    device = ((lax.axis_index("z") * 2 + y) * 2 + x) * 2 + c
    place = jnp.stack([c, x, y]).astype(jnp.int32)
    part_a, part_b = pack_weights(*weights, c, device)
    at_a, at_b = 2 * ROWS, 4 * ROWS
    along_x = swap(jnp.concatenate([part_a[1, :at_a], part_b[1, :at_b]]), "x")
    along_y = swap(jnp.concatenate([part_a[1, at_a:], part_b[1, at_b:]]), "y")
    g0 = SpreadGather(jnp.concatenate([part_a[0], part_b[0]]))
    g1a = MixedGather(part_a[1], at_a, along_x[:at_a], along_y[: PART_A - at_a])
    g1b = MixedGather(part_b[1], at_b, along_x[at_a:], along_y[PART_A - at_a :])

    tok = g0.plane((along_x, along_y))
    tok = g1a.line(tok)
    tok = g1b.line(tok)
    tok = g1a.arrive(tok)
    tok = g0.forward(tok)
    tok = g0.across(tok)
    tok = g1a.plane(tok)
    tok = g1a.near(tok)
    part_a0, part_b0 = (Spread(0), g0.pieces), (Spread(PART_A), g0.pieces)
    p0, m0, xt0, mt0, stat0, vec0 = attend(encoder_input, lengths, buckets, place, part_a0, tok, 0)
    tok = g1b.near((stat0,))
    tok = g1b.plane((*tok, g1a.own_c))
    tok = g1a.across(tok)
    enc_out, *saved0, xd, xdl, y1t0, gt0, give0 = feed(
        True, encoder_input, m0, vec0, place, part_a0, part_b0, tok, corrupted, buckets
    )
    given0 = swap(give0, "c")
    xt0, mt0 = gate([xt0, mt0], (enc_out,))
    xt0_other, mt0_other = swap(xt0, "c"), swap(mt0, "c")
    part_a1 = g1a.part
    p1, m1, xt1, mt1, stat1, vec1 = attend(
        xdl, lengths, buckets, place, part_a1, (xt0,), 0
    )
    xt1_other, mt1_other = swap(xt1, "c"), swap(mt1, "c")
    tok = g1b.across((stat1,))
    part_b1 = g1b.part
    dec_out, *saved1, y1t1, gt1, give1 = feed(
        False, xd, m1, vec1, place, part_a1, part_b1, (xt0_other, mt0_other, xt1_other, mt1_other)
    )
    given1 = swap(give1, "c")

    n1, r1, n2, r2, gp = saved1
    dr2l, dr1, dml, small, dul, dul_give, dr1l, resid = feed_back(
        False, decoder_cot, n2, r2, vec1, gp, n1, r1, place, part_a1, part_b1, (dec_out, given0)
    )
    resid, dul_other = swap(resid, "c"), swap(dul_give, "c")
    s1, q1 = Scatter(("do", "u"), place), Scatter(("q",), place)
    tok = s1.keep(
        (gt1, dr2l, resid, given1, mt1, mt1_other, dr1l, y1t1, dul, dul_other, given1), (dr1,)
    )
    part, low, high, small = attend_back(p1, dml, stat1, small, lengths, buckets, place, tok)
    part_other = [swap(low, "c"), swap(high, "c")]
    dxd, cor_grad = input_back(False, (part, low, high), dr1, place, part_a1, (small,), buckets)
    tok = q1.keep((xt1, xt1_other, part, *part_other, small), (cor_grad,))

    n1, r1, n2, r2, gp = saved0
    dr2l, dr1, dml, small, dul, dul_give, dr1l, resid = feed_back(
        True, encoder_cot, n2, r2, vec0, gp, n1, r1, place, part_a0, part_b0, tok, dxd, buckets
    )
    resid, dul_other = swap(resid, "c"), swap(dul_give, "c")
    tok = s1.next((dr1,))
    tok = q1.next(tok)
    s0, q0 = Scatter(("do", "u"), place), Scatter(("q",), place)
    tok = s0.keep(
        (gt0, dr2l, resid, given0, mt0, mt0_other, dr1l, y1t0, dul, dul_other, given0), tok
    )
    tok, feed1 = finish([s1], place, tok)
    tok, attend1 = finish([q1], place, tok)
    part, low, high, small = attend_back(p0, dml, stat0, small, lengths, buckets, place, tok)
    part_other = [swap(low, "c"), swap(high, "c")]
    tok = q0.keep((xt0, xt0_other, part, *part_other, small), (small,))
    tok = s0.next(tok)
    (enc_grad,) = input_back(True, (part, low, high), dr1, place, part_a0, tok)
    tok = q0.next((enc_grad,))
    tok, both0 = finish([s0, q0], place, tok)
    feed1, attend1 = gate([feed1, attend1], tok)

    def rows_of(feed_part, attend_part):
        panels = jnp.concatenate([attend_part[:144], feed_part[192:]], axis=0)
        panels = panels.reshape(8, 2, rows, HALF)
        mine = pick(panels, c, 1)
        got = swap(pick(panels, 1 - c, 1), "c")
        panels = jnp.concatenate([jnp.where(c == 0, mine, got), jnp.where(c == 0, got, mine)], axis=2)
        qkv_grad = jnp.concatenate([panels[0], panels[1], panels[2]], axis=1)
        up_grad = jnp.concatenate([panels[4], panels[5], panels[6], panels[7]], axis=1)
        down_grad = jnp.concatenate([feed_part[:96], feed_part[96:192]], axis=1)
        small = jnp.concatenate([attend_part[144:160], attend_part[160:]], axis=1)
        heads = lax.dynamic_slice(small, (0, device * rows), (8, rows))
        up_b_grad = lax.dynamic_slice(small, (8 + device // 8, device % 8 * (4 * rows)), (1, 4 * rows))
        return qkv_grad, panels[3], up_grad, down_grad, heads[:2], heads[2:], up_b_grad[0]

    dec_grads = rows_of(feed1, attend1)
    enc_grads = rows_of(both0[:432], both0[432:])
    grads_out = [jnp.stack(pair).astype(F32) for pair in zip(enc_grads, dec_grads)]
    if extra > 1:
        grads_out = [
            lax.psum_scatter(v, "e", scatter_dimension=at, tiled=True)
            for v, at in zip(grads_out, (1, 1, 1, 1, 2, 2, 1))
        ]
    return (enc_out, dec_out, enc_grad, cor_grad, *grads_out)


def solution(mesh):
    devices = mesh.devices.reshape(4, 2, 2, 2, -1)
    inner = Mesh(devices, AXES)
    token = P(AXES, None)
    line = P(AXES)
    wide = P(None, AXES, None)
    vector = P(None, None, AXES)
    return jax.shard_map(
        body,
        mesh=inner,
        in_specs=(
            token, token, line, line, wide, wide, wide, wide, vector, vector, P(None, AXES), token, token,
        ),
        out_specs=(
            token, token, token, token, wide, wide, wide, wide, vector, vector, P(None, AXES),
        ),
        check_vma=False,
    )
```

```python
import functools

import jax
import jax.numpy as jnp
from jax import lax
from jax.experimental import pallas as pl
from jax.experimental.pallas import tpu as pltpu
from jax.sharding import Mesh
from jax.sharding import PartitionSpec as P

HD = 64
SLOT = 128
EPSILON = 1e-06
NEGATIVE = -1e30
F32 = jnp.float32
BF16 = jnp.bfloat16
VMEM_LIMIT = 64 * 1024 * 1024

T = 512
D = 768
HALF = D // 2
ROWS = 48
DROWS = 192
O_AT, SMALL_AT, PART_A = 144, 192, 224
D_AT, PART_B = 192, 384

NORM_ROWS = 256
ATTEND_BACK_PAIRS = 2
SM = pl.BlockSpec(memory_space=pltpu.SMEM)
HBM = pl.BlockSpec(memory_space=pl.ANY)
SPAN = {
    "feed": 20,
    "add_next": 12,
    "add_mid": 16,
}


def dot(left, right):
    return lax.dot_general(left, right, (((1,), (0,)), ((), ())), preferred_element_type=F32)


def dot_rt(left, right):
    return lax.dot_general(left, right, (((1,), (1,)), ((), ())), preferred_element_type=F32)


def sds(shape, dtype):
    return jax.ShapeDtypeStruct(shape, dtype)


class In:
    def __init__(self, source, held, sem, late):
        self.held, self.copy, self.there = held, pltpu.make_async_copy(source, held, sem), False
        self.begun = False
        if not late:
            self.start()

    def start(self):
        self.begun = True
        self.copy.start()

    def __call__(self):
        if not self.begun:
            self.start()
        if not self.there:
            self.copy.wait()
            self.there = True
        return self.held


class Out:
    def __init__(self, target, held, sems):
        self.target, self.held, self.sems, self.copies = target, held, sems, []

    def send(self, index=None):
        source = self.held if index is None else self.held.at[index]
        target = self.target if index is None else self.target.at[index]
        copy = pltpu.make_async_copy(source, target, self.sems.at[len(self.copies)])
        copy.start()
        self.copies.append(copy)

    def wait(self):
        for copy in self.copies:
            copy.wait()


def call(kernel, name, args, in_kinds, outs, out_kinds, scratch, after=(), aliases=None, span=None):
    n, m, k = len(args), len(after), len(outs)
    spec = {"i": HBM, "l": HBM, "o": HBM, "h": HBM, "s": SM}
    ins = [a for a, kind in zip(args, in_kinds) if kind in "il"]
    sent = [o for o, kind in zip(outs, out_kinds) if kind == "o"]

    def ordered(*refs):
        inputs, results, rest = refs[:n], refs[n + m : n + m + k], refs[n + m + k :]
        held_in, held_out = rest[: len(ins)], rest[len(ins) : len(ins) + len(sent)]
        own = rest[len(ins) + len(sent) : len(ins) + len(sent) + len(scratch)]
        sems = rest[len(ins) + len(sent) + len(scratch) :]
        lazy, at = [], 0
        for ref, kind in zip(inputs, in_kinds):
            if kind in "il":
                ref, at = In(ref, held_in[at], sems[0].at[at], kind == "l"), at + 1
            lazy.append(ref)
        flow, at = [], 0
        for ref, kind in zip(results, out_kinds):
            if kind == "o":
                ref, at = Out(ref, held_out[at], sems[-1].at[at]), at + 1
            flow.append(ref)
        kernel(*lazy, *flow, *own)
        for ref in lazy:
            if isinstance(ref, In):
                ref()
        flow = [ref for ref in flow if isinstance(ref, Out)]
        for ref in flow:
            if not ref.copies:
                ref.send()
        for ref in flow:
            ref.wait()

    sems = []
    if ins:
        sems.append(pltpu.SemaphoreType.DMA((len(ins),)))
    if sent:
        sems.append(pltpu.SemaphoreType.DMA((len(sent), 4)))
    return pl.pallas_call(
        ordered,
        out_shape=outs,
        in_specs=[*(spec[kind] for kind in in_kinds), *([HBM] * m)],
        out_specs=[HBM] * k,
        scratch_shapes=[
            *(pltpu.VMEM(a.shape, a.dtype) for a in ins),
            *(pltpu.VMEM(o.shape, o.dtype) for o in sent),
            *scratch,
            *sems,
        ],
        input_output_aliases=aliases or {},
        compiler_params=pltpu.CompilerParams(vmem_limit_bytes=VMEM_LIMIT),
        cost_estimate=pl.CostEstimate(
            flops=int(1000 + 1.1e9 * (SPAN.get(name, 0) if span is None else span)), bytes_accessed=1000, transcendentals=0
        ),
        name=name,
    )(*args, *after)


def start(copies):
    for copy in copies:
        copy.start()


def wait(copies):
    for copy in copies:
        copy.wait()


class Spread:
    count = 10

    def __init__(self, base):
        self.base = base

    def slabs(self, refs, place, row_at, rows):
        c, x, y = place[0], place[1], place[2]
        across = 2 * (1 - y) + (1 - x)
        slots = ((2 * y + x, 0, 4), (2 * y + 1 - x, 0, 4), (2 * (1 - y) + x, 0, 4), (across, 0, 2), (across, 2, 4))
        first = self.base + row_at
        for half, group in ((c, refs[:5]), (1 - c, refs[5:])):
            for ref, (at, low, high) in zip(group, slots):
                yield ref.at[:, first : first + rows, :], at, low, high, half


class Mixed:
    count = 6

    def __init__(self, cut, size):
        self.cut, self.size = cut, size

    def slabs(self, refs, place, row_at, rows):
        c, x, y = place[0], place[1], place[2]
        own, near_x, near_y = 2 * y + x, 2 * y + 1 - x, 2 * (1 - y) + x
        across = 2 * (1 - y) + (1 - x)
        rest = self.size - self.cut
        for half, (line, low, high) in ((c, refs[:3]), (1 - c, refs[3:])):
            if row_at < self.cut:
                places = ((line, row_at, own), (line, self.cut + row_at, near_x))
                places += ((low, row_at, near_y), (low, self.cut + row_at, across))
            else:
                first, base = row_at - self.cut, 2 * self.cut
                places = ((line, base + first, own), (line, base + rest + first, near_y))
                places += ((high, first, near_x), (high, rest + first, across))
            for ref, first, at in places:
                yield ref.at[:, first : first + rows, :], at, 0, 4, half


def half_cols(h):
    return pl.ds(pl.multiple_of(h * HALF, HALF), HALF)


def panel_copies(layout, refs, place, dst, sems, row_at, rows):
    copies = []
    for n, (src, at, low, high, half) in enumerate(layout.slabs(refs, place, row_at, rows)):
        copies.append(
            pltpu.make_async_copy(src, dst.at[low:high, at, :, half_cols(half)], sems.at[n])
        )
    return copies


def fill_bias(bias, lens, buck):
    bucket = buck[0]
    key = lax.broadcasted_iota(jnp.int32, (T, T), 0)
    query = lax.broadcasted_iota(jnp.int32, (T, T), 1)
    shift = bucket + 7
    same = lax.shift_right_logical(key, shift) == lax.shift_right_logical(query, shift)
    position = jnp.bitwise_and(key, lax.shift_left(jnp.int32(SLOT), bucket) - 1)
    slot = lax.shift_right_logical(key, 7)
    length = jnp.where(
        slot < 2,
        jnp.where(slot == 0, lens[0], lens[1]),
        jnp.where(slot == 2, lens[2], lens[3]),
    )
    bias[...] = jnp.where(same & (position < length), 0.0, NEGATIVE)


def first_tokens(buck, low, size):
    span = lax.shift_left(jnp.int32(SLOT), buck[0])
    token = lax.broadcasted_iota(jnp.int32, (size, 1), 0) + low
    return jnp.bitwise_and(token, span - 1) == 0


def halves(block):
    lane = lax.broadcasted_iota(jnp.int32, block.shape, 1)
    zero = jnp.zeros_like(block)
    return jnp.where(lane < HD, block, zero), jnp.where(lane < HD, zero, block)


def row_loop(size, body):
    if size == T:
        return body(pl.ds(0, T))

    def step(i, carry):
        body(pl.ds(pl.multiple_of(i * size, size), size))
        return carry

    lax.fori_loop(0, T // size, step, 0)


def attend_kernel(layout, *refs):
    x, lens, buck, place = refs[:4]
    pieces, refs = refs[4 : 4 + layout.count], refs[4 + layout.count :]
    flow, (wq, bias, heap, sems) = refs[:6], refs[6:]
    p, m, xt, mt, stat, vec = (ref.held for ref in flow)
    copies = [
        panel_copies(layout, pieces, place, wq.at[j], sems.at[j], j * ROWS, ROWS) for j in range(3)
    ]
    smalls, at = [], 0
    for n, (src, _, low, high, _) in enumerate(layout.slabs(pieces, place, SMALL_AT, 32)):
        smalls.append(pltpu.make_async_copy(src, heap.at[at : at + high - low], sems.at[3, n]))
        at += high - low
    start(smalls)
    for group in copies:
        start(group)
    fill_bias(bias, lens, buck)
    x = x()
    xt[...] = x[...].T
    flow[2].send()
    wait(smalls)
    total = heap[0].astype(F32)
    for n in range(1, 32):
        total = total + heap[n].astype(F32)
    vec[...] = jnp.concatenate([total[:16], total[16:]], axis=1)
    flow[5].send()
    for j in range(3):
        wait(copies[j])
        weight = wq[j].reshape(D, D)
        for half in range(2):
            rows = slice(half * 256, half * 256 + 256)
            out = dot(x[rows, :], weight)
            if j != 1:
                out = out + (vec[2:3, :] if j == 0 else vec[3:4, :])
            out = out.astype(BF16)
            for s in range(6):
                p[6 * j + s, rows, :] = out[:, 128 * s : 128 * s + 128]
        flow[0].send(slice(6 * j, 6 * j + 6))

    def pair(i):
        q = p[i] * jnp.asarray(HD**-0.5, BF16)
        v_t = p[12 + i].T
        both = dot_rt(jnp.concatenate(halves(p[6 + i]), axis=0), q)
        mixed = []
        for a in range(2):
            scores = both[T * a : T * a + T] + bias[...]
            peak = jnp.max(scores, axis=0, keepdims=True)
            weights = jnp.exp(scores - peak)
            inverse = 1.0 / jnp.sum(weights, axis=0, keepdims=True)
            stat[2 * i + a, 0:1, :] = peak
            stat[2 * i + a, 1:2, :] = inverse
            soft = (weights * inverse).astype(BF16)
            mixed.append(dot(v_t[HD * a : HD * a + HD, :], soft))
        mixed = jnp.concatenate(mixed, axis=0)
        mt[pl.ds(pl.multiple_of(i * 128, 128), 128), :] = mixed.astype(BF16)
        m[i] = mixed.T.astype(BF16)

    def pairs(n, carry):
        for k in range(3):
            pair(3 * n + k)
        return carry

    lax.fori_loop(0, 2, pairs, 0)


def attend(x, lens, buck, place, part, after, span):
    layout, pieces = part
    return call(
        functools.partial(attend_kernel, layout),
        "attend",
        (x, lens, buck, place, *pieces),
        "isss" + "h" * layout.count,
        [
            sds((18, T, 128), BF16),
            sds((6, T, 128), BF16),
            sds((D, T), BF16),
            sds((D, T), BF16),
            sds((12, 8, T), F32),
            sds((16, D), F32),
        ],
        "o" * 6,
        [
            pltpu.VMEM((3, 4, 4, ROWS, D), BF16),
            pltpu.VMEM((T, T), F32),
            pltpu.VMEM((32, 32, HALF), BF16),
            pltpu.SemaphoreType.DMA((4, 10)),
        ],
        after,
        span=span,
    )


def unit_norm(resid):
    center = jnp.mean(resid, axis=-1, keepdims=True)
    shifted = resid - center
    spread = jnp.mean(shifted * shifted, axis=-1, keepdims=True)
    inverse = lax.rsqrt(spread + EPSILON)
    return shifted * inverse, inverse


def feed_kernel(encoder, layout_a, layout_b, *refs):
    x, m, vec, place = refs[:4]
    refs = refs[4:]
    if encoder:
        cor, buck = refs[:2]
        refs = refs[2:]
    pieces_a, refs = refs[: layout_a.count], refs[layout_a.count :]
    pieces_b, refs = refs[: layout_b.count], refs[layout_b.count :]
    flow, refs = refs[: 8 if encoder else 6], refs[8 if encoder else 6 :]
    out, n1, r1, n2, r2, gp = (ref.held for ref in flow[:6])
    if encoder:
        xd, xdl = (ref.held for ref in flow[6:])
    y1t_out, gt_out, give_out, wo, wu, wd, scr, y1, y1l, g, y1t, gt, sems, out_sems = refs
    c = place[0]
    sent = []

    def send(source, target):
        copy = pltpu.make_async_copy(source, target, out_sems.at[len(sent)])
        copy.start()
        sent.append(copy)

    o_copies = panel_copies(layout_a, pieces_a, place, wo, sems.at[0], O_AT, ROWS)
    u_copies = [
        panel_copies(layout_b, pieces_b, place, wu.at[j], sems.at[1 + j], j * ROWS, ROWS)
        for j in range(4)
    ]
    d_copies = panel_copies(layout_b, pieces_b, place, wd, sems.at[5], D_AT, DROWS)
    start(o_copies)
    for group in u_copies:
        start(group)
    start(d_copies)
    wait(o_copies)
    m, x, vec = m(), x(), vec()
    weight = wo[...].reshape(D, D)
    for half in range(2):
        rows = slice(half * 256, half * 256 + 256)
        left = jnp.concatenate([m[s, rows, :] for s in range(6)], axis=1)
        scr[rows, :] = dot(left, weight)

    def first(rows):
        resid = x[rows, :].astype(F32) + (scr[rows, :] + vec[4:5, :])
        unit, inverse = unit_norm(resid)
        n1[rows, :] = unit
        r1[rows, :] = jnp.broadcast_to(inverse, (inverse.shape[0], 128))
        normed = unit * vec[0:1, :] + vec[5:6, :]
        y1[rows, :] = normed
        y1l[rows, :] = normed.astype(BF16)

    row_loop(NORM_ROWS, first)
    y1t[...] = y1l[...].T.reshape(8, 96, T)
    send(y1t, y1t_out)
    send(y1t, give_out.at[0:8])
    for n in (1, 2):
        flow[n].send()

    for j in range(4):
        wait(u_copies[j])

        def up(rows, j=j):
            left = y1l[rows, :]
            for k in range(3):
                cols = slice(256 * k, 256 * k + 256)
                right = wu[j, :, :, :, cols].reshape(D, 256)
                hidden = dot(left, right) + vec[8 + j : 9 + j, cols]
                cdf = 0.5 * (1.0 + lax.erf(hidden * (0.5**0.5)))
                g[j, rows, cols] = (hidden * cdf).astype(BF16)
                density = jnp.exp(hidden * hidden * -0.5) * 0.3989422804014327
                gp[j, rows, cols] = (cdf + hidden * density).astype(BF16)

        row_loop(128, up)
        gt[j] = g[j].T.reshape(4, 2, 96, T)
        send(gt.at[j, :, c], gt_out.at[j])
        send(gt.at[j, :, 1 - c], give_out.at[8 + 4 * j : 12 + 4 * j])
        flow[5].send(j)

    wait(d_copies)
    if encoder:
        cor = cor()
    for half in range(2):
        rows = slice(half * 256, half * 256 + 256)
        total = dot(g[0, rows, :], wd[0].reshape(D, D))
        for j in range(1, 4):
            total = total + dot(g[j, rows, :], wd[j].reshape(D, D))
        scr[rows, :] = total

    def second(rows):
        resid = y1[rows, :] + (scr[rows, :] + vec[6:7, :])
        unit, inverse = unit_norm(resid)
        n2[rows, :] = unit
        r2[rows, :] = jnp.broadcast_to(inverse, (inverse.shape[0], 128))
        result = unit * vec[1:2, :] + vec[7:8, :]
        out[rows, :] = result.astype(BF16)
        if encoder:
            mixed = jnp.where(
                first_tokens(buck, rows.start, NORM_ROWS), result, cor[rows, :].astype(F32)
            )
            xd[rows, :] = mixed
            xdl[rows, :] = mixed.astype(BF16)

    row_loop(NORM_ROWS, second)
    wait(sent)


def feed(encoder, x, m, vec, place, part_a, part_b, after, cor=None, buck=None):
    (layout_a, pieces_a), (layout_b, pieces_b) = part_a, part_b
    args, kinds = (x, m, vec, place), "iiis"
    outs = [
        sds((T, D), BF16),
        sds((T, D), F32),
        sds((T, 128), F32),
        sds((T, D), F32),
        sds((T, 128), F32),
        sds((4, T, D), BF16),
    ]
    if encoder:
        args, kinds = (*args, cor, buck), kinds + "is"
        outs = [*outs, sds((T, D), F32), sds((T, D), BF16)]
    return call(
        functools.partial(feed_kernel, encoder, layout_a, layout_b),
        "feed",
        (*args, *pieces_a, *pieces_b),
        kinds + "h" * (layout_a.count + layout_b.count),
        [*outs, sds((8, 96, T), BF16), sds((4, 4, 96, T), BF16), sds((24, 96, T), BF16)],
        "o" * len(outs) + "hhh",
        [
            pltpu.VMEM((4, 4, ROWS, D), BF16),
            pltpu.VMEM((4, 4, 4, ROWS, D), BF16),
            pltpu.VMEM((4, 4, DROWS, D), BF16),
            pltpu.VMEM((T, D), F32),
            pltpu.VMEM((T, D), F32),
            pltpu.VMEM((T, D), BF16),
            pltpu.VMEM((4, T, D), BF16),
            pltpu.VMEM((8, 96, T), BF16),
            pltpu.VMEM((4, 4, 2, 96, T), BF16),
            pltpu.SemaphoreType.DMA((6, 10)),
            pltpu.SemaphoreType.DMA((10,)),
        ],
        after,
    )


def norm_back(grad, unit, inverse, gain):
    scaled = grad * gain
    mean = jnp.mean(scaled, axis=-1, keepdims=True)
    along = jnp.mean(scaled * unit, axis=-1, keepdims=True)
    return inverse * (scaled - mean - unit * along)


def column_sum(value):
    return jnp.sum(value, axis=0, keepdims=True)


GROUPS = {"do": (240, "iiihlll"), "u": (192, "lllh"), "q": (176, "iiiiii")}


def down_out_grads(more, block, at, held, sems, gt, dr2l, resid_other, given, xm, xm_other, dr1l):
    copies = [
        pltpu.make_async_copy(given.at[8 + 4 * j : 12 + 4 * j], held.at[4 * j : 4 * j + 4], sems.at[j])
        for j in range(4)
    ]
    start(copies)
    gt, dr2l, resid_other = gt(), dr2l(), resid_other()
    for ref in (xm, xm_other, dr1l, *more):
        ref.start()
    dr2l_other = jnp.concatenate([resid_other[0], resid_other[1]], axis=1)
    for j in range(4):
        mine = dot(gt[j].reshape(4 * 96, T), dr2l[...])
        copies[j].wait()
        other = dot(held[4 * j : 4 * j + 4].reshape(4 * 96, T), dr2l_other)
        value = (mine + other).astype(BF16)
        for half in range(2):
            rows = slice(at + 96 * half, at + 96 * half + 96)
            block[j, :, rows] = value[:, half * HALF : half * HALF + HALF].reshape(4, 96, HALF)
    xm, xm_other, dr1l = xm(), xm_other(), dr1l()
    panel_grad(block, at + 192, dot(xm[...], dr1l[...]), dot(xm_other[...], resid_other[2]))


def panel_grad(block, at, mine, other):
    block[:, :, at : at + ROWS] = (mine + other).astype(BF16).reshape(4, 4, ROWS, HALF)


def up_grads(more, block, at, held, sems, y1t, dul, dul_other, given):
    copy = pltpu.make_async_copy(given.at[0:8], held.at[16:24], sems.at[4])
    copy.start()
    y1t, dul, dul_other = y1t(), dul(), dul_other()
    left = y1t[...].reshape(D, T)
    copy.wait()
    left_other = held[16:24].reshape(D, T)
    for j in range(4):
        panel_grad(block, at + j * ROWS, dot(left, dul[j]), dot(left_other, dul_other[j]))


def qkv_grads(more, block, at, held, sems, xt, xt_other, part, part_low, part_high, small):
    xt, xt_other, part = xt(), xt_other(), part()
    part_other = [p[s] for p in (part_low(), part_high()) for s in range(5)]
    for j in range(3):
        mine, other = (
            jnp.concatenate([p[s] for s in range(3 * j, 3 * j + 3)], axis=1)
            for p in (part, part_other)
        )
        panel_grad(block, at + j * ROWS, dot(xt[...], mine), dot(xt_other[...], other))
    other = [part_other[9][16 * k : 16 * k + 16, :].astype(F32) for k in range(6)]
    small = small()[...] + jnp.concatenate(other, axis=1)
    small = jnp.concatenate([small[:, :HALF], small[:, HALF:]], axis=0)
    block[:, :, at + 144 : at + 176] = jnp.broadcast_to(small.astype(BF16), (4, 4, 32, HALF))


FILLS = {"do": down_out_grads, "u": up_grads, "q": qkv_grads}


def send_spread(block, part, place, outs):
    x, y = place[1], place[2]
    a_send, a_keep, b_send, b_keep = outs
    for side, a, b in ((1, a_send, b_send), (0, a_keep, b_keep)):
        for n in range(2):
            yield block.at[0:2, 2 * n + lax.bitwise_xor(x, side), part], a.at[n, :, part]
            yield block.at[2:4, 2 * lax.bitwise_xor(y, side) + n, part], b.at[n, :, part]


def send_mixed(cut, block, part, place, outs):
    x, y = place[1], place[2]
    a_send, a_keep, b_send, b_keep = outs
    low = slice(part.start, min(part.stop, cut))
    high = slice(max(part.start, cut), part.stop)
    for side, a, b in ((1, a_send, b_send), (0, a_keep, b_keep)):
        for n in range(2):
            if low.start < low.stop:
                yield block.at[:, 2 * n + lax.bitwise_xor(x, side), low], a.at[:, n, low]
            if high.start < high.stop:
                to = slice(high.start - cut, high.stop - cut)
                yield block.at[:, 2 * lax.bitwise_xor(y, side) + n, high], b.at[:, n, to]


def keep_kernel(groups, send, *refs):
    count = sum(len(GROUPS[g][1]) for g in groups)
    inputs, refs = refs[:count], refs[count:]
    place, outs, (block, held, sems, out_sems) = refs[0], refs[1:5], refs[5:]
    copies, at, first = [], 0, 0
    for g in groups:
        rows, kinds = GROUPS[g]
        more = [ref for ref in inputs[first + len(kinds) :] if isinstance(ref, In)]
        FILLS[g](more, block, at, held, sems, *inputs[first : first + len(kinds)])
        new = [
            pltpu.make_async_copy(src, dst, out_sems.at[len(copies) + n])
            for n, (src, dst) in enumerate(send(block, slice(at, at + rows), place, outs))
        ]
        start(new)
        copies += new
        at, first = at + rows, first + len(kinds)
    wait(copies)


def keep(groups, inputs, place, after, cut=None):
    rows = sum(GROUPS[g][0] for g in groups)
    if cut is None:
        send, outs = send_spread, [sds((2, 2, rows, HALF), BF16)] * 4
    else:
        send = functools.partial(send_mixed, cut)
        outs = [sds((4, 2, cut, HALF), BF16)] * 2 + [sds((4, 2, rows - cut, HALF), BF16)] * 2
    return call(
        functools.partial(keep_kernel, groups, send),
        "keep_grads",
        (*inputs, place),
        "".join(GROUPS[g][1] for g in groups) + "s",
        outs,
        "hhhh",
        [
            pltpu.VMEM((4, 4, rows, HALF), BF16),
            pltpu.VMEM((24, 96, T), BF16),
            pltpu.SemaphoreType.DMA((5,)),
            pltpu.SemaphoreType.DMA((16 * len(groups),)),
        ],
        after,
    )


def add_mid_kernel(sizes, *refs):
    pairs, line, blocks, sems = refs[: 2 * len(sizes)], refs[2 * len(sizes)], refs[2 * len(sizes) + 1 : -1], refs[-1]
    copies = [
        pltpu.make_async_copy(ref, blocks[n // 2].at[n % 2], sems.at[n]) for n, ref in enumerate(pairs)
    ]
    start(copies)
    at = 0
    for g, size in enumerate(sizes):
        wait(copies[2 * g : 2 * g + 2])
        total = (blocks[g][0].astype(F32) + blocks[g][1].astype(F32)).astype(BF16)
        line.held[:, at : at + 2 * size] = total.reshape(4, 2 * size, HALF)
        at += 2 * size


def add_mid(pairs, after):
    sizes = [keep.shape[2] for keep, _ in pairs]
    (line,) = call(
        functools.partial(add_mid_kernel, sizes),
        "add_mid",
        tuple(array for pair in pairs for array in pair),
        "h" * (2 * len(pairs)),
        [sds((4, 2 * sum(sizes), HALF), BF16)],
        "o",
        [
            *(pltpu.VMEM((2, 4, 2, size, HALF), BF16) for size in sizes),
            pltpu.SemaphoreType.DMA((2 * len(sizes),)),
        ],
        after,
    )
    return line


def part_slices(cuts, place):
    x, y = place[1], place[2]
    slices, base = [], 0
    for g, (cut, rows) in enumerate(cuts):
        for size, mine in ((cut, y), (rows - cut, x)):
            own, other = (
                pl.ds(pl.multiple_of(base + side * size, 16), size) for side in (mine, 1 - mine)
            )
            slices.append((g, size, own, other))
            base += 2 * size
    return slices


def part_kernel(cuts, total, place, *refs):
    n = 2 * len(cuts)
    outs, held, sems = refs[:n], refs[n : 2 * n], refs[-1]
    into, out = [], []
    for k, (_, _, _, other) in enumerate(part_slices(cuts, place)):
        into.append(pltpu.make_async_copy(total.at[other], held[k], sems.at[2 * k]))
        out.append(pltpu.make_async_copy(held[k], outs[k], sems.at[2 * k + 1]))
    start(into)
    for k, copy in enumerate(into):
        copy.wait()
        out[k].start()
    wait(out)


def part_rows(total, cuts, place, after):
    shapes = [sds((size, HALF), BF16) for cut, rows in cuts for size in (cut, rows - cut)]
    return call(
        functools.partial(part_kernel, cuts),
        "part",
        (total, place),
        "hs",
        shapes,
        "h" * len(shapes),
        [
            *(pltpu.VMEM(shape.shape, BF16) for shape in shapes),
            pltpu.SemaphoreType.DMA((2 * len(shapes),)),
        ],
        after,
    )


def close_kernel(cuts, total, *refs):
    n = len(cuts)
    got, place, flow = refs[: 2 * n], refs[2 * n], refs[2 * n + 1 : 3 * n + 1]
    held, sems = refs[3 * n + 1 : -1], refs[-1]
    slices = part_slices(cuts, place)
    copies = [
        pltpu.make_async_copy(total.at[own], held[k], sems.at[k])
        for k, (_, _, own, _) in enumerate(slices)
    ]
    start(copies)
    at = 0
    for k, (g, size, _, _) in enumerate(slices):
        copies[k].wait()
        at = 0 if k % 2 == 0 else at
        value = held[k][...].astype(F32) + got[k]()[...].astype(F32)
        flow[g].held[at : at + size] = value.astype(BF16)
        at += size


def close(total, got, cuts, place, after):
    shapes = [sds((rows, HALF), BF16) for _, rows in cuts]
    sizes = [size for cut, rows in cuts for size in (cut, rows - cut)]
    return call(
        functools.partial(close_kernel, cuts),
        "close",
        (total, *got, place),
        "h" + "i" * len(got) + "s",
        shapes,
        "o" * len(shapes),
        [
            *(pltpu.VMEM((size, HALF), BF16) for size in sizes),
            pltpu.SemaphoreType.DMA((len(sizes),)),
        ],
        after,
    )


def add_next_kernel(a_keep, a_got, b_keep, b_got, place, a_next, b_next, blocks, sems):
    x, y = place[1], place[2]
    refs = (a_keep.at[1 - y], a_got.at[1 - y], b_keep.at[1 - x], b_got.at[1 - x])
    copies = [pltpu.make_async_copy(ref, blocks.at[n], sems.at[n]) for n, ref in enumerate(refs)]
    start(copies)
    for n, out in enumerate((a_next, b_next)):
        wait(copies[2 * n : 2 * n + 2])
        out.held[...] = (blocks[2 * n].astype(F32) + blocks[2 * n + 1].astype(F32)).astype(BF16)
        out.send()


def add_next(a_keep, a_got, b_keep, b_got, place, after):
    shape = a_keep.shape[2:]
    return call(
        add_next_kernel,
        "add_next",
        (a_keep, a_got, b_keep, b_got, place),
        "hhhhs",
        [sds((2, *shape), BF16)] * 2,
        "oo",
        [pltpu.VMEM((4, 2, *shape), BF16), pltpu.SemaphoreType.DMA((4,))],
        after,
    )


def add_last_kernel(sizes, *refs):
    place, line, sems = refs[6 * len(sizes)], refs[6 * len(sizes) + 1], refs[-1]
    blocks = refs[6 * len(sizes) + 2 : -1]
    x, y = place[1], place[2]
    copies = []
    for g in range(len(sizes)):
        a_keep, a_got, a_last, b_keep, b_got, b_last = refs[6 * g : 6 * g + 6]
        for n, ref in enumerate((a_keep.at[y], a_got.at[y], a_last, b_keep.at[x], b_got.at[x], b_last)):
            copies.append(pltpu.make_async_copy(ref, blocks[g].at[n], sems.at[6 * g + n]))
    start(copies)
    at = 0
    for g, rows in enumerate(sizes):
        for n in range(2):
            wait(copies[6 * g + 3 * n : 6 * g + 3 * n + 3])
            block = blocks[g]
            total = block[3 * n].astype(F32) + block[3 * n + 1].astype(F32)
            total = total + block[3 * n + 2].astype(F32)
            line.held[2 * n : 2 * n + 2, at : at + rows] = total.astype(BF16)
        at += rows


def add_last(groups, place, after):
    sizes = [group[0].shape[2] for group in groups]
    (line,) = call(
        functools.partial(add_last_kernel, sizes),
        "add_last",
        (*(array for group in groups for array in group), place),
        "h" * (6 * len(groups)) + "s",
        [sds((4, sum(sizes), HALF), BF16)],
        "o",
        [
            *(pltpu.VMEM((6, 2, rows, HALF), BF16) for rows in sizes),
            pltpu.SemaphoreType.DMA((6 * len(groups),)),
        ],
        after,
    )
    return line


def feed_back_kernel(encoder, layout_a, layout_b, *refs):
    cot, n2, r2, vec, gp, n1, r1, place = refs[:8]
    refs = refs[8:]
    if encoder:
        dxd, buck = refs[:2]
        refs = refs[2:]
    pieces_a, refs = refs[: layout_a.count], refs[layout_a.count :]
    pieces_b, refs = refs[: layout_b.count], refs[layout_b.count :]
    flow, refs = refs[:4], refs[4:]
    dr2l, dr1, dml, small = (ref.held for ref in flow)
    dul_keep, dul_give, dr1_keep, resid_give, wo, wu, wd, scr, dul, dr1l, sems, out_sems = refs
    c = place[0]
    sent = []

    def send(source, target):
        sent.append(pltpu.make_async_copy(source, target, out_sems.at[len(sent)]))
        sent[-1].start()

    d_copies = panel_copies(layout_b, pieces_b, place, wd, sems.at[5], D_AT, DROWS)
    u_copies = [
        panel_copies(layout_b, pieces_b, place, wu.at[j], sems.at[1 + j], j * ROWS, ROWS)
        for j in range(4)
    ]
    o_copies = panel_copies(layout_a, pieces_a, place, wo, sems.at[0], O_AT, ROWS)
    start(d_copies)
    gp.start()
    for group in u_copies:
        start(group)
    n1.start()
    r1.start()
    start(o_copies)
    small[...] = jnp.zeros_like(small)
    cot, n2, r2, vec = cot(), n2(), r2(), vec()
    if encoder:
        dxd = dxd()

    def second(rows):
        grad = cot[rows, :].astype(F32)
        if encoder:
            grad = grad + jnp.where(first_tokens(buck, rows.start, NORM_ROWS), dxd[rows, :], 0.0)
        unit = n2[rows, :]
        resid = norm_back(grad, unit, r2[rows, 0:1], vec[1:2, :])
        small[1:2, :] += column_sum(grad * unit)
        small[7:8, :] += column_sum(grad)
        small[6:7, :] += column_sum(resid)
        scr[rows, :] = resid
        dr2l[rows, :] = resid.astype(BF16)

    row_loop(NORM_ROWS, second)
    flow[0].send()
    for half in range(2):
        send(dr2l.at[:, half * HALF : half * HALF + HALF], resid_give.at[half])
    wait(d_copies)
    gp = gp()
    for j in range(4):

        def up(rows, j=j):
            left = dr2l[rows, :]
            weight = wd[j].reshape(D, D)
            for k in range(3):
                cols = slice(256 * k, 256 * k + 256)
                grad = dot_rt(left, weight[cols, :])
                hidden = (grad * gp[j, rows, cols].astype(F32)).astype(BF16)
                dul[j, rows, cols] = hidden
                small[8 + j : 9 + j, cols] += column_sum(hidden.astype(F32))

        row_loop(256, up)
        send(dul.at[j, :, half_cols(1 - c)], dul_give.at[j])
        send(dul.at[j, :, half_cols(c)], dul_keep.at[j])
        wait(u_copies[j])
        for half in range(2):
            rows = slice(half * 256, half * 256 + 256)
            scr[rows, :] += dot_rt(dul[j, rows, :], wu[j].reshape(D, D))
    n1, r1 = n1(), r1()

    def first(rows):
        grad = scr[rows, :]
        unit = n1[rows, :]
        resid = norm_back(grad, unit, r1[rows, 0:1], vec[0:1, :])
        small[0:1, :] += column_sum(grad * unit)
        small[5:6, :] += column_sum(grad)
        small[4:5, :] += column_sum(resid)
        dr1[rows, :] = resid
        dr1l[rows, :] = resid.astype(BF16)

    row_loop(NORM_ROWS, first)
    send(dr1l.at[:, half_cols(1 - c)], resid_give.at[2])
    send(dr1l.at[:, half_cols(c)], dr1_keep)
    for n in (1, 3):
        flow[n].send()
    wait(o_copies)
    weight = wo[...].reshape(D, D)
    for half in range(2):
        rows = slice(half * 256, half * 256 + 256)
        out = dot_rt(dr1l[rows, :], weight).astype(BF16)
        for s in range(6):
            dml[s, rows, :] = out[:, 128 * s : 128 * s + 128]
    wait(sent)


def feed_back(encoder, cot, n2, r2, vec, gp, n1, r1, place, part_a, part_b, after, dxd=None, buck=None):
    (layout_a, pieces_a), (layout_b, pieces_b) = part_a, part_b
    args, kinds = (cot, n2, r2, vec, gp, n1, r1, place), "iiiillls"
    if encoder:
        args, kinds = (*args, dxd, buck), kinds + "is"
    half = sds((4, T, HALF), BF16)
    narrow = sds((T, HALF), BF16)
    return call(
        functools.partial(feed_back_kernel, encoder, layout_a, layout_b),
        "feed_back",
        (*args, *pieces_a, *pieces_b),
        kinds + "h" * (layout_a.count + layout_b.count),
        [
            sds((T, D), BF16),
            sds((T, D), F32),
            sds((6, T, 128), BF16),
            sds((16, D), F32),
            half,
            half,
            narrow,
            sds((3, T, HALF), BF16),
        ],
        "oooohhhh",
        [
            pltpu.VMEM((4, 4, ROWS, D), BF16),
            pltpu.VMEM((4, 4, 4, ROWS, D), BF16),
            pltpu.VMEM((4, 4, DROWS, D), BF16),
            pltpu.VMEM((T, D), F32),
            pltpu.VMEM((4, T, D), BF16),
            pltpu.VMEM((T, D), BF16),
            pltpu.SemaphoreType.DMA((6, 10)),
            pltpu.SemaphoreType.DMA((12,)),
        ],
        after,
        span=12 if encoder else 0,
    )


def attend_back_kernel(*refs):
    p, dml, stat, small_in, lens, buck, place = refs[:7]
    keep_out, low_out, high_out, small_out, dpl, slab, bias, out_sems = refs[7:]
    small = small_out.held
    c = place[0]
    fill_bias(bias, lens, buck)
    p, dml, stat = p(), dml(), stat()
    scale = jnp.asarray(HD**-0.5, BF16)
    small[...] = small_in()[...]

    def pair(i):
        q = p[i] * scale
        k_t = p[6 + i].T
        both = dot_rt(jnp.concatenate(halves(p[6 + i]), axis=0), q)
        grad = dml[i]
        dboth = dot_rt(jnp.concatenate(halves(p[12 + i]), axis=0), grad)
        softs, dscores, dq = [], [], []
        for a in range(2):
            scores = both[T * a : T * a + T] + bias[...]
            peak = stat[2 * i + a, 0:1, :]
            inverse = stat[2 * i + a, 1:2, :]
            soft = jnp.exp(scores - peak) * inverse
            dsoft = dboth[T * a : T * a + T]
            total = jnp.sum(soft * dsoft, axis=0, keepdims=True)
            dscore = (soft * (dsoft - total)).astype(BF16)
            softs.append(soft.astype(BF16))
            dscores.append(dscore)
            dq.append(dot(k_t[HD * a : HD * a + HD, :], dscore))
        grads, queries = halves(grad), halves(q)
        dv = (dot(softs[0], grads[0]) + dot(softs[1], grads[1])).astype(BF16)
        dk = (dot(dscores[0], queries[0]) + dot(dscores[1], queries[1])).astype(BF16)
        dq = (jnp.concatenate(dq, axis=0).T * (HD**-0.5)).astype(BF16)
        dpl[i] = dq
        dpl[6 + i] = dk
        dpl[12 + i] = dv
        cols = pl.ds(pl.multiple_of(i * 128, 128), 128)
        small[2:3, cols] = column_sum(dq.astype(F32))
        small[3:4, cols] = column_sum(dv.astype(F32))

    def pairs(n, carry):
        for k in range(ATTEND_BACK_PAIRS):
            pair(ATTEND_BACK_PAIRS * n + k)
        return carry

    lax.fori_loop(0, 6 // ATTEND_BACK_PAIRS, pairs, 0)
    slab[...] = jnp.zeros_like(slab)
    for k in range(6):
        slab[16 * k : 16 * k + 16, :] = small[:, 128 * k : 128 * k + 128].astype(BF16)
    h = 3 * (1 - c)
    sent = [
        (dpl.at[pl.ds(h, 3)], low_out.at[0:3]),
        (dpl.at[pl.ds(6 + h, 2)], low_out.at[3:5]),
        (dpl.at[pl.ds(8 + h, 1)], high_out.at[0:1]),
        (dpl.at[pl.ds(12 + h, 3)], high_out.at[1:4]),
        (slab, high_out.at[4]),
    ]
    for j in range(3):
        sent.append((dpl.at[pl.ds(6 * j + 3 * c, 3)], keep_out.at[3 * j : 3 * j + 3]))
    sent = [pltpu.make_async_copy(src, dst, out_sems.at[n]) for n, (src, dst) in enumerate(sent)]
    start(sent)
    wait(sent)


def attend_back(p, dml, stat, small, lens, buck, place, after):
    return call(
        attend_back_kernel,
        "attend_back",
        (p, dml, stat, small, lens, buck, place),
        "iiiisss",
        [sds((9, T, 128), BF16), sds((5, T, 128), BF16), sds((5, T, 128), BF16), sds((16, D), F32)],
        "hhho",
        [
            pltpu.VMEM((18, T, 128), BF16),
            pltpu.VMEM((T, 128), BF16),
            pltpu.VMEM((T, T), F32),
            pltpu.SemaphoreType.DMA((10,)),
        ],
        after,
    )


def input_back_kernel(encoder, layout, *refs):
    dpl_keep, dpl_low, dpl_high, dr1, place = refs[:5]
    refs = refs[5:]
    if not encoder:
        buck, refs = refs[0], refs[1:]
    pieces, refs = refs[: layout.count], refs[layout.count :]
    if not encoder:
        dxd_out, refs = refs[0], refs[1:]
        dxd = dxd_out.held
    out_flow, dpl, wq, sems = refs
    out = out_flow.held
    c = place[0]
    copies = []
    for j in range(3):
        group = panel_copies(layout, pieces, place, wq.at[j], sems.at[j], j * ROWS, ROWS)
        other = 6 * j + 3 * (1 - c)
        pairs = [(dpl_keep.at[3 * j : 3 * j + 3], pl.ds(6 * j + 3 * c, 3))]
        if j == 0:
            pairs.append((dpl_low.at[0:3], pl.ds(other, 3)))
        elif j == 1:
            pairs += [(dpl_low.at[3:5], pl.ds(other, 2)), (dpl_high.at[0:1], pl.ds(other + 2, 1))]
        else:
            pairs.append((dpl_high.at[1:4], pl.ds(other, 3)))
        for n, (src, at) in enumerate(pairs):
            group.append(pltpu.make_async_copy(src, dpl.at[at], sems.at[j, 10 + n]))
        start(group)
        copies.append(group)
    dr1 = dr1()
    for group in copies:
        wait(group)
    for half in range(2):
        rows = slice(half * 256, half * 256 + 256)
        total = dr1[rows, :]
        for j in range(3):
            left = jnp.concatenate([dpl[6 * j + s, rows, :] for s in range(6)], axis=1)
            total = total + dot_rt(left, wq[j].reshape(D, D))
        if encoder:
            out[rows, :] = total.astype(BF16)
        else:
            dxd[rows, :] = total
            out[rows, :] = jnp.where(first_tokens(buck, half * 256, 256), 0.0, total).astype(BF16)
            dxd_out.send(rows)
        out_flow.send(rows)


def input_back(encoder, slabs, dr1, place, part_a, after, buck=None):
    layout, pieces = part_a
    args, kinds = (*slabs, dr1, place), "hhhis"
    outs = [sds((T, D), BF16)]
    if not encoder:
        args, kinds = (*args, buck), kinds + "s"
        outs = [sds((T, D), F32), *outs]
    return call(
        functools.partial(input_back_kernel, encoder, layout),
        "input_back",
        (*args, *pieces),
        kinds + "h" * layout.count,
        outs,
        "o" * len(outs),
        [
            pltpu.VMEM((18, T, 128), BF16),
            pltpu.VMEM((3, 4, 4, ROWS, D), BF16),
            pltpu.SemaphoreType.DMA((3, 13)),
        ],
        after,
        span=30 if encoder else 0,
    )


def gate_kernel(*refs):
    pass


def gate(values, after):
    outs = call(
        gate_kernel,
        "gate",
        tuple(values),
        "h" * len(values),
        [sds(v.shape, v.dtype) for v in values],
        "h" * len(values),
        [],
        after,
        {n: n for n in range(len(values))},
    )
    return list(outs)


def split_kernel(bx, by, ax, ay, held, sems):
    refs = ((bx.at[0:2], held.at[0], ax), (by.at[2:4], held.at[1], ay))
    into = [pltpu.make_async_copy(src, mid, sems.at[n]) for n, (src, mid, _) in enumerate(refs)]
    out = [pltpu.make_async_copy(mid, dst, sems.at[2 + n]) for n, (_, mid, dst) in enumerate(refs)]
    start(into)
    for n in range(2):
        into[n].wait()
        out[n].start()
    wait(out)


def split(bx, by, after):
    shape = (2, *bx.shape[1:])
    return call(
        split_kernel,
        "split",
        (bx, by),
        "hh",
        [sds(shape, BF16)] * 2,
        "hh",
        [pltpu.VMEM((2, *shape), BF16), pltpu.SemaphoreType.DMA((4,))],
        after,
    )


def cut_kernel(at, line, low, high, held, sems):
    into, out = [], []
    for n, (rows, dst) in enumerate(((slice(0, at), low), (slice(at, held.shape[1]), high))):
        into.append(pltpu.make_async_copy(line.at[:, rows], held.at[:, rows], sems.at[n]))
        out.append(pltpu.make_async_copy(held.at[:, rows], dst, sems.at[2 + n]))
    start(into)
    for n in range(2):
        into[n].wait()
        out[n].start()
    wait(out)


def cut(line, at, after):
    rows = line.shape[1]
    return call(
        functools.partial(cut_kernel, at),
        "cut",
        (line,),
        "h",
        [sds((4, at, HALF), BF16), sds((4, rows - at, HALF), BF16)],
        "hh",
        [pltpu.VMEM((4, rows, HALF), BF16), pltpu.SemaphoreType.DMA((4,))],
        after,
    )


AXES = ("z", "y", "x", "c", "e")


def swap(value, axis):
    return lax.ppermute(value, axis, [(0, 1), (1, 0)])


def pick(value, index, axis):
    return lax.dynamic_index_in_dim(value, index, axis, keepdims=False)


class SpreadGather:
    def __init__(self, rows):
        self.own = lax.all_gather(rows, "z", axis=0, tiled=False)

    def plane(self, after):
        (self.own,) = gate([self.own], after)
        self.bx, self.by = swap(self.own, "x"), swap(self.own, "y")
        self.own_c = swap(self.own, "c")
        return (self.own,)

    def forward(self, after):
        ax, ay = split(self.bx, self.by, (*after, self.own_c))
        self.dx, self.dy = swap(ax, "y"), swap(ay, "x")
        self.bx_c, self.by_c = swap(self.bx, "c"), swap(self.by, "c")
        return (ax,)

    def across(self):
        there = (self.own, self.bx, self.by, self.dx, self.dy)
        self.pieces = (*there, self.own_c, self.bx_c, self.by_c, swap(self.dx, "c"), swap(self.dy, "c"))


class MixedGather:
    def __init__(self, rows, at, along_x, along_y):
        self.at, self.size = at, rows.shape[0]
        self.rows = jnp.concatenate([rows[:at], along_x, rows[at:], along_y])

    def line(self, after):
        (rows,) = gate([self.rows], after)
        self.own = lax.all_gather(rows, "z", axis=0, tiled=False)
        return (rows,)

    def arrive(self, after):
        (self.own,) = gate([self.own], after)
        return (self.own,)

    def plane(self, after):
        self.low, self.high = cut(self.own, 2 * self.at, after)
        return (self.low,)

    def last(self, after=()):
        low, high = self.low, self.high
        if after:
            low, high = gate([low, high], after)
        self.low, self.high = swap(low, "y"), swap(high, "x")
        return (low,)

    def near(self, after):
        tok = self.arrive(after)
        self.own_c = swap(self.own, "c")
        return tok

    def across(self, after):
        self.low, self.high = gate([self.low, self.high], after)
        self.low_c, self.high_c = swap(self.low, "c"), swap(self.high, "c")
        self.pieces = (self.own, self.low, self.high, self.own_c, self.low_c, self.high_c)
        self.part = (Mixed(self.at, self.size), self.pieces)
        return (self.low,)


class Scatter:
    def __init__(self, groups, place, cut=None):
        self.groups, self.place, self.cut = groups, place, cut

    def keep(self, inputs, after):
        a_send, self.a_keep, b_send, self.b_keep = keep(
            self.groups, inputs, self.place, after, self.cut
        )
        self.a_got, self.b_got = swap(a_send, "x"), swap(b_send, "y")
        return (a_send,)

    def next(self, after):
        a_next, b_next = add_next(
            self.a_keep, self.a_got, self.b_keep, self.b_got, self.place, after
        )
        self.a_last, self.b_last = swap(a_next, "y"), swap(b_next, "x")
        return (a_next,)

    def sums(self):
        return (self.a_keep, self.a_got, self.a_last, self.b_keep, self.b_got, self.b_last)


def along_z(scatters, after):
    pairs = []
    for scatter in scatters:
        pairs += [(scatter.a_keep, scatter.a_got), (scatter.b_keep, scatter.b_got)]
    line = add_mid(pairs, after)
    return (line,), lax.psum_scatter(line, "z", scatter_dimension=0, tiled=False)


def finish(scatters, place, after):
    line = add_last([scatter.sums() for scatter in scatters], place, after)
    return (line,), lax.psum_scatter(line, "z", scatter_dimension=0, tiled=False)


def pack_weights(qkv, out, up, down, gains, biases, up_b, c, device):
    rows = out.shape[1]
    panels = jnp.concatenate([qkv, out, up], axis=2).reshape(2, rows, 8, 2, HALF)
    panels = jnp.transpose(panels, (0, 3, 2, 1, 4)).reshape(2, 2, 8 * rows, HALF)
    downs = jnp.transpose(down.reshape(2, 4 * rows, 2, HALF), (0, 2, 1, 3))
    both = jnp.concatenate([panels, downs], axis=2)
    mine = pick(both, c, 1)
    got = swap(pick(both, 1 - c, 1), "c")
    low = jnp.where(c == 0, mine, got)
    high = jnp.where(c == 0, got, mine)
    panels = jnp.stack(
        [low[:, : 8 * rows].reshape(2, 8, rows, HALF), high[:, : 8 * rows].reshape(2, 8, rows, HALF)],
        axis=2,
    ).reshape(2, 16 * rows, HALF)
    downs = jnp.concatenate([low[:, 8 * rows :], high[:, 8 * rows :]], axis=1)
    small = jnp.zeros((2, 16, D), BF16)
    small = lax.dynamic_update_slice(
        small, jnp.concatenate([gains, biases], axis=1), (0, 0, device * rows)
    )
    small = lax.dynamic_update_slice(
        small, up_b[:, None, :], (0, 8 + device // 8, device % 8 * (4 * rows))
    )
    small = jnp.concatenate([small[:, :, :HALF], small[:, :, HALF:]], axis=1)
    part_a = jnp.concatenate([panels[:, : 8 * rows], small], axis=1)
    part_b = jnp.concatenate([panels[:, 8 * rows :], downs], axis=1)
    return part_a, part_b


def body(
    encoder_input,
    corrupted,
    lengths,
    buckets,
    qkv_weight,
    out_weight,
    up_weight,
    down_weight,
    norm_gains,
    bias_rows,
    up_bias,
    encoder_cot,
    decoder_cot,
):
    extra = lax.axis_size("e")
    weights = [qkv_weight, out_weight, up_weight, down_weight, norm_gains, bias_rows, up_bias]
    if extra > 1:
        weights = [
            lax.all_gather(w, "e", axis=at, tiled=True)
            for w, at in zip(weights, (1, 1, 1, 1, 2, 2, 1))
        ]
    rows = weights[1].shape[1]
    x, y, c = lax.axis_index("x"), lax.axis_index("y"), lax.axis_index("c")
    device = ((lax.axis_index("z") * 2 + y) * 2 + x) * 2 + c
    place = jnp.stack([c, x, y]).astype(jnp.int32)
    part_a, part_b = pack_weights(*weights, c, device)
    at_a, at_b = 2 * ROWS, 4 * ROWS
    along_x = swap(jnp.concatenate([part_a[1, :at_a], part_b[1, :at_b]]), "x")
    along_y = swap(jnp.concatenate([part_a[1, at_a:], part_b[1, at_b:]]), "y")
    g0 = SpreadGather(jnp.concatenate([part_a[0], part_b[0]]))
    g1a = MixedGather(part_a[1], at_a, along_x[:at_a], along_y[: PART_A - at_a])
    g1b = MixedGather(part_b[1], at_b, along_x[at_a:], along_y[PART_A - at_a :])

    tok = g0.plane((along_x, along_y))
    tok = g1a.line(tok)
    tok = g1b.line(tok)
    tok = g0.forward(tok)
    g1a.plane(tok)
    g0.across()
    part_a0, part_b0 = (Spread(0), g0.pieces), (Spread(PART_A), g0.pieces)
    tok = g1a.last((g0.dx, g0.dy))
    tok = g1a.near(tok)
    p0, m0, xt0, mt0, stat0, vec0 = attend(encoder_input, lengths, buckets, place, part_a0, tok, 0)
    tok = g1b.near((stat0,))
    tok = g1b.plane((*tok, g1a.own_c))
    g1b.last()
    tok = g1a.across(tok)
    enc_out, *saved0, xd, xdl, y1t0, gt0, give0 = feed(
        True, encoder_input, m0, vec0, place, part_a0, part_b0, tok, corrupted, buckets
    )
    given0 = swap(give0, "c")
    xt0_other, mt0_other = swap(xt0, "c"), swap(mt0, "c")
    part_a1 = g1a.part
    p1, m1, xt1, mt1, stat1, vec1 = attend(
        xdl, lengths, buckets, place, part_a1, (enc_out,), 0
    )
    xt1_other, mt1_other = swap(xt1, "c"), swap(mt1, "c")
    tok = g1b.across((stat1,))
    part_b1 = g1b.part
    dec_out, *saved1, y1t1, gt1, give1 = feed(
        False, xd, m1, vec1, place, part_a1, part_b1, tok
    )
    given1 = swap(give1, "c")

    n1, r1, n2, r2, gp = saved1
    dr2l, dr1, dml, small, dul, dul_give, dr1l, resid = feed_back(
        False, decoder_cot, n2, r2, vec1, gp, n1, r1, place, part_a1, part_b1, (dec_out, given0)
    )
    resid, dul_other = swap(resid, "c"), swap(dul_give, "c")
    cuts = ((208, 432), (96, 176))
    s1, q1 = Scatter(("do", "u"), place, cuts[0][0]), Scatter(("q",), place, cuts[1][0])
    part, low, high, small = attend_back(p1, dml, stat1, small, lengths, buckets, place, (dr1,))
    part_other = [swap(low, "c"), swap(high, "c")]
    tok = s1.keep(
        (gt1, dr2l, resid, given1, mt1, mt1_other, dr1l, y1t1, dul, dul_other, given1), (small,)
    )
    tok = q1.keep((xt1, xt1_other, part, *part_other, small), tok)
    dxd, cor_grad = input_back(False, (part, low, high), dr1, place, part_a1, tok, buckets)
    tok = (cor_grad,)

    n1, r1, n2, r2, gp = saved0
    dr2l, dr1, dml, small, dul, dul_give, dr1l, resid = feed_back(
        True, encoder_cot, n2, r2, vec0, gp, n1, r1, place, part_a0, part_b0, tok, dxd, buckets
    )
    resid, dul_other = swap(resid, "c"), swap(dul_give, "c")
    tok, dec_total = along_z([s1, q1], (dr1,))
    s0, q0 = Scatter(("do", "u"), place), Scatter(("q",), place)
    tok = s0.keep(
        (gt0, dr2l, resid, given0, mt0, mt0_other, dr1l, y1t0, dul, dul_other, given0), tok
    )
    part, low, high, small = attend_back(p0, dml, stat0, small, lengths, buckets, place, tok)
    part_other = [swap(low, "c"), swap(high, "c")]
    tok = q0.keep((xt0, xt0_other, part, *part_other, small), (small,))
    tok = s0.next(tok)
    (enc_grad,) = input_back(True, (part, low, high), dr1, place, part_a0, tok)
    tok = q0.next((enc_grad,))
    (dec_total,) = gate([dec_total], tok)
    tok, both0 = finish([s0, q0], place, (dec_total,))
    sent = part_rows(dec_total, cuts, place, tok)
    got = [swap(value, "yx"[n % 2]) for n, value in enumerate(sent)]
    feed1, attend1 = close(dec_total, got, cuts, place, ())

    def rows_of(feed_part, attend_part):
        panels = jnp.concatenate([attend_part[:144], feed_part[192:]], axis=0)
        panels = panels.reshape(8, 2, rows, HALF)
        mine = pick(panels, c, 1)
        got = swap(pick(panels, 1 - c, 1), "c")
        panels = jnp.concatenate([jnp.where(c == 0, mine, got), jnp.where(c == 0, got, mine)], axis=2)
        qkv_grad = jnp.concatenate([panels[0], panels[1], panels[2]], axis=1)
        up_grad = jnp.concatenate([panels[4], panels[5], panels[6], panels[7]], axis=1)
        down_grad = jnp.concatenate([feed_part[:96], feed_part[96:192]], axis=1)
        small = jnp.concatenate([attend_part[144:160], attend_part[160:]], axis=1)
        heads = lax.dynamic_slice(small, (0, device * rows), (8, rows))
        up_b_grad = lax.dynamic_slice(small, (8 + device // 8, device % 8 * (4 * rows)), (1, 4 * rows))
        return qkv_grad, panels[3], up_grad, down_grad, heads[:2], heads[2:], up_b_grad[0]

    dec_grads = rows_of(feed1, attend1)
    enc_grads = rows_of(both0[:432], both0[432:])
    grads_out = [jnp.stack(pair).astype(F32) for pair in zip(enc_grads, dec_grads)]
    if extra > 1:
        grads_out = [
            lax.psum_scatter(v, "e", scatter_dimension=at, tiled=True)
            for v, at in zip(grads_out, (1, 1, 1, 1, 2, 2, 1))
        ]
    return (enc_out, dec_out, enc_grad, cor_grad, *grads_out)


def solution(mesh):
    devices = mesh.devices.reshape(4, 2, 2, 2, -1)
    inner = Mesh(devices, AXES)
    token = P(AXES, None)
    line = P(AXES)
    wide = P(None, AXES, None)
    vector = P(None, None, AXES)
    return jax.shard_map(
        body,
        mesh=inner,
        in_specs=(
            token, token, line, line, wide, wide, wide, wide, vector, vector, P(None, AXES), token, token,
        ),
        out_specs=(
            token, token, token, token, wide, wide, wide, wide, vector, vector, P(None, AXES),
        ),
        check_vma=False,
    )
```

```python
import functools

import jax
import jax.numpy as jnp
from jax import lax
from jax.experimental import pallas as pl
from jax.experimental.pallas import tpu as pltpu
from jax.sharding import Mesh
from jax.sharding import PartitionSpec as P

HD = 64
SLOT = 128
EPSILON = 1e-06
NEGATIVE = -1e30
F32 = jnp.float32
BF16 = jnp.bfloat16
VMEM_LIMIT = 64 * 1024 * 1024

T = 512
D = 768
HALF = D // 2
ROWS = 48
DROWS = 192
O_AT, SMALL_AT, PART_A = 144, 192, 224
D_AT, PART_B = 192, 384

NORM_ROWS = 256
ATTEND_BACK_PAIRS = 2
SM = pl.BlockSpec(memory_space=pltpu.SMEM)
HBM = pl.BlockSpec(memory_space=pl.ANY)
SPAN = {
    "feed": 20,
    "add_next": 12,
    "add_mid": 16,
}


def dot(left, right):
    return lax.dot_general(left, right, (((1,), (0,)), ((), ())), preferred_element_type=F32)


def dot_rt(left, right):
    return lax.dot_general(left, right, (((1,), (1,)), ((), ())), preferred_element_type=F32)


def sds(shape, dtype):
    return jax.ShapeDtypeStruct(shape, dtype)


class In:
    def __init__(self, source, held, sem, late):
        self.held, self.copy, self.there = held, pltpu.make_async_copy(source, held, sem), False
        self.begun = False
        if not late:
            self.start()

    def start(self):
        self.begun = True
        self.copy.start()

    def __call__(self):
        if not self.begun:
            self.start()
        if not self.there:
            self.copy.wait()
            self.there = True
        return self.held


class Out:
    def __init__(self, target, held, sems):
        self.target, self.held, self.sems, self.copies = target, held, sems, []

    def send(self, index=None):
        source = self.held if index is None else self.held.at[index]
        target = self.target if index is None else self.target.at[index]
        copy = pltpu.make_async_copy(source, target, self.sems.at[len(self.copies)])
        copy.start()
        self.copies.append(copy)

    def wait(self):
        for copy in self.copies:
            copy.wait()


def call(kernel, name, args, in_kinds, outs, out_kinds, scratch, after=(), aliases=None, span=None):
    n, m, k = len(args), len(after), len(outs)
    spec = {"i": HBM, "l": HBM, "o": HBM, "h": HBM, "s": SM}
    ins = [a for a, kind in zip(args, in_kinds) if kind in "il"]
    sent = [o for o, kind in zip(outs, out_kinds) if kind == "o"]

    def ordered(*refs):
        inputs, results, rest = refs[:n], refs[n + m : n + m + k], refs[n + m + k :]
        held_in, held_out = rest[: len(ins)], rest[len(ins) : len(ins) + len(sent)]
        own = rest[len(ins) + len(sent) : len(ins) + len(sent) + len(scratch)]
        sems = rest[len(ins) + len(sent) + len(scratch) :]
        lazy, at = [], 0
        for ref, kind in zip(inputs, in_kinds):
            if kind in "il":
                ref, at = In(ref, held_in[at], sems[0].at[at], kind == "l"), at + 1
            lazy.append(ref)
        flow, at = [], 0
        for ref, kind in zip(results, out_kinds):
            if kind == "o":
                ref, at = Out(ref, held_out[at], sems[-1].at[at]), at + 1
            flow.append(ref)
        kernel(*lazy, *flow, *own)
        for ref in lazy:
            if isinstance(ref, In):
                ref()
        flow = [ref for ref in flow if isinstance(ref, Out)]
        for ref in flow:
            if not ref.copies:
                ref.send()
        for ref in flow:
            ref.wait()

    sems = []
    if ins:
        sems.append(pltpu.SemaphoreType.DMA((len(ins),)))
    if sent:
        sems.append(pltpu.SemaphoreType.DMA((len(sent), 4)))
    return pl.pallas_call(
        ordered,
        out_shape=outs,
        in_specs=[*(spec[kind] for kind in in_kinds), *([HBM] * m)],
        out_specs=[HBM] * k,
        scratch_shapes=[
            *(pltpu.VMEM(a.shape, a.dtype) for a in ins),
            *(pltpu.VMEM(o.shape, o.dtype) for o in sent),
            *scratch,
            *sems,
        ],
        input_output_aliases=aliases or {},
        compiler_params=pltpu.CompilerParams(vmem_limit_bytes=VMEM_LIMIT),
        cost_estimate=pl.CostEstimate(
            flops=int(1000 + 1.1e9 * (SPAN.get(name, 0) if span is None else span)), bytes_accessed=1000, transcendentals=0
        ),
        name=name,
    )(*args, *after)


def start(copies):
    for copy in copies:
        copy.start()


def wait(copies):
    for copy in copies:
        copy.wait()


class Spread:
    count = 10

    def __init__(self, base):
        self.base = base

    def slabs(self, refs, place, row_at, rows):
        c, x, y = place[0], place[1], place[2]
        across = 2 * (1 - y) + (1 - x)
        slots = ((2 * y + x, 0, 4), (2 * y + 1 - x, 0, 4), (2 * (1 - y) + x, 0, 4), (across, 0, 2), (across, 2, 4))
        first = self.base + row_at
        for half, group in ((c, refs[:5]), (1 - c, refs[5:])):
            for ref, (at, low, high) in zip(group, slots):
                yield ref.at[:, first : first + rows, :], at, low, high, half


class Mixed:
    count = 6

    def __init__(self, cut, size):
        self.cut, self.size = cut, size

    def slabs(self, refs, place, row_at, rows):
        c, x, y = place[0], place[1], place[2]
        own, near_x, near_y = 2 * y + x, 2 * y + 1 - x, 2 * (1 - y) + x
        across = 2 * (1 - y) + (1 - x)
        rest = self.size - self.cut
        for half, (line, low, high) in ((c, refs[:3]), (1 - c, refs[3:])):
            if row_at < self.cut:
                places = ((line, row_at, own), (line, self.cut + row_at, near_x))
                places += ((low, row_at, near_y), (low, self.cut + row_at, across))
            else:
                first, base = row_at - self.cut, 2 * self.cut
                places = ((line, base + first, own), (line, base + rest + first, near_y))
                places += ((high, first, near_x), (high, rest + first, across))
            for ref, first, at in places:
                yield ref.at[:, first : first + rows, :], at, 0, 4, half


def half_cols(h):
    return pl.ds(pl.multiple_of(h * HALF, HALF), HALF)


def panel_copies(layout, refs, place, dst, sems, row_at, rows):
    copies = []
    for n, (src, at, low, high, half) in enumerate(layout.slabs(refs, place, row_at, rows)):
        copies.append(
            pltpu.make_async_copy(src, dst.at[low:high, at, :, half_cols(half)], sems.at[n])
        )
    return copies


def fill_bias(bias, lens, buck):
    bucket = buck[0]
    key = lax.broadcasted_iota(jnp.int32, (T, T), 0)
    query = lax.broadcasted_iota(jnp.int32, (T, T), 1)
    shift = bucket + 7
    same = lax.shift_right_logical(key, shift) == lax.shift_right_logical(query, shift)
    position = jnp.bitwise_and(key, lax.shift_left(jnp.int32(SLOT), bucket) - 1)
    slot = lax.shift_right_logical(key, 7)
    length = jnp.where(
        slot < 2,
        jnp.where(slot == 0, lens[0], lens[1]),
        jnp.where(slot == 2, lens[2], lens[3]),
    )
    bias[...] = jnp.where(same & (position < length), 0.0, NEGATIVE)


def first_tokens(buck, low, size):
    span = lax.shift_left(jnp.int32(SLOT), buck[0])
    token = lax.broadcasted_iota(jnp.int32, (size, 1), 0) + low
    return jnp.bitwise_and(token, span - 1) == 0


def halves(block):
    lane = lax.broadcasted_iota(jnp.int32, block.shape, 1)
    zero = jnp.zeros_like(block)
    return jnp.where(lane < HD, block, zero), jnp.where(lane < HD, zero, block)


def row_loop(size, body):
    if size == T:
        return body(pl.ds(0, T))

    def step(i, carry):
        body(pl.ds(pl.multiple_of(i * size, size), size))
        return carry

    lax.fori_loop(0, T // size, step, 0)


def attend_kernel(layout, *refs):
    x, lens, buck, place = refs[:4]
    pieces, refs = refs[4 : 4 + layout.count], refs[4 + layout.count :]
    flow, (wq, bias, heap, sems) = refs[:6], refs[6:]
    p, m, xt, mt, stat, vec = (ref.held for ref in flow)
    copies = [
        panel_copies(layout, pieces, place, wq.at[j], sems.at[j], j * ROWS, ROWS) for j in range(3)
    ]
    smalls, at = [], 0
    for n, (src, _, low, high, _) in enumerate(layout.slabs(pieces, place, SMALL_AT, 32)):
        smalls.append(pltpu.make_async_copy(src, heap.at[at : at + high - low], sems.at[3, n]))
        at += high - low
    start(smalls)
    for group in copies:
        start(group)
    fill_bias(bias, lens, buck)
    x = x()
    xt[...] = x[...].T
    flow[2].send()
    wait(smalls)
    total = heap[0].astype(F32)
    for n in range(1, 32):
        total = total + heap[n].astype(F32)
    vec[...] = jnp.concatenate([total[:16], total[16:]], axis=1)
    flow[5].send()
    for j in range(3):
        wait(copies[j])
        weight = wq[j].reshape(D, D)
        for half in range(2):
            rows = slice(half * 256, half * 256 + 256)
            out = dot(x[rows, :], weight)
            if j != 1:
                out = out + (vec[2:3, :] if j == 0 else vec[3:4, :])
            out = out.astype(BF16)
            for s in range(6):
                p[6 * j + s, rows, :] = out[:, 128 * s : 128 * s + 128]
        flow[0].send(slice(6 * j, 6 * j + 6))

    def pair(i):
        q = p[i] * jnp.asarray(HD**-0.5, BF16)
        v_t = p[12 + i].T
        both = dot_rt(jnp.concatenate(halves(p[6 + i]), axis=0), q)
        mixed = []
        for a in range(2):
            scores = both[T * a : T * a + T] + bias[...]
            peak = jnp.max(scores, axis=0, keepdims=True)
            weights = jnp.exp(scores - peak)
            inverse = 1.0 / jnp.sum(weights, axis=0, keepdims=True)
            stat[2 * i + a, 0:1, :] = peak
            stat[2 * i + a, 1:2, :] = inverse
            soft = (weights * inverse).astype(BF16)
            mixed.append(dot(v_t[HD * a : HD * a + HD, :], soft))
        mixed = jnp.concatenate(mixed, axis=0)
        mt[pl.ds(pl.multiple_of(i * 128, 128), 128), :] = mixed.astype(BF16)
        m[i] = mixed.T.astype(BF16)

    def pairs(n, carry):
        for k in range(3):
            pair(3 * n + k)
        return carry

    lax.fori_loop(0, 2, pairs, 0)


def attend(x, lens, buck, place, part, after, span):
    layout, pieces = part
    return call(
        functools.partial(attend_kernel, layout),
        "attend",
        (x, lens, buck, place, *pieces),
        "isss" + "h" * layout.count,
        [
            sds((18, T, 128), BF16),
            sds((6, T, 128), BF16),
            sds((D, T), BF16),
            sds((D, T), BF16),
            sds((12, 8, T), F32),
            sds((16, D), F32),
        ],
        "o" * 6,
        [
            pltpu.VMEM((3, 4, 4, ROWS, D), BF16),
            pltpu.VMEM((T, T), F32),
            pltpu.VMEM((32, 32, HALF), BF16),
            pltpu.SemaphoreType.DMA((4, 10)),
        ],
        after,
        span=span,
    )


def unit_norm(resid):
    center = jnp.mean(resid, axis=-1, keepdims=True)
    shifted = resid - center
    spread = jnp.mean(shifted * shifted, axis=-1, keepdims=True)
    inverse = lax.rsqrt(spread + EPSILON)
    return shifted * inverse, inverse


def weight_copies(layout_a, layout_b, pieces_a, pieces_b, place, wo, wu, wd, sems):
    o_copies = panel_copies(layout_a, pieces_a, place, wo, sems.at[0], O_AT, ROWS)
    u_copies = [
        panel_copies(layout_b, pieces_b, place, wu.at[j], sems.at[1 + j], j * ROWS, ROWS)
        for j in range(4)
    ]
    return o_copies, u_copies, panel_copies(layout_b, pieces_b, place, wd, sems.at[5], D_AT, DROWS)


class Sender:
    def __init__(self, sems):
        self.sems, self.copies = sems, []

    def __call__(self, source, target):
        self.copies.append(pltpu.make_async_copy(source, target, self.sems.at[len(self.copies)]))
        self.copies[-1].start()

    def wait(self):
        wait(self.copies)


def feed_rows(x, m, vec, copies, weights, saved, work, first_done, panel_done, result):
    o_copies, u_copies, d_copies = copies
    wo, wu, wd = weights
    n1, r1, n2, r2, gp = saved
    scr, y1, y1l, g = work
    wait(o_copies)
    m, x, vec = m(), x(), vec()
    weight = wo[...].reshape(D, D)
    for half in range(2):
        rows = slice(half * 256, half * 256 + 256)
        left = jnp.concatenate([m[s, rows, :] for s in range(6)], axis=1)
        scr[rows, :] = dot(left, weight)

    def first(rows):
        resid = x[rows, :].astype(F32) + (scr[rows, :] + vec[4:5, :])
        unit, inverse = unit_norm(resid)
        n1[rows, :] = unit
        r1[rows, :] = jnp.broadcast_to(inverse, (inverse.shape[0], 128))
        normed = unit * vec[0:1, :] + vec[5:6, :]
        y1[rows, :] = normed
        y1l[rows, :] = normed.astype(BF16)

    row_loop(NORM_ROWS, first)
    first_done()
    for j in range(4):
        wait(u_copies[j])

        def up(rows, j=j):
            left = y1l[rows, :]
            for k in range(3):
                cols = slice(256 * k, 256 * k + 256)
                right = wu[j, :, :, :, cols].reshape(D, 256)
                hidden = dot(left, right) + vec[8 + j : 9 + j, cols]
                cdf = 0.5 * (1.0 + lax.erf(hidden * (0.5**0.5)))
                g[j, rows, cols] = (hidden * cdf).astype(BF16)
                density = jnp.exp(hidden * hidden * -0.5) * 0.3989422804014327
                gp[j, rows, cols] = (cdf + hidden * density).astype(BF16)

        row_loop(256, up)
        panel_done(j)
    wait(d_copies)
    for half in range(2):
        rows = slice(half * 256, half * 256 + 256)
        total = dot(g[0, rows, :], wd[0].reshape(D, D))
        for j in range(1, 4):
            total = total + dot(g[j, rows, :], wd[j].reshape(D, D))
        scr[rows, :] = total

    def second(rows):
        resid = y1[rows, :] + (scr[rows, :] + vec[6:7, :])
        unit, inverse = unit_norm(resid)
        n2[rows, :] = unit
        r2[rows, :] = jnp.broadcast_to(inverse, (inverse.shape[0], 128))
        result(rows, unit * vec[1:2, :] + vec[7:8, :])

    row_loop(NORM_ROWS, second)


def feed_back_rows(output_grad, vec, small, copies, weights, saved, work, outs, send, c):
    o_copies, u_copies, d_copies = copies
    wo, wu, wd = weights
    n1, r1, n2, r2, gp = saved
    scr, dul, dr1l = work
    dr2l, dr1, dml, dul_keep, dul_give, dr1_keep, resid_give = outs
    small[...] = jnp.zeros_like(small)
    vec, n2, r2 = vec(), n2(), r2()

    def second(rows):
        grad = output_grad(rows)
        unit = n2[rows, :]
        resid = norm_back(grad, unit, r2[rows, 0:1], vec[1:2, :])
        small[1:2, :] += column_sum(grad * unit)
        small[7:8, :] += column_sum(grad)
        small[6:7, :] += column_sum(resid)
        scr[rows, :] = resid
        dr2l.held[rows, :] = resid.astype(BF16)

    row_loop(NORM_ROWS, second)
    dr2l.send()
    for half in range(2):
        send(dr2l.held.at[:, half * HALF : half * HALF + HALF], resid_give.at[half])
    wait(d_copies)
    gp = gp()
    for j in range(4):

        def up(rows, j=j):
            left = dr2l.held[rows, :]
            weight = wd[j].reshape(D, D)
            for k in range(3):
                cols = slice(256 * k, 256 * k + 256)
                grad = dot_rt(left, weight[cols, :])
                hidden = (grad * gp[j, rows, cols].astype(F32)).astype(BF16)
                dul[j, rows, cols] = hidden
                small[8 + j : 9 + j, cols] += column_sum(hidden.astype(F32))

        row_loop(256, up)
        send(dul.at[j, :, half_cols(1 - c)], dul_give.at[j])
        send(dul.at[j, :, half_cols(c)], dul_keep.at[j])
        wait(u_copies[j])
        for half in range(2):
            rows = slice(half * 256, half * 256 + 256)
            scr[rows, :] += dot_rt(dul[j, rows, :], wu[j].reshape(D, D))
    n1, r1 = n1(), r1()

    def first(rows):
        grad = scr[rows, :]
        unit = n1[rows, :]
        resid = norm_back(grad, unit, r1[rows, 0:1], vec[0:1, :])
        small[0:1, :] += column_sum(grad * unit)
        small[5:6, :] += column_sum(grad)
        small[4:5, :] += column_sum(resid)
        dr1.held[rows, :] = resid
        dr1l[rows, :] = resid.astype(BF16)

    row_loop(NORM_ROWS, first)
    send(dr1l.at[:, half_cols(1 - c)], resid_give.at[2])
    send(dr1l.at[:, half_cols(c)], dr1_keep)
    dr1.send()
    wait(o_copies)
    weight = wo[...].reshape(D, D)
    for half in range(2):
        rows = slice(half * 256, half * 256 + 256)
        out = dot_rt(dr1l[rows, :], weight).astype(BF16)
        for s in range(6):
            dml.held[s, rows, :] = out[:, 128 * s : 128 * s + 128]


def send_transposed(send, y1l, g, y1t, gt, outs, c):
    y1t_out, gt_out, give_out = outs

    def first_done():
        y1t[...] = y1l[...].T.reshape(8, 96, T)
        send(y1t, y1t_out)
        send(y1t, give_out.at[0:8])

    def panel_done(j):
        gt[j] = g[j].T.reshape(4, 2, 96, T)
        send(gt.at[j, :, c], gt_out.at[j])
        send(gt.at[j, :, 1 - c], give_out.at[8 + 4 * j : 12 + 4 * j])

    return first_done, panel_done


TRANSPOSED = [sds((8, 96, T), BF16), sds((4, 4, 96, T), BF16), sds((24, 96, T), BF16)]
WEIGHTS = [
    pltpu.VMEM((4, 4, ROWS, D), BF16),
    pltpu.VMEM((4, 4, 4, ROWS, D), BF16),
    pltpu.VMEM((4, 4, DROWS, D), BF16),
]


def feed_kernel(layout_a, layout_b, *refs):
    x, m, vec, place, cor, buck = refs[:6]
    pieces_a, refs = refs[6 : 6 + layout_a.count], refs[6 + layout_a.count :]
    pieces_b, refs = refs[: layout_b.count], refs[layout_b.count :]
    flow, transposed, refs = refs[:8], refs[8:11], refs[11:]
    out, n1, r1, n2, r2, gp, xd, xdl = (ref.held for ref in flow)
    wo, wu, wd, scr, y1, y1l, g, y1t, gt, sems, out_sems = refs
    c = place[0]
    send = Sender(out_sems)
    copies = weight_copies(layout_a, layout_b, pieces_a, pieces_b, place, wo, wu, wd, sems)
    start(copies[0])
    for group in copies[1]:
        start(group)
    start(copies[2])
    first_sent, panel_sent = send_transposed(send, y1l, g, y1t, gt, transposed, c)

    def first_done():
        first_sent()
        flow[1].send()
        flow[2].send()

    def panel_done(j):
        panel_sent(j)
        flow[5].send(j)

    def result(rows, value):
        out[rows, :] = value.astype(BF16)
        mixed = jnp.where(
            first_tokens(buck, rows.start, NORM_ROWS), value, cor()[rows, :].astype(F32)
        )
        xd[rows, :] = mixed
        xdl[rows, :] = mixed.astype(BF16)

    cor()
    feed_rows(
        x, m, vec, copies, (wo, wu, wd), (n1, r1, n2, r2, gp), (scr, y1, y1l, g), first_done, panel_done, result
    )
    send.wait()


def feed(x, m, vec, place, part_a, part_b, after, cor, buck):
    (layout_a, pieces_a), (layout_b, pieces_b) = part_a, part_b
    outs = [
        sds((T, D), BF16),
        sds((T, D), F32),
        sds((T, 128), F32),
        sds((T, D), F32),
        sds((T, 128), F32),
        sds((4, T, D), BF16),
        sds((T, D), F32),
        sds((T, D), BF16),
    ]
    return call(
        functools.partial(feed_kernel, layout_a, layout_b),
        "feed",
        (x, m, vec, place, cor, buck, *pieces_a, *pieces_b),
        "iiisis" + "h" * (layout_a.count + layout_b.count),
        [*outs, *TRANSPOSED],
        "o" * len(outs) + "hhh",
        [
            *WEIGHTS,
            pltpu.VMEM((T, D), F32),
            pltpu.VMEM((T, D), F32),
            pltpu.VMEM((T, D), BF16),
            pltpu.VMEM((4, T, D), BF16),
            pltpu.VMEM((8, 96, T), BF16),
            pltpu.VMEM((4, 4, 2, 96, T), BF16),
            pltpu.SemaphoreType.DMA((6, 10)),
            pltpu.SemaphoreType.DMA((10,)),
        ],
        after,
        span=0,
    )


def norm_back(grad, unit, inverse, gain):
    scaled = grad * gain
    mean = jnp.mean(scaled, axis=-1, keepdims=True)
    along = jnp.mean(scaled * unit, axis=-1, keepdims=True)
    return inverse * (scaled - mean - unit * along)


def column_sum(value):
    return jnp.sum(value, axis=0, keepdims=True)


GROUPS = {"do": (240, "iiihlll"), "u": (192, "lllh"), "q": (176, "iiiiii")}


def down_out_grads(more, block, at, held, sems, gt, dr2l, resid_other, given, xm, xm_other, dr1l):
    copies = [
        pltpu.make_async_copy(given.at[8 + 4 * j : 12 + 4 * j], held.at[4 * j : 4 * j + 4], sems.at[j])
        for j in range(4)
    ]
    start(copies)
    gt, dr2l, resid_other = gt(), dr2l(), resid_other()
    for ref in (xm, xm_other, dr1l, *more):
        ref.start()
    dr2l_other = jnp.concatenate([resid_other[0], resid_other[1]], axis=1)
    for j in range(4):
        mine = dot(gt[j].reshape(4 * 96, T), dr2l[...])
        copies[j].wait()
        other = dot(held[4 * j : 4 * j + 4].reshape(4 * 96, T), dr2l_other)
        value = (mine + other).astype(BF16)
        for half in range(2):
            rows = slice(at + 96 * half, at + 96 * half + 96)
            block[j, :, rows] = value[:, half * HALF : half * HALF + HALF].reshape(4, 96, HALF)
    xm, xm_other, dr1l = xm(), xm_other(), dr1l()
    panel_grad(block, at + 192, dot(xm[...], dr1l[...]), dot(xm_other[...], resid_other[2]))


def panel_grad(block, at, mine, other):
    block[:, :, at : at + ROWS] = (mine + other).astype(BF16).reshape(4, 4, ROWS, HALF)


def up_grads(more, block, at, held, sems, y1t, dul, dul_other, given):
    copy = pltpu.make_async_copy(given.at[0:8], held.at[16:24], sems.at[4])
    copy.start()
    y1t, dul, dul_other = y1t(), dul(), dul_other()
    left = y1t[...].reshape(D, T)
    copy.wait()
    left_other = held[16:24].reshape(D, T)
    for j in range(4):
        panel_grad(block, at + j * ROWS, dot(left, dul[j]), dot(left_other, dul_other[j]))


def qkv_grads(more, block, at, held, sems, xt, xt_other, part, part_low, part_high, small):
    xt, xt_other, part = xt(), xt_other(), part()
    part_other = [p[s] for p in (part_low(), part_high()) for s in range(5)]
    for j in range(3):
        mine, other = (
            jnp.concatenate([p[s] for s in range(3 * j, 3 * j + 3)], axis=1)
            for p in (part, part_other)
        )
        panel_grad(block, at + j * ROWS, dot(xt[...], mine), dot(xt_other[...], other))
    other = [part_other[9][16 * k : 16 * k + 16, :].astype(F32) for k in range(6)]
    small = small()[...] + jnp.concatenate(other, axis=1)
    small = jnp.concatenate([small[:, :HALF], small[:, HALF:]], axis=0)
    block[:, :, at + 144 : at + 176] = jnp.broadcast_to(small.astype(BF16), (4, 4, 32, HALF))


FILLS = {"do": down_out_grads, "u": up_grads, "q": qkv_grads}


def send_spread(block, part, place, outs):
    x, y = place[1], place[2]
    a_send, a_keep, b_send, b_keep = outs
    for side, a, b in ((1, a_send, b_send), (0, a_keep, b_keep)):
        for n in range(2):
            yield block.at[0:2, 2 * n + lax.bitwise_xor(x, side), part], a.at[n, :, part]
            yield block.at[2:4, 2 * lax.bitwise_xor(y, side) + n, part], b.at[n, :, part]


def send_mixed(cut, block, part, place, outs):
    x, y = place[1], place[2]
    a_send, a_keep, b_send, b_keep = outs
    low = slice(part.start, min(part.stop, cut))
    high = slice(max(part.start, cut), part.stop)
    for side, a, b in ((1, a_send, b_send), (0, a_keep, b_keep)):
        for n in range(2):
            if low.start < low.stop:
                yield block.at[:, 2 * n + lax.bitwise_xor(x, side), low], a.at[:, n, low]
            if high.start < high.stop:
                to = slice(high.start - cut, high.stop - cut)
                yield block.at[:, 2 * lax.bitwise_xor(y, side) + n, high], b.at[:, n, to]


def keep_kernel(groups, send, *refs):
    count = sum(len(GROUPS[g][1]) for g in groups)
    inputs, refs = refs[:count], refs[count:]
    place, outs, (block, held, sems, out_sems) = refs[0], refs[1:5], refs[5:]
    copies, at, first = [], 0, 0
    for g in groups:
        rows, kinds = GROUPS[g]
        more = [ref for ref in inputs[first + len(kinds) :] if isinstance(ref, In)]
        FILLS[g](more, block, at, held, sems, *inputs[first : first + len(kinds)])
        new = [
            pltpu.make_async_copy(src, dst, out_sems.at[len(copies) + n])
            for n, (src, dst) in enumerate(send(block, slice(at, at + rows), place, outs))
        ]
        start(new)
        copies += new
        at, first = at + rows, first + len(kinds)
    wait(copies)


def keep(groups, inputs, place, after, cut=None):
    rows = sum(GROUPS[g][0] for g in groups)
    if cut is None:
        send, outs = send_spread, [sds((2, 2, rows, HALF), BF16)] * 4
    else:
        send = functools.partial(send_mixed, cut)
        outs = [sds((4, 2, cut, HALF), BF16)] * 2 + [sds((4, 2, rows - cut, HALF), BF16)] * 2
    return call(
        functools.partial(keep_kernel, groups, send),
        "keep_grads",
        (*inputs, place),
        "".join(GROUPS[g][1] for g in groups) + "s",
        outs,
        "hhhh",
        [
            pltpu.VMEM((4, 4, rows, HALF), BF16),
            pltpu.VMEM((24, 96, T), BF16),
            pltpu.SemaphoreType.DMA((5,)),
            pltpu.SemaphoreType.DMA((16 * len(groups),)),
        ],
        after,
    )


def add_mid_kernel(sizes, *refs):
    pairs, line, blocks, sems = refs[: 2 * len(sizes)], refs[2 * len(sizes)], refs[2 * len(sizes) + 1 : -1], refs[-1]
    copies = [
        pltpu.make_async_copy(ref, blocks[n // 2].at[n % 2], sems.at[n]) for n, ref in enumerate(pairs)
    ]
    start(copies)
    at = 0
    for g, size in enumerate(sizes):
        wait(copies[2 * g : 2 * g + 2])
        total = (blocks[g][0].astype(F32) + blocks[g][1].astype(F32)).astype(BF16)
        line.held[:, at : at + 2 * size] = total.reshape(4, 2 * size, HALF)
        at += 2 * size


def add_mid(pairs, after):
    sizes = [keep.shape[2] for keep, _ in pairs]
    (line,) = call(
        functools.partial(add_mid_kernel, sizes),
        "add_mid",
        tuple(array for pair in pairs for array in pair),
        "h" * (2 * len(pairs)),
        [sds((4, 2 * sum(sizes), HALF), BF16)],
        "o",
        [
            *(pltpu.VMEM((2, 4, 2, size, HALF), BF16) for size in sizes),
            pltpu.SemaphoreType.DMA((2 * len(sizes),)),
        ],
        after,
    )
    return line


def part_slices(cuts, place):
    x, y = place[1], place[2]
    slices, base = [], 0
    for g, (cut, rows) in enumerate(cuts):
        for size, mine in ((cut, y), (rows - cut, x)):
            own, other = (
                pl.ds(pl.multiple_of(base + side * size, 16), size) for side in (mine, 1 - mine)
            )
            slices.append((g, size, own, other))
            base += 2 * size
    return slices


def part_kernel(cuts, total, place, *refs):
    n = 2 * len(cuts)
    outs, held, sems = refs[:n], refs[n : 2 * n], refs[-1]
    into, out = [], []
    for k, (_, _, _, other) in enumerate(part_slices(cuts, place)):
        into.append(pltpu.make_async_copy(total.at[other], held[k], sems.at[2 * k]))
        out.append(pltpu.make_async_copy(held[k], outs[k], sems.at[2 * k + 1]))
    start(into)
    for k, copy in enumerate(into):
        copy.wait()
        out[k].start()
    wait(out)


def part_rows(total, cuts, place, after):
    shapes = [sds((size, HALF), BF16) for cut, rows in cuts for size in (cut, rows - cut)]
    return call(
        functools.partial(part_kernel, cuts),
        "part",
        (total, place),
        "hs",
        shapes,
        "h" * len(shapes),
        [
            *(pltpu.VMEM(shape.shape, BF16) for shape in shapes),
            pltpu.SemaphoreType.DMA((2 * len(shapes),)),
        ],
        after,
    )


def close_kernel(cuts, total, *refs):
    n = len(cuts)
    got, place, flow = refs[: 2 * n], refs[2 * n], refs[2 * n + 1 : 3 * n + 1]
    held, sems = refs[3 * n + 1 : -1], refs[-1]
    slices = part_slices(cuts, place)
    copies = [
        pltpu.make_async_copy(total.at[own], held[k], sems.at[k])
        for k, (_, _, own, _) in enumerate(slices)
    ]
    start(copies)
    at = 0
    for k, (g, size, _, _) in enumerate(slices):
        copies[k].wait()
        at = 0 if k % 2 == 0 else at
        value = held[k][...].astype(F32) + got[k]()[...].astype(F32)
        flow[g].held[at : at + size] = value.astype(BF16)
        at += size


def close(total, got, cuts, place, after):
    shapes = [sds((rows, HALF), BF16) for _, rows in cuts]
    sizes = [size for cut, rows in cuts for size in (cut, rows - cut)]
    return call(
        functools.partial(close_kernel, cuts),
        "close",
        (total, *got, place),
        "h" + "i" * len(got) + "s",
        shapes,
        "o" * len(shapes),
        [
            *(pltpu.VMEM((size, HALF), BF16) for size in sizes),
            pltpu.SemaphoreType.DMA((len(sizes),)),
        ],
        after,
    )


def add_next_kernel(a_keep, a_got, b_keep, b_got, place, a_next, b_next, blocks, sems):
    x, y = place[1], place[2]
    refs = (a_keep.at[1 - y], a_got.at[1 - y], b_keep.at[1 - x], b_got.at[1 - x])
    copies = [pltpu.make_async_copy(ref, blocks.at[n], sems.at[n]) for n, ref in enumerate(refs)]
    start(copies)
    for n, out in enumerate((a_next, b_next)):
        wait(copies[2 * n : 2 * n + 2])
        out.held[...] = (blocks[2 * n].astype(F32) + blocks[2 * n + 1].astype(F32)).astype(BF16)
        out.send()


def add_next(a_keep, a_got, b_keep, b_got, place, after):
    shape = a_keep.shape[2:]
    return call(
        add_next_kernel,
        "add_next",
        (a_keep, a_got, b_keep, b_got, place),
        "hhhhs",
        [sds((2, *shape), BF16)] * 2,
        "oo",
        [pltpu.VMEM((4, 2, *shape), BF16), pltpu.SemaphoreType.DMA((4,))],
        after,
    )


def add_last_kernel(sizes, *refs):
    place, line, sems = refs[6 * len(sizes)], refs[6 * len(sizes) + 1], refs[-1]
    blocks = refs[6 * len(sizes) + 2 : -1]
    x, y = place[1], place[2]
    copies = []
    for g in range(len(sizes)):
        a_keep, a_got, a_last, b_keep, b_got, b_last = refs[6 * g : 6 * g + 6]
        for n, ref in enumerate((a_keep.at[y], a_got.at[y], a_last, b_keep.at[x], b_got.at[x], b_last)):
            copies.append(pltpu.make_async_copy(ref, blocks[g].at[n], sems.at[6 * g + n]))
    start(copies)
    at = 0
    for g, rows in enumerate(sizes):
        for n in range(2):
            wait(copies[6 * g + 3 * n : 6 * g + 3 * n + 3])
            block = blocks[g]
            total = block[3 * n].astype(F32) + block[3 * n + 1].astype(F32)
            total = total + block[3 * n + 2].astype(F32)
            line.held[2 * n : 2 * n + 2, at : at + rows] = total.astype(BF16)
        at += rows


def add_last(groups, place, after):
    sizes = [group[0].shape[2] for group in groups]
    (line,) = call(
        functools.partial(add_last_kernel, sizes),
        "add_last",
        (*(array for group in groups for array in group), place),
        "h" * (6 * len(groups)) + "s",
        [sds((4, sum(sizes), HALF), BF16)],
        "o",
        [
            *(pltpu.VMEM((6, 2, rows, HALF), BF16) for rows in sizes),
            pltpu.SemaphoreType.DMA((6 * len(groups),)),
        ],
        after,
    )
    return line


BACK_OUTS = [
    sds((T, D), BF16),
    sds((T, D), F32),
    sds((6, T, 128), BF16),
    sds((16, D), F32),
    sds((4, T, HALF), BF16),
    sds((4, T, HALF), BF16),
    sds((T, HALF), BF16),
    sds((3, T, HALF), BF16),
]


def feed_back_kernel(layout_a, layout_b, *refs):
    cot, n2, r2, vec, gp, n1, r1, place, dxd, buck = refs[:10]
    refs = refs[10:]
    pieces_a, refs = refs[: layout_a.count], refs[layout_a.count :]
    pieces_b, refs = refs[: layout_b.count], refs[layout_b.count :]
    (dr2l, dr1, dml, small), outs, refs = refs[:4], refs[4:8], refs[8:]
    wo, wu, wd, scr, dul, dr1l, sems, out_sems = refs
    send = Sender(out_sems)
    copies = weight_copies(layout_a, layout_b, pieces_a, pieces_b, place, wo, wu, wd, sems)
    start(copies[2])
    gp.start()
    for group in copies[1]:
        start(group)
    n1.start()
    r1.start()
    start(copies[0])
    cot, dxd = cot(), dxd()

    def output_grad(rows):
        first = first_tokens(buck, rows.start, NORM_ROWS)
        return cot[rows, :].astype(F32) + jnp.where(first, dxd[rows, :], 0.0)

    feed_back_rows(
        output_grad, vec, small.held, copies, (wo, wu, wd), (n1, r1, n2, r2, gp), (scr, dul, dr1l),
        (dr2l, dr1, dml, *outs), send, place[0],
    )
    send.wait()


def feed_back(cot, n2, r2, vec, gp, n1, r1, place, part_a, part_b, after, dxd, buck):
    (layout_a, pieces_a), (layout_b, pieces_b) = part_a, part_b
    return call(
        functools.partial(feed_back_kernel, layout_a, layout_b),
        "feed_back",
        (cot, n2, r2, vec, gp, n1, r1, place, dxd, buck, *pieces_a, *pieces_b),
        "iiiillls" + "is" + "h" * (layout_a.count + layout_b.count),
        BACK_OUTS,
        "oooohhhh",
        [
            *WEIGHTS,
            pltpu.VMEM((T, D), F32),
            pltpu.VMEM((4, T, D), BF16),
            pltpu.VMEM((T, D), BF16),
            pltpu.SemaphoreType.DMA((6, 10)),
            pltpu.SemaphoreType.DMA((12,)),
        ],
        after,
        span=12,
    )


def feed_both_kernel(layout_a, layout_b, *refs):
    x, m, vec, place, cot = refs[:5]
    refs = refs[5:]
    pieces_a, refs = refs[: layout_a.count], refs[layout_a.count :]
    pieces_b, refs = refs[: layout_b.count], refs[layout_b.count :]
    out, transposed, refs = refs[0], refs[1:4], refs[4:]
    (dr2l, dr1, dml, small), outs, refs = refs[:4], refs[4:8], refs[8:]
    wo, wu, wd, scr, y1, y1l, g, y1t, gt, n1, r1, n2, r2, gp, dul, sems, out_sems = refs
    c = place[0]
    send = Sender(out_sems)
    copies = weight_copies(layout_a, layout_b, pieces_a, pieces_b, place, wo, wu, wd, sems)
    start(copies[0])
    for group in copies[1]:
        start(group)
    start(copies[2])
    cot.start()
    first_done, panel_done = send_transposed(send, y1l, g, y1t, gt, transposed, c)

    def result(rows, value):
        out.held[rows, :] = value.astype(BF16)

    feed_rows(
        x, m, vec, copies, (wo, wu, wd), (n1, r1, n2, r2, gp), (scr, y1, y1l, g), first_done, panel_done, result
    )
    out.send()
    cot = cot()
    saved = [lambda ref=ref: ref for ref in (n1, r1, n2, r2, gp)]
    feed_back_rows(
        lambda rows: cot[rows, :].astype(F32), vec, small.held, ([], [[]] * 4, []), (wo, wu, wd), saved,
        (scr, dul, y1l), (dr2l, dr1, dml, *outs), send, c,
    )
    send.wait()


def feed_both(x, m, vec, place, cot, part_a, part_b, after):
    (layout_a, pieces_a), (layout_b, pieces_b) = part_a, part_b
    return call(
        functools.partial(feed_both_kernel, layout_a, layout_b),
        "feed_both",
        (x, m, vec, place, cot, *pieces_a, *pieces_b),
        "iiisl" + "h" * (layout_a.count + layout_b.count),
        [sds((T, D), BF16), *TRANSPOSED, *BACK_OUTS],
        "ohhhoooohhhh",
        [
            *WEIGHTS,
            pltpu.VMEM((T, D), F32),
            pltpu.VMEM((T, D), F32),
            pltpu.VMEM((T, D), BF16),
            pltpu.VMEM((4, T, D), BF16),
            pltpu.VMEM((8, 96, T), BF16),
            pltpu.VMEM((4, 4, 2, 96, T), BF16),
            pltpu.VMEM((T, D), F32),
            pltpu.VMEM((T, 128), F32),
            pltpu.VMEM((T, D), F32),
            pltpu.VMEM((T, 128), F32),
            pltpu.VMEM((4, T, D), BF16),
            pltpu.VMEM((4, T, D), BF16),
            pltpu.SemaphoreType.DMA((6, 10)),
            pltpu.SemaphoreType.DMA((24,)),
        ],
        after,
        span=20,
    )


def attend_back_kernel(*refs):
    p, dml, stat, small_in, lens, buck, place = refs[:7]
    keep_out, low_out, high_out, small_out, dpl, slab, bias, out_sems = refs[7:]
    small = small_out.held
    c = place[0]
    fill_bias(bias, lens, buck)
    p, dml, stat = p(), dml(), stat()
    scale = jnp.asarray(HD**-0.5, BF16)
    small[...] = small_in()[...]

    def pair(i):
        q = p[i] * scale
        k_t = p[6 + i].T
        both = dot_rt(jnp.concatenate(halves(p[6 + i]), axis=0), q)
        grad = dml[i]
        dboth = dot_rt(jnp.concatenate(halves(p[12 + i]), axis=0), grad)
        softs, dscores, dq = [], [], []
        for a in range(2):
            scores = both[T * a : T * a + T] + bias[...]
            peak = stat[2 * i + a, 0:1, :]
            inverse = stat[2 * i + a, 1:2, :]
            soft = jnp.exp(scores - peak) * inverse
            dsoft = dboth[T * a : T * a + T]
            total = jnp.sum(soft * dsoft, axis=0, keepdims=True)
            dscore = (soft * (dsoft - total)).astype(BF16)
            softs.append(soft.astype(BF16))
            dscores.append(dscore)
            dq.append(dot(k_t[HD * a : HD * a + HD, :], dscore))
        grads, queries = halves(grad), halves(q)
        dv = (dot(softs[0], grads[0]) + dot(softs[1], grads[1])).astype(BF16)
        dk = (dot(dscores[0], queries[0]) + dot(dscores[1], queries[1])).astype(BF16)
        dq = (jnp.concatenate(dq, axis=0).T * (HD**-0.5)).astype(BF16)
        dpl[i] = dq
        dpl[6 + i] = dk
        dpl[12 + i] = dv
        cols = pl.ds(pl.multiple_of(i * 128, 128), 128)
        small[2:3, cols] = column_sum(dq.astype(F32))
        small[3:4, cols] = column_sum(dv.astype(F32))

    def pairs(n, carry):
        for k in range(ATTEND_BACK_PAIRS):
            pair(ATTEND_BACK_PAIRS * n + k)
        return carry

    lax.fori_loop(0, 6 // ATTEND_BACK_PAIRS, pairs, 0)
    slab[...] = jnp.zeros_like(slab)
    for k in range(6):
        slab[16 * k : 16 * k + 16, :] = small[:, 128 * k : 128 * k + 128].astype(BF16)
    h = 3 * (1 - c)
    sent = [
        (dpl.at[pl.ds(h, 3)], low_out.at[0:3]),
        (dpl.at[pl.ds(6 + h, 2)], low_out.at[3:5]),
        (dpl.at[pl.ds(8 + h, 1)], high_out.at[0:1]),
        (dpl.at[pl.ds(12 + h, 3)], high_out.at[1:4]),
        (slab, high_out.at[4]),
    ]
    for j in range(3):
        sent.append((dpl.at[pl.ds(6 * j + 3 * c, 3)], keep_out.at[3 * j : 3 * j + 3]))
    sent = [pltpu.make_async_copy(src, dst, out_sems.at[n]) for n, (src, dst) in enumerate(sent)]
    start(sent)
    wait(sent)


def attend_back(p, dml, stat, small, lens, buck, place, after):
    return call(
        attend_back_kernel,
        "attend_back",
        (p, dml, stat, small, lens, buck, place),
        "iiiisss",
        [sds((9, T, 128), BF16), sds((5, T, 128), BF16), sds((5, T, 128), BF16), sds((16, D), F32)],
        "hhho",
        [
            pltpu.VMEM((18, T, 128), BF16),
            pltpu.VMEM((T, 128), BF16),
            pltpu.VMEM((T, T), F32),
            pltpu.SemaphoreType.DMA((10,)),
        ],
        after,
    )


def input_back_kernel(encoder, layout, *refs):
    dpl_keep, dpl_low, dpl_high, dr1, place = refs[:5]
    refs = refs[5:]
    if not encoder:
        buck, refs = refs[0], refs[1:]
    pieces, refs = refs[: layout.count], refs[layout.count :]
    if not encoder:
        dxd_out, refs = refs[0], refs[1:]
        dxd = dxd_out.held
    out_flow, dpl, wq, sems = refs
    out = out_flow.held
    c = place[0]
    copies = []
    for j in range(3):
        group = panel_copies(layout, pieces, place, wq.at[j], sems.at[j], j * ROWS, ROWS)
        other = 6 * j + 3 * (1 - c)
        pairs = [(dpl_keep.at[3 * j : 3 * j + 3], pl.ds(6 * j + 3 * c, 3))]
        if j == 0:
            pairs.append((dpl_low.at[0:3], pl.ds(other, 3)))
        elif j == 1:
            pairs += [(dpl_low.at[3:5], pl.ds(other, 2)), (dpl_high.at[0:1], pl.ds(other + 2, 1))]
        else:
            pairs.append((dpl_high.at[1:4], pl.ds(other, 3)))
        for n, (src, at) in enumerate(pairs):
            group.append(pltpu.make_async_copy(src, dpl.at[at], sems.at[j, 10 + n]))
        start(group)
        copies.append(group)
    dr1 = dr1()
    for group in copies:
        wait(group)
    for half in range(2):
        rows = slice(half * 256, half * 256 + 256)
        total = dr1[rows, :]
        for j in range(3):
            left = jnp.concatenate([dpl[6 * j + s, rows, :] for s in range(6)], axis=1)
            total = total + dot_rt(left, wq[j].reshape(D, D))
        if encoder:
            out[rows, :] = total.astype(BF16)
        else:
            dxd[rows, :] = total
            out[rows, :] = jnp.where(first_tokens(buck, half * 256, 256), 0.0, total).astype(BF16)
            dxd_out.send(rows)
        out_flow.send(rows)


def input_back(encoder, slabs, dr1, place, part_a, after, buck=None):
    layout, pieces = part_a
    args, kinds = (*slabs, dr1, place), "hhhis"
    outs = [sds((T, D), BF16)]
    if not encoder:
        args, kinds = (*args, buck), kinds + "s"
        outs = [sds((T, D), F32), *outs]
    return call(
        functools.partial(input_back_kernel, encoder, layout),
        "input_back",
        (*args, *pieces),
        kinds + "h" * layout.count,
        outs,
        "o" * len(outs),
        [
            pltpu.VMEM((18, T, 128), BF16),
            pltpu.VMEM((3, 4, 4, ROWS, D), BF16),
            pltpu.SemaphoreType.DMA((3, 13)),
        ],
        after,
        span=30 if encoder else 0,
    )


def gate_kernel(*refs):
    pass


def gate(values, after):
    outs = call(
        gate_kernel,
        "gate",
        tuple(values),
        "h" * len(values),
        [sds(v.shape, v.dtype) for v in values],
        "h" * len(values),
        [],
        after,
        {n: n for n in range(len(values))},
    )
    return list(outs)


def split_kernel(bx, by, ax, ay, held, sems):
    refs = ((bx.at[0:2], held.at[0], ax), (by.at[2:4], held.at[1], ay))
    into = [pltpu.make_async_copy(src, mid, sems.at[n]) for n, (src, mid, _) in enumerate(refs)]
    out = [pltpu.make_async_copy(mid, dst, sems.at[2 + n]) for n, (_, mid, dst) in enumerate(refs)]
    start(into)
    for n in range(2):
        into[n].wait()
        out[n].start()
    wait(out)


def split(bx, by, after):
    shape = (2, *bx.shape[1:])
    return call(
        split_kernel,
        "split",
        (bx, by),
        "hh",
        [sds(shape, BF16)] * 2,
        "hh",
        [pltpu.VMEM((2, *shape), BF16), pltpu.SemaphoreType.DMA((4,))],
        after,
    )


def cut_kernel(at, line, low, high, held, sems):
    into, out = [], []
    for n, (rows, dst) in enumerate(((slice(0, at), low), (slice(at, held.shape[1]), high))):
        into.append(pltpu.make_async_copy(line.at[:, rows], held.at[:, rows], sems.at[n]))
        out.append(pltpu.make_async_copy(held.at[:, rows], dst, sems.at[2 + n]))
    start(into)
    for n in range(2):
        into[n].wait()
        out[n].start()
    wait(out)


def cut(line, at, after):
    rows = line.shape[1]
    return call(
        functools.partial(cut_kernel, at),
        "cut",
        (line,),
        "h",
        [sds((4, at, HALF), BF16), sds((4, rows - at, HALF), BF16)],
        "hh",
        [pltpu.VMEM((4, rows, HALF), BF16), pltpu.SemaphoreType.DMA((4,))],
        after,
    )


AXES = ("z", "y", "x", "c", "e")


def swap(value, axis):
    return lax.ppermute(value, axis, [(0, 1), (1, 0)])


def pick(value, index, axis):
    return lax.dynamic_index_in_dim(value, index, axis, keepdims=False)


class SpreadGather:
    def __init__(self, rows):
        self.own = lax.all_gather(rows, "z", axis=0, tiled=False)

    def plane(self, after):
        (self.own,) = gate([self.own], after)
        self.bx, self.by = swap(self.own, "x"), swap(self.own, "y")
        self.own_c = swap(self.own, "c")
        return (self.own,)

    def forward(self, after):
        ax, ay = split(self.bx, self.by, (*after, self.own_c))
        self.dx, self.dy = swap(ax, "y"), swap(ay, "x")
        self.bx_c, self.by_c = swap(self.bx, "c"), swap(self.by, "c")
        return (ax,)

    def across(self):
        there = (self.own, self.bx, self.by, self.dx, self.dy)
        self.pieces = (*there, self.own_c, self.bx_c, self.by_c, swap(self.dx, "c"), swap(self.dy, "c"))


class MixedGather:
    def __init__(self, rows, at, along_x, along_y):
        self.at, self.size = at, rows.shape[0]
        self.rows = jnp.concatenate([rows[:at], along_x, rows[at:], along_y])

    def line(self, after):
        (rows,) = gate([self.rows], after)
        self.own = lax.all_gather(rows, "z", axis=0, tiled=False)
        return (rows,)

    def arrive(self, after):
        (self.own,) = gate([self.own], after)
        return (self.own,)

    def plane(self, after):
        self.low, self.high = cut(self.own, 2 * self.at, after)
        return (self.low,)

    def last(self, after=()):
        low, high = self.low, self.high
        if after:
            low, high = gate([low, high], after)
        self.low, self.high = swap(low, "y"), swap(high, "x")
        return (low,)

    def near(self, after):
        tok = self.arrive(after)
        self.own_c = swap(self.own, "c")
        return tok

    def across(self, after):
        self.low, self.high = gate([self.low, self.high], after)
        self.low_c, self.high_c = swap(self.low, "c"), swap(self.high, "c")
        self.pieces = (self.own, self.low, self.high, self.own_c, self.low_c, self.high_c)
        self.part = (Mixed(self.at, self.size), self.pieces)
        return (self.low,)


class Scatter:
    def __init__(self, groups, place, cut=None):
        self.groups, self.place, self.cut = groups, place, cut

    def keep(self, inputs, after):
        a_send, self.a_keep, b_send, self.b_keep = keep(
            self.groups, inputs, self.place, after, self.cut
        )
        self.a_got, self.b_got = swap(a_send, "x"), swap(b_send, "y")
        return (a_send,)

    def next(self, after):
        a_next, b_next = add_next(
            self.a_keep, self.a_got, self.b_keep, self.b_got, self.place, after
        )
        self.a_last, self.b_last = swap(a_next, "y"), swap(b_next, "x")
        return (a_next,)

    def sums(self):
        return (self.a_keep, self.a_got, self.a_last, self.b_keep, self.b_got, self.b_last)


def along_z(scatters, after):
    pairs = []
    for scatter in scatters:
        pairs += [(scatter.a_keep, scatter.a_got), (scatter.b_keep, scatter.b_got)]
    line = add_mid(pairs, after)
    return (line,), lax.psum_scatter(line, "z", scatter_dimension=0, tiled=False)


def finish(scatters, place, after):
    line = add_last([scatter.sums() for scatter in scatters], place, after)
    return (line,), lax.psum_scatter(line, "z", scatter_dimension=0, tiled=False)


def pack_weights(qkv, out, up, down, gains, biases, up_b, c, device):
    rows = out.shape[1]
    panels = jnp.concatenate([qkv, out, up], axis=2).reshape(2, rows, 8, 2, HALF)
    panels = jnp.transpose(panels, (0, 3, 2, 1, 4)).reshape(2, 2, 8 * rows, HALF)
    downs = jnp.transpose(down.reshape(2, 4 * rows, 2, HALF), (0, 2, 1, 3))
    both = jnp.concatenate([panels, downs], axis=2)
    mine = pick(both, c, 1)
    got = swap(pick(both, 1 - c, 1), "c")
    low = jnp.where(c == 0, mine, got)
    high = jnp.where(c == 0, got, mine)
    panels = jnp.stack(
        [low[:, : 8 * rows].reshape(2, 8, rows, HALF), high[:, : 8 * rows].reshape(2, 8, rows, HALF)],
        axis=2,
    ).reshape(2, 16 * rows, HALF)
    downs = jnp.concatenate([low[:, 8 * rows :], high[:, 8 * rows :]], axis=1)
    small = jnp.zeros((2, 16, D), BF16)
    small = lax.dynamic_update_slice(
        small, jnp.concatenate([gains, biases], axis=1), (0, 0, device * rows)
    )
    small = lax.dynamic_update_slice(
        small, up_b[:, None, :], (0, 8 + device // 8, device % 8 * (4 * rows))
    )
    small = jnp.concatenate([small[:, :, :HALF], small[:, :, HALF:]], axis=1)
    part_a = jnp.concatenate([panels[:, : 8 * rows], small], axis=1)
    part_b = jnp.concatenate([panels[:, 8 * rows :], downs], axis=1)
    return part_a, part_b


def body(
    encoder_input,
    corrupted,
    lengths,
    buckets,
    qkv_weight,
    out_weight,
    up_weight,
    down_weight,
    norm_gains,
    bias_rows,
    up_bias,
    encoder_cot,
    decoder_cot,
):
    extra = lax.axis_size("e")
    weights = [qkv_weight, out_weight, up_weight, down_weight, norm_gains, bias_rows, up_bias]
    if extra > 1:
        weights = [
            lax.all_gather(w, "e", axis=at, tiled=True)
            for w, at in zip(weights, (1, 1, 1, 1, 2, 2, 1))
        ]
    rows = weights[1].shape[1]
    x, y, c = lax.axis_index("x"), lax.axis_index("y"), lax.axis_index("c")
    device = ((lax.axis_index("z") * 2 + y) * 2 + x) * 2 + c
    place = jnp.stack([c, x, y]).astype(jnp.int32)
    part_a, part_b = pack_weights(*weights, c, device)
    at_a, at_b = 2 * ROWS, 4 * ROWS
    along_x = swap(jnp.concatenate([part_a[1, :at_a], part_b[1, :at_b]]), "x")
    along_y = swap(jnp.concatenate([part_a[1, at_a:], part_b[1, at_b:]]), "y")
    g0 = SpreadGather(jnp.concatenate([part_a[0], part_b[0]]))
    g1a = MixedGather(part_a[1], at_a, along_x[:at_a], along_y[: PART_A - at_a])
    g1b = MixedGather(part_b[1], at_b, along_x[at_a:], along_y[PART_A - at_a :])

    tok = g0.plane((along_x, along_y))
    tok = g1a.line(tok)
    tok = g1b.line(tok)
    tok = g0.forward(tok)
    g1a.plane(tok)
    g0.across()
    part_a0, part_b0 = (Spread(0), g0.pieces), (Spread(PART_A), g0.pieces)
    tok = g1a.last((g0.dx, g0.dy))
    tok = g1a.near(tok)
    p0, m0, xt0, mt0, stat0, vec0 = attend(encoder_input, lengths, buckets, place, part_a0, tok, 0)
    tok = g1b.near((stat0,))
    tok = g1b.plane((*tok, g1a.own_c))
    g1b.last()
    tok = g1a.across(tok)
    enc_out, *saved0, xd, xdl, y1t0, gt0, give0 = feed(
        encoder_input, m0, vec0, place, part_a0, part_b0, tok, corrupted, buckets
    )
    given0 = swap(give0, "c")
    xt0_other, mt0_other = swap(xt0, "c"), swap(mt0, "c")
    part_a1 = g1a.part
    p1, m1, xt1, mt1, stat1, vec1 = attend(
        xdl, lengths, buckets, place, part_a1, (enc_out,), 0
    )
    xt1_other, mt1_other = swap(xt1, "c"), swap(mt1, "c")
    tok = g1b.across((stat1,))
    part_b1 = g1b.part
    dec_out, y1t1, gt1, give1, dr2l, dr1, dml, small, dul, dul_give, dr1l, resid = feed_both(
        xd, m1, vec1, place, decoder_cot, part_a1, part_b1, tok
    )

    given1 = swap(give1, "c")
    resid, dul_other = swap(resid, "c"), swap(dul_give, "c")
    cuts = ((208, 432), (96, 176))
    s1, q1 = Scatter(("do", "u"), place, cuts[0][0]), Scatter(("q",), place, cuts[1][0])
    part, low, high, small = attend_back(
        p1, dml, stat1, small, lengths, buckets, place, (dr1, given0)
    )
    part_other = [swap(low, "c"), swap(high, "c")]
    tok = s1.keep(
        (gt1, dr2l, resid, given1, mt1, mt1_other, dr1l, y1t1, dul, dul_other, given1), (small,)
    )
    tok = q1.keep((xt1, xt1_other, part, *part_other, small), tok)
    dxd, cor_grad = input_back(False, (part, low, high), dr1, place, part_a1, tok, buckets)
    tok = (cor_grad,)

    n1, r1, n2, r2, gp = saved0
    dr2l, dr1, dml, small, dul, dul_give, dr1l, resid = feed_back(
        encoder_cot, n2, r2, vec0, gp, n1, r1, place, part_a0, part_b0, tok, dxd, buckets
    )
    resid, dul_other = swap(resid, "c"), swap(dul_give, "c")
    tok, dec_total = along_z([s1, q1], (dr1,))
    s0, q0 = Scatter(("do", "u"), place), Scatter(("q",), place)
    tok = s0.keep(
        (gt0, dr2l, resid, given0, mt0, mt0_other, dr1l, y1t0, dul, dul_other, given0), tok
    )
    part, low, high, small = attend_back(p0, dml, stat0, small, lengths, buckets, place, tok)
    part_other = [swap(low, "c"), swap(high, "c")]
    tok = q0.keep((xt0, xt0_other, part, *part_other, small), (small,))
    tok = s0.next(tok)
    (enc_grad,) = input_back(True, (part, low, high), dr1, place, part_a0, tok)
    tok = q0.next((enc_grad,))
    (dec_total,) = gate([dec_total], tok)
    tok, both0 = finish([s0, q0], place, (dec_total,))
    sent = part_rows(dec_total, cuts, place, tok)
    got = [swap(value, "yx"[n % 2]) for n, value in enumerate(sent)]
    feed1, attend1 = close(dec_total, got, cuts, place, ())

    def rows_of(feed_part, attend_part):
        panels = jnp.concatenate([attend_part[:144], feed_part[192:]], axis=0)
        panels = panels.reshape(8, 2, rows, HALF)
        mine = pick(panels, c, 1)
        got = swap(pick(panels, 1 - c, 1), "c")
        panels = jnp.concatenate([jnp.where(c == 0, mine, got), jnp.where(c == 0, got, mine)], axis=2)
        qkv_grad = jnp.concatenate([panels[0], panels[1], panels[2]], axis=1)
        up_grad = jnp.concatenate([panels[4], panels[5], panels[6], panels[7]], axis=1)
        down_grad = jnp.concatenate([feed_part[:96], feed_part[96:192]], axis=1)
        small = jnp.concatenate([attend_part[144:160], attend_part[160:]], axis=1)
        heads = lax.dynamic_slice(small, (0, device * rows), (8, rows))
        up_b_grad = lax.dynamic_slice(small, (8 + device // 8, device % 8 * (4 * rows)), (1, 4 * rows))
        return qkv_grad, panels[3], up_grad, down_grad, heads[:2], heads[2:], up_b_grad[0]

    dec_grads = rows_of(feed1, attend1)
    enc_grads = rows_of(both0[:432], both0[432:])
    grads_out = [jnp.stack(pair).astype(F32) for pair in zip(enc_grads, dec_grads)]
    if extra > 1:
        grads_out = [
            lax.psum_scatter(v, "e", scatter_dimension=at, tiled=True)
            for v, at in zip(grads_out, (1, 1, 1, 1, 2, 2, 1))
        ]
    return (enc_out, dec_out, enc_grad, cor_grad, *grads_out)


def solution(mesh):
    devices = mesh.devices.reshape(4, 2, 2, 2, -1)
    inner = Mesh(devices, AXES)
    token = P(AXES, None)
    line = P(AXES)
    wide = P(None, AXES, None)
    vector = P(None, None, AXES)
    return jax.shard_map(
        body,
        mesh=inner,
        in_specs=(
            token, token, line, line, wide, wide, wide, wide, vector, vector, P(None, AXES), token, token,
        ),
        out_specs=(
            token, token, token, token, wide, wide, wide, wide, vector, vector, P(None, AXES),
        ),
        check_vma=False,
    )
```

```python
import functools

import jax
import jax.numpy as jnp
from jax import lax
from jax.experimental import pallas as pl
from jax.experimental.pallas import tpu as pltpu
from jax.sharding import Mesh
from jax.sharding import PartitionSpec as P

HD = 64
SLOT = 128
EPSILON = 1e-06
NEGATIVE = -1e30
F32 = jnp.float32
BF16 = jnp.bfloat16
VMEM_LIMIT = 64 * 1024 * 1024

T = 512
D = 768
HALF = D // 2
ROWS = 48
DROWS = 192
O_AT, SMALL_AT, PART_A = 144, 192, 224
D_AT, PART_B = 192, 384

NORM_ROWS = 256
ATTEND_BACK_PAIRS = 2
SM = pl.BlockSpec(memory_space=pltpu.SMEM)
HBM = pl.BlockSpec(memory_space=pl.ANY)
SPAN = {
    "feed": 20,
    "add_next": 12,
    "add_mid": 16,
}


def dot(left, right):
    return lax.dot_general(left, right, (((1,), (0,)), ((), ())), preferred_element_type=F32)


def dot_rt(left, right):
    return lax.dot_general(left, right, (((1,), (1,)), ((), ())), preferred_element_type=F32)


def sds(shape, dtype):
    return jax.ShapeDtypeStruct(shape, dtype)


class In:
    def __init__(self, source, held, sem, late):
        self.held, self.copy, self.there = held, pltpu.make_async_copy(source, held, sem), False
        self.begun = False
        if not late:
            self.start()

    def start(self):
        self.begun = True
        self.copy.start()

    def __call__(self):
        if not self.begun:
            self.start()
        if not self.there:
            self.copy.wait()
            self.there = True
        return self.held


class Out:
    def __init__(self, target, held, sems):
        self.target, self.held, self.sems, self.copies = target, held, sems, []

    def send(self, index=None):
        source = self.held if index is None else self.held.at[index]
        target = self.target if index is None else self.target.at[index]
        copy = pltpu.make_async_copy(source, target, self.sems.at[len(self.copies)])
        copy.start()
        self.copies.append(copy)

    def wait(self):
        for copy in self.copies:
            copy.wait()


def call(kernel, name, args, in_kinds, outs, out_kinds, scratch, after=(), aliases=None, span=None):
    n, m, k = len(args), len(after), len(outs)
    spec = {"i": HBM, "l": HBM, "o": HBM, "h": HBM, "s": SM}
    ins = [a for a, kind in zip(args, in_kinds) if kind in "il"]
    sent = [o for o, kind in zip(outs, out_kinds) if kind == "o"]

    def ordered(*refs):
        inputs, results, rest = refs[:n], refs[n + m : n + m + k], refs[n + m + k :]
        held_in, held_out = rest[: len(ins)], rest[len(ins) : len(ins) + len(sent)]
        own = rest[len(ins) + len(sent) : len(ins) + len(sent) + len(scratch)]
        sems = rest[len(ins) + len(sent) + len(scratch) :]
        lazy, at = [], 0
        for ref, kind in zip(inputs, in_kinds):
            if kind in "il":
                ref, at = In(ref, held_in[at], sems[0].at[at], kind == "l"), at + 1
            lazy.append(ref)
        flow, at = [], 0
        for ref, kind in zip(results, out_kinds):
            if kind == "o":
                ref, at = Out(ref, held_out[at], sems[-1].at[at]), at + 1
            flow.append(ref)
        kernel(*lazy, *flow, *own)
        for ref in lazy:
            if isinstance(ref, In):
                ref()
        flow = [ref for ref in flow if isinstance(ref, Out)]
        for ref in flow:
            if not ref.copies:
                ref.send()
        for ref in flow:
            ref.wait()

    sems = []
    if ins:
        sems.append(pltpu.SemaphoreType.DMA((len(ins),)))
    if sent:
        sems.append(pltpu.SemaphoreType.DMA((len(sent), 4)))
    return pl.pallas_call(
        ordered,
        out_shape=outs,
        in_specs=[*(spec[kind] for kind in in_kinds), *([HBM] * m)],
        out_specs=[HBM] * k,
        scratch_shapes=[
            *(pltpu.VMEM(a.shape, a.dtype) for a in ins),
            *(pltpu.VMEM(o.shape, o.dtype) for o in sent),
            *scratch,
            *sems,
        ],
        input_output_aliases=aliases or {},
        compiler_params=pltpu.CompilerParams(vmem_limit_bytes=VMEM_LIMIT),
        cost_estimate=pl.CostEstimate(
            flops=int(1000 + 1.1e9 * (SPAN.get(name, 0) if span is None else span)), bytes_accessed=1000, transcendentals=0
        ),
        name=name,
    )(*args, *after)


def start(copies):
    for copy in copies:
        copy.start()


def wait(copies):
    for copy in copies:
        copy.wait()


class Spread:
    count = 10

    def __init__(self, base):
        self.base = base

    def slabs(self, refs, place, row_at, rows):
        c, x, y = place[0], place[1], place[2]
        across = 2 * (1 - y) + (1 - x)
        slots = ((2 * y + x, 0, 4), (2 * y + 1 - x, 0, 4), (2 * (1 - y) + x, 0, 4), (across, 0, 2), (across, 2, 4))
        first = self.base + row_at
        for half, group in ((c, refs[:5]), (1 - c, refs[5:])):
            for ref, (at, low, high) in zip(group, slots):
                yield ref.at[:, first : first + rows, :], at, low, high, half


class Mixed:
    count = 6

    def __init__(self, cut, size):
        self.cut, self.size = cut, size

    def slabs(self, refs, place, row_at, rows):
        c, x, y = place[0], place[1], place[2]
        own, near_x, near_y = 2 * y + x, 2 * y + 1 - x, 2 * (1 - y) + x
        across = 2 * (1 - y) + (1 - x)
        rest = self.size - self.cut
        for half, (line, low, high) in ((c, refs[:3]), (1 - c, refs[3:])):
            if row_at < self.cut:
                places = ((line, row_at, own), (line, self.cut + row_at, near_x))
                places += ((low, row_at, near_y), (low, self.cut + row_at, across))
            else:
                first, base = row_at - self.cut, 2 * self.cut
                places = ((line, base + first, own), (line, base + rest + first, near_y))
                places += ((high, first, near_x), (high, rest + first, across))
            for ref, first, at in places:
                yield ref.at[:, first : first + rows, :], at, 0, 4, half


def half_cols(h):
    return pl.ds(pl.multiple_of(h * HALF, HALF), HALF)


def panel_copies(layout, refs, place, dst, sems, row_at, rows):
    copies = []
    for n, (src, at, low, high, half) in enumerate(layout.slabs(refs, place, row_at, rows)):
        copies.append(
            pltpu.make_async_copy(src, dst.at[low:high, at, :, half_cols(half)], sems.at[n])
        )
    return copies


def fill_bias(bias, lens, buck):
    bucket = buck[0]
    key = lax.broadcasted_iota(jnp.int32, (T, T), 0)
    query = lax.broadcasted_iota(jnp.int32, (T, T), 1)
    shift = bucket + 7
    same = lax.shift_right_logical(key, shift) == lax.shift_right_logical(query, shift)
    position = jnp.bitwise_and(key, lax.shift_left(jnp.int32(SLOT), bucket) - 1)
    slot = lax.shift_right_logical(key, 7)
    length = jnp.where(
        slot < 2,
        jnp.where(slot == 0, lens[0], lens[1]),
        jnp.where(slot == 2, lens[2], lens[3]),
    )
    bias[...] = jnp.where(same & (position < length), 0.0, NEGATIVE)


def first_tokens(buck, low, size):
    span = lax.shift_left(jnp.int32(SLOT), buck[0])
    token = lax.broadcasted_iota(jnp.int32, (size, 1), 0) + low
    return jnp.bitwise_and(token, span - 1) == 0


def halves(block):
    lane = lax.broadcasted_iota(jnp.int32, block.shape, 1)
    zero = jnp.zeros_like(block)
    return jnp.where(lane < HD, block, zero), jnp.where(lane < HD, zero, block)


def row_loop(size, body):
    if size == T:
        return body(pl.ds(0, T))

    def step(i, carry):
        body(pl.ds(pl.multiple_of(i * size, size), size))
        return carry

    lax.fori_loop(0, T // size, step, 0)


def attend_kernel(layout, *refs):
    x, lens, buck, place = refs[:4]
    pieces, refs = refs[4 : 4 + layout.count], refs[4 + layout.count :]
    flow, (wq, bias, heap, sems) = refs[:6], refs[6:]
    p, m, xt, mt, stat, vec = (ref.held for ref in flow)
    copies = [
        panel_copies(layout, pieces, place, wq.at[j], sems.at[j], j * ROWS, ROWS) for j in range(3)
    ]
    smalls, at = [], 0
    for n, (src, _, low, high, _) in enumerate(layout.slabs(pieces, place, SMALL_AT, 32)):
        smalls.append(pltpu.make_async_copy(src, heap.at[at : at + high - low], sems.at[3, n]))
        at += high - low
    start(smalls)
    for group in copies:
        start(group)
    fill_bias(bias, lens, buck)
    x = x()
    xt[...] = x[...].T
    flow[2].send()
    wait(smalls)
    total = heap[0].astype(F32)
    for n in range(1, 32):
        total = total + heap[n].astype(F32)
    vec[...] = jnp.concatenate([total[:16], total[16:]], axis=1)
    flow[5].send()
    for j in range(3):
        wait(copies[j])
        weight = wq[j].reshape(D, D)
        for half in range(2):
            rows = slice(half * 256, half * 256 + 256)
            out = dot(x[rows, :], weight)
            if j != 1:
                out = out + (vec[2:3, :] if j == 0 else vec[3:4, :])
            out = out.astype(BF16)
            for s in range(6):
                p[6 * j + s, rows, :] = out[:, 128 * s : 128 * s + 128]
        flow[0].send(slice(6 * j, 6 * j + 6))

    def pair(i):
        q = p[i] * jnp.asarray(HD**-0.5, BF16)
        v_t = p[12 + i].T
        both = dot_rt(jnp.concatenate(halves(p[6 + i]), axis=0), q)
        mixed = []
        for a in range(2):
            scores = both[T * a : T * a + T] + bias[...]
            peak = jnp.max(scores, axis=0, keepdims=True)
            weights = jnp.exp(scores - peak)
            inverse = 1.0 / jnp.sum(weights, axis=0, keepdims=True)
            stat[2 * i + a, 0:1, :] = peak
            stat[2 * i + a, 1:2, :] = inverse
            soft = (weights * inverse).astype(BF16)
            mixed.append(dot(v_t[HD * a : HD * a + HD, :], soft))
        mixed = jnp.concatenate(mixed, axis=0)
        mt[i * 128 : i * 128 + 128, :] = mixed.astype(BF16)
        m[i] = mixed.T.astype(BF16)

    for i in range(6):
        pair(i)


def attend(x, lens, buck, place, part, after, span):
    layout, pieces = part
    return call(
        functools.partial(attend_kernel, layout),
        "attend",
        (x, lens, buck, place, *pieces),
        "isss" + "h" * layout.count,
        [
            sds((18, T, 128), BF16),
            sds((6, T, 128), BF16),
            sds((D, T), BF16),
            sds((D, T), BF16),
            sds((12, 8, T), F32),
            sds((16, D), F32),
        ],
        "o" * 6,
        [
            pltpu.VMEM((3, 4, 4, ROWS, D), BF16),
            pltpu.VMEM((T, T), F32),
            pltpu.VMEM((32, 32, HALF), BF16),
            pltpu.SemaphoreType.DMA((4, 10)),
        ],
        after,
        span=span,
    )


def unit_norm(resid):
    center = jnp.mean(resid, axis=-1, keepdims=True)
    shifted = resid - center
    spread = jnp.mean(shifted * shifted, axis=-1, keepdims=True)
    inverse = lax.rsqrt(spread + EPSILON)
    return shifted * inverse, inverse


def weight_copies(layout_a, layout_b, pieces_a, pieces_b, place, wo, wu, wd, sems):
    o_copies = panel_copies(layout_a, pieces_a, place, wo, sems.at[0], O_AT, ROWS)
    u_copies = [
        panel_copies(layout_b, pieces_b, place, wu.at[j], sems.at[1 + j], j * ROWS, ROWS)
        for j in range(4)
    ]
    return o_copies, u_copies, panel_copies(layout_b, pieces_b, place, wd, sems.at[5], D_AT, DROWS)


class Sender:
    def __init__(self, sems):
        self.sems, self.copies = sems, []

    def __call__(self, source, target):
        self.copies.append(pltpu.make_async_copy(source, target, self.sems.at[len(self.copies)]))
        self.copies[-1].start()

    def wait(self):
        wait(self.copies)


def feed_rows(x, m, vec, copies, weights, saved, work, first_done, panel_done, result):
    o_copies, u_copies, d_copies = copies
    wo, wu, wd = weights
    n1, r1, n2, r2, gp = saved
    scr, y1, y1l, g = work
    wait(o_copies)
    m, x, vec = m(), x(), vec()
    weight = wo[...].reshape(D, D)
    for half in range(2):
        rows = slice(half * 256, half * 256 + 256)
        left = jnp.concatenate([m[s, rows, :] for s in range(6)], axis=1)
        scr[rows, :] = dot(left, weight)

    def first(rows):
        resid = x[rows, :].astype(F32) + (scr[rows, :] + vec[4:5, :])
        unit, inverse = unit_norm(resid)
        n1[rows, :] = unit
        r1[rows, :] = jnp.broadcast_to(inverse, (inverse.shape[0], 128))
        normed = unit * vec[0:1, :] + vec[5:6, :]
        y1[rows, :] = normed
        y1l[rows, :] = normed.astype(BF16)

    row_loop(NORM_ROWS, first)
    first_done()
    for j in range(4):
        wait(u_copies[j])

        def up(rows, j=j):
            left = y1l[rows, :]
            for k in range(3):
                cols = slice(256 * k, 256 * k + 256)
                right = wu[j, :, :, :, cols].reshape(D, 256)
                hidden = dot(left, right) + vec[8 + j : 9 + j, cols]
                cdf = 0.5 * (1.0 + lax.erf(hidden * (0.5**0.5)))
                g[j, rows, cols] = (hidden * cdf).astype(BF16)
                density = jnp.exp(hidden * hidden * -0.5) * 0.3989422804014327
                gp[j, rows, cols] = (cdf + hidden * density).astype(BF16)

        row_loop(256, up)
        panel_done(j)
    wait(d_copies)
    for half in range(2):
        rows = slice(half * 256, half * 256 + 256)
        total = dot(g[0, rows, :], wd[0].reshape(D, D))
        for j in range(1, 4):
            total = total + dot(g[j, rows, :], wd[j].reshape(D, D))
        scr[rows, :] = total

    def second(rows):
        resid = y1[rows, :] + (scr[rows, :] + vec[6:7, :])
        unit, inverse = unit_norm(resid)
        n2[rows, :] = unit
        r2[rows, :] = jnp.broadcast_to(inverse, (inverse.shape[0], 128))
        result(rows, unit * vec[1:2, :] + vec[7:8, :])

    row_loop(NORM_ROWS, second)


def feed_back_rows(output_grad, vec, small, copies, weights, saved, work, outs, send, c):
    o_copies, u_copies, d_copies = copies
    wo, wu, wd = weights
    n1, r1, n2, r2, gp = saved
    scr, dul, dr1l = work
    dr2l, dr1, dml, dul_keep, dul_give, dr1_keep, resid_give = outs
    small[...] = jnp.zeros_like(small)
    vec, n2, r2 = vec(), n2(), r2()

    def second(rows):
        grad = output_grad(rows)
        unit = n2[rows, :]
        resid = norm_back(grad, unit, r2[rows, 0:1], vec[1:2, :])
        small[1:2, :] += column_sum(grad * unit)
        small[7:8, :] += column_sum(grad)
        small[6:7, :] += column_sum(resid)
        scr[rows, :] = resid
        dr2l.held[rows, :] = resid.astype(BF16)

    row_loop(NORM_ROWS, second)
    dr2l.send()
    for half in range(2):
        send(dr2l.held.at[:, half * HALF : half * HALF + HALF], resid_give.at[half])
    wait(d_copies)
    gp = gp()
    for j in range(4):

        def up(rows, j=j):
            left = dr2l.held[rows, :]
            weight = wd[j].reshape(D, D)
            for k in range(3):
                cols = slice(256 * k, 256 * k + 256)
                grad = dot_rt(left, weight[cols, :])
                hidden = (grad * gp[j, rows, cols].astype(F32)).astype(BF16)
                dul[j, rows, cols] = hidden
                small[8 + j : 9 + j, cols] += column_sum(hidden.astype(F32))

        row_loop(T, up)
        send(dul.at[j, :, half_cols(1 - c)], dul_give.at[j])
        send(dul.at[j, :, half_cols(c)], dul_keep.at[j])
        wait(u_copies[j])
        for half in range(2):
            rows = slice(half * 256, half * 256 + 256)
            scr[rows, :] += dot_rt(dul[j, rows, :], wu[j].reshape(D, D))
    n1, r1 = n1(), r1()

    def first(rows):
        grad = scr[rows, :]
        unit = n1[rows, :]
        resid = norm_back(grad, unit, r1[rows, 0:1], vec[0:1, :])
        small[0:1, :] += column_sum(grad * unit)
        small[5:6, :] += column_sum(grad)
        small[4:5, :] += column_sum(resid)
        dr1.held[rows, :] = resid
        dr1l[rows, :] = resid.astype(BF16)

    row_loop(NORM_ROWS, first)
    send(dr1l.at[:, half_cols(1 - c)], resid_give.at[2])
    send(dr1l.at[:, half_cols(c)], dr1_keep)
    dr1.send()
    wait(o_copies)
    weight = wo[...].reshape(D, D)
    for half in range(2):
        rows = slice(half * 256, half * 256 + 256)
        out = dot_rt(dr1l[rows, :], weight).astype(BF16)
        for s in range(6):
            dml.held[s, rows, :] = out[:, 128 * s : 128 * s + 128]


def send_transposed(send, y1l, g, y1t, gt, outs, c):
    y1t_out, gt_out, give_out = outs

    def first_done():
        y1t[...] = y1l[...].T.reshape(8, 96, T)
        send(y1t, y1t_out)
        send(y1t, give_out.at[0:8])

    def panel_done(j):
        gt[j] = g[j].T.reshape(4, 2, 96, T)
        send(gt.at[j, :, c], gt_out.at[j])
        send(gt.at[j, :, 1 - c], give_out.at[8 + 4 * j : 12 + 4 * j])

    return first_done, panel_done


TRANSPOSED = [sds((8, 96, T), BF16), sds((4, 4, 96, T), BF16), sds((24, 96, T), BF16)]
WEIGHTS = [
    pltpu.VMEM((4, 4, ROWS, D), BF16),
    pltpu.VMEM((4, 4, 4, ROWS, D), BF16),
    pltpu.VMEM((4, 4, DROWS, D), BF16),
]


def feed_kernel(layout_a, layout_b, *refs):
    x, m, vec, place, cor, buck = refs[:6]
    pieces_a, refs = refs[6 : 6 + layout_a.count], refs[6 + layout_a.count :]
    pieces_b, refs = refs[: layout_b.count], refs[layout_b.count :]
    flow, transposed, refs = refs[:8], refs[8:11], refs[11:]
    out, n1, r1, n2, r2, gp, xd, xdl = (ref.held for ref in flow)
    wo, wu, wd, scr, y1, y1l, g, y1t, gt, sems, out_sems = refs
    c = place[0]
    send = Sender(out_sems)
    copies = weight_copies(layout_a, layout_b, pieces_a, pieces_b, place, wo, wu, wd, sems)
    start(copies[0])
    for group in copies[1]:
        start(group)
    start(copies[2])
    first_sent, panel_sent = send_transposed(send, y1l, g, y1t, gt, transposed, c)

    def first_done():
        first_sent()
        flow[1].send()
        flow[2].send()

    def panel_done(j):
        panel_sent(j)
        flow[5].send(j)

    def result(rows, value):
        out[rows, :] = value.astype(BF16)
        mixed = jnp.where(
            first_tokens(buck, rows.start, NORM_ROWS), value, cor()[rows, :].astype(F32)
        )
        xd[rows, :] = mixed
        xdl[rows, :] = mixed.astype(BF16)

    cor()
    feed_rows(
        x, m, vec, copies, (wo, wu, wd), (n1, r1, n2, r2, gp), (scr, y1, y1l, g), first_done, panel_done, result
    )
    send.wait()


def feed(x, m, vec, place, part_a, part_b, after, cor, buck):
    (layout_a, pieces_a), (layout_b, pieces_b) = part_a, part_b
    outs = [
        sds((T, D), BF16),
        sds((T, D), F32),
        sds((T, 128), F32),
        sds((T, D), F32),
        sds((T, 128), F32),
        sds((4, T, D), BF16),
        sds((T, D), F32),
        sds((T, D), BF16),
    ]
    return call(
        functools.partial(feed_kernel, layout_a, layout_b),
        "feed",
        (x, m, vec, place, cor, buck, *pieces_a, *pieces_b),
        "iiisis" + "h" * (layout_a.count + layout_b.count),
        [*outs, *TRANSPOSED],
        "o" * len(outs) + "hhh",
        [
            *WEIGHTS,
            pltpu.VMEM((T, D), F32),
            pltpu.VMEM((T, D), F32),
            pltpu.VMEM((T, D), BF16),
            pltpu.VMEM((4, T, D), BF16),
            pltpu.VMEM((8, 96, T), BF16),
            pltpu.VMEM((4, 4, 2, 96, T), BF16),
            pltpu.SemaphoreType.DMA((6, 10)),
            pltpu.SemaphoreType.DMA((10,)),
        ],
        after,
        span=0,
    )


def norm_back(grad, unit, inverse, gain):
    scaled = grad * gain
    mean = jnp.mean(scaled, axis=-1, keepdims=True)
    along = jnp.mean(scaled * unit, axis=-1, keepdims=True)
    return inverse * (scaled - mean - unit * along)


def column_sum(value):
    return jnp.sum(value, axis=0, keepdims=True)


GROUPS = {"do": (240, "iiihlll"), "u": (192, "lllh"), "q": (176, "iiiiii")}


def down_out_grads(more, block, at, held, sems, gt, dr2l, resid_other, given, xm, xm_other, dr1l):
    copies = [
        pltpu.make_async_copy(given.at[8 + 4 * j : 12 + 4 * j], held.at[4 * j : 4 * j + 4], sems.at[j])
        for j in range(4)
    ]
    start(copies)
    gt, dr2l, resid_other = gt(), dr2l(), resid_other()
    for ref in (xm, xm_other, dr1l, *more):
        ref.start()
    dr2l_other = jnp.concatenate([resid_other[0], resid_other[1]], axis=1)
    for j in range(4):
        mine = dot(gt[j].reshape(4 * 96, T), dr2l[...])
        copies[j].wait()
        other = dot(held[4 * j : 4 * j + 4].reshape(4 * 96, T), dr2l_other)
        value = (mine + other).astype(BF16)
        for half in range(2):
            rows = slice(at + 96 * half, at + 96 * half + 96)
            block[j, :, rows] = value[:, half * HALF : half * HALF + HALF].reshape(4, 96, HALF)
    xm, xm_other, dr1l = xm(), xm_other(), dr1l()
    panel_grad(block, at + 192, dot(xm[...], dr1l[...]), dot(xm_other[...], resid_other[2]))


def panel_grad(block, at, mine, other):
    block[:, :, at : at + ROWS] = (mine + other).astype(BF16).reshape(4, 4, ROWS, HALF)


def up_grads(more, block, at, held, sems, y1t, dul, dul_other, given):
    copy = pltpu.make_async_copy(given.at[0:8], held.at[16:24], sems.at[4])
    copy.start()
    y1t, dul, dul_other = y1t(), dul(), dul_other()
    left = y1t[...].reshape(D, T)
    copy.wait()
    left_other = held[16:24].reshape(D, T)
    for j in range(4):
        panel_grad(block, at + j * ROWS, dot(left, dul[j]), dot(left_other, dul_other[j]))


def qkv_grads(more, block, at, held, sems, xt, xt_other, part, part_low, part_high, small):
    xt, xt_other, part = xt(), xt_other(), part()
    part_other = [p[s] for p in (part_low(), part_high()) for s in range(5)]
    for j in range(3):
        mine, other = (
            jnp.concatenate([p[s] for s in range(3 * j, 3 * j + 3)], axis=1)
            for p in (part, part_other)
        )
        panel_grad(block, at + j * ROWS, dot(xt[...], mine), dot(xt_other[...], other))
    other = [part_other[9][16 * k : 16 * k + 16, :].astype(F32) for k in range(6)]
    small = small()[...] + jnp.concatenate(other, axis=1)
    small = jnp.concatenate([small[:, :HALF], small[:, HALF:]], axis=0)
    block[:, :, at + 144 : at + 176] = jnp.broadcast_to(small.astype(BF16), (4, 4, 32, HALF))


FILLS = {"do": down_out_grads, "u": up_grads, "q": qkv_grads}


def send_spread(block, part, place, outs):
    x, y = place[1], place[2]
    a_send, a_keep, b_send, b_keep = outs
    for side, a, b in ((1, a_send, b_send), (0, a_keep, b_keep)):
        for n in range(2):
            yield block.at[0:2, 2 * n + lax.bitwise_xor(x, side), part], a.at[n, :, part]
            yield block.at[2:4, 2 * lax.bitwise_xor(y, side) + n, part], b.at[n, :, part]


def send_mixed(cut, block, part, place, outs):
    x, y = place[1], place[2]
    a_send, a_keep, b_send, b_keep = outs
    low = slice(part.start, min(part.stop, cut))
    high = slice(max(part.start, cut), part.stop)
    for side, a, b in ((1, a_send, b_send), (0, a_keep, b_keep)):
        for n in range(2):
            if low.start < low.stop:
                yield block.at[:, 2 * n + lax.bitwise_xor(x, side), low], a.at[:, n, low]
            if high.start < high.stop:
                to = slice(high.start - cut, high.stop - cut)
                yield block.at[:, 2 * lax.bitwise_xor(y, side) + n, high], b.at[:, n, to]


def keep_kernel(groups, send, *refs):
    count = sum(len(GROUPS[g][1]) for g in groups)
    inputs, refs = refs[:count], refs[count:]
    place, outs, (block, held, sems, out_sems) = refs[0], refs[1:5], refs[5:]
    copies, at, first = [], 0, 0
    for g in groups:
        rows, kinds = GROUPS[g]
        more = [ref for ref in inputs[first + len(kinds) :] if isinstance(ref, In)]
        FILLS[g](more, block, at, held, sems, *inputs[first : first + len(kinds)])
        new = [
            pltpu.make_async_copy(src, dst, out_sems.at[len(copies) + n])
            for n, (src, dst) in enumerate(send(block, slice(at, at + rows), place, outs))
        ]
        start(new)
        copies += new
        at, first = at + rows, first + len(kinds)
    wait(copies)


def keep(groups, inputs, place, after, cut=None):
    rows = sum(GROUPS[g][0] for g in groups)
    if cut is None:
        send, outs = send_spread, [sds((2, 2, rows, HALF), BF16)] * 4
    else:
        send = functools.partial(send_mixed, cut)
        outs = [sds((4, 2, cut, HALF), BF16)] * 2 + [sds((4, 2, rows - cut, HALF), BF16)] * 2
    return call(
        functools.partial(keep_kernel, groups, send),
        "keep_grads",
        (*inputs, place),
        "".join(GROUPS[g][1] for g in groups) + "s",
        outs,
        "hhhh",
        [
            pltpu.VMEM((4, 4, rows, HALF), BF16),
            pltpu.VMEM((24, 96, T), BF16),
            pltpu.SemaphoreType.DMA((5,)),
            pltpu.SemaphoreType.DMA((16 * len(groups),)),
        ],
        after,
    )


def add_mid_kernel(sizes, *refs):
    pairs, line, blocks, sems = refs[: 2 * len(sizes)], refs[2 * len(sizes)], refs[2 * len(sizes) + 1 : -1], refs[-1]
    copies = [
        pltpu.make_async_copy(ref, blocks[n // 2].at[n % 2], sems.at[n]) for n, ref in enumerate(pairs)
    ]
    start(copies)
    at = 0
    for g, size in enumerate(sizes):
        wait(copies[2 * g : 2 * g + 2])
        total = (blocks[g][0].astype(F32) + blocks[g][1].astype(F32)).astype(BF16)
        line.held[:, at : at + 2 * size] = total.reshape(4, 2 * size, HALF)
        at += 2 * size


def add_mid(pairs, after):
    sizes = [keep.shape[2] for keep, _ in pairs]
    (line,) = call(
        functools.partial(add_mid_kernel, sizes),
        "add_mid",
        tuple(array for pair in pairs for array in pair),
        "h" * (2 * len(pairs)),
        [sds((4, 2 * sum(sizes), HALF), BF16)],
        "o",
        [
            *(pltpu.VMEM((2, 4, 2, size, HALF), BF16) for size in sizes),
            pltpu.SemaphoreType.DMA((2 * len(sizes),)),
        ],
        after,
    )
    return line


def part_slices(cuts, place):
    x, y = place[1], place[2]
    slices, base = [], 0
    for g, (cut, rows) in enumerate(cuts):
        for size, mine in ((cut, y), (rows - cut, x)):
            own, other = (
                pl.ds(pl.multiple_of(base + side * size, 16), size) for side in (mine, 1 - mine)
            )
            slices.append((g, size, own, other))
            base += 2 * size
    return slices


def part_kernel(cuts, total, place, *refs):
    n = 2 * len(cuts)
    outs, held, sems = refs[:n], refs[n : 2 * n], refs[-1]
    into, out = [], []
    for k, (_, _, _, other) in enumerate(part_slices(cuts, place)):
        into.append(pltpu.make_async_copy(total.at[other], held[k], sems.at[2 * k]))
        out.append(pltpu.make_async_copy(held[k], outs[k], sems.at[2 * k + 1]))
    start(into)
    for k, copy in enumerate(into):
        copy.wait()
        out[k].start()
    wait(out)


def part_rows(total, cuts, place, after):
    shapes = [sds((size, HALF), BF16) for cut, rows in cuts for size in (cut, rows - cut)]
    return call(
        functools.partial(part_kernel, cuts),
        "part",
        (total, place),
        "hs",
        shapes,
        "h" * len(shapes),
        [
            *(pltpu.VMEM(shape.shape, BF16) for shape in shapes),
            pltpu.SemaphoreType.DMA((2 * len(shapes),)),
        ],
        after,
    )


def close_kernel(cuts, total, *refs):
    n = len(cuts)
    got, place, flow = refs[: 2 * n], refs[2 * n], refs[2 * n + 1]
    held, sems = refs[2 * n + 2 : -1], refs[-1]
    slices = part_slices(cuts, place)
    copies = [
        pltpu.make_async_copy(total.at[own], held[k], sems.at[k])
        for k, (_, _, own, _) in enumerate(slices)
    ]
    start(copies)
    at = 0
    for k, (_, size, _, _) in enumerate(slices):
        copies[k].wait()
        value = held[k][...].astype(F32) + got[k]()[...].astype(F32)
        flow.held[at : at + size] = value.astype(BF16)
        at += size


def close(total, got, cuts, place, after):
    rows = sum(rows for _, rows in cuts)
    sizes = [size for cut, rows in cuts for size in (cut, rows - cut)]
    (sums,) = call(
        functools.partial(close_kernel, cuts),
        "close",
        (total, *got, place),
        "h" + "i" * len(got) + "s",
        [sds((rows, HALF), BF16)],
        "o",
        [
            *(pltpu.VMEM((size, HALF), BF16) for size in sizes),
            pltpu.SemaphoreType.DMA((len(sizes),)),
        ],
        after,
    )
    return sums


def spread_out_kernel(place, *refs):
    parts, outs = refs[:4], refs[4:]
    first = place[0] == 0
    qkv, out, up, down, gains, biases, up_b = (ref.held for ref in outs)
    device = place[3]

    def columns(first, count):
        row = lax.broadcasted_iota(jnp.int32, (D, count), 0)
        return (row == lax.broadcasted_iota(jnp.int32, (D, count), 1) + first).astype(BF16)

    def panel(l, at):
        mine, got = (
            jnp.where(first, value[:24], value[24:])
            for value in (ref()[at : at + ROWS].astype(F32) for ref in parts[2 * l : 2 * l + 2])
        )
        return jnp.concatenate([jnp.where(first, mine, got), jnp.where(first, got, mine)], axis=1)

    for l in (1, 0):
        mine = parts[2 * l]()
        down[l] = jnp.concatenate([mine[0:96], mine[96:192]], axis=1).astype(F32)
        out[l] = panel(l, 192)
        for j in range(4):
            up[l, :, j * D : j * D + D] = panel(l, 240 + j * ROWS)
        for j in range(3):
            qkv[l, :, j * D : j * D + D] = panel(l, 432 + j * ROWS)
        small = jnp.concatenate([mine[576:592], mine[592:608]], axis=1)
        heads = dot(small, columns(24 * device, 24))
        gains[l] = heads[0:2]
        for k in range(6):
            biases[k, l : l + 1, :] = heads[2 + k : 3 + k]
        tail = dot(small, columns(96 * lax.rem(device, 8), 96))
        row = lax.broadcasted_iota(jnp.int32, (16, 96), 0)
        up_b[l : l + 1] = column_sum(jnp.where(row == 8 + lax.div(device, 8), tail, 0.0))
        for ref in outs[:4]:
            ref.send(l)


def spread_out(place, enc, enc_other, dec, dec_other, after):
    return call(
        spread_out_kernel,
        "spread_out",
        (place, enc, enc_other, dec, dec_other),
        "siiii",
        [
            sds((2, 24, 3 * D), F32),
            sds((2, 24, D), F32),
            sds((2, 24, 4 * D), F32),
            sds((2, 96, D), F32),
            sds((2, 2, 24), F32),
            sds((6, 2, 24), F32),
            sds((2, 96), F32),
        ],
        "ooooooo",
        [],
        after,
    )


def add_next_kernel(a_keep, a_got, b_keep, b_got, place, a_next, b_next, blocks, sems):
    x, y = place[1], place[2]
    refs = (a_keep.at[1 - y], a_got.at[1 - y], b_keep.at[1 - x], b_got.at[1 - x])
    copies = [pltpu.make_async_copy(ref, blocks.at[n], sems.at[n]) for n, ref in enumerate(refs)]
    start(copies)
    for n, out in enumerate((a_next, b_next)):
        wait(copies[2 * n : 2 * n + 2])
        out.held[...] = (blocks[2 * n].astype(F32) + blocks[2 * n + 1].astype(F32)).astype(BF16)
        out.send()


def add_next(a_keep, a_got, b_keep, b_got, place, after):
    shape = a_keep.shape[2:]
    return call(
        add_next_kernel,
        "add_next",
        (a_keep, a_got, b_keep, b_got, place),
        "hhhhs",
        [sds((2, *shape), BF16)] * 2,
        "oo",
        [pltpu.VMEM((4, 2, *shape), BF16), pltpu.SemaphoreType.DMA((4,))],
        after,
    )


def add_last_kernel(sizes, *refs):
    place, line, sems = refs[6 * len(sizes)], refs[6 * len(sizes) + 1], refs[-1]
    blocks = refs[6 * len(sizes) + 2 : -1]
    x, y = place[1], place[2]
    copies = []
    for g in range(len(sizes)):
        a_keep, a_got, a_last, b_keep, b_got, b_last = refs[6 * g : 6 * g + 6]
        for n, ref in enumerate((a_keep.at[y], a_got.at[y], a_last, b_keep.at[x], b_got.at[x], b_last)):
            copies.append(pltpu.make_async_copy(ref, blocks[g].at[n], sems.at[6 * g + n]))
    start(copies)
    at = 0
    for g, rows in enumerate(sizes):
        for n in range(2):
            wait(copies[6 * g + 3 * n : 6 * g + 3 * n + 3])
            block = blocks[g]
            total = block[3 * n].astype(F32) + block[3 * n + 1].astype(F32)
            total = total + block[3 * n + 2].astype(F32)
            line.held[2 * n : 2 * n + 2, at : at + rows] = total.astype(BF16)
        at += rows


def add_last(groups, place, after):
    sizes = [group[0].shape[2] for group in groups]
    (line,) = call(
        functools.partial(add_last_kernel, sizes),
        "add_last",
        (*(array for group in groups for array in group), place),
        "h" * (6 * len(groups)) + "s",
        [sds((4, sum(sizes), HALF), BF16)],
        "o",
        [
            *(pltpu.VMEM((6, 2, rows, HALF), BF16) for rows in sizes),
            pltpu.SemaphoreType.DMA((6 * len(groups),)),
        ],
        after,
    )
    return line


BACK_OUTS = [
    sds((T, D), BF16),
    sds((T, D), F32),
    sds((6, T, 128), BF16),
    sds((16, D), F32),
    sds((4, T, HALF), BF16),
    sds((4, T, HALF), BF16),
    sds((T, HALF), BF16),
    sds((3, T, HALF), BF16),
]


def feed_back_kernel(layout_a, layout_b, *refs):
    cot, n2, r2, vec, gp, n1, r1, place, dxd, buck = refs[:10]
    refs = refs[10:]
    pieces_a, refs = refs[: layout_a.count], refs[layout_a.count :]
    pieces_b, refs = refs[: layout_b.count], refs[layout_b.count :]
    (dr2l, dr1, dml, small), outs, refs = refs[:4], refs[4:8], refs[8:]
    wo, wu, wd, scr, dul, dr1l, sems, out_sems = refs
    send = Sender(out_sems)
    copies = weight_copies(layout_a, layout_b, pieces_a, pieces_b, place, wo, wu, wd, sems)
    start(copies[2])
    gp.start()
    for group in copies[1]:
        start(group)
    n1.start()
    r1.start()
    start(copies[0])
    cot, dxd = cot(), dxd()

    def output_grad(rows):
        first = first_tokens(buck, rows.start, NORM_ROWS)
        return cot[rows, :].astype(F32) + jnp.where(first, dxd[rows, :], 0.0)

    feed_back_rows(
        output_grad, vec, small.held, copies, (wo, wu, wd), (n1, r1, n2, r2, gp), (scr, dul, dr1l),
        (dr2l, dr1, dml, *outs), send, place[0],
    )
    send.wait()


def feed_back(cot, n2, r2, vec, gp, n1, r1, place, part_a, part_b, after, dxd, buck):
    (layout_a, pieces_a), (layout_b, pieces_b) = part_a, part_b
    return call(
        functools.partial(feed_back_kernel, layout_a, layout_b),
        "feed_back",
        (cot, n2, r2, vec, gp, n1, r1, place, dxd, buck, *pieces_a, *pieces_b),
        "iiiillls" + "is" + "h" * (layout_a.count + layout_b.count),
        BACK_OUTS,
        "oooohhhh",
        [
            *WEIGHTS,
            pltpu.VMEM((T, D), F32),
            pltpu.VMEM((4, T, D), BF16),
            pltpu.VMEM((T, D), BF16),
            pltpu.SemaphoreType.DMA((6, 10)),
            pltpu.SemaphoreType.DMA((12,)),
        ],
        after,
        span=12,
    )


def feed_both_kernel(layout_a, layout_b, *refs):
    x, m, vec, place, cot = refs[:5]
    refs = refs[5:]
    pieces_a, refs = refs[: layout_a.count], refs[layout_a.count :]
    pieces_b, refs = refs[: layout_b.count], refs[layout_b.count :]
    out, transposed, refs = refs[0], refs[1:4], refs[4:]
    (dr2l, dr1, dml, small), outs, refs = refs[:4], refs[4:8], refs[8:]
    wo, wu, wd, scr, y1, y1l, g, y1t, gt, n1, r1, n2, r2, gp, dul, sems, out_sems = refs
    c = place[0]
    send = Sender(out_sems)
    copies = weight_copies(layout_a, layout_b, pieces_a, pieces_b, place, wo, wu, wd, sems)
    start(copies[0])
    for group in copies[1]:
        start(group)
    start(copies[2])
    cot.start()
    first_done, panel_done = send_transposed(send, y1l, g, y1t, gt, transposed, c)

    def result(rows, value):
        out.held[rows, :] = value.astype(BF16)

    feed_rows(
        x, m, vec, copies, (wo, wu, wd), (n1, r1, n2, r2, gp), (scr, y1, y1l, g), first_done, panel_done, result
    )
    out.send()
    cot = cot()
    saved = [lambda ref=ref: ref for ref in (n1, r1, n2, r2, gp)]
    feed_back_rows(
        lambda rows: cot[rows, :].astype(F32), vec, small.held, ([], [[]] * 4, []), (wo, wu, wd), saved,
        (scr, dul, y1l), (dr2l, dr1, dml, *outs), send, c,
    )
    send.wait()


def feed_both(x, m, vec, place, cot, part_a, part_b, after):
    (layout_a, pieces_a), (layout_b, pieces_b) = part_a, part_b
    return call(
        functools.partial(feed_both_kernel, layout_a, layout_b),
        "feed_both",
        (x, m, vec, place, cot, *pieces_a, *pieces_b),
        "iiisl" + "h" * (layout_a.count + layout_b.count),
        [sds((T, D), BF16), *TRANSPOSED, *BACK_OUTS],
        "ohhhoooohhhh",
        [
            *WEIGHTS,
            pltpu.VMEM((T, D), F32),
            pltpu.VMEM((T, D), F32),
            pltpu.VMEM((T, D), BF16),
            pltpu.VMEM((4, T, D), BF16),
            pltpu.VMEM((8, 96, T), BF16),
            pltpu.VMEM((4, 4, 2, 96, T), BF16),
            pltpu.VMEM((T, D), F32),
            pltpu.VMEM((T, 128), F32),
            pltpu.VMEM((T, D), F32),
            pltpu.VMEM((T, 128), F32),
            pltpu.VMEM((4, T, D), BF16),
            pltpu.VMEM((4, T, D), BF16),
            pltpu.SemaphoreType.DMA((6, 10)),
            pltpu.SemaphoreType.DMA((24,)),
        ],
        after,
        span=20,
    )


def attend_back_kernel(*refs):
    p, dml, stat, small_in, lens, buck, place = refs[:7]
    keep_out, low_out, high_out, small_out, dpl, slab, bias, out_sems = refs[7:]
    small = small_out.held
    c = place[0]
    fill_bias(bias, lens, buck)
    p, dml, stat = p(), dml(), stat()
    scale = jnp.asarray(HD**-0.5, BF16)
    small[...] = small_in()[...]

    def pair(i):
        q = p[i] * scale
        k_t = p[6 + i].T
        both = dot_rt(jnp.concatenate(halves(p[6 + i]), axis=0), q)
        grad = dml[i]
        dboth = dot_rt(jnp.concatenate(halves(p[12 + i]), axis=0), grad)
        softs, dscores, dq = [], [], []
        for a in range(2):
            scores = both[T * a : T * a + T] + bias[...]
            peak = stat[2 * i + a, 0:1, :]
            inverse = stat[2 * i + a, 1:2, :]
            soft = jnp.exp(scores - peak) * inverse
            dsoft = dboth[T * a : T * a + T]
            total = jnp.sum(soft * dsoft, axis=0, keepdims=True)
            dscore = (soft * (dsoft - total)).astype(BF16)
            softs.append(soft.astype(BF16))
            dscores.append(dscore)
            dq.append(dot(k_t[HD * a : HD * a + HD, :], dscore))
        grads, queries = halves(grad), halves(q)
        dv = (dot(softs[0], grads[0]) + dot(softs[1], grads[1])).astype(BF16)
        dk = (dot(dscores[0], queries[0]) + dot(dscores[1], queries[1])).astype(BF16)
        dq = (jnp.concatenate(dq, axis=0).T * (HD**-0.5)).astype(BF16)
        dpl[i] = dq
        dpl[6 + i] = dk
        dpl[12 + i] = dv
        cols = pl.ds(pl.multiple_of(i * 128, 128), 128)
        small[2:3, cols] = column_sum(dq.astype(F32))
        small[3:4, cols] = column_sum(dv.astype(F32))

    def pairs(n, carry):
        for k in range(ATTEND_BACK_PAIRS):
            pair(ATTEND_BACK_PAIRS * n + k)
        return carry

    lax.fori_loop(0, 6 // ATTEND_BACK_PAIRS, pairs, 0)
    slab[...] = jnp.zeros_like(slab)
    for k in range(6):
        slab[16 * k : 16 * k + 16, :] = small[:, 128 * k : 128 * k + 128].astype(BF16)
    h = 3 * (1 - c)
    sent = [
        (dpl.at[pl.ds(h, 3)], low_out.at[0:3]),
        (dpl.at[pl.ds(6 + h, 2)], low_out.at[3:5]),
        (dpl.at[pl.ds(8 + h, 1)], high_out.at[0:1]),
        (dpl.at[pl.ds(12 + h, 3)], high_out.at[1:4]),
        (slab, high_out.at[4]),
    ]
    for j in range(3):
        sent.append((dpl.at[pl.ds(6 * j + 3 * c, 3)], keep_out.at[3 * j : 3 * j + 3]))
    sent = [pltpu.make_async_copy(src, dst, out_sems.at[n]) for n, (src, dst) in enumerate(sent)]
    start(sent)
    wait(sent)


def attend_back(p, dml, stat, small, lens, buck, place, after):
    return call(
        attend_back_kernel,
        "attend_back",
        (p, dml, stat, small, lens, buck, place),
        "iiiisss",
        [sds((9, T, 128), BF16), sds((5, T, 128), BF16), sds((5, T, 128), BF16), sds((16, D), F32)],
        "hhho",
        [
            pltpu.VMEM((18, T, 128), BF16),
            pltpu.VMEM((T, 128), BF16),
            pltpu.VMEM((T, T), F32),
            pltpu.SemaphoreType.DMA((10,)),
        ],
        after,
    )


def input_back_kernel(encoder, layout, *refs):
    dpl_keep, dpl_low, dpl_high, dr1, place = refs[:5]
    refs = refs[5:]
    if not encoder:
        buck, refs = refs[0], refs[1:]
    pieces, refs = refs[: layout.count], refs[layout.count :]
    if not encoder:
        dxd_out, refs = refs[0], refs[1:]
        dxd = dxd_out.held
    out_flow, dpl, wq, sems = refs
    out = out_flow.held
    c = place[0]
    copies = []
    for j in range(3):
        group = panel_copies(layout, pieces, place, wq.at[j], sems.at[j], j * ROWS, ROWS)
        other = 6 * j + 3 * (1 - c)
        pairs = [(dpl_keep.at[3 * j : 3 * j + 3], pl.ds(6 * j + 3 * c, 3))]
        if j == 0:
            pairs.append((dpl_low.at[0:3], pl.ds(other, 3)))
        elif j == 1:
            pairs += [(dpl_low.at[3:5], pl.ds(other, 2)), (dpl_high.at[0:1], pl.ds(other + 2, 1))]
        else:
            pairs.append((dpl_high.at[1:4], pl.ds(other, 3)))
        for n, (src, at) in enumerate(pairs):
            group.append(pltpu.make_async_copy(src, dpl.at[at], sems.at[j, 10 + n]))
        start(group)
        copies.append(group)
    dr1 = dr1()
    for group in copies:
        wait(group)
    for half in range(2):
        rows = slice(half * 256, half * 256 + 256)
        total = dr1[rows, :]
        for j in range(3):
            left = jnp.concatenate([dpl[6 * j + s, rows, :] for s in range(6)], axis=1)
            total = total + dot_rt(left, wq[j].reshape(D, D))
        if encoder:
            out[rows, :] = total.astype(BF16)
        else:
            dxd[rows, :] = total
            out[rows, :] = jnp.where(first_tokens(buck, half * 256, 256), 0.0, total).astype(BF16)
            dxd_out.send(rows)
        out_flow.send(rows)


def input_back(encoder, slabs, dr1, place, part_a, after, buck=None):
    layout, pieces = part_a
    args, kinds = (*slabs, dr1, place), "hhhis"
    outs = [sds((T, D), BF16)]
    if not encoder:
        args, kinds = (*args, buck), kinds + "s"
        outs = [sds((T, D), F32), *outs]
    return call(
        functools.partial(input_back_kernel, encoder, layout),
        "input_back",
        (*args, *pieces),
        kinds + "h" * layout.count,
        outs,
        "o" * len(outs),
        [
            pltpu.VMEM((18, T, 128), BF16),
            pltpu.VMEM((3, 4, 4, ROWS, D), BF16),
            pltpu.SemaphoreType.DMA((3, 13)),
        ],
        after,
        span=30 if encoder else 0,
    )


def gate_kernel(*refs):
    pass


def gate(values, after):
    outs = call(
        gate_kernel,
        "gate",
        tuple(values),
        "h" * len(values),
        [sds(v.shape, v.dtype) for v in values],
        "h" * len(values),
        [],
        after,
        {n: n for n in range(len(values))},
    )
    return list(outs)


def split_kernel(bx, by, ax, ay, held, sems):
    refs = ((bx.at[0:2], held.at[0], ax), (by.at[2:4], held.at[1], ay))
    into = [pltpu.make_async_copy(src, mid, sems.at[n]) for n, (src, mid, _) in enumerate(refs)]
    out = [pltpu.make_async_copy(mid, dst, sems.at[2 + n]) for n, (_, mid, dst) in enumerate(refs)]
    start(into)
    for n in range(2):
        into[n].wait()
        out[n].start()
    wait(out)


def split(bx, by, after):
    shape = (2, *bx.shape[1:])
    return call(
        split_kernel,
        "split",
        (bx, by),
        "hh",
        [sds(shape, BF16)] * 2,
        "hh",
        [pltpu.VMEM((2, *shape), BF16), pltpu.SemaphoreType.DMA((4,))],
        after,
    )


def cut_kernel(at, line, low, high, held, sems):
    into, out = [], []
    for n, (rows, dst) in enumerate(((slice(0, at), low), (slice(at, held.shape[1]), high))):
        into.append(pltpu.make_async_copy(line.at[:, rows], held.at[:, rows], sems.at[n]))
        out.append(pltpu.make_async_copy(held.at[:, rows], dst, sems.at[2 + n]))
    start(into)
    for n in range(2):
        into[n].wait()
        out[n].start()
    wait(out)


def cut(line, at, after):
    rows = line.shape[1]
    return call(
        functools.partial(cut_kernel, at),
        "cut",
        (line,),
        "h",
        [sds((4, at, HALF), BF16), sds((4, rows - at, HALF), BF16)],
        "hh",
        [pltpu.VMEM((4, rows, HALF), BF16), pltpu.SemaphoreType.DMA((4,))],
        after,
    )


AXES = ("z", "y", "x", "c", "e")


def swap(value, axis):
    return lax.ppermute(value, axis, [(0, 1), (1, 0)])


def pick(value, index, axis):
    return lax.dynamic_index_in_dim(value, index, axis, keepdims=False)


class SpreadGather:
    def __init__(self, rows):
        self.own = lax.all_gather(rows, "z", axis=0, tiled=False)

    def plane(self, after):
        (self.own,) = gate([self.own], after)
        self.bx, self.by = swap(self.own, "x"), swap(self.own, "y")
        self.own_c = swap(self.own, "c")
        return (self.own,)

    def forward(self, after):
        ax, ay = split(self.bx, self.by, (*after, self.own_c))
        self.dx, self.dy = swap(ax, "y"), swap(ay, "x")
        self.bx_c, self.by_c = swap(self.bx, "c"), swap(self.by, "c")
        return (ax,)

    def across(self):
        there = (self.own, self.bx, self.by, self.dx, self.dy)
        self.pieces = (*there, self.own_c, self.bx_c, self.by_c, swap(self.dx, "c"), swap(self.dy, "c"))


class MixedGather:
    def __init__(self, rows, at, along_x, along_y):
        self.at, self.size = at, rows.shape[0]
        self.rows = jnp.concatenate([rows[:at], along_x, rows[at:], along_y])

    def line(self, after):
        (rows,) = gate([self.rows], after)
        self.own = lax.all_gather(rows, "z", axis=0, tiled=False)
        return (rows,)

    def arrive(self, after):
        (self.own,) = gate([self.own], after)
        return (self.own,)

    def plane(self, after):
        self.low, self.high = cut(self.own, 2 * self.at, after)
        return (self.low,)

    def last(self, after=()):
        low, high = self.low, self.high
        if after:
            low, high = gate([low, high], after)
        self.low, self.high = swap(low, "y"), swap(high, "x")
        return (low,)

    def near(self, after):
        tok = self.arrive(after)
        self.own_c = swap(self.own, "c")
        return tok

    def across(self, after):
        self.low, self.high = gate([self.low, self.high], after)
        self.low_c, self.high_c = swap(self.low, "c"), swap(self.high, "c")
        self.pieces = (self.own, self.low, self.high, self.own_c, self.low_c, self.high_c)
        self.part = (Mixed(self.at, self.size), self.pieces)
        return (self.low,)


class Scatter:
    def __init__(self, groups, place, cut=None):
        self.groups, self.place, self.cut = groups, place, cut

    def keep(self, inputs, after):
        a_send, self.a_keep, b_send, self.b_keep = keep(
            self.groups, inputs, self.place, after, self.cut
        )
        self.a_got, self.b_got = swap(a_send, "x"), swap(b_send, "y")
        return (a_send,)

    def next(self, after):
        a_next, b_next = add_next(
            self.a_keep, self.a_got, self.b_keep, self.b_got, self.place, after
        )
        self.a_last, self.b_last = swap(a_next, "y"), swap(b_next, "x")
        return (a_next,)

    def sums(self):
        return (self.a_keep, self.a_got, self.a_last, self.b_keep, self.b_got, self.b_last)


def along_z(scatters, after):
    pairs = []
    for scatter in scatters:
        pairs += [(scatter.a_keep, scatter.a_got), (scatter.b_keep, scatter.b_got)]
    line = add_mid(pairs, after)
    return (line,), lax.psum_scatter(line, "z", scatter_dimension=0, tiled=False)


def finish(scatters, place, after):
    line = add_last([scatter.sums() for scatter in scatters], place, after)
    return (line,), lax.psum_scatter(line, "z", scatter_dimension=0, tiled=False)


def pack_weights(qkv, out, up, down, gains, biases, up_b, c, device):
    rows = out.shape[1]
    panels = jnp.concatenate([qkv, out, up], axis=2).reshape(2, rows, 8, 2, HALF)
    panels = jnp.transpose(panels, (0, 3, 2, 1, 4)).reshape(2, 2, 8 * rows, HALF)
    downs = jnp.transpose(down.reshape(2, 4 * rows, 2, HALF), (0, 2, 1, 3))
    both = jnp.concatenate([panels, downs], axis=2)
    mine = pick(both, c, 1)
    got = swap(pick(both, 1 - c, 1), "c")
    low = jnp.where(c == 0, mine, got)
    high = jnp.where(c == 0, got, mine)
    panels = jnp.stack(
        [low[:, : 8 * rows].reshape(2, 8, rows, HALF), high[:, : 8 * rows].reshape(2, 8, rows, HALF)],
        axis=2,
    ).reshape(2, 16 * rows, HALF)
    downs = jnp.concatenate([low[:, 8 * rows :], high[:, 8 * rows :]], axis=1)
    small = jnp.zeros((2, 16, D), BF16)
    small = lax.dynamic_update_slice(
        small, jnp.concatenate([gains, biases], axis=1), (0, 0, device * rows)
    )
    small = lax.dynamic_update_slice(
        small, up_b[:, None, :], (0, 8 + device // 8, device % 8 * (4 * rows))
    )
    small = jnp.concatenate([small[:, :, :HALF], small[:, :, HALF:]], axis=1)
    part_a = jnp.concatenate([panels[:, : 8 * rows], small], axis=1)
    part_b = jnp.concatenate([panels[:, 8 * rows :], downs], axis=1)
    return part_a, part_b


def body(
    encoder_input,
    corrupted,
    lengths,
    buckets,
    qkv_weight,
    out_weight,
    up_weight,
    down_weight,
    norm_gains,
    bias_rows,
    up_bias,
    encoder_cot,
    decoder_cot,
):
    extra = lax.axis_size("e")
    weights = [qkv_weight, out_weight, up_weight, down_weight, norm_gains, bias_rows, up_bias]
    if extra > 1:
        weights = [
            lax.all_gather(w, "e", axis=at, tiled=True)
            for w, at in zip(weights, (1, 1, 1, 1, 2, 2, 1))
        ]
    rows = weights[1].shape[1]
    x, y, c = lax.axis_index("x"), lax.axis_index("y"), lax.axis_index("c")
    device = ((lax.axis_index("z") * 2 + y) * 2 + x) * 2 + c
    place = jnp.stack([c, x, y, device]).astype(jnp.int32)
    part_a, part_b = pack_weights(*weights, c, device)
    at_a, at_b = 2 * ROWS, 4 * ROWS
    along_x = swap(jnp.concatenate([part_a[1, :at_a], part_b[1, :at_b]]), "x")
    along_y = swap(jnp.concatenate([part_a[1, at_a:], part_b[1, at_b:]]), "y")
    g0 = SpreadGather(jnp.concatenate([part_a[0], part_b[0]]))
    g1a = MixedGather(part_a[1], at_a, along_x[:at_a], along_y[: PART_A - at_a])
    g1b = MixedGather(part_b[1], at_b, along_x[at_a:], along_y[PART_A - at_a :])

    tok = g0.plane((along_x, along_y))
    tok = g1a.line(tok)
    tok = g1b.line(tok)
    tok = g0.forward(tok)
    g1a.plane(tok)
    g0.across()
    part_a0, part_b0 = (Spread(0), g0.pieces), (Spread(PART_A), g0.pieces)
    tok = g1a.last((g0.dx, g0.dy))
    tok = g1a.near(tok)
    p0, m0, xt0, mt0, stat0, vec0 = attend(encoder_input, lengths, buckets, place, part_a0, tok, 0)
    tok = g1b.near((stat0,))
    tok = g1b.plane((*tok, g1a.own_c))
    g1b.last()
    tok = g1a.across(tok)
    enc_out, *saved0, xd, xdl, y1t0, gt0, give0 = feed(
        encoder_input, m0, vec0, place, part_a0, part_b0, tok, corrupted, buckets
    )
    given0 = swap(give0, "c")
    xt0_other, mt0_other = swap(xt0, "c"), swap(mt0, "c")
    part_a1 = g1a.part
    p1, m1, xt1, mt1, stat1, vec1 = attend(
        xdl, lengths, buckets, place, part_a1, (enc_out,), 0
    )
    xt1_other, mt1_other = swap(xt1, "c"), swap(mt1, "c")
    tok = g1b.across((stat1,))
    part_b1 = g1b.part
    dec_out, y1t1, gt1, give1, dr2l, dr1, dml, small, dul, dul_give, dr1l, resid = feed_both(
        xd, m1, vec1, place, decoder_cot, part_a1, part_b1, tok
    )

    given1 = swap(give1, "c")
    resid, dul_other = swap(resid, "c"), swap(dul_give, "c")
    cuts = ((208, 432), (96, 176))
    s1, q1 = Scatter(("do", "u"), place, cuts[0][0]), Scatter(("q",), place, cuts[1][0])
    part, low, high, small = attend_back(
        p1, dml, stat1, small, lengths, buckets, place, (dr1, given0)
    )
    part_other = [swap(low, "c"), swap(high, "c")]
    tok = s1.keep(
        (gt1, dr2l, resid, given1, mt1, mt1_other, dr1l, y1t1, dul, dul_other, given1), (small,)
    )
    tok = q1.keep((xt1, xt1_other, part, *part_other, small), tok)
    dxd, cor_grad = input_back(False, (part, low, high), dr1, place, part_a1, tok, buckets)
    tok = (cor_grad,)

    n1, r1, n2, r2, gp = saved0
    dr2l, dr1, dml, small, dul, dul_give, dr1l, resid = feed_back(
        encoder_cot, n2, r2, vec0, gp, n1, r1, place, part_a0, part_b0, tok, dxd, buckets
    )
    resid, dul_other = swap(resid, "c"), swap(dul_give, "c")
    tok, dec_total = along_z([s1, q1], (dr1,))
    s0, q0 = Scatter(("do", "u"), place), Scatter(("q",), place)
    tok = s0.keep(
        (gt0, dr2l, resid, given0, mt0, mt0_other, dr1l, y1t0, dul, dul_other, given0), tok
    )
    part, low, high, small = attend_back(p0, dml, stat0, small, lengths, buckets, place, tok)
    part_other = [swap(low, "c"), swap(high, "c")]
    tok = q0.keep((xt0, xt0_other, part, *part_other, small), (small,))
    tok = s0.next(tok)
    (enc_grad,) = input_back(True, (part, low, high), dr1, place, part_a0, tok)
    tok = q0.next((enc_grad,))
    (dec_total,) = gate([dec_total], tok)
    tok, both0 = finish([s0, q0], place, (dec_total,))
    sent = part_rows(dec_total, cuts, place, tok)
    got = [swap(value, "yx"[n % 2]) for n, value in enumerate(sent)]
    dec_rows = close(dec_total, got, cuts, place, ())
    grads_out = list(
        spread_out(place, both0, swap(both0, "c"), dec_rows, swap(dec_rows, "c"), ())
    )
    grads_out[5] = jnp.transpose(grads_out[5], (1, 0, 2))
    if extra > 1:
        grads_out = [
            lax.psum_scatter(v, "e", scatter_dimension=at, tiled=True)
            for v, at in zip(grads_out, (1, 1, 1, 1, 2, 2, 1))
        ]
    return (enc_out, dec_out, enc_grad, cor_grad, *grads_out)


def solution(mesh):
    devices = mesh.devices.reshape(4, 2, 2, 2, -1)
    inner = Mesh(devices, AXES)
    token = P(AXES, None)
    line = P(AXES)
    wide = P(None, AXES, None)
    vector = P(None, None, AXES)
    return jax.shard_map(
        body,
        mesh=inner,
        in_specs=(
            token, token, line, line, wide, wide, wide, wide, vector, vector, P(None, AXES), token, token,
        ),
        out_specs=(
            token, token, token, token, wide, wide, wide, wide, vector, vector, P(None, AXES),
        ),
        check_vma=False,
    )
```

```python
import functools

import jax
import jax.numpy as jnp
from jax import lax
from jax.experimental import pallas as pl
from jax.experimental.pallas import tpu as pltpu
from jax.sharding import Mesh
from jax.sharding import PartitionSpec as P

HD = 64
SLOT = 128
EPSILON = 1e-06
NEGATIVE = -1e30
F32 = jnp.float32
BF16 = jnp.bfloat16
VMEM_LIMIT = 64 * 1024 * 1024

T = 512
D = 768
HALF = D // 2
ROWS = 48
DROWS = 192
O_AT, SMALL_AT, PART_A = 144, 192, 224
D_AT, PART_B = 192, 384

NORM_ROWS = 256
ATTEND_BACK_PAIRS = 2
SM = pl.BlockSpec(memory_space=pltpu.SMEM)
HBM = pl.BlockSpec(memory_space=pl.ANY)
SPAN = {
    "feed": 20,
    "add_next": 12,
    "add_mid": 16,
}


def dot(left, right):
    return lax.dot_general(left, right, (((1,), (0,)), ((), ())), preferred_element_type=F32)


def dot_rt(left, right):
    return lax.dot_general(left, right, (((1,), (1,)), ((), ())), preferred_element_type=F32)


def sds(shape, dtype):
    return jax.ShapeDtypeStruct(shape, dtype)


class In:
    def __init__(self, source, held, sem, late):
        self.held, self.copy, self.there = held, pltpu.make_async_copy(source, held, sem), False
        self.begun = False
        if not late:
            self.start()

    def start(self):
        if not self.begun:
            self.begun = True
            self.copy.start()

    def __call__(self):
        if not self.begun:
            self.start()
        if not self.there:
            self.copy.wait()
            self.there = True
        return self.held


class Out:
    def __init__(self, target, held, sems):
        self.target, self.held, self.sems, self.copies = target, held, sems, []

    def send(self, index=None):
        source = self.held if index is None else self.held.at[index]
        target = self.target if index is None else self.target.at[index]
        copy = pltpu.make_async_copy(source, target, self.sems.at[len(self.copies)])
        copy.start()
        self.copies.append(copy)

    def wait(self):
        for copy in self.copies:
            copy.wait()


def call(kernel, name, args, in_kinds, outs, out_kinds, scratch, after=(), aliases=None, span=None):
    n, m, k = len(args), len(after), len(outs)
    spec = {"i": HBM, "l": HBM, "o": HBM, "h": HBM, "s": SM}
    ins = [a for a, kind in zip(args, in_kinds) if kind in "il"]
    sent = [o for o, kind in zip(outs, out_kinds) if kind == "o"]

    def ordered(*refs):
        inputs, results, rest = refs[:n], refs[n + m : n + m + k], refs[n + m + k :]
        held_in, held_out = rest[: len(ins)], rest[len(ins) : len(ins) + len(sent)]
        own = rest[len(ins) + len(sent) : len(ins) + len(sent) + len(scratch)]
        sems = rest[len(ins) + len(sent) + len(scratch) :]
        lazy, at = [], 0
        for ref, kind in zip(inputs, in_kinds):
            if kind in "il":
                ref, at = In(ref, held_in[at], sems[0].at[at], kind == "l"), at + 1
            lazy.append(ref)
        flow, at = [], 0
        for ref, kind in zip(results, out_kinds):
            if kind == "o":
                ref, at = Out(ref, held_out[at], sems[-1].at[at]), at + 1
            flow.append(ref)
        kernel(*lazy, *flow, *own)
        for ref in lazy:
            if isinstance(ref, In):
                ref()
        flow = [ref for ref in flow if isinstance(ref, Out)]
        for ref in flow:
            if not ref.copies:
                ref.send()
        for ref in flow:
            ref.wait()

    sems = []
    if ins:
        sems.append(pltpu.SemaphoreType.DMA((len(ins),)))
    if sent:
        sems.append(pltpu.SemaphoreType.DMA((len(sent), 4)))
    return pl.pallas_call(
        ordered,
        out_shape=outs,
        in_specs=[*(spec[kind] for kind in in_kinds), *([HBM] * m)],
        out_specs=[HBM] * k,
        scratch_shapes=[
            *(pltpu.VMEM(a.shape, a.dtype) for a in ins),
            *(pltpu.VMEM(o.shape, o.dtype) for o in sent),
            *scratch,
            *sems,
        ],
        input_output_aliases=aliases or {},
        compiler_params=pltpu.CompilerParams(vmem_limit_bytes=VMEM_LIMIT),
        cost_estimate=pl.CostEstimate(
            flops=int(1000 + 1.1e9 * (SPAN.get(name, 0) if span is None else span)), bytes_accessed=1000, transcendentals=0
        ),
        name=name,
    )(*args, *after)


def start(copies):
    for copy in copies:
        copy.start()


def wait(copies):
    for copy in copies:
        copy.wait()


class Spread:
    count = 10

    def __init__(self, base):
        self.base = base

    def slabs(self, refs, place, row_at, rows):
        c, x, y = place[0], place[1], place[2]
        across = 2 * (1 - y) + (1 - x)
        slots = ((2 * y + x, 0, 4), (2 * y + 1 - x, 0, 4), (2 * (1 - y) + x, 0, 4), (across, 0, 2), (across, 2, 4))
        first = self.base + row_at
        for half, group in ((c, refs[:5]), (1 - c, refs[5:])):
            for ref, (at, low, high) in zip(group, slots):
                yield ref.at[:, first : first + rows, :], at, low, high, half


class Mixed:
    count = 6

    def __init__(self, cut, size):
        self.cut, self.size = cut, size

    def slabs(self, refs, place, row_at, rows):
        c, x, y = place[0], place[1], place[2]
        own, near_x, near_y = 2 * y + x, 2 * y + 1 - x, 2 * (1 - y) + x
        across = 2 * (1 - y) + (1 - x)
        rest = self.size - self.cut
        for half, (line, low, high) in ((c, refs[:3]), (1 - c, refs[3:])):
            if row_at < self.cut:
                places = ((line, row_at, own), (line, self.cut + row_at, near_x))
                places += ((low, row_at, near_y), (low, self.cut + row_at, across))
            else:
                first, base = row_at - self.cut, 2 * self.cut
                places = ((line, base + first, own), (line, base + rest + first, near_y))
                places += ((high, first, near_x), (high, rest + first, across))
            for ref, first, at in places:
                yield ref.at[:, first : first + rows, :], at, 0, 4, half


def half_cols(h):
    return pl.ds(pl.multiple_of(h * HALF, HALF), HALF)


def panel_copies(layout, refs, place, dst, sems, row_at, rows):
    copies = []
    for n, (src, at, low, high, half) in enumerate(layout.slabs(refs, place, row_at, rows)):
        copies.append(
            pltpu.make_async_copy(src, dst.at[low:high, at, :, half_cols(half)], sems.at[n])
        )
    return copies


def fill_bias(bias, lens, buck):
    bucket = buck[0]
    key = lax.broadcasted_iota(jnp.int32, (T, T), 0)
    query = lax.broadcasted_iota(jnp.int32, (T, T), 1)
    shift = bucket + 7
    same = lax.shift_right_logical(key, shift) == lax.shift_right_logical(query, shift)
    position = jnp.bitwise_and(key, lax.shift_left(jnp.int32(SLOT), bucket) - 1)
    slot = lax.shift_right_logical(key, 7)
    length = jnp.where(
        slot < 2,
        jnp.where(slot == 0, lens[0], lens[1]),
        jnp.where(slot == 2, lens[2], lens[3]),
    )
    bias[...] = jnp.where(same & (position < length), 0.0, NEGATIVE)


def first_tokens(buck, low, size):
    span = lax.shift_left(jnp.int32(SLOT), buck[0])
    token = lax.broadcasted_iota(jnp.int32, (size, 1), 0) + low
    return jnp.bitwise_and(token, span - 1) == 0


def halves(block):
    lane = lax.broadcasted_iota(jnp.int32, block.shape, 1)
    zero = jnp.zeros_like(block)
    return jnp.where(lane < HD, block, zero), jnp.where(lane < HD, zero, block)


def row_loop(size, body):
    if size == T:
        return body(pl.ds(0, T))

    def step(i, carry):
        body(pl.ds(pl.multiple_of(i * size, size), size))
        return carry

    lax.fori_loop(0, T // size, step, 0)


def attend_kernel(layout, *refs):
    x, lens, buck, place = refs[:4]
    pieces, refs = refs[4 : 4 + layout.count], refs[4 + layout.count :]
    flow, (wq, bias, heap, sems) = refs[:6], refs[6:]
    p, m, xt, mt, stat, vec = (ref.held for ref in flow)
    copies = [
        panel_copies(layout, pieces, place, wq.at[j], sems.at[j], j * ROWS, ROWS) for j in range(3)
    ]
    smalls, at = [], 0
    for n, (src, _, low, high, _) in enumerate(layout.slabs(pieces, place, SMALL_AT, 32)):
        smalls.append(pltpu.make_async_copy(src, heap.at[at : at + high - low], sems.at[3, n]))
        at += high - low
    start(smalls)
    for group in copies:
        start(group)
    fill_bias(bias, lens, buck)
    x = x()
    xt[...] = x[...].T
    flow[2].send()
    wait(smalls)
    total = heap[0].astype(F32)
    for n in range(1, 32):
        total = total + heap[n].astype(F32)
    vec[...] = jnp.concatenate([total[:16], total[16:]], axis=1)
    flow[5].send()
    for j in range(3):
        wait(copies[j])
        weight = wq[j].reshape(D, D)
        for half in range(2):
            rows = slice(half * 256, half * 256 + 256)
            out = dot(x[rows, :], weight)
            if j != 1:
                out = out + (vec[2:3, :] if j == 0 else vec[3:4, :])
            out = out.astype(BF16)
            for s in range(6):
                p[6 * j + s, rows, :] = out[:, 128 * s : 128 * s + 128]
        flow[0].send(slice(6 * j, 6 * j + 6))

    def pair(i):
        q = p[i] * jnp.asarray(HD**-0.5, BF16)
        v_t = p[12 + i].T
        both = dot_rt(jnp.concatenate(halves(p[6 + i]), axis=0), q)
        mixed = []
        for a in range(2):
            scores = both[T * a : T * a + T] + bias[...]
            peak = jnp.max(scores, axis=0, keepdims=True)
            weights = jnp.exp(scores - peak)
            inverse = 1.0 / jnp.sum(weights, axis=0, keepdims=True)
            stat[2 * i + a, 0:1, :] = peak
            stat[2 * i + a, 1:2, :] = inverse
            soft = (weights * inverse).astype(BF16)
            mixed.append(dot(v_t[HD * a : HD * a + HD, :], soft))
        mixed = jnp.concatenate(mixed, axis=0)
        mt[i * 128 : i * 128 + 128, :] = mixed.astype(BF16)
        m[i] = mixed.T.astype(BF16)

    for i in range(6):
        pair(i)


def attend(x, lens, buck, place, part, after, span):
    layout, pieces = part
    return call(
        functools.partial(attend_kernel, layout),
        "attend",
        (x, lens, buck, place, *pieces),
        "isss" + "h" * layout.count,
        [
            sds((18, T, 128), BF16),
            sds((6, T, 128), BF16),
            sds((D, T), BF16),
            sds((D, T), BF16),
            sds((12, 8, T), F32),
            sds((16, D), F32),
        ],
        "o" * 6,
        [
            pltpu.VMEM((3, 4, 4, ROWS, D), BF16),
            pltpu.VMEM((T, T), F32),
            pltpu.VMEM((32, 32, HALF), BF16),
            pltpu.SemaphoreType.DMA((4, 10)),
        ],
        after,
        span=span,
    )


def unit_norm(resid):
    center = jnp.mean(resid, axis=-1, keepdims=True)
    shifted = resid - center
    spread = jnp.mean(shifted * shifted, axis=-1, keepdims=True)
    inverse = lax.rsqrt(spread + EPSILON)
    return shifted * inverse, inverse


def weight_copies(layout_a, layout_b, pieces_a, pieces_b, place, wo, wu, wd, sems):
    o_copies = panel_copies(layout_a, pieces_a, place, wo, sems.at[0], O_AT, ROWS)
    u_copies = [
        panel_copies(layout_b, pieces_b, place, wu.at[j], sems.at[1 + j], j * ROWS, ROWS)
        for j in range(4)
    ]
    return o_copies, u_copies, panel_copies(layout_b, pieces_b, place, wd, sems.at[5], D_AT, DROWS)


class Sender:
    def __init__(self, sems):
        self.sems, self.copies = sems, []

    def __call__(self, source, target):
        self.copies.append(pltpu.make_async_copy(source, target, self.sems.at[len(self.copies)]))
        self.copies[-1].start()

    def wait(self):
        wait(self.copies)


def feed_rows(x, m, vec, copies, weights, saved, work, first_done, panel_done, result):
    o_copies, u_copies, d_copies = copies
    wo, wu, wd = weights
    n1, r1, n2, r2, gp = saved
    scr, y1, y1l, g = work
    wait(o_copies)
    m, x, vec = m(), x(), vec()
    weight = wo[...].reshape(D, D)
    for half in range(2):
        rows = slice(half * 256, half * 256 + 256)
        left = jnp.concatenate([m[s, rows, :] for s in range(6)], axis=1)
        scr[rows, :] = dot(left, weight)

    def first(rows):
        resid = x[rows, :].astype(F32) + (scr[rows, :] + vec[4:5, :])
        unit, inverse = unit_norm(resid)
        n1[rows, :] = unit
        r1[rows, :] = jnp.broadcast_to(inverse, (inverse.shape[0], 128))
        normed = unit * vec[0:1, :] + vec[5:6, :]
        y1[rows, :] = normed
        y1l[rows, :] = normed.astype(BF16)

    row_loop(NORM_ROWS, first)
    first_done()
    for j in range(4):
        wait(u_copies[j])

        def up(rows, j=j):
            left = y1l[rows, :]
            for k in range(3):
                cols = slice(256 * k, 256 * k + 256)
                right = wu[j, :, :, :, cols].reshape(D, 256)
                hidden = dot(left, right) + vec[8 + j : 9 + j, cols]
                cdf = 0.5 * (1.0 + lax.erf(hidden * (0.5**0.5)))
                g[j, rows, cols] = (hidden * cdf).astype(BF16)
                density = jnp.exp(hidden * hidden * -0.5) * 0.3989422804014327
                gp[j, rows, cols] = (cdf + hidden * density).astype(BF16)

        row_loop(256, up)
        panel_done(j)
    wait(d_copies)
    for half in range(2):
        rows = slice(half * 256, half * 256 + 256)
        total = dot(g[0, rows, :], wd[0].reshape(D, D))
        for j in range(1, 4):
            total = total + dot(g[j, rows, :], wd[j].reshape(D, D))
        scr[rows, :] = total

    def second(rows):
        resid = y1[rows, :] + (scr[rows, :] + vec[6:7, :])
        unit, inverse = unit_norm(resid)
        n2[rows, :] = unit
        r2[rows, :] = jnp.broadcast_to(inverse, (inverse.shape[0], 128))
        result(rows, unit * vec[1:2, :] + vec[7:8, :])

    row_loop(NORM_ROWS, second)


def feed_back_rows(output_grad, vec, small, copies, weights, saved, work, outs, send, c):
    o_copies, u_copies, d_copies = copies
    wo, wu, wd = weights
    n1, r1, n2, r2, gp = saved
    scr, dul, dr1l = work
    dr2l, dr1, dml, dul_keep, dul_give, dr1_keep, resid_give = outs
    small[...] = jnp.zeros_like(small)
    vec, n2, r2 = vec(), n2(), r2()

    def second(rows):
        grad = output_grad(rows)
        unit = n2[rows, :]
        resid = norm_back(grad, unit, r2[rows, 0:1], vec[1:2, :])
        small[1:2, :] += column_sum(grad * unit)
        small[7:8, :] += column_sum(grad)
        small[6:7, :] += column_sum(resid)
        scr[rows, :] = resid
        dr2l.held[rows, :] = resid.astype(BF16)

    row_loop(NORM_ROWS, second)
    dr2l.send()
    for half in range(2):
        send(dr2l.held.at[:, half * HALF : half * HALF + HALF], resid_give.at[half])
    wait(d_copies)
    gp = gp()
    for j in range(4):

        def up(rows, j=j):
            left = dr2l.held[rows, :]
            weight = wd[j].reshape(D, D)
            for k in range(3):
                cols = slice(256 * k, 256 * k + 256)
                grad = dot_rt(left, weight[cols, :])
                hidden = (grad * gp[j, rows, cols].astype(F32)).astype(BF16)
                dul[j, rows, cols] = hidden
                small[8 + j : 9 + j, cols] += column_sum(hidden.astype(F32))

        row_loop(T, up)
        send(dul.at[j, :, half_cols(1 - c)], dul_give.at[j])
        send(dul.at[j, :, half_cols(c)], dul_keep.at[j])
        wait(u_copies[j])
        for half in range(2):
            rows = slice(half * 256, half * 256 + 256)
            scr[rows, :] += dot_rt(dul[j, rows, :], wu[j].reshape(D, D))
    n1, r1 = n1(), r1()

    def first(rows):
        grad = scr[rows, :]
        unit = n1[rows, :]
        resid = norm_back(grad, unit, r1[rows, 0:1], vec[0:1, :])
        small[0:1, :] += column_sum(grad * unit)
        small[5:6, :] += column_sum(grad)
        small[4:5, :] += column_sum(resid)
        dr1.held[rows, :] = resid
        dr1l[rows, :] = resid.astype(BF16)

    row_loop(NORM_ROWS, first)
    send(dr1l.at[:, half_cols(1 - c)], resid_give.at[2])
    send(dr1l.at[:, half_cols(c)], dr1_keep)
    dr1.send()
    wait(o_copies)
    weight = wo[...].reshape(D, D)
    for half in range(2):
        rows = slice(half * 256, half * 256 + 256)
        out = dot_rt(dr1l[rows, :], weight).astype(BF16)
        for s in range(6):
            dml.held[s, rows, :] = out[:, 128 * s : 128 * s + 128]


def send_transposed(send, y1l, g, y1t, gt, outs, c):
    y1t_out, gt_out, give_out = outs

    def first_done():
        y1t[...] = y1l[...].T.reshape(8, 96, T)
        send(y1t, y1t_out)
        send(y1t, give_out.at[0:8])

    def panel_done(j):
        gt[j] = g[j].T.reshape(4, 2, 96, T)
        send(gt.at[j, :, c], gt_out.at[j])
        send(gt.at[j, :, 1 - c], give_out.at[8 + 4 * j : 12 + 4 * j])

    return first_done, panel_done


TRANSPOSED = [sds((8, 96, T), BF16), sds((4, 4, 96, T), BF16), sds((24, 96, T), BF16)]
WEIGHTS = [
    pltpu.VMEM((4, 4, ROWS, D), BF16),
    pltpu.VMEM((4, 4, 4, ROWS, D), BF16),
    pltpu.VMEM((4, 4, DROWS, D), BF16),
]


def feed_kernel(layout_a, layout_b, *refs):
    x, m, vec, place, cor, buck = refs[:6]
    pieces_a, refs = refs[6 : 6 + layout_a.count], refs[6 + layout_a.count :]
    pieces_b, refs = refs[: layout_b.count], refs[layout_b.count :]
    flow, transposed, refs = refs[:8], refs[8:11], refs[11:]
    out, n1, r1, n2, r2, gp, xd, xdl = (ref.held for ref in flow)
    wo, wu, wd, scr, y1, y1l, g, y1t, gt, sems, out_sems = refs
    c = place[0]
    send = Sender(out_sems)
    copies = weight_copies(layout_a, layout_b, pieces_a, pieces_b, place, wo, wu, wd, sems)
    start(copies[0])
    for group in copies[1]:
        start(group)
    start(copies[2])
    first_sent, panel_sent = send_transposed(send, y1l, g, y1t, gt, transposed, c)

    def first_done():
        first_sent()
        flow[1].send()
        flow[2].send()

    def panel_done(j):
        panel_sent(j)
        flow[5].send(j)

    def result(rows, value):
        out[rows, :] = value.astype(BF16)
        mixed = jnp.where(
            first_tokens(buck, rows.start, NORM_ROWS), value, cor()[rows, :].astype(F32)
        )
        xd[rows, :] = mixed
        xdl[rows, :] = mixed.astype(BF16)

    cor()
    feed_rows(
        x, m, vec, copies, (wo, wu, wd), (n1, r1, n2, r2, gp), (scr, y1, y1l, g), first_done, panel_done, result
    )
    send.wait()


def feed(x, m, vec, place, part_a, part_b, after, cor, buck):
    (layout_a, pieces_a), (layout_b, pieces_b) = part_a, part_b
    outs = [
        sds((T, D), BF16),
        sds((T, D), F32),
        sds((T, 128), F32),
        sds((T, D), F32),
        sds((T, 128), F32),
        sds((4, T, D), BF16),
        sds((T, D), F32),
        sds((T, D), BF16),
    ]
    return call(
        functools.partial(feed_kernel, layout_a, layout_b),
        "feed",
        (x, m, vec, place, cor, buck, *pieces_a, *pieces_b),
        "iiisis" + "h" * (layout_a.count + layout_b.count),
        [*outs, *TRANSPOSED],
        "o" * len(outs) + "hhh",
        [
            *WEIGHTS,
            pltpu.VMEM((T, D), F32),
            pltpu.VMEM((T, D), F32),
            pltpu.VMEM((T, D), BF16),
            pltpu.VMEM((4, T, D), BF16),
            pltpu.VMEM((8, 96, T), BF16),
            pltpu.VMEM((4, 4, 2, 96, T), BF16),
            pltpu.SemaphoreType.DMA((6, 10)),
            pltpu.SemaphoreType.DMA((10,)),
        ],
        after,
        span=0,
    )


def norm_back(grad, unit, inverse, gain):
    scaled = grad * gain
    mean = jnp.mean(scaled, axis=-1, keepdims=True)
    along = jnp.mean(scaled * unit, axis=-1, keepdims=True)
    return inverse * (scaled - mean - unit * along)


def column_sum(value):
    return jnp.sum(value, axis=0, keepdims=True)


GROUPS = {"d": (192, "iiih"), "o": (48, "iiii"), "do": (240, "iiihlll"), "u": (192, "lllh"), "q": (176, "iiiiii")}


def down_grads(more, block, at, held, sems, gt, dr2l, resid_other, given):
    copies = [
        pltpu.make_async_copy(given.at[8 + 4 * j : 12 + 4 * j], held.at[4 * j : 4 * j + 4], sems.at[j])
        for j in range(4)
    ]
    start(copies)
    gt, dr2l, resid_other = gt(), dr2l(), resid_other()
    for ref in more:
        ref.start()
    dr2l_other = jnp.concatenate([resid_other[0], resid_other[1]], axis=1)
    for j in range(4):
        mine = dot(gt[j].reshape(4 * 96, T), dr2l[...])
        copies[j].wait()
        other = dot(held[4 * j : 4 * j + 4].reshape(4 * 96, T), dr2l_other)
        value = (mine + other).astype(BF16)
        for half in range(2):
            rows = slice(at + 96 * half, at + 96 * half + 96)
            block[j, :, rows] = value[:, half * HALF : half * HALF + HALF].reshape(4, 96, HALF)


def out_grads(more, block, at, held, sems, mt, mt_other, dr1l, resid_other):
    mt, mt_other, dr1l, resid_other = mt(), mt_other(), dr1l(), resid_other()
    panel_grad(block, at, dot(mt[...], dr1l[...]), dot(mt_other[...], resid_other[2]))


def down_out_grads(more, block, at, held, sems, gt, dr2l, resid_other, given, mt, mt_other, dr1l):
    down_grads((mt, mt_other, dr1l, *more), block, at, held, sems, gt, dr2l, resid_other, given)
    out_grads((), block, at + 192, held, sems, mt, mt_other, dr1l, resid_other)


def panel_grad(block, at, mine, other):
    block[:, :, at : at + ROWS] = (mine + other).astype(BF16).reshape(4, 4, ROWS, HALF)


def up_grads(more, block, at, held, sems, y1t, dul, dul_other, given):
    copy = pltpu.make_async_copy(given.at[0:8], held.at[16:24], sems.at[4])
    copy.start()
    y1t, dul, dul_other = y1t(), dul(), dul_other()
    left = y1t[...].reshape(D, T)
    copy.wait()
    left_other = held[16:24].reshape(D, T)
    for j in range(4):
        panel_grad(block, at + j * ROWS, dot(left, dul[j]), dot(left_other, dul_other[j]))


def qkv_grads(more, block, at, held, sems, xt, xt_other, part, part_low, part_high, small):
    for ref in more:
        ref.start()
    xt, xt_other, part = xt(), xt_other(), part()
    part_other = [p[s] for p in (part_low(), part_high()) for s in range(5)]
    for j in range(3):
        mine, other = (
            jnp.concatenate([p[s] for s in range(3 * j, 3 * j + 3)], axis=1)
            for p in (part, part_other)
        )
        panel_grad(block, at + j * ROWS, dot(xt[...], mine), dot(xt_other[...], other))
    other = [part_other[9][16 * k : 16 * k + 16, :].astype(F32) for k in range(6)]
    small = small()[...] + jnp.concatenate(other, axis=1)
    small = jnp.concatenate([small[:, :HALF], small[:, HALF:]], axis=0)
    block[:, :, at + 144 : at + 176] = jnp.broadcast_to(small.astype(BF16), (4, 4, 32, HALF))


FILLS = {"d": down_grads, "o": out_grads, "do": down_out_grads, "u": up_grads, "q": qkv_grads}


def send_spread(block, part, place, outs):
    x, y = place[1], place[2]
    a_send, a_keep, b_send, b_keep = outs
    for side, a, b in ((1, a_send, b_send), (0, a_keep, b_keep)):
        for n in range(2):
            yield block.at[0:2, 2 * n + lax.bitwise_xor(x, side), part], a.at[n, :, part]
            yield block.at[2:4, 2 * lax.bitwise_xor(y, side) + n, part], b.at[n, :, part]


def send_mixed(cut, block, part, place, outs):
    x, y = place[1], place[2]
    a_send, a_keep, b_send, b_keep = outs
    low = slice(part.start, min(part.stop, cut))
    high = slice(max(part.start, cut), part.stop)
    for side, a, b in ((1, a_send, b_send), (0, a_keep, b_keep)):
        for n in range(2):
            if low.start < low.stop:
                yield block.at[:, 2 * n + lax.bitwise_xor(x, side), low], a.at[:, n, low]
            if high.start < high.stop:
                to = slice(high.start - cut, high.stop - cut)
                yield block.at[:, 2 * lax.bitwise_xor(y, side) + n, high], b.at[:, n, to]


def keep_kernel(groups, send, *refs):
    count = sum(len(GROUPS[g][1]) for g in groups)
    inputs, refs = refs[:count], refs[count:]
    place, outs, (block, held, sems, out_sems) = refs[0], refs[1:5], refs[5:]
    copies, at, first = [], 0, 0
    for g in groups:
        rows, kinds = GROUPS[g]
        more = [ref for ref in inputs[first + len(kinds) :] if isinstance(ref, In)]
        FILLS[g](more, block, at, held, sems, *inputs[first : first + len(kinds)])
        new = [
            pltpu.make_async_copy(src, dst, out_sems.at[len(copies) + n])
            for n, (src, dst) in enumerate(send(block, slice(at, at + rows), place, outs))
        ]
        start(new)
        copies += new
        at, first = at + rows, first + len(kinds)
    wait(copies)


def keep(groups, inputs, place, after, cut=None):
    rows = sum(GROUPS[g][0] for g in groups)
    if cut is None:
        send, outs = send_spread, [sds((2, 2, rows, HALF), BF16)] * 4
    else:
        send = functools.partial(send_mixed, cut)
        outs = [sds((4, 2, cut, HALF), BF16)] * 2 + [sds((4, 2, rows - cut, HALF), BF16)] * 2
    return call(
        functools.partial(keep_kernel, groups, send),
        "keep_grads",
        (*inputs, place),
        "".join(GROUPS[g][1] for g in groups) + "s",
        outs,
        "hhhh",
        [
            pltpu.VMEM((4, 4, rows, HALF), BF16),
            pltpu.VMEM((24, 96, T), BF16),
            pltpu.SemaphoreType.DMA((5,)),
            pltpu.SemaphoreType.DMA((16 * len(groups),)),
        ],
        after,
    )


def add_mid_kernel(sizes, *refs):
    pairs, line, blocks, sems = refs[: 2 * len(sizes)], refs[2 * len(sizes)], refs[2 * len(sizes) + 1 : -1], refs[-1]
    copies = [
        pltpu.make_async_copy(ref, blocks[n // 2].at[n % 2], sems.at[n]) for n, ref in enumerate(pairs)
    ]
    start(copies)
    at = 0
    for g, size in enumerate(sizes):
        wait(copies[2 * g : 2 * g + 2])
        total = (blocks[g][0].astype(F32) + blocks[g][1].astype(F32)).astype(BF16)
        line.held[:, at : at + 2 * size] = total.reshape(4, 2 * size, HALF)
        at += 2 * size


def add_mid(pairs, after):
    sizes = [keep.shape[2] for keep, _ in pairs]
    (line,) = call(
        functools.partial(add_mid_kernel, sizes),
        "add_mid",
        tuple(array for pair in pairs for array in pair),
        "h" * (2 * len(pairs)),
        [sds((4, 2 * sum(sizes), HALF), BF16)],
        "o",
        [
            *(pltpu.VMEM((2, 4, 2, size, HALF), BF16) for size in sizes),
            pltpu.SemaphoreType.DMA((2 * len(sizes),)),
        ],
        after,
    )
    return line


def part_slices(cuts, place):
    x, y = place[1], place[2]
    slices, base = [], 0
    for g, (cut, rows) in enumerate(cuts):
        for size, mine in ((cut, y), (rows - cut, x)):
            own, other = (
                pl.ds(pl.multiple_of(base + side * size, 16), size) for side in (mine, 1 - mine)
            )
            slices.append((g, size, own, other))
            base += 2 * size
    return slices


def part_kernel(cuts, total, place, *refs):
    n = 2 * len(cuts)
    outs, held, sems = refs[:n], refs[n : 2 * n], refs[-1]
    into, out = [], []
    for k, (_, _, _, other) in enumerate(part_slices(cuts, place)):
        into.append(pltpu.make_async_copy(total.at[other], held[k], sems.at[2 * k]))
        out.append(pltpu.make_async_copy(held[k], outs[k], sems.at[2 * k + 1]))
    start(into)
    for k, copy in enumerate(into):
        copy.wait()
        out[k].start()
    wait(out)


def part_rows(total, cuts, place, after):
    shapes = [sds((size, HALF), BF16) for cut, rows in cuts for size in (cut, rows - cut)]
    return call(
        functools.partial(part_kernel, cuts),
        "part",
        (total, place),
        "hs",
        shapes,
        "h" * len(shapes),
        [
            *(pltpu.VMEM(shape.shape, BF16) for shape in shapes),
            pltpu.SemaphoreType.DMA((2 * len(shapes),)),
        ],
        after,
    )


def close_kernel(cuts, total, *refs):
    n = len(cuts)
    got, place, flow = refs[: 2 * n], refs[2 * n], refs[2 * n + 1]
    held, sems = refs[2 * n + 2 : -1], refs[-1]
    slices = part_slices(cuts, place)
    copies = [
        pltpu.make_async_copy(total.at[own], held[k], sems.at[k])
        for k, (_, _, own, _) in enumerate(slices)
    ]
    start(copies)
    at = 0
    for k, (_, size, _, _) in enumerate(slices):
        copies[k].wait()
        value = held[k][...].astype(F32) + got[k]()[...].astype(F32)
        flow.held[at : at + size] = value.astype(BF16)
        at += size


def close(total, got, cuts, place, after):
    rows = sum(rows for _, rows in cuts)
    sizes = [size for cut, rows in cuts for size in (cut, rows - cut)]
    (sums,) = call(
        functools.partial(close_kernel, cuts),
        "close",
        (total, *got, place),
        "h" + "i" * len(got) + "s",
        [sds((rows, HALF), BF16)],
        "o",
        [
            *(pltpu.VMEM((size, HALF), BF16) for size in sizes),
            pltpu.SemaphoreType.DMA((len(sizes),)),
        ],
        after,
    )
    return sums


def spread_out_kernel(place, *refs):
    parts, outs = refs[:4], refs[4:]
    first = place[0] == 0
    qkv, out, up, down, gains, biases, up_b = (ref.held for ref in outs)
    device = place[3]

    def columns(first, count):
        row = lax.broadcasted_iota(jnp.int32, (D, count), 0)
        return (row == lax.broadcasted_iota(jnp.int32, (D, count), 1) + first).astype(BF16)

    def panel(l, at):
        mine, got = (
            jnp.where(first, value[:24], value[24:])
            for value in (ref()[at : at + ROWS].astype(F32) for ref in parts[2 * l : 2 * l + 2])
        )
        return jnp.concatenate([jnp.where(first, mine, got), jnp.where(first, got, mine)], axis=1)

    for l, (o_at, u_at, q_at, small_at) in ((1, (560, 368, 192, 336)), (0, (192, 240, 432, 576))):
        mine = parts[2 * l]()
        down[l] = jnp.concatenate([mine[0:96], mine[96:192]], axis=1).astype(F32)
        out[l] = panel(l, o_at)
        for j in range(4):
            up[l, :, j * D : j * D + D] = panel(l, u_at + j * ROWS)
        for j in range(3):
            qkv[l, :, j * D : j * D + D] = panel(l, q_at + j * ROWS)
        small = jnp.concatenate(
            [mine[small_at : small_at + 16], mine[small_at + 16 : small_at + 32]], axis=1
        )
        heads = dot(small, columns(24 * device, 24))
        gains[l] = heads[0:2]
        for k in range(6):
            biases[k, l : l + 1, :] = heads[2 + k : 3 + k]
        tail = dot(small, columns(96 * lax.rem(device, 8), 96))
        row = lax.broadcasted_iota(jnp.int32, (16, 96), 0)
        up_b[l : l + 1] = column_sum(jnp.where(row == 8 + lax.div(device, 8), tail, 0.0))
        for ref in outs[:4]:
            ref.send(l)


def spread_out(place, enc, enc_other, dec, dec_other, after):
    return call(
        spread_out_kernel,
        "spread_out",
        (place, enc, enc_other, dec, dec_other),
        "siiii",
        [
            sds((2, 24, 3 * D), F32),
            sds((2, 24, D), F32),
            sds((2, 24, 4 * D), F32),
            sds((2, 96, D), F32),
            sds((2, 2, 24), F32),
            sds((6, 2, 24), F32),
            sds((2, 96), F32),
        ],
        "ooooooo",
        [],
        after,
    )


def add_next_kernel(a_keep, a_got, b_keep, b_got, place, a_next, b_next, blocks, sems):
    x, y = place[1], place[2]
    refs = (a_keep.at[1 - y], a_got.at[1 - y], b_keep.at[1 - x], b_got.at[1 - x])
    copies = [pltpu.make_async_copy(ref, blocks.at[n], sems.at[n]) for n, ref in enumerate(refs)]
    start(copies)
    for n, out in enumerate((a_next, b_next)):
        wait(copies[2 * n : 2 * n + 2])
        out.held[...] = (blocks[2 * n].astype(F32) + blocks[2 * n + 1].astype(F32)).astype(BF16)
        out.send()


def add_next(a_keep, a_got, b_keep, b_got, place, after):
    shape = a_keep.shape[2:]
    return call(
        add_next_kernel,
        "add_next",
        (a_keep, a_got, b_keep, b_got, place),
        "hhhhs",
        [sds((2, *shape), BF16)] * 2,
        "oo",
        [pltpu.VMEM((4, 2, *shape), BF16), pltpu.SemaphoreType.DMA((4,))],
        after,
    )


def add_last_kernel(sizes, *refs):
    place, line, sems = refs[6 * len(sizes)], refs[6 * len(sizes) + 1], refs[-1]
    blocks = refs[6 * len(sizes) + 2 : -1]
    x, y = place[1], place[2]
    copies = []
    for g in range(len(sizes)):
        a_keep, a_got, a_last, b_keep, b_got, b_last = refs[6 * g : 6 * g + 6]
        for n, ref in enumerate((a_keep.at[y], a_got.at[y], a_last, b_keep.at[x], b_got.at[x], b_last)):
            copies.append(pltpu.make_async_copy(ref, blocks[g].at[n], sems.at[6 * g + n]))
    start(copies)
    at = 0
    for g, rows in enumerate(sizes):
        for n in range(2):
            wait(copies[6 * g + 3 * n : 6 * g + 3 * n + 3])
            block = blocks[g]
            total = block[3 * n].astype(F32) + block[3 * n + 1].astype(F32)
            total = total + block[3 * n + 2].astype(F32)
            line.held[2 * n : 2 * n + 2, at : at + rows] = total.astype(BF16)
        at += rows


def add_last(groups, place, after):
    sizes = [group[0].shape[2] for group in groups]
    (line,) = call(
        functools.partial(add_last_kernel, sizes),
        "add_last",
        (*(array for group in groups for array in group), place),
        "h" * (6 * len(groups)) + "s",
        [sds((4, sum(sizes), HALF), BF16)],
        "o",
        [
            *(pltpu.VMEM((6, 2, rows, HALF), BF16) for rows in sizes),
            pltpu.SemaphoreType.DMA((6 * len(groups),)),
        ],
        after,
    )
    return line


BACK_OUTS = [
    sds((T, D), BF16),
    sds((T, D), F32),
    sds((6, T, 128), BF16),
    sds((16, D), F32),
    sds((4, T, HALF), BF16),
    sds((4, T, HALF), BF16),
    sds((T, HALF), BF16),
    sds((3, T, HALF), BF16),
]


def feed_back_kernel(layout_a, layout_b, *refs):
    cot, n2, r2, vec, gp, n1, r1, place, dxd, buck = refs[:10]
    refs = refs[10:]
    pieces_a, refs = refs[: layout_a.count], refs[layout_a.count :]
    pieces_b, refs = refs[: layout_b.count], refs[layout_b.count :]
    (dr2l, dr1, dml, small), outs, refs = refs[:4], refs[4:8], refs[8:]
    wo, wu, wd, scr, dul, dr1l, sems, out_sems = refs
    send = Sender(out_sems)
    copies = weight_copies(layout_a, layout_b, pieces_a, pieces_b, place, wo, wu, wd, sems)
    start(copies[2])
    gp.start()
    for group in copies[1]:
        start(group)
    n1.start()
    r1.start()
    start(copies[0])
    cot, dxd = cot(), dxd()

    def output_grad(rows):
        first = first_tokens(buck, rows.start, NORM_ROWS)
        return cot[rows, :].astype(F32) + jnp.where(first, dxd[rows, :], 0.0)

    feed_back_rows(
        output_grad, vec, small.held, copies, (wo, wu, wd), (n1, r1, n2, r2, gp), (scr, dul, dr1l),
        (dr2l, dr1, dml, *outs), send, place[0],
    )
    send.wait()


def feed_back(cot, n2, r2, vec, gp, n1, r1, place, part_a, part_b, after, dxd, buck):
    (layout_a, pieces_a), (layout_b, pieces_b) = part_a, part_b
    return call(
        functools.partial(feed_back_kernel, layout_a, layout_b),
        "feed_back",
        (cot, n2, r2, vec, gp, n1, r1, place, dxd, buck, *pieces_a, *pieces_b),
        "iiiillls" + "is" + "h" * (layout_a.count + layout_b.count),
        BACK_OUTS,
        "oooohhhh",
        [
            *WEIGHTS,
            pltpu.VMEM((T, D), F32),
            pltpu.VMEM((4, T, D), BF16),
            pltpu.VMEM((T, D), BF16),
            pltpu.SemaphoreType.DMA((6, 10)),
            pltpu.SemaphoreType.DMA((12,)),
        ],
        after,
        span=12,
    )


def feed_both_kernel(layout_a, layout_b, *refs):
    x, m, vec, place, cot = refs[:5]
    refs = refs[5:]
    pieces_a, refs = refs[: layout_a.count], refs[layout_a.count :]
    pieces_b, refs = refs[: layout_b.count], refs[layout_b.count :]
    out, transposed, refs = refs[0], refs[1:4], refs[4:]
    (dr2l, dr1, dml, small), outs, refs = refs[:4], refs[4:8], refs[8:]
    wo, wu, wd, scr, y1, y1l, g, y1t, gt, n1, r1, n2, r2, gp, dul, sems, out_sems = refs
    c = place[0]
    send = Sender(out_sems)
    copies = weight_copies(layout_a, layout_b, pieces_a, pieces_b, place, wo, wu, wd, sems)
    start(copies[0])
    for group in copies[1]:
        start(group)
    start(copies[2])
    cot.start()
    first_done, panel_done = send_transposed(send, y1l, g, y1t, gt, transposed, c)

    def result(rows, value):
        out.held[rows, :] = value.astype(BF16)

    feed_rows(
        x, m, vec, copies, (wo, wu, wd), (n1, r1, n2, r2, gp), (scr, y1, y1l, g), first_done, panel_done, result
    )
    out.send()
    cot = cot()
    saved = [lambda ref=ref: ref for ref in (n1, r1, n2, r2, gp)]
    feed_back_rows(
        lambda rows: cot[rows, :].astype(F32), vec, small.held, ([], [[]] * 4, []), (wo, wu, wd), saved,
        (scr, dul, y1l), (dr2l, dr1, dml, *outs), send, c,
    )
    send.wait()


def feed_both(x, m, vec, place, cot, part_a, part_b, after):
    (layout_a, pieces_a), (layout_b, pieces_b) = part_a, part_b
    return call(
        functools.partial(feed_both_kernel, layout_a, layout_b),
        "feed_both",
        (x, m, vec, place, cot, *pieces_a, *pieces_b),
        "iiisl" + "h" * (layout_a.count + layout_b.count),
        [sds((T, D), BF16), *TRANSPOSED, *BACK_OUTS],
        "ohhhoooohhhh",
        [
            *WEIGHTS,
            pltpu.VMEM((T, D), F32),
            pltpu.VMEM((T, D), F32),
            pltpu.VMEM((T, D), BF16),
            pltpu.VMEM((4, T, D), BF16),
            pltpu.VMEM((8, 96, T), BF16),
            pltpu.VMEM((4, 4, 2, 96, T), BF16),
            pltpu.VMEM((T, D), F32),
            pltpu.VMEM((T, 128), F32),
            pltpu.VMEM((T, D), F32),
            pltpu.VMEM((T, 128), F32),
            pltpu.VMEM((4, T, D), BF16),
            pltpu.VMEM((4, T, D), BF16),
            pltpu.SemaphoreType.DMA((6, 10)),
            pltpu.SemaphoreType.DMA((24,)),
        ],
        after,
        span=20,
    )


def attend_back_kernel(*refs):
    p, dml, stat, small_in, lens, buck, place = refs[:7]
    keep_out, low_out, high_out, small_out, dpl, slab, bias, out_sems = refs[7:]
    small = small_out.held
    c = place[0]
    fill_bias(bias, lens, buck)
    p, dml, stat = p(), dml(), stat()
    scale = jnp.asarray(HD**-0.5, BF16)
    small[...] = small_in()[...]

    def pair(i):
        q = p[i] * scale
        k_t = p[6 + i].T
        both = dot_rt(jnp.concatenate(halves(p[6 + i]), axis=0), q)
        grad = dml[i]
        dboth = dot_rt(jnp.concatenate(halves(p[12 + i]), axis=0), grad)
        softs, dscores, dq = [], [], []
        for a in range(2):
            scores = both[T * a : T * a + T] + bias[...]
            peak = stat[2 * i + a, 0:1, :]
            inverse = stat[2 * i + a, 1:2, :]
            soft = jnp.exp(scores - peak) * inverse
            dsoft = dboth[T * a : T * a + T]
            total = jnp.sum(soft * dsoft, axis=0, keepdims=True)
            dscore = (soft * (dsoft - total)).astype(BF16)
            softs.append(soft.astype(BF16))
            dscores.append(dscore)
            dq.append(dot(k_t[HD * a : HD * a + HD, :], dscore))
        grads, queries = halves(grad), halves(q)
        dv = (dot(softs[0], grads[0]) + dot(softs[1], grads[1])).astype(BF16)
        dk = (dot(dscores[0], queries[0]) + dot(dscores[1], queries[1])).astype(BF16)
        dq = (jnp.concatenate(dq, axis=0).T * (HD**-0.5)).astype(BF16)
        dpl[i] = dq
        dpl[6 + i] = dk
        dpl[12 + i] = dv
        cols = pl.ds(pl.multiple_of(i * 128, 128), 128)
        small[2:3, cols] = column_sum(dq.astype(F32))
        small[3:4, cols] = column_sum(dv.astype(F32))

    def pairs(n, carry):
        for k in range(ATTEND_BACK_PAIRS):
            pair(ATTEND_BACK_PAIRS * n + k)
        return carry

    lax.fori_loop(0, 6 // ATTEND_BACK_PAIRS, pairs, 0)
    slab[...] = jnp.zeros_like(slab)
    for k in range(6):
        slab[16 * k : 16 * k + 16, :] = small[:, 128 * k : 128 * k + 128].astype(BF16)
    h = 3 * (1 - c)
    sent = [
        (dpl.at[pl.ds(h, 3)], low_out.at[0:3]),
        (dpl.at[pl.ds(6 + h, 2)], low_out.at[3:5]),
        (dpl.at[pl.ds(8 + h, 1)], high_out.at[0:1]),
        (dpl.at[pl.ds(12 + h, 3)], high_out.at[1:4]),
        (slab, high_out.at[4]),
    ]
    for j in range(3):
        sent.append((dpl.at[pl.ds(6 * j + 3 * c, 3)], keep_out.at[3 * j : 3 * j + 3]))
    sent = [pltpu.make_async_copy(src, dst, out_sems.at[n]) for n, (src, dst) in enumerate(sent)]
    start(sent)
    wait(sent)


def attend_back(p, dml, stat, small, lens, buck, place, after):
    return call(
        attend_back_kernel,
        "attend_back",
        (p, dml, stat, small, lens, buck, place),
        "iiiisss",
        [sds((9, T, 128), BF16), sds((5, T, 128), BF16), sds((5, T, 128), BF16), sds((16, D), F32)],
        "hhho",
        [
            pltpu.VMEM((18, T, 128), BF16),
            pltpu.VMEM((T, 128), BF16),
            pltpu.VMEM((T, T), F32),
            pltpu.SemaphoreType.DMA((10,)),
        ],
        after,
    )


def input_back_kernel(encoder, layout, *refs):
    dpl_keep, dpl_low, dpl_high, dr1, place = refs[:5]
    refs = refs[5:]
    if not encoder:
        buck, refs = refs[0], refs[1:]
    pieces, refs = refs[: layout.count], refs[layout.count :]
    if not encoder:
        dxd_out, refs = refs[0], refs[1:]
        dxd = dxd_out.held
    out_flow, dpl, wq, sems = refs
    out = out_flow.held
    c = place[0]
    copies = []
    for j in range(3):
        group = panel_copies(layout, pieces, place, wq.at[j], sems.at[j], j * ROWS, ROWS)
        other = 6 * j + 3 * (1 - c)
        pairs = [(dpl_keep.at[3 * j : 3 * j + 3], pl.ds(6 * j + 3 * c, 3))]
        if j == 0:
            pairs.append((dpl_low.at[0:3], pl.ds(other, 3)))
        elif j == 1:
            pairs += [(dpl_low.at[3:5], pl.ds(other, 2)), (dpl_high.at[0:1], pl.ds(other + 2, 1))]
        else:
            pairs.append((dpl_high.at[1:4], pl.ds(other, 3)))
        for n, (src, at) in enumerate(pairs):
            group.append(pltpu.make_async_copy(src, dpl.at[at], sems.at[j, 10 + n]))
        start(group)
        copies.append(group)
    dr1 = dr1()
    for group in copies:
        wait(group)
    for half in range(2):
        rows = slice(half * 256, half * 256 + 256)
        total = dr1[rows, :]
        for j in range(3):
            left = jnp.concatenate([dpl[6 * j + s, rows, :] for s in range(6)], axis=1)
            total = total + dot_rt(left, wq[j].reshape(D, D))
        if encoder:
            out[rows, :] = total.astype(BF16)
        else:
            dxd[rows, :] = total
            out[rows, :] = jnp.where(first_tokens(buck, half * 256, 256), 0.0, total).astype(BF16)
            dxd_out.send(rows)
        out_flow.send(rows)


def input_back(encoder, slabs, dr1, place, part_a, after, buck=None):
    layout, pieces = part_a
    args, kinds = (*slabs, dr1, place), "hhhis"
    outs = [sds((T, D), BF16)]
    if not encoder:
        args, kinds = (*args, buck), kinds + "s"
        outs = [sds((T, D), F32), *outs]
    return call(
        functools.partial(input_back_kernel, encoder, layout),
        "input_back",
        (*args, *pieces),
        kinds + "h" * layout.count,
        outs,
        "o" * len(outs),
        [
            pltpu.VMEM((18, T, 128), BF16),
            pltpu.VMEM((3, 4, 4, ROWS, D), BF16),
            pltpu.SemaphoreType.DMA((3, 13)),
        ],
        after,
        span=30 if encoder else 0,
    )


def gate_kernel(*refs):
    pass


def gate(values, after):
    outs = call(
        gate_kernel,
        "gate",
        tuple(values),
        "h" * len(values),
        [sds(v.shape, v.dtype) for v in values],
        "h" * len(values),
        [],
        after,
        {n: n for n in range(len(values))},
    )
    return list(outs)


def split_kernel(bx, by, ax, ay, held, sems):
    refs = ((bx.at[0:2], held.at[0], ax), (by.at[2:4], held.at[1], ay))
    into = [pltpu.make_async_copy(src, mid, sems.at[n]) for n, (src, mid, _) in enumerate(refs)]
    out = [pltpu.make_async_copy(mid, dst, sems.at[2 + n]) for n, (_, mid, dst) in enumerate(refs)]
    start(into)
    for n in range(2):
        into[n].wait()
        out[n].start()
    wait(out)


def split(bx, by, after):
    shape = (2, *bx.shape[1:])
    return call(
        split_kernel,
        "split",
        (bx, by),
        "hh",
        [sds(shape, BF16)] * 2,
        "hh",
        [pltpu.VMEM((2, *shape), BF16), pltpu.SemaphoreType.DMA((4,))],
        after,
    )


def cut_kernel(at, line, low, high, held, sems):
    into, out = [], []
    for n, (rows, dst) in enumerate(((slice(0, at), low), (slice(at, held.shape[1]), high))):
        into.append(pltpu.make_async_copy(line.at[:, rows], held.at[:, rows], sems.at[n]))
        out.append(pltpu.make_async_copy(held.at[:, rows], dst, sems.at[2 + n]))
    start(into)
    for n in range(2):
        into[n].wait()
        out[n].start()
    wait(out)


def cut(line, at, after):
    rows = line.shape[1]
    return call(
        functools.partial(cut_kernel, at),
        "cut",
        (line,),
        "h",
        [sds((4, at, HALF), BF16), sds((4, rows - at, HALF), BF16)],
        "hh",
        [pltpu.VMEM((4, rows, HALF), BF16), pltpu.SemaphoreType.DMA((4,))],
        after,
    )


AXES = ("z", "y", "x", "c", "e")


def swap(value, axis):
    return lax.ppermute(value, axis, [(0, 1), (1, 0)])


def pick(value, index, axis):
    return lax.dynamic_index_in_dim(value, index, axis, keepdims=False)


class SpreadGather:
    def __init__(self, rows):
        self.own = lax.all_gather(rows, "z", axis=0, tiled=False)

    def plane(self, after):
        (self.own,) = gate([self.own], after)
        self.bx, self.by = swap(self.own, "x"), swap(self.own, "y")
        self.own_c = swap(self.own, "c")
        return (self.own,)

    def forward(self, after):
        ax, ay = split(self.bx, self.by, (*after, self.own_c))
        self.dx, self.dy = swap(ax, "y"), swap(ay, "x")
        self.bx_c, self.by_c = swap(self.bx, "c"), swap(self.by, "c")
        return (ax,)

    def across(self):
        there = (self.own, self.bx, self.by, self.dx, self.dy)
        self.pieces = (*there, self.own_c, self.bx_c, self.by_c, swap(self.dx, "c"), swap(self.dy, "c"))


class MixedGather:
    def __init__(self, rows, at, along_x, along_y):
        self.at, self.size = at, rows.shape[0]
        self.rows = jnp.concatenate([rows[:at], along_x, rows[at:], along_y])

    def line(self, after):
        (rows,) = gate([self.rows], after)
        self.own = lax.all_gather(rows, "z", axis=0, tiled=False)
        return (rows,)

    def arrive(self, after):
        (self.own,) = gate([self.own], after)
        return (self.own,)

    def plane(self, after):
        self.low, self.high = cut(self.own, 2 * self.at, after)
        return (self.low,)

    def last(self, after=()):
        low, high = self.low, self.high
        if after:
            low, high = gate([low, high], after)
        self.low, self.high = swap(low, "y"), swap(high, "x")
        return (low,)

    def near(self, after):
        tok = self.arrive(after)
        self.own_c = swap(self.own, "c")
        return tok

    def across(self, after):
        self.low, self.high = gate([self.low, self.high], after)
        self.low_c, self.high_c = swap(self.low, "c"), swap(self.high, "c")
        self.pieces = (self.own, self.low, self.high, self.own_c, self.low_c, self.high_c)
        self.part = (Mixed(self.at, self.size), self.pieces)
        return (self.low,)


class Scatter:
    def __init__(self, groups, place, cut=None):
        self.groups, self.place, self.cut = groups, place, cut

    def keep(self, inputs, after):
        a_send, self.a_keep, b_send, self.b_keep = keep(
            self.groups, inputs, self.place, after, self.cut
        )
        self.a_got, self.b_got = swap(a_send, "x"), swap(b_send, "y")
        return (a_send,)

    def next(self, after):
        a_next, b_next = add_next(
            self.a_keep, self.a_got, self.b_keep, self.b_got, self.place, after
        )
        self.a_last, self.b_last = swap(a_next, "y"), swap(b_next, "x")
        return (a_next,)

    def sums(self):
        return (self.a_keep, self.a_got, self.a_last, self.b_keep, self.b_got, self.b_last)


def along_z(scatters, after):
    pairs = []
    for scatter in scatters:
        pairs += [(scatter.a_keep, scatter.a_got), (scatter.b_keep, scatter.b_got)]
    line = add_mid(pairs, after)
    return (line,), lax.psum_scatter(line, "z", scatter_dimension=0, tiled=False)


def finish(scatters, place, after):
    line = add_last([scatter.sums() for scatter in scatters], place, after)
    return (line,), lax.psum_scatter(line, "z", scatter_dimension=0, tiled=False)


def pack_weights(qkv, out, up, down, gains, biases, up_b, c, device):
    rows = out.shape[1]
    panels = jnp.concatenate([qkv, out, up], axis=2).reshape(2, rows, 8, 2, HALF)
    panels = jnp.transpose(panels, (0, 3, 2, 1, 4)).reshape(2, 2, 8 * rows, HALF)
    downs = jnp.transpose(down.reshape(2, 4 * rows, 2, HALF), (0, 2, 1, 3))
    both = jnp.concatenate([panels, downs], axis=2)
    mine = pick(both, c, 1)
    got = swap(pick(both, 1 - c, 1), "c")
    low = jnp.where(c == 0, mine, got)
    high = jnp.where(c == 0, got, mine)
    panels = jnp.stack(
        [low[:, : 8 * rows].reshape(2, 8, rows, HALF), high[:, : 8 * rows].reshape(2, 8, rows, HALF)],
        axis=2,
    ).reshape(2, 16 * rows, HALF)
    downs = jnp.concatenate([low[:, 8 * rows :], high[:, 8 * rows :]], axis=1)
    small = jnp.zeros((2, 16, D), BF16)
    small = lax.dynamic_update_slice(
        small, jnp.concatenate([gains, biases], axis=1), (0, 0, device * rows)
    )
    small = lax.dynamic_update_slice(
        small, up_b[:, None, :], (0, 8 + device // 8, device % 8 * (4 * rows))
    )
    small = jnp.concatenate([small[:, :, :HALF], small[:, :, HALF:]], axis=1)
    part_a = jnp.concatenate([panels[:, : 8 * rows], small], axis=1)
    part_b = jnp.concatenate([panels[:, 8 * rows :], downs], axis=1)
    return part_a, part_b


def body(
    encoder_input,
    corrupted,
    lengths,
    buckets,
    qkv_weight,
    out_weight,
    up_weight,
    down_weight,
    norm_gains,
    bias_rows,
    up_bias,
    encoder_cot,
    decoder_cot,
):
    extra = lax.axis_size("e")
    weights = [qkv_weight, out_weight, up_weight, down_weight, norm_gains, bias_rows, up_bias]
    if extra > 1:
        weights = [
            lax.all_gather(w, "e", axis=at, tiled=True)
            for w, at in zip(weights, (1, 1, 1, 1, 2, 2, 1))
        ]
    rows = weights[1].shape[1]
    x, y, c = lax.axis_index("x"), lax.axis_index("y"), lax.axis_index("c")
    device = ((lax.axis_index("z") * 2 + y) * 2 + x) * 2 + c
    place = jnp.stack([c, x, y, device]).astype(jnp.int32)
    part_a, part_b = pack_weights(*weights, c, device)
    at_a, at_b = 2 * ROWS, 4 * ROWS
    along_x = swap(jnp.concatenate([part_a[1, :at_a], part_b[1, :at_b]]), "x")
    along_y = swap(jnp.concatenate([part_a[1, at_a:], part_b[1, at_b:]]), "y")
    g0 = SpreadGather(jnp.concatenate([part_a[0], part_b[0]]))
    g1a = MixedGather(part_a[1], at_a, along_x[:at_a], along_y[: PART_A - at_a])
    g1b = MixedGather(part_b[1], at_b, along_x[at_a:], along_y[PART_A - at_a :])

    tok = g0.plane((along_x, along_y))
    tok = g1a.line(tok)
    tok = g1b.line(tok)
    tok = g0.forward(tok)
    g1a.plane(tok)
    g0.across()
    part_a0, part_b0 = (Spread(0), g0.pieces), (Spread(PART_A), g0.pieces)
    tok = g1a.last((g0.dx, g0.dy))
    tok = g1a.near(tok)
    p0, m0, xt0, mt0, stat0, vec0 = attend(encoder_input, lengths, buckets, place, part_a0, tok, 0)
    tok = g1b.near((stat0,))
    tok = g1b.plane((*tok, g1a.own_c))
    g1b.last()
    tok = g1a.across(tok)
    enc_out, *saved0, xd, xdl, y1t0, gt0, give0 = feed(
        encoder_input, m0, vec0, place, part_a0, part_b0, tok, corrupted, buckets
    )
    given0 = swap(give0, "c")
    xt0_other, mt0_other = swap(xt0, "c"), swap(mt0, "c")
    part_a1 = g1a.part
    p1, m1, xt1, mt1, stat1, vec1 = attend(
        xdl, lengths, buckets, place, part_a1, (enc_out,), 0
    )
    tok = g1b.across((stat1,))
    part_b1 = g1b.part
    dec_out, y1t1, gt1, give1, dr2l, dr1, dml, small, dul, dul_give, dr1l, resid = feed_both(
        xd, m1, vec1, place, decoder_cot, part_a1, part_b1, tok
    )

    given1 = swap(give1, "c")
    resid, dul_other = swap(resid, "c"), swap(dul_give, "c")
    cuts = ((96, 192), (208, 416))
    s1, q1 = Scatter(("d",), place, cuts[0][0]), Scatter(("q", "u", "o"), place, cuts[1][0])
    part, low, high, small = attend_back(
        p1, dml, stat1, small, lengths, buckets, place, (dr1, given0)
    )
    part_other = [swap(low, "c"), swap(high, "c")]
    xt1_other, mt1_other = swap(xt1, "c"), swap(mt1, "c")
    tok = s1.keep((gt1, dr2l, resid, given1), (small,))
    tok = q1.keep(
        (
            *(xt1, xt1_other, part, *part_other, small),
            *(y1t1, dul, dul_other, given1),
            *(mt1, mt1_other, dr1l, resid),
        ),
        tok,
    )
    dxd, cor_grad = input_back(False, (part, low, high), dr1, place, part_a1, tok, buckets)
    s1.a_got, s1.b_got = gate([s1.a_got, s1.b_got], (cor_grad,))
    tok = (s1.a_got,)

    n1, r1, n2, r2, gp = saved0
    dr2l, dr1, dml, small, dul, dul_give, dr1l, resid = feed_back(
        encoder_cot, n2, r2, vec0, gp, n1, r1, place, part_a0, part_b0, tok, dxd, buckets
    )
    resid, dul_other = swap(resid, "c"), swap(dul_give, "c")
    tok, dec_total = along_z([s1, q1], (dr1,))
    s0, q0 = Scatter(("do", "u"), place), Scatter(("q",), place)
    tok = s0.keep(
        (gt0, dr2l, resid, given0, mt0, mt0_other, dr1l, y1t0, dul, dul_other, given0), tok
    )
    part, low, high, small = attend_back(p0, dml, stat0, small, lengths, buckets, place, tok)
    part_other = [swap(low, "c"), swap(high, "c")]
    tok = q0.keep((xt0, xt0_other, part, *part_other, small), (small,))
    tok = s0.next(tok)
    (enc_grad,) = input_back(True, (part, low, high), dr1, place, part_a0, tok)
    tok = q0.next((enc_grad,))
    (dec_total,) = gate([dec_total], tok)
    tok, both0 = finish([s0, q0], place, (dec_total,))
    sent = part_rows(dec_total, cuts, place, tok)
    got = [swap(value, "yx"[n % 2]) for n, value in enumerate(sent)]
    dec_rows = close(dec_total, got, cuts, place, ())
    grads_out = list(
        spread_out(place, both0, swap(both0, "c"), dec_rows, swap(dec_rows, "c"), ())
    )
    grads_out[5] = jnp.transpose(grads_out[5], (1, 0, 2))
    if extra > 1:
        grads_out = [
            lax.psum_scatter(v, "e", scatter_dimension=at, tiled=True)
            for v, at in zip(grads_out, (1, 1, 1, 1, 2, 2, 1))
        ]
    return (enc_out, dec_out, enc_grad, cor_grad, *grads_out)


def solution(mesh):
    devices = mesh.devices.reshape(4, 2, 2, 2, -1)
    inner = Mesh(devices, AXES)
    token = P(AXES, None)
    line = P(AXES)
    wide = P(None, AXES, None)
    vector = P(None, None, AXES)
    return jax.shard_map(
        body,
        mesh=inner,
        in_specs=(
            token, token, line, line, wide, wide, wide, wide, vector, vector, P(None, AXES), token, token,
        ),
        out_specs=(
            token, token, token, token, wide, wide, wide, wide, vector, vector, P(None, AXES),
        ),
        check_vma=False,
    )
```
